32 devices in a mesh: ctx: 8 (over z, y), fsdp: 4 (over x, core).
Axes of the slice: x: 2, y: 2, z: 4, core: 2. Of those that a mesh axis runs over, the one named last changes fastest.
Arguments:
- tokens: bfloat16 [8, 1024, 1536], P('fsdp', 'ctx'), may hold values from -6 to 6
- cotangent: bfloat16 [8, 1024, 1536], P('fsdp', 'ctx'), may hold values from -6 to 6
- lengths: int32 [8], replicated, may hold values from 256 to 1024, as said below
- slot_adapter_index: int32 [8], replicated, may hold values from 0 to 7
- attention_norm_gain: float32 [1536], replicated, may hold values from 0.1 to 1.9
- feedforward_norm_gain: float32 [1536], replicated, may hold values from 0.1 to 1.9
- query_weight: bfloat16 [1536, 1536], P(None, 'fsdp'), may hold values from -0.15625 to 0.15625
- key_weight: bfloat16 [1536, 768], P(None, 'fsdp'), may hold values from -0.15625 to 0.15625
- value_weight: bfloat16 [1536, 768], P(None, 'fsdp'), may hold values from -0.15625 to 0.15625
- output_weight: bfloat16 [1536, 1536], P('fsdp'), may hold values from -1.25 to 1.25
- gate_weight: bfloat16 [1536, 4096], P(None, 'fsdp'), may hold values from -0.15625 to 0.15625
- up_weight: bfloat16 [1536, 4096], P(None, 'fsdp'), may hold values from -0.15625 to 0.15625
- down_weight: bfloat16 [4096, 1536], P('fsdp'), may hold values from -0.09375 to 0.09375
- adapter_input_first: bfloat16 [8, 5, 1536, 16], replicated, may hold values from -0.15625 to 0.15625
- adapter_output_first: bfloat16 [8, 1536, 16], replicated, may hold values from -1.25 to 1.25
- adapter_down_first: bfloat16 [8, 4096, 16], replicated, may hold values from -0.09375 to 0.09375
- adapter_query_second: bfloat16 [8, 16, 1536], replicated, may hold values from -1.5 to 1.5
- adapter_key_value_second: bfloat16 [8, 2, 16, 768], replicated, may hold values from -1.5 to 1.5
- adapter_output_second: bfloat16 [8, 16, 1536], replicated, may hold values from -1.5 to 1.5
- adapter_gate_up_second: bfloat16 [8, 2, 16, 4096], replicated, may hold values from -1.5 to 1.5
- adapter_down_second: bfloat16 [8, 16, 1536], replicated, may hold values from -1.5 to 1.5
Outputs:
- out_tokens: bfloat16 [8, 1024, 1536], P('fsdp', 'ctx')
- grad_tokens: float32 [8, 1024, 1536], P('fsdp', 'ctx')
- grad_in_a: float32 [8, 5, 1536, 16], replicated
- grad_o_a: float32 [8, 1536, 16], replicated
- grad_d_a: float32 [8, 4096, 16], replicated
- grad_q_b: float32 [8, 16, 1536], replicated
- grad_kv_b: float32 [8, 2, 16, 768], replicated
- grad_o_b: float32 [8, 16, 1536], replicated
- grad_gu_b: float32 [8, 2, 16, 4096], replicated
- grad_d_b: float32 [8, 16, 1536], replicated
The draws below stay inside these ranges and needn't reach their ends.
Inputs may be any that keep to these rules, and one draw needn't show every extreme that they name: `lengths`: in each aligned group of 2 slots one slot, drawn from the seed, has all 1024 positions live.
All inputs are finite; a program needn't handle non-finite values.
Results may differ from the reference program's by a relative error of at most 0.02.
Values may be sent and summed in bfloat16 or wider, within the bound.
A program may use at most 256 MiB of HBM per device.

```python
import jax
import jax.numpy as jnp
from jax import lax

MODEL_DIM = 1536
QUERY_HEADS = 16
KEY_VALUE_HEADS = 8
HEAD_DIM = 96
HIDDEN_UNITS = 4096
ADAPTER_RANK = 16
ADAPTER_CHOICES = 8
SHARD_SLOTS = 2
QUERY_FEATURES = 1536
KEY_FEATURES = 768
SLOT_POSITIONS = 1024
TOTAL_SLOTS = 8


def draw_lengths(key, part):
    key = jax.random.fold_in(key, 7)
    key_length, complete_keys = jax.random.split(key)
    sampled_values = jax.random.randint(key_length, (TOTAL_SLOTS,), SLOT_POSITIONS // 4, SLOT_POSITIONS + 1)
    complete_slot = jax.random.randint(complete_keys, (TOTAL_SLOTS // SHARD_SLOTS,), 0, SHARD_SLOTS)
    slot_labels = jnp.arange(TOTAL_SLOTS, dtype=jnp.int32)
    picked = jnp.repeat(complete_slot, SHARD_SLOTS)
    return jnp.where(slot_labels % SHARD_SLOTS == picked, SLOT_POSITIONS, sampled_values).astype(jnp.int32)


def with_ends(entries, rng, smallest, top_value):
    place = [jax.random.randint(jax.random.fold_in(rng, axis), (), 0, length) for axis, length in enumerate(entries.shape)]
    widest = entries.shape.index(max(entries.shape))
    neighbour = place[:widest] + [(place[widest] + 1) % entries.shape[widest]] + place[widest + 1:]
    return entries.at[tuple(place)].set(smallest).at[tuple(neighbour)].set(top_value)


def block_levels(rng, extent, pieces, smallest, top_value):
    factor_of, own = 1.0, jax.random.fold_in(rng, 6)
    for position, blocks in pieces:
        heights = jnp.exp(jax.random.uniform(jax.random.fold_in(own, position), (blocks,), jnp.float32, smallest / len(pieces), top_value / len(pieces)))
        factor_of = factor_of * jnp.repeat(heights, extent[position] // blocks).reshape([-1 if axis == position else 1 for axis in range(len(extent))])
    return factor_of


def bell_draw(stream_key, extent, scale, bound, pieces=(), held_as=jnp.bfloat16):
    values = scale * jax.random.normal(stream_key, extent, jnp.float32)
    if pieces:
        values = values * block_levels(stream_key, extent, pieces, -0.22, 0.18)
    return jnp.clip(values, -bound, bound).astype(held_as)


def setup_inputs(seed: int = 0) -> dict:
    seeds = jax.random.split(jax.random.key(seed), 22)
    return {
        "tokens": bell_draw(seeds[0], (TOTAL_SLOTS, SLOT_POSITIONS, MODEL_DIM), 1.0, 6.0, ((0, 4), (1, 8))),
        "cotangent": bell_draw(seeds[1], (TOTAL_SLOTS, SLOT_POSITIONS, MODEL_DIM), 1.0, 6.0, ((0, 4), (1, 8))),
        "lengths": draw_lengths(jax.random.fold_in(seeds[21], 71), 0),
        "slot_adapter_index": with_ends(jax.random.randint(seeds[3], (TOTAL_SLOTS,), 0, ADAPTER_CHOICES), jax.random.fold_in(seeds[3], 1), 0, ADAPTER_CHOICES - 1).astype(jnp.int32),
        "attention_norm_gain": jnp.clip(1.0 + 0.18 * jax.random.normal(seeds[4], (MODEL_DIM,), jnp.float32), 0.1, 1.9),
        "feedforward_norm_gain": jnp.clip(1.0 + 0.18 * jax.random.normal(seeds[5], (MODEL_DIM,), jnp.float32), 0.1, 1.9),
        "query_weight": bell_draw(seeds[6], (MODEL_DIM, QUERY_FEATURES), MODEL_DIM ** -0.5, 0.15625, ((1, 4),)),
        "key_weight": bell_draw(seeds[7], (MODEL_DIM, KEY_FEATURES), MODEL_DIM ** -0.5, 0.15625, ((1, 4),)),
        "value_weight": bell_draw(seeds[8], (MODEL_DIM, KEY_FEATURES), MODEL_DIM ** -0.5, 0.15625, ((1, 4),)),
        "output_weight": bell_draw(seeds[9], (QUERY_FEATURES, MODEL_DIM), (max(QUERY_FEATURES * 16 // SLOT_POSITIONS, 1)) ** -0.5, 1.25, ((0, 4),)),
        "gate_weight": bell_draw(seeds[10], (MODEL_DIM, HIDDEN_UNITS), MODEL_DIM ** -0.5, 0.15625, ((1, 4),)),
        "up_weight": bell_draw(seeds[11], (MODEL_DIM, HIDDEN_UNITS), MODEL_DIM ** -0.5, 0.15625, ((1, 4),)),
        "down_weight": bell_draw(seeds[12], (HIDDEN_UNITS, MODEL_DIM), HIDDEN_UNITS ** -0.5, 0.09375, ((0, 4),)),
        "adapter_input_first": bell_draw(seeds[13], (ADAPTER_CHOICES, 5, MODEL_DIM, ADAPTER_RANK), MODEL_DIM ** -0.5, 0.15625),
        "adapter_output_first": bell_draw(seeds[14], (ADAPTER_CHOICES, QUERY_FEATURES, ADAPTER_RANK), (max(QUERY_FEATURES * 16 // SLOT_POSITIONS, 1)) ** -0.5, 1.25),
        "adapter_down_first": bell_draw(seeds[15], (ADAPTER_CHOICES, HIDDEN_UNITS, ADAPTER_RANK), HIDDEN_UNITS ** -0.5, 0.09375),
        "adapter_query_second": bell_draw(seeds[16], (ADAPTER_CHOICES, ADAPTER_RANK, QUERY_FEATURES), ADAPTER_RANK ** -0.5, 1.5),
        "adapter_key_value_second": bell_draw(seeds[17], (ADAPTER_CHOICES, 2, ADAPTER_RANK, KEY_FEATURES), ADAPTER_RANK ** -0.5, 1.5),
        "adapter_output_second": bell_draw(seeds[18], (ADAPTER_CHOICES, ADAPTER_RANK, MODEL_DIM), ADAPTER_RANK ** -0.5, 1.5),
        "adapter_gate_up_second": bell_draw(seeds[19], (ADAPTER_CHOICES, 2, ADAPTER_RANK, HIDDEN_UNITS), ADAPTER_RANK ** -0.5, 1.5),
        "adapter_down_second": bell_draw(seeds[20], (ADAPTER_CHOICES, ADAPTER_RANK, MODEL_DIM), ADAPTER_RANK ** -0.5, 1.5),
    }


EPSILON = 1e-05
NEGATIVE = -1e+30
ADAPTER_SCALE = 0.5
ROPE_BASE = 100000.0
TOP_PRECISION = lax.Precision.HIGHEST

@jax.custom_vjp
def low_rank_rows(v):
    return lax.optimization_barrier(v.astype(jnp.bfloat16)).astype(jnp.float32)

@jax.custom_vjp
def low_back(v):
    return v

def low_keep(v):
    return (low_rank_rows(v), None)

def low_pass(kept, grad):
    return (grad,)

def back_keep(v):
    return (v, None)

def back_low(kept, grad):
    return (low_rank_rows(grad),)
low_rank_rows.defvjp(low_keep, low_pass)
low_back.defvjp(back_keep, back_low)

def rope_tables(positions, head_size):
    half_size = head_size // 2
    freqs = ROPE_BASE ** (-(jnp.arange(half_size, dtype=jnp.float32) * 2.0 / head_size))
    angles = positions.astype(jnp.float32)[:, None] * freqs[None, :]
    return (jnp.cos(angles)[:, None, :], jnp.sin(angles)[:, None, :])

def apply_rotation(values, cosine_table, sine_table):
    half_size = values.shape[-1] // 2
    first_half = values[..., :half_size]
    second_half = values[..., half_size:]
    return jnp.concatenate([first_half * cosine_table - second_half * sine_table, second_half * cosine_table + first_half * sine_table], axis=-1)

def rms_norm(values, gain):
    return values * lax.rsqrt(lax.optimization_barrier(jnp.mean(values * values, axis=-1, keepdims=True)) + EPSILON) * gain

def matrix_product(left, right):
    return jnp.dot(left, right, precision=TOP_PRECISION)

def adapted(input_rows, weight_matrix, down, upward_rows):
    inner_rows = low_rank_rows(low_back(matrix_product(input_rows, down)))
    return matrix_product(input_rows, weight_matrix) + ADAPTER_SCALE * matrix_product(inner_rows, upward_rows)

def attention(query_head_rows, key_head_rows, value_head_rows, length):
    block_rows = min(512, SLOT_POSITIONS)
    positions = jnp.arange(SLOT_POSITIONS, dtype=jnp.int32)
    key_live = positions < length
    scale = HEAD_DIM ** (-0.5)

    def one_block(block_index):
        rows = lax.dynamic_slice_in_dim(query_head_rows, block_index * block_rows, block_rows, 0)
        row_pos = block_index * block_rows + jnp.arange(block_rows, dtype=jnp.int32)
        scores = jnp.einsum('qhgd,khd->hgqk', rows, key_head_rows, precision=TOP_PRECISION) * scale
        scores = low_back(scores)
        allowed = (positions[None, :] <= row_pos[:, None]) & key_live[None, :]
        masked = jnp.where(allowed, scores, NEGATIVE)
        top_score = lax.optimization_barrier(jnp.max(masked, axis=-1, keepdims=True))
        weights = jnp.where(allowed, jnp.exp(masked - top_score), 0.0)
        probs = low_rank_rows(weights / lax.optimization_barrier(jnp.sum(weights, axis=-1, keepdims=True)))
        return jnp.einsum('hgqk,khd->qhgd', probs, value_head_rows, precision=TOP_PRECISION)
    block_list = lax.map(jax.checkpoint(one_block), jnp.arange(SLOT_POSITIONS // block_rows, dtype=jnp.int32))
    return block_list.reshape(SLOT_POSITIONS, KEY_VALUE_HEADS, QUERY_HEADS // KEY_VALUE_HEADS, HEAD_DIM)

def slot_layer(input_rows, rotation_tables, frozen, length, index):
    gain_attn, gain_mlp, weight_q, weight_k, weight_v, weight_o, weight_gate, weight_up, weight_down = frozen
    input_first, output_first, down_first, query_second, key_value_second, output_second, gate_up_second, down_second = rotation_tables
    positions = jnp.arange(SLOT_POSITIONS, dtype=jnp.int32)
    cosine_table, sine_table = rope_tables(positions, HEAD_DIM)
    normed_one = low_rank_rows(low_back(rms_norm(input_rows, gain_attn)))
    projected_queries = low_back(adapted(normed_one, weight_q, input_first[index, 0], query_second[index]))
    projected_keys = low_back(adapted(normed_one, weight_k, input_first[index, 1], key_value_second[index, 0]))
    projected_values = low_back(adapted(normed_one, weight_v, input_first[index, 2], key_value_second[index, 1]))
    query_head_rows = low_rank_rows(apply_rotation(projected_queries.reshape(SLOT_POSITIONS, QUERY_HEADS, HEAD_DIM), cosine_table, sine_table)).reshape(SLOT_POSITIONS, KEY_VALUE_HEADS, QUERY_HEADS // KEY_VALUE_HEADS, HEAD_DIM)
    key_head_rows = low_rank_rows(apply_rotation(projected_keys.reshape(SLOT_POSITIONS, KEY_VALUE_HEADS, HEAD_DIM), cosine_table, sine_table))
    value_head_rows = low_rank_rows(projected_values).reshape(SLOT_POSITIONS, KEY_VALUE_HEADS, HEAD_DIM)
    attended = attention(query_head_rows, key_head_rows, value_head_rows, length).reshape(SLOT_POSITIONS, QUERY_HEADS * HEAD_DIM)
    attn_b = low_rank_rows(low_back(attended))
    resid = input_rows + low_back(adapted(attn_b, weight_o, output_first[index], output_second[index]))
    normed_two = low_rank_rows(low_back(rms_norm(resid, gain_mlp)))
    gate = low_back(adapted(normed_two, weight_gate, input_first[index, 3], gate_up_second[index, 0]))
    up_proj = low_back(adapted(normed_two, weight_up, input_first[index, 4], gate_up_second[index, 1]))
    hidden = low_rank_rows(jax.nn.silu(gate) * up_proj)
    output = resid + adapted(hidden, weight_down, down_first[index], down_second[index])
    live = positions < length
    return jnp.where(live[:, None], output, 0.0)

def reference(tokens, cotangent, lengths, slot_adapter_index, attention_norm_gain, feedforward_norm_gain, query_weight, key_weight, value_weight, output_weight, gate_weight, up_weight, down_weight, adapter_input_first, adapter_output_first, adapter_down_first, adapter_query_second, adapter_key_value_second, adapter_output_second, adapter_gate_up_second, adapter_down_second):
    frozen = tuple((entry_item.astype(jnp.float32) for entry_item in (attention_norm_gain, feedforward_norm_gain, query_weight, key_weight, value_weight, output_weight, gate_weight, up_weight, down_weight)))
    rotation_tables = tuple((entry_item.astype(jnp.float32) for entry_item in (adapter_input_first, adapter_output_first, adapter_down_first, adapter_query_second, adapter_key_value_second, adapter_output_second, adapter_gate_up_second, adapter_down_second)))

    def slot_step(totals, entry_item):
        input_rows, grad_output, length, index = entry_item

        def layer(input_values, table_values):
            return slot_layer(input_values, table_values, frozen, length, index)
        output, pullback = jax.vjp(layer, input_rows.astype(jnp.float32), rotation_tables)
        grad_inputs, grad_tables = pullback(grad_output.astype(jnp.float32))
        totals = jax.tree.map(lambda left, right: left + right, totals, grad_tables)
        return (totals, (output.astype(jnp.bfloat16), grad_inputs))
    zeros = jax.tree.map(jnp.zeros_like, rotation_tables)
    totals, (outputs, gradient_tree) = lax.scan(slot_step, zeros, (tokens, cotangent, lengths, slot_adapter_index))
    return (outputs, gradient_tree, totals[0], totals[1], totals[2], totals[3], totals[4], totals[5], totals[6], totals[7])
```

```python
import math

import jax
import jax.numpy as jnp
from jax import lax
from jax.experimental import pallas as pl
from jax.experimental.pallas import tpu as pltpu
from jax.sharding import PartitionSpec as P

QUERY_HEADS = 16
KEY_VALUE_HEADS = 8
HEAD_DIM = 96


EPSILON = 1e-05
NEGATIVE = -1e30
ADAPTER_SCALE = 0.5
ROPE_BASE = 100000.0


def from_behind(x, axis, by):
    size = lax.axis_size(axis)
    return lax.ppermute(x, axis, [(i, (i + by) % size) for i in range(size)])


def rope_tables(positions, head_size):
    half_size = head_size // 2
    freqs = ROPE_BASE ** (-(jnp.arange(half_size, dtype=jnp.float32) * 2.0 / head_size))
    angles = positions.astype(jnp.float32)[:, None] * freqs[None, :]
    return (jnp.cos(angles)[:, None, :], jnp.sin(angles)[:, None, :])


def apply_rotation(values, cosine_table, sine_table):
    half_size = values.shape[-1] // 2
    first_half = values[..., :half_size]
    second_half = values[..., half_size:]
    return jnp.concatenate(
        [
            first_half * cosine_table - second_half * sine_table,
            second_half * cosine_table + first_half * sine_table,
        ],
        axis=-1,
    )


def rotate_back(gradient_tree, cosine_table, sine_table):
    half_size = gradient_tree.shape[-1] // 2
    first_half = gradient_tree[..., :half_size]
    second_half = gradient_tree[..., half_size:]
    return jnp.concatenate(
        [
            first_half * cosine_table + second_half * sine_table,
            second_half * cosine_table - first_half * sine_table,
        ],
        axis=-1,
    )


def rms_factor(values):
    return lax.rsqrt(jnp.mean(values * values, axis=-1, keepdims=True) + EPSILON)


def norm_back(values, factor, gain, grad_norm):
    scaled = grad_norm * gain
    return factor * scaled - values * factor**3 * jnp.mean(scaled * values, axis=-1, keepdims=True)


def pick_rows(onehot, table):
    return jnp.einsum("sa,a...->s...", onehot, table, preferred_element_type=jnp.float32).astype(
        jnp.bfloat16
    )


def spread_rows(onehot, gradient_tree):
    return jnp.einsum("sa,s...->a...", onehot, gradient_tree, precision=lax.Precision.HIGHEST)


def direct_product(input_rows, weight_matrix):
    return jnp.einsum("std,do->sto", input_rows, weight_matrix, preferred_element_type=jnp.float32)


def direct_back(gradient_tree, weight_matrix):
    return jnp.einsum(
        "sto,do->std", gradient_tree, weight_matrix, preferred_element_type=jnp.float32
    )


def inner_product_part(input_rows, down):
    return jnp.einsum("std,sdr->str", input_rows, down, preferred_element_type=jnp.float32)


def inner_back(gradient_tree, upward_rows):
    return ADAPTER_SCALE * jnp.einsum(
        "sto,sro->str", gradient_tree, upward_rows, preferred_element_type=jnp.float32
    )


def through_down(grad_inner, down):
    return jnp.einsum("str,sdr->std", grad_inner, down, preferred_element_type=jnp.float32)


def down_grad(input_rows, grad_inner):
    return jnp.einsum("std,str->sdr", input_rows, grad_inner, preferred_element_type=jnp.float32)


def upward_grad(inner_rows, gradient_tree):
    return ADAPTER_SCALE * jnp.einsum(
        "jvp,jvx->jpx", inner_rows, gradient_tree, preferred_element_type=jnp.float32
    )


def upward_apply(inner_rows, upward_rows):
    return ADAPTER_SCALE * jnp.einsum(
        "str,sro->sto", inner_rows, upward_rows, preferred_element_type=jnp.float32
    )


def project(input_rows, weight_matrix, down, upward_rows):
    inner_rows = inner_product_part(input_rows, down).astype(jnp.bfloat16)
    return (
        inner_rows,
        direct_product(input_rows, weight_matrix) + upward_apply(inner_rows, upward_rows),
    )


def project_back(input_rows, grad_output, weight_matrix, down, upward_rows, inner_rows):
    grad_upward = upward_grad(inner_rows, grad_output)
    grad_inner = inner_back(grad_output, upward_rows).astype(jnp.bfloat16)
    grad_down = down_grad(input_rows, grad_inner)
    grad_inputs = direct_back(grad_output, weight_matrix) + through_down(grad_inner, down)
    return (grad_inputs, grad_down, grad_upward)


def allowed_mask(key_start, key_count, query_pos, lengths):
    key_pos = key_start + jnp.arange(key_count, dtype=jnp.int32)
    causal = key_pos[None, :] <= query_pos[:, None]
    live = key_pos[None, :] < lengths[:, None]
    return (causal[None, :, :] & live[:, None, :])[:, None, None, :, :]


def attend_block(state, key_block, value_block, key_start, query_head_rows, query_pos, lengths):
    run_max, run_sum, run_acc = state
    scale = query_head_rows.shape[-1] ** (-0.5)
    scores = (
        jnp.einsum(
            "sqhgd,skhd->shgqk", query_head_rows, key_block, preferred_element_type=jnp.float32
        )
        * scale
    )
    allowed = allowed_mask(key_start, key_block.shape[1], query_pos, lengths)
    new_max = jnp.maximum(run_max, jnp.max(jnp.where(allowed, scores, NEGATIVE), axis=-1))
    weights = jnp.where(allowed, jnp.exp(scores - new_max[..., None]), 0.0)
    factor = jnp.exp(run_max - new_max)
    new_sum = run_sum * factor + jnp.sum(weights, axis=-1)
    update = jnp.einsum(
        "shgqk,skhd->shgqd",
        weights.astype(jnp.bfloat16),
        value_block,
        preferred_element_type=jnp.float32,
    )
    return (new_max, new_sum, run_acc * factor[..., None] + update)


def attend_back(
    key_block,
    value_block,
    key_start,
    query_head_rows,
    grad_heads,
    log_total,
    row_dot,
    query_pos,
    lengths,
):
    scale = query_head_rows.shape[-1] ** (-0.5)
    scores = (
        jnp.einsum(
            "sqhgd,skhd->shgqk", query_head_rows, key_block, preferred_element_type=jnp.float32
        )
        * scale
    )
    allowed = allowed_mask(key_start, key_block.shape[1], query_pos, lengths)
    probs = jnp.where(allowed, jnp.exp(scores - log_total[..., None]), 0.0)
    grad_probs = jnp.einsum(
        "sqhgd,skhd->shgqk", grad_heads, value_block, preferred_element_type=jnp.float32
    )
    grad_scores = (probs * (grad_probs - row_dot[..., None])).astype(jnp.bfloat16)
    grad_query = scale * jnp.einsum(
        "shgqk,skhd->sqhgd", grad_scores, key_block, preferred_element_type=jnp.float32
    )
    grad_key = scale * jnp.einsum(
        "shgqk,sqhgd->skhd", grad_scores, query_head_rows, preferred_element_type=jnp.float32
    )
    grad_value = jnp.einsum(
        "shgqk,sqhgd->skhd",
        probs.astype(jnp.bfloat16),
        grad_heads,
        preferred_element_type=jnp.float32,
    )
    return (grad_query, grad_key, grad_value)


def attend_forward(query_head_rows, key_head_rows, value_head_rows, lengths_used, query_pos):
    slots, rows, kv_heads, group_size, head_size = query_head_rows.shape
    key_flat = key_head_rows.reshape(slots, rows, kv_heads * head_size)
    value_flat = value_head_rows.reshape(slots, rows, kv_heads * head_size)
    stat_shape = (slots, kv_heads, group_size, rows)
    initial = (
        jnp.full(stat_shape, NEGATIVE, jnp.float32),
        jnp.zeros(stat_shape, jnp.float32),
        jnp.zeros(stat_shape + (head_size,), jnp.float32),
    )
    part_keys = lax.all_gather(key_flat, "ctx", axis=1, tiled=True)
    part_values = lax.all_gather(value_flat, "ctx", axis=1, tiled=True)
    piece_rows = part_keys.shape[1]
    part_keys = part_keys.reshape(slots, piece_rows, kv_heads, head_size)
    part_values = part_values.reshape(slots, piece_rows, kv_heads, head_size)
    span_rows = math.gcd(piece_rows, 4 * rows)

    def inner_step(block_index, inner_state):
        sub_keys = lax.dynamic_slice_in_dim(part_keys, block_index * span_rows, span_rows, 1)
        sub_values = lax.dynamic_slice_in_dim(part_values, block_index * span_rows, span_rows, 1)
        return attend_block(
            inner_state,
            sub_keys,
            sub_values,
            block_index * span_rows,
            query_head_rows,
            query_pos,
            lengths_used,
        )

    run_max, run_sum, run_acc = lax.fori_loop(0, piece_rows // span_rows, inner_step, initial)
    log_total = run_max + jnp.log(run_sum)
    attended = jnp.transpose(run_acc / run_sum[..., None], (0, 3, 1, 2, 4))
    return (attended, log_total)


def attend_backward(
    query_head_rows,
    key_head_rows,
    value_head_rows,
    grad_heads,
    attended,
    log_total,
    lengths_used,
    query_pos,
):
    ctx_count = lax.axis_size("ctx")
    own_index = lax.axis_index("ctx")
    rows = query_head_rows.shape[1]
    row_dot = jnp.transpose(
        jnp.sum(grad_heads.astype(jnp.float32) * attended, axis=-1), (0, 2, 3, 1)
    )

    def cycle_step(step_index, carried):
        carried_keys, carried_values, grad_query, grad_key, grad_value = carried
        block_id = (own_index + step_index) % ctx_count
        query_part, key_part, value_part = attend_back(
            carried_keys,
            carried_values,
            block_id * rows,
            query_head_rows,
            grad_heads,
            log_total,
            row_dot,
            query_pos,
            lengths_used,
        )
        grad_key, grad_value = (
            from_behind((grad_key + key_part).astype(jnp.bfloat16), "ctx", -1).astype(jnp.float32),
            from_behind((grad_value + value_part).astype(jnp.bfloat16), "ctx", -1).astype(
                jnp.float32
            ),
        )
        carried_keys, carried_values = from_behind((carried_keys, carried_values), "ctx", -1)
        return (carried_keys, carried_values, grad_query + query_part, grad_key, grad_value)

    key_zeros = jnp.zeros(key_head_rows.shape, jnp.float32)
    start_state = (
        key_head_rows,
        value_head_rows,
        jnp.zeros(query_head_rows.shape, jnp.float32),
        key_zeros,
        key_zeros,
    )
    carried = lax.fori_loop(0, ctx_count, cycle_step, start_state)
    return (carried[2], carried[3], carried[4])


def table_total(rotation_tables):
    return lax.psum(rotation_tables, ("ctx", "fsdp"))


def local(
    tokens,
    cotangent,
    lengths,
    slot_adapter_index,
    attention_norm_gain,
    feedforward_norm_gain,
    query_weight,
    key_weight,
    value_weight,
    output_weight,
    gate_weight,
    up_weight,
    down_weight,
    adapter_input_first,
    adapter_output_first,
    adapter_down_first,
    adapter_query_second,
    adapter_key_value_second,
    adapter_output_second,
    adapter_gate_up_second,
    adapter_down_second,
):
    slot_count, tok_rows, model_width = tokens.shape
    head_groups = QUERY_HEADS // KEY_VALUE_HEADS
    own_index = lax.axis_index("ctx")
    fsdp_index = lax.axis_index("fsdp")
    query_pos = own_index * tok_rows + jnp.arange(tok_rows, dtype=jnp.int32)
    cosine_table, sine_table = rope_tables(query_pos, HEAD_DIM)
    own_lengths = lax.dynamic_slice_in_dim(lengths, fsdp_index * slot_count, slot_count, 0)
    own_adapters = lax.dynamic_slice_in_dim(
        slot_adapter_index, fsdp_index * slot_count, slot_count, 0
    )
    valid = query_pos[None, :] < own_lengths[:, None]
    adapter_labels = jnp.arange(adapter_input_first.shape[0], dtype=jnp.int32)
    onehot_own = own_adapters[:, None] == adapter_labels[None, :]
    owned_low_rank = onehot_own.astype(jnp.bfloat16)
    own_full = onehot_own.astype(jnp.float32)
    tokens_f = tokens.astype(jnp.float32)
    factor_one = rms_factor(tokens_f)
    normed_one = (tokens_f * factor_one * attention_norm_gain).astype(jnp.bfloat16)
    grad_out = jnp.where(valid[..., None], cotangent, jnp.zeros((), jnp.bfloat16))
    input_first = pick_rows(owned_low_rank, adapter_input_first)
    output_second = pick_rows(owned_low_rank, adapter_output_second)
    down_second = pick_rows(owned_low_rank, adapter_down_second)
    output_first = pick_rows(owned_low_rank, adapter_output_first)
    down_first = pick_rows(owned_low_rank, adapter_down_first)
    query_second = pick_rows(owned_low_rank, adapter_query_second)
    key_value_second = pick_rows(owned_low_rank, adapter_key_value_second)
    gate_up_second = pick_rows(owned_low_rank, adapter_gate_up_second)
    weight_q, weight_k, weight_v, weight_gate, weight_up, weight_o, weight_down = (
        lax.all_gather(query_weight, "fsdp", axis=1, tiled=True),
        lax.all_gather(key_weight, "fsdp", axis=1, tiled=True),
        lax.all_gather(value_weight, "fsdp", axis=1, tiled=True),
        lax.all_gather(gate_weight, "fsdp", axis=1, tiled=True),
        lax.all_gather(up_weight, "fsdp", axis=1, tiled=True),
        lax.all_gather(output_weight, "fsdp", axis=0, tiled=True),
        lax.all_gather(down_weight, "fsdp", axis=0, tiled=True),
    )
    inner_q, projected_queries = project(normed_one, weight_q, input_first[:, 0], query_second)
    inner_k, projected_keys = project(
        normed_one, weight_k, input_first[:, 1], key_value_second[:, 0]
    )
    inner_v, projected_values = project(
        normed_one, weight_v, input_first[:, 2], key_value_second[:, 1]
    )
    query_head_rows = apply_rotation(
        projected_queries.reshape(slot_count, tok_rows, -1, HEAD_DIM), cosine_table, sine_table
    ).astype(jnp.bfloat16)
    query_head_rows = query_head_rows.reshape(slot_count, tok_rows, -1, head_groups, HEAD_DIM)
    key_head_rows = apply_rotation(
        projected_keys.reshape(slot_count, tok_rows, -1, HEAD_DIM), cosine_table, sine_table
    ).astype(jnp.bfloat16)
    value_head_rows = projected_values.astype(jnp.bfloat16).reshape(
        slot_count, tok_rows, -1, HEAD_DIM
    )
    attended, log_total = attend_forward(
        query_head_rows, key_head_rows, value_head_rows, own_lengths, query_pos
    )
    attn_b = attended.reshape(slot_count, tok_rows, -1).astype(jnp.bfloat16)
    inner_o, proj_o = project(attn_b, weight_o, output_first, output_second)
    resid = tokens_f + proj_o
    factor_two = rms_factor(resid)
    normed_two = (resid * factor_two * feedforward_norm_gain).astype(jnp.bfloat16)
    inner_gate, gate = project(normed_two, weight_gate, input_first[:, 3], gate_up_second[:, 0])
    inner_up, up_proj = project(normed_two, weight_up, input_first[:, 4], gate_up_second[:, 1])
    sigmoid_gate = jax.nn.sigmoid(gate)
    hidden = (gate * sigmoid_gate * up_proj).astype(jnp.bfloat16)
    inner_down, proj_down = project(hidden, weight_down, down_first, down_second)
    out_tokens = jnp.where(valid[..., None], resid + proj_down, 0.0).astype(jnp.bfloat16)
    grad_hidden, grad_da, grad_db = project_back(
        hidden, grad_out, weight_down, down_first, down_second, inner_down
    )
    grad_gate = (grad_hidden * up_proj * sigmoid_gate * (1.0 + gate * (1.0 - sigmoid_gate))).astype(
        jnp.bfloat16
    )
    grad_up = (grad_hidden * gate * sigmoid_gate).astype(jnp.bfloat16)
    from_gate, grad_ga, grad_gb = project_back(
        normed_two, grad_gate, weight_gate, input_first[:, 3], gate_up_second[:, 0], inner_gate
    )
    from_up, grad_ua, grad_ub = project_back(
        normed_two, grad_up, weight_up, input_first[:, 4], gate_up_second[:, 1], inner_up
    )
    grad_normed_two = (from_gate + from_up).astype(jnp.bfloat16).astype(jnp.float32)
    grad_resid = grad_out.astype(jnp.float32) + norm_back(
        resid, factor_two, feedforward_norm_gain, grad_normed_two
    )
    grad_resid_low = grad_resid.astype(jnp.bfloat16)
    from_attn, grad_oa, grad_ob = project_back(
        attn_b, grad_resid_low, weight_o, output_first, output_second, inner_o
    )
    grad_heads = from_attn.astype(jnp.bfloat16).reshape(attended.shape)
    grad_query, grad_key, grad_value = attend_backward(
        query_head_rows,
        key_head_rows,
        value_head_rows,
        grad_heads,
        attended,
        log_total,
        own_lengths,
        query_pos,
    )
    grad_proj_q = (
        rotate_back(
            grad_query.reshape(slot_count, tok_rows, -1, HEAD_DIM), cosine_table, sine_table
        )
        .astype(jnp.bfloat16)
        .reshape(slot_count, tok_rows, -1)
    )
    grad_proj_k = (
        rotate_back(grad_key, cosine_table, sine_table)
        .astype(jnp.bfloat16)
        .reshape(slot_count, tok_rows, -1)
    )
    grad_proj_v = grad_value.astype(jnp.bfloat16).reshape(slot_count, tok_rows, -1)
    from_query, grad_qa, grad_qb = project_back(
        normed_one, grad_proj_q, weight_q, input_first[:, 0], query_second, inner_q
    )
    from_key, grad_ka, grad_kb = project_back(
        normed_one, grad_proj_k, weight_k, input_first[:, 1], key_value_second[:, 0], inner_k
    )
    from_value, grad_va, grad_vb = project_back(
        normed_one, grad_proj_v, weight_v, input_first[:, 2], key_value_second[:, 1], inner_v
    )
    grad_normed_one = (from_query + from_key + from_value).astype(jnp.bfloat16).astype(jnp.float32)
    grad_tokens = grad_resid + norm_back(tokens_f, factor_one, attention_norm_gain, grad_normed_one)
    slot_grads = (
        jnp.stack([grad_qa, grad_ka, grad_va, grad_ga, grad_ua], axis=1),
        grad_oa,
        grad_da,
        grad_qb,
        jnp.stack([grad_kb, grad_vb], axis=1),
        grad_ob,
        jnp.stack([grad_gb, grad_ub], axis=1),
        grad_db,
    )
    summed = table_total(tuple((spread_rows(own_full, entry_item) for entry_item in slot_grads)))
    return (
        out_tokens,
        grad_tokens,
        summed[0],
        summed[1],
        summed[2],
        summed[3],
        summed[4],
        summed[5],
        summed[6],
        summed[7],
    )


BF16 = jnp.bfloat16
F32 = jnp.float32
MESH_ID = pl.DeviceIdType.MESH
RANK = 16
SIDE = 128
PAD_HEAD = 128
HALF_PAD = 64


def _sem(count):
    return pltpu.SemaphoreType.DMA((count,))


def _place():
    c = lax.axis_index("ctx")
    f = lax.axis_index("fsdp")
    x = f // 2
    core = f % 2
    return c, f, x, core, (c, 2 * x + 1 - core), (c, 2 * (1 - x) + core)


def _greet(targets):
    barrier = pltpu.get_barrier_semaphore()
    for target in targets:
        pl.semaphore_signal(barrier, inc=1, device_id=target, device_id_type=MESH_ID)
    pl.semaphore_wait(barrier, len(targets))


def _remote(src, dst, send, recv, target):
    return pltpu.make_async_remote_copy(
        src_ref=src, dst_ref=dst, send_sem=send, recv_sem=recv, device_id=target, device_id_type=MESH_ID
    )


def _comm_call(kernel, ins, outs, scratch, cid, name, in_space=pl.ANY, out_space=pl.ANY, vmem=None):
    return pl.pallas_call(
        kernel,
        out_shape=outs,
        in_specs=[pl.BlockSpec(memory_space=in_space)] * len(ins),
        out_specs=jax.tree.map(lambda _: pl.BlockSpec(memory_space=out_space), outs),
        scratch_shapes=scratch,
        compiler_params=pltpu.CompilerParams(
            collective_id=cid, has_side_effects=True, vmem_limit_bytes=vmem
        ),
        name=name,
    )(*ins)


def _gather_body(ins, outs, own_sem, send_sem, recv_sem, place):
    c, f, x, core, core_peer, x_peer = place
    h = 1 - core
    count = len(ins)
    local = []
    sends = []
    for i in range(count):
        for j in range(2):
            k = i * 2 + j
            cp = _remote(
                ins[i].at[j], outs[i].at[h, j, x], send_sem.at[k], recv_sem.at[k], x_peer
            )
            cp.start()
            sends.append(cp)
    for i in range(count):
        for j in range(2):
            k = i * 2 + j
            cp = _remote(
                ins[i].at[j],
                outs[i].at[h, j, x],
                send_sem.at[2 * count + k],
                recv_sem.at[2 * count + k],
                core_peer,
            )
            cp.start()
            sends.append(cp)
            lc = pltpu.make_async_copy(ins[i].at[j], outs[i].at[h, j, x], own_sem.at[k])
            lc.start()
            local.append(lc)
    forwards = []
    for i in range(count):
        for j in range(2):
            k = i * 2 + j
            sends[k].wait_recv()
            cp = _remote(
                outs[i].at[h, j, 1 - x],
                outs[i].at[h, j, 1 - x],
                send_sem.at[4 * count + k],
                recv_sem.at[4 * count + k],
                core_peer,
            )
            cp.start()
            forwards.append(cp)
    for k in range(2 * count):
        sends[2 * count + k].wait_recv()
        forwards[k].wait_recv()
    for cp in sends + forwards:
        cp.wait_send()
    for lc in local:
        lc.wait()


def group_gather(arrays, cid, name):
    count = len(arrays)

    def kernel(*refs):
        ins, outs = refs[:count], refs[count : 2 * count]
        own_sem, send_sem, recv_sem = refs[2 * count :]
        place = _place()
        _greet([place[4], place[5]])
        _gather_body(ins, outs, own_sem, send_sem, recv_sem, place)

    outs = [jax.ShapeDtypeStruct((2, 2, 2) + a.shape[1:], a.dtype) for a in arrays]
    return _comm_call(
        kernel, arrays, outs, [_sem(2 * count), _sem(6 * count), _sem(6 * count)], cid, name
    )


def group_scatter(arrays, cid, name):
    count = len(arrays)

    def kernel(*refs):
        ins, outs = refs[:count], refs[count : 2 * count]
        first, staged, second = (
            refs[2 * count : 3 * count],
            refs[3 * count : 4 * count],
            refs[4 * count : 5 * count],
        )
        send_sem, recv_sem = refs[5 * count :]
        c, f, x, core, core_peer, x_peer = _place()
        h = 1 - core
        _greet([core_peer, x_peer])
        one, two = {}, {}
        for far in (1, 0):
            for j in range(2):
                for i in range(count):
                    k = (i * 2 + j) * 2 + far
                    xx = 1 - x if far else x
                    cp = _remote(
                        ins[i].at[1 - h, j, xx],
                        first[i].at[far, j],
                        send_sem.at[k],
                        recv_sem.at[k],
                        core_peer,
                    )
                    cp.start()
                    one[(i, j, far)] = cp
        for j in range(2):
            for i in range(count):
                one[(i, j, 1)].wait_recv()
                staged[i][j] = (
                    ins[i][h, j, 1 - x].astype(F32) + first[i][1, j].astype(F32)
                ).astype(BF16)
                k = 4 * count + i * 2 + j
                cp = _remote(
                    staged[i].at[j], second[i].at[j], send_sem.at[k], recv_sem.at[k], x_peer
                )
                cp.start()
                two[(i, j)] = cp
        for j in range(2):
            for i in range(count):
                one[(i, j, 0)].wait_recv()
                outs[i][j] = ins[i][h, j, x].astype(F32) + first[i][0, j].astype(F32)
        for j in range(2):
            for i in range(count):
                two[(i, j)].wait_recv()
                outs[i][j] = outs[i][j] + second[i][j].astype(F32)
        for cp in list(one.values()) + list(two.values()):
            cp.wait_send()

    outs = [jax.ShapeDtypeStruct((2,) + a.shape[3:], F32) for a in arrays]
    rows = [a.shape[3:] for a in arrays]
    scratch = (
        [pltpu.VMEM((2, 2) + r, BF16) for r in rows]
        + [pltpu.VMEM((2,) + r, BF16) for r in rows]
        + [pltpu.VMEM((2,) + r, BF16) for r in rows]
        + [_sem(6 * count), _sem(6 * count)]
    )
    return _comm_call(
        kernel, arrays, outs, scratch, cid, name, pltpu.VMEM, pltpu.VMEM, 40 * 1024 * 1024
    )


def take_in(tokens, cotangent, cid):
    def kernel(tok, cot, tok_own, cot_own, tok_all, cot_all, land_s, land_r, own_sem, send_sem, recv_sem):
        place = _place()
        c, f, x, core, core_peer, x_peer = place
        h = 1 - core
        slot = c // 2 + 4 * (c % 2)
        barrier = pltpu.get_barrier_semaphore()
        for j in range(2):
            pl.semaphore_signal(
                barrier, inc=1, device_id=(x + 2 * j + 4 * h, slot // 2), device_id_type=MESH_ID
            )
        for target in (core_peer, x_peer):
            pl.semaphore_signal(barrier, inc=1, device_id=target, device_id_type=MESH_ID)
        pl.semaphore_wait(barrier, 4)
        to_f = 2 * (c % 2) + 1 - c // 4
        to_j = (c // 2) % 2
        moves = []
        for a, (src, dst) in enumerate(((tok, tok_own), (cot, cot_own))):
            for half in range(2):
                s = 2 * f + half
                to_c = (s % 4) * 2 + s // 4
                cp = _remote(
                    src.at[half], dst.at[to_j], land_s.at[2 * a + half], land_r.at[2 * a + to_j], (to_c, to_f)
                )
                cp.start()
                moves.append(cp)
        for a in range(2):
            for j in range(2):
                dst = (tok_own, cot_own)[a]
                pltpu.make_async_copy(dst.at[j], dst.at[j], land_r.at[2 * a + j]).wait()
        _gather_body((tok_own, cot_own), (tok_all, cot_all), own_sem, send_sem, recv_sem, place)
        for cp in moves:
            cp.wait_send()

    own = jax.ShapeDtypeStruct(tokens.shape, tokens.dtype)
    whole = jax.ShapeDtypeStruct((2, 2, 2) + tokens.shape[1:], tokens.dtype)
    return _comm_call(
        kernel,
        [tokens, cotangent],
        [own, own, whole, whole],
        [_sem(4), _sem(4), _sem(4), _sem(12), _sem(12)],
        cid,
        "take_in",
    )


def give_back(arrays, smalls, cid):
    count, extra = len(arrays), len(smalls)

    def kernel(*refs):
        ins, small_in = refs[:count], refs[count : count + extra]
        outs = refs[count + extra : 2 * count + extra]
        small_out = refs[2 * count + extra : 2 * count + 2 * extra]
        out_s, out_r, own_sem, send_sem, recv_sem = refs[2 * count + 2 * extra :]
        place = _place()
        c, f, x, core, core_peer, x_peer = place
        h = 1 - core
        slot = c // 2 + 4 * (c % 2)
        barrier = pltpu.get_barrier_semaphore()
        from_f = 2 * (c % 2) + 1 - c // 4
        for half in range(2):
            s = 2 * f + half
            pl.semaphore_signal(
                barrier, inc=1, device_id=((s % 4) * 2 + s // 4, from_f), device_id_type=MESH_ID
            )
        for target in (core_peer, x_peer):
            pl.semaphore_signal(barrier, inc=1, device_id=target, device_id_type=MESH_ID)
        pl.semaphore_wait(barrier, 4)
        moves = []
        place_in = slot % 2
        for i in range(count):
            for j in range(2):
                cp = _remote(
                    ins[i].at[j],
                    outs[i].at[place_in],
                    out_s.at[2 * i + j],
                    out_r.at[2 * i + place_in],
                    (x + 2 * j + 4 * h, slot // 2),
                )
                cp.start()
                moves.append(cp)
        _gather_body(small_in, small_out, own_sem, send_sem, recv_sem, place)
        for i in range(count):
            for half in range(2):
                pltpu.make_async_copy(
                    outs[i].at[half], outs[i].at[half], out_r.at[2 * i + half]
                ).wait()
        for cp in moves:
            cp.wait_send()

    outs = [jax.ShapeDtypeStruct(a.shape, a.dtype) for a in arrays]
    outs += [jax.ShapeDtypeStruct((2, 2, 2) + a.shape[1:], a.dtype) for a in smalls]
    return _comm_call(
        kernel,
        list(arrays) + list(smalls),
        outs,
        [_sem(2 * count), _sem(2 * count), _sem(2 * extra), _sem(6 * extra), _sem(6 * extra)],
        cid,
        "give_back",
    )


def attend_call(proj, cosine, sine, length):
    rows = proj.shape[0]
    step = 256
    scale = HEAD_DIM ** (-0.5)
    lane = PAD_HEAD

    def kernel(len_ref, proj_ref, cos_ref, sin_ref, att_ref, qkv_ref, lse_ref):
        live = len_ref[0]
        for part in range(6):
            cols = slice(part * lane, (part + 1) * lane)
            v = proj_ref[:, cols]
            v = v * cos_ref[...] + pltpu.roll(v, HALF_PAD, 1) * sin_ref[...]
            qkv_ref[:, cols] = v.astype(BF16)
        qkv_ref[:, 6 * lane :] = proj_ref[:, 6 * lane :].astype(BF16)
        for block in range(rows // step):
            keys = (block + 1) * step
            row = pl.ds(block * step, step)
            qpos = block * step + lax.broadcasted_iota(jnp.int32, (step, keys), 0)
            kpos = lax.broadcasted_iota(jnp.int32, (step, keys), 1)
            allowed = (kpos <= qpos) & (kpos < live)
            pieces = []
            stats = jnp.zeros((step, lane), F32)
            lanes = lax.broadcasted_iota(jnp.int32, (step, lane), 1)
            for head in range(4):
                q = qkv_ref[row, head * lane : (head + 1) * lane]
                kv = head // 2
                k = qkv_ref[:keys, (4 + kv) * lane : (5 + kv) * lane]
                v = qkv_ref[:keys, (6 + kv) * lane : (7 + kv) * lane]
                s = lax.dot_general(q, k, (((1,), (1,)), ((), ())), preferred_element_type=F32)
                s = jnp.where(allowed, s * scale, NEGATIVE)
                top = jnp.max(s, axis=1, keepdims=True)
                p = jnp.where(allowed, jnp.exp(s - top), 0.0)
                total = jnp.sum(p, axis=1, keepdims=True)
                o = jnp.dot(p.astype(BF16), v, preferred_element_type=F32) / total
                pieces.append(o[:, :HEAD_DIM])
                stats = jnp.where(lanes == head, top + jnp.log(total), stats)
            att_ref[row, :] = jnp.concatenate(pieces, axis=1).astype(BF16)
            lse_ref[row, :] = stats

    vmem = pl.BlockSpec(memory_space=pltpu.VMEM)
    return pl.pallas_call(
        kernel,
        out_shape=(
            jax.ShapeDtypeStruct((rows, 4 * HEAD_DIM), BF16),
            jax.ShapeDtypeStruct(proj.shape, BF16),
            jax.ShapeDtypeStruct((rows, lane), F32),
        ),
        in_specs=[pl.BlockSpec(memory_space=pltpu.SMEM), vmem, vmem, vmem],
        out_specs=(vmem, vmem, vmem),
        compiler_params=pltpu.CompilerParams(vmem_limit_bytes=48 * 1024 * 1024),
        name="attend",
    )(length, proj, cosine, sine)


def attend_back_call(qkv, stats, grad_att, cosine, sine, length):
    rows = qkv.shape[0]
    step = 256
    scale = HEAD_DIM ** (-0.5)
    lane = PAD_HEAD

    def kernel(len_ref, qkv_ref, lse_ref, g_ref, cos_ref, sin_ref, out_ref, dk_ref, dv_ref, do_ref):
        live = len_ref[0]
        pad = jnp.zeros((rows, lane - HEAD_DIM), BF16)
        for head in range(4):
            do_ref[head] = jnp.concatenate(
                [g_ref[:, head * HEAD_DIM : (head + 1) * HEAD_DIM], pad], axis=1
            )
        dk_ref[...] = jnp.zeros_like(dk_ref)
        dv_ref[...] = jnp.zeros_like(dv_ref)
        for block in range(rows // step):
            keys = (block + 1) * step
            row = pl.ds(block * step, step)
            qpos = block * step + lax.broadcasted_iota(jnp.int32, (step, keys), 0)
            kpos = lax.broadcasted_iota(jnp.int32, (step, keys), 1)
            allowed = (kpos <= qpos) & (kpos < live)
            cos, sin = cos_ref[row, :], sin_ref[row, :]
            for head in range(4):
                kv = head // 2
                q = qkv_ref[row, head * lane : (head + 1) * lane]
                k = qkv_ref[:keys, (4 + kv) * lane : (5 + kv) * lane]
                v = qkv_ref[:keys, (6 + kv) * lane : (7 + kv) * lane]
                do = do_ref[head, row, :]
                s = lax.dot_general(q, k, (((1,), (1,)), ((), ())), preferred_element_type=F32)
                p = jnp.where(allowed, jnp.exp(s * scale - lse_ref[row, head : head + 1]), 0.0)
                dp = lax.dot_general(do, v, (((1,), (1,)), ((), ())), preferred_element_type=F32)
                dot = jnp.sum(p * dp, axis=1, keepdims=True)
                ds = (p * (dp - dot)).astype(BF16)
                dq = scale * jnp.dot(ds, k, preferred_element_type=F32)
                dq = dq * cos - pltpu.roll(dq, HALF_PAD, 1) * sin
                out_ref[row, head * lane : (head + 1) * lane] = dq.astype(BF16)
                dk_ref[kv, :keys] += lax.dot_general(
                    ds, q, (((0,), (0,)), ((), ())), preferred_element_type=F32
                )
                dv_ref[kv, :keys] += lax.dot_general(
                    p.astype(BF16), do, (((0,), (0,)), ((), ())), preferred_element_type=F32
                )
        for kv in range(2):
            dk = scale * dk_ref[kv]
            dk = dk * cos_ref[...] - pltpu.roll(dk, HALF_PAD, 1) * sin_ref[...]
            out_ref[:, (4 + kv) * lane : (5 + kv) * lane] = dk.astype(BF16)
            out_ref[:, (6 + kv) * lane : (7 + kv) * lane] = dv_ref[kv].astype(BF16)

    vmem = pl.BlockSpec(memory_space=pltpu.VMEM)
    return pl.pallas_call(
        kernel,
        out_shape=jax.ShapeDtypeStruct(qkv.shape, BF16),
        in_specs=[pl.BlockSpec(memory_space=pltpu.SMEM)] + [vmem] * 5,
        out_specs=vmem,
        scratch_shapes=[
            pltpu.VMEM((2, rows, lane), F32),
            pltpu.VMEM((2, rows, lane), F32),
            pltpu.VMEM((4, rows, lane), BF16),
        ],
        compiler_params=pltpu.CompilerParams(vmem_limit_bytes=48 * 1024 * 1024),
        name="attend_back",
    )(length, qkv, stats, grad_att, cosine, sine)


def gather_all(piece, cid):
    def kernel(src, out, own_sem, send_sem, recv_sem):
        c = lax.axis_index("ctx")
        f = lax.axis_index("fsdp")
        me = c * 4 + f
        barrier = pltpu.get_barrier_semaphore()

        def greet(step, carry):
            to = lax.rem(me + step, 32)
            pl.semaphore_signal(barrier, inc=1, device_id=(to // 4, to % 4), device_id_type=MESH_ID)
            return carry

        lax.fori_loop(1, 32, greet, 0)
        pl.semaphore_wait(barrier, 31)
        lc = pltpu.make_async_copy(src, out.at[c, f], own_sem)
        lc.start()

        def copy(step):
            to = lax.rem(me + step, 32)
            return _remote(
                src, out.at[c, f], send_sem.at[step], recv_sem.at[step], (to // 4, to % 4)
            )

        def send(step, carry):
            copy(step).start()
            return carry

        lax.fori_loop(1, 32, send, 0)

        def done(step, carry):
            copy(step).wait_recv()
            copy(step).wait_send()
            return carry

        lax.fori_loop(1, 32, done, 0)
        lc.wait()

    return _comm_call(
        kernel,
        [piece],
        jax.ShapeDtypeStruct((8, 4) + piece.shape, piece.dtype),
        [pltpu.SemaphoreType.DMA(()), _sem(32), _sem(32)],
        cid,
        "gather_all",
    )


def dot(left, right):
    return jnp.dot(left, right, preferred_element_type=F32)


def dot_t(left, right):
    return lax.dot_general(left, right, (((1,), (1,)), ((), ())), preferred_element_type=F32)


def dot_rows(left, right):
    return lax.dot_general(left, right, (((0,), (0,)), ((), ())), preferred_element_type=F32)


def side_pad(value):
    return jnp.pad(value, ((0, 0), (0, SIDE - value.shape[1])))


def blocks(value):
    return value.reshape(2, 2, 2, 128, value.shape[-1])


def own_blocks(value):
    return value.reshape(2, 128, value.shape[-1])


def flat(value):
    return value.reshape(-1, value.shape[-1])


def slot_local(
    tokens,
    cotangent,
    lengths,
    slot_adapter_index,
    attention_norm_gain,
    feedforward_norm_gain,
    query_weight,
    key_weight,
    value_weight,
    output_weight,
    gate_weight,
    up_weight,
    down_weight,
    adapter_input_first,
    adapter_output_first,
    adapter_down_first,
    adapter_query_second,
    adapter_key_value_second,
    adapter_output_second,
    adapter_gate_up_second,
    adapter_down_second,
):
    width = tokens.shape[-1]
    hidden_units = gate_weight.shape[1]
    quarter = width // 4
    c = lax.axis_index("ctx")
    f = lax.axis_index("fsdp")
    x, core = f // 2, f % 2
    slot = c // 2 + 4 * (c % 2)
    length = lax.dynamic_slice_in_dim(lengths, slot, 1, 0)
    adapter = slot_adapter_index[slot]

    def pick(table):
        return lax.dynamic_index_in_dim(table, adapter, 0, keepdims=False)

    def cut(value, axis, size):
        return lax.dynamic_slice_in_dim(value, f * size, size, axis)

    first_in = pick(adapter_input_first)
    first_out = pick(adapter_output_first)
    first_down = pick(adapter_down_first)
    second_q = cut(pick(adapter_query_second), 1, query_weight.shape[1])
    second_kv = cut(pick(adapter_key_value_second), 2, key_weight.shape[1])
    second_o = pick(adapter_output_second)
    second_gu = cut(pick(adapter_gate_up_second), 2, hidden_units)
    second_d = pick(adapter_down_second)
    first_o_own = cut(first_out, 0, output_weight.shape[0])
    first_d_own = cut(first_down, 0, hidden_units)

    def pad_turned(w):
        rows = w.shape[0]
        w = w.reshape(rows, -1, 2, HEAD_DIM // 2)
        w = jnp.pad(w, ((0, 0), (0, 0), (0, 0), (0, HALF_PAD - HEAD_DIM // 2)))
        return w.reshape(rows, -1)

    def pad_plain(w):
        rows = w.shape[0]
        w = w.reshape(rows, -1, HEAD_DIM)
        w = jnp.pad(w, ((0, 0), (0, 0), (0, PAD_HEAD - HEAD_DIM)))
        return w.reshape(rows, -1)

    def unpad_turned(g):
        rows = g.shape[0]
        return g.reshape(rows, -1, 2, HALF_PAD)[..., : HEAD_DIM // 2].reshape(rows, -1)

    def unpad_plain(g):
        rows = g.shape[0]
        return g.reshape(rows, -1, PAD_HEAD)[..., :HEAD_DIM].reshape(rows, -1)

    weight_all = jnp.concatenate(
        [pad_turned(query_weight), pad_turned(key_weight), pad_plain(value_weight)], axis=1
    )
    zero_q = jnp.zeros((RANK, 4 * PAD_HEAD), BF16)
    zero_k = jnp.zeros((RANK, 2 * PAD_HEAD), BF16)
    second_all = jnp.concatenate(
        [
            jnp.concatenate([pad_turned(second_q), zero_k, zero_k], axis=1),
            jnp.concatenate([zero_q, pad_turned(second_kv[0]), zero_k], axis=1),
            jnp.concatenate([zero_q, zero_k, pad_plain(second_kv[1])], axis=1),
        ],
        axis=0,
    )
    first_all = jnp.concatenate([first_in[0], first_in[1], first_in[2]], axis=1)
    first_gu = jnp.concatenate([first_in[3], first_in[4]], axis=1)

    half = HEAD_DIM // 2
    rows = 4 * 2 * tokens.shape[1]
    freqs = ROPE_BASE ** (-(jnp.arange(half, dtype=F32) * 2.0 / HEAD_DIM))
    angles = jnp.arange(rows, dtype=jnp.int32).astype(F32)[:, None] * freqs[None, :]
    gap = jnp.zeros((rows, HALF_PAD - half), F32)
    cos, sin = jnp.cos(angles), jnp.sin(angles)
    cosine = jnp.concatenate([cos, gap, cos, gap], axis=1)
    sine = jnp.concatenate([-sin, gap, sin, gap], axis=1)

    tok_own, cot_own, tok_all, cot_all = take_in(tokens, cotangent, 0)
    live_rows = (jnp.arange(rows, dtype=jnp.int32) < length[0])[:, None]
    block_of = x + 4 * (1 - core) + 2 * jnp.arange(2, dtype=jnp.int32)
    own_pos = (block_of[:, None] * 128 + jnp.arange(128, dtype=jnp.int32)[None, :]).reshape(-1)
    own_live = (own_pos < length[0])[:, None]
    grad_out = jnp.where(live_rows, flat(cot_all), jnp.zeros((), BF16))
    grad_out_own = jnp.where(own_live, flat(cot_own), jnp.zeros((), BF16))

    tokens_f = flat(tok_all).astype(F32)
    normed_one = (tokens_f * rms_factor(tokens_f) * attention_norm_gain).astype(BF16)
    inner_qkv = dot(normed_one, first_all).astype(BF16)
    proj = dot(normed_one, weight_all) + ADAPTER_SCALE * dot(inner_qkv, second_all)
    attn_b, qkv, stats = attend_call(proj, cosine, sine, length)

    sums, side = group_scatter(
        [
            blocks(dot(attn_b, output_weight).astype(BF16)),
            blocks(side_pad(dot(attn_b, first_o_own)).astype(BF16)),
        ],
        1,
        "scatter_o",
    )
    inner_o_own = flat(side)[:, :RANK].astype(BF16)
    own_f = flat(tok_own).astype(F32)
    resid = own_f + flat(sums) + ADAPTER_SCALE * dot(inner_o_own, second_o)
    factor_two = rms_factor(resid)
    normed_two_own = (resid * factor_two * feedforward_norm_gain).astype(BF16)
    normed_two, side_all = group_gather(
        [own_blocks(normed_two_own), own_blocks(side_pad(inner_o_own))], 2, "gather_two"
    )
    normed_two = flat(normed_two)
    inner_o = flat(side_all)[:, :RANK]

    inner_gu = dot(normed_two, first_gu).astype(BF16)
    gate = dot(normed_two, gate_weight) + ADAPTER_SCALE * dot(inner_gu[:, :RANK], second_gu[0])
    up_proj = dot(normed_two, up_weight) + ADAPTER_SCALE * dot(inner_gu[:, RANK:], second_gu[1])
    sigmoid_gate = jax.nn.sigmoid(gate)
    hidden = (gate * sigmoid_gate * up_proj).astype(BF16)
    grad_inner_d = (ADAPTER_SCALE * dot_t(grad_out, second_d)).astype(BF16)
    grad_hidden = dot_t(grad_out, down_weight) + dot_t(grad_inner_d, first_d_own)
    grad_gate = (grad_hidden * up_proj * sigmoid_gate * (1.0 + gate * (1.0 - sigmoid_gate))).astype(
        BF16
    )
    grad_up = (grad_hidden * gate * sigmoid_gate).astype(BF16)
    grad_two = (dot_t(grad_gate, gate_weight) + dot_t(grad_up, up_weight)).astype(BF16)
    side_gu = ADAPTER_SCALE * jnp.concatenate(
        [dot_t(grad_gate, second_gu[0]), dot_t(grad_up, second_gu[1])], axis=1
    )
    sums, side = group_scatter(
        [blocks(grad_two), blocks(side_pad(side_gu).astype(BF16))], 3, "scatter_two"
    )
    grad_inner_gu_own = flat(side)[:, : 2 * RANK].astype(BF16)
    grad_normed_two = (
        (flat(sums) + dot_t(grad_inner_gu_own, first_gu)).astype(BF16).astype(F32)
    )
    grad_resid = grad_out_own.astype(F32) + norm_back(
        resid, factor_two, feedforward_norm_gain, grad_normed_two
    )
    grad_low_own = grad_resid.astype(BF16)

    out_sums, out_side = group_scatter(
        [
            blocks(dot(hidden, down_weight).astype(BF16)),
            blocks(side_pad(dot(hidden, first_d_own)).astype(BF16)),
        ],
        4,
        "scatter_out",
    )
    inner_d_own = flat(out_side)[:, :RANK].astype(BF16)
    out_own = jnp.where(
        own_live, resid + flat(out_sums) + ADAPTER_SCALE * dot(inner_d_own, second_d), 0.0
    ).astype(BF16)

    grad_low, side_all = group_gather(
        [
            own_blocks(grad_low_own),
            own_blocks(side_pad(jnp.concatenate([grad_inner_gu_own, inner_d_own], axis=1))),
        ],
        5,
        "gather_resid",
    )
    grad_low = flat(grad_low)
    side_all = flat(side_all)
    grad_inner_gu = side_all[:, : 2 * RANK]
    inner_d = side_all[:, 2 * RANK : 3 * RANK]
    grad_inner_o = (ADAPTER_SCALE * dot_t(grad_low, second_o)).astype(BF16)
    grad_att = (dot_t(grad_low, output_weight) + dot_t(grad_inner_o, first_o_own)).astype(BF16)
    grad_qkv = attend_back_call(qkv, stats, grad_att, cosine, sine, length)
    grad_one = dot_t(grad_qkv, weight_all).astype(BF16)
    side_qkv = ADAPTER_SCALE * dot_t(grad_qkv, second_all)
    sums, side = group_scatter(
        [blocks(grad_one), blocks(side_pad(side_qkv).astype(BF16))], 6, "scatter_one"
    )
    grad_inner_own = flat(side)[:, : 3 * RANK].astype(BF16)
    grad_normed_one = (flat(sums) + dot_t(grad_inner_own, first_all)).astype(BF16).astype(F32)
    grad_tok_own = grad_resid + norm_back(
        own_f, rms_factor(own_f), attention_norm_gain, grad_normed_one
    )
    out_tokens, grad_tokens, side_all = give_back(
        [own_blocks(out_own), own_blocks(grad_tok_own.astype(BF16))],
        [own_blocks(side_pad(grad_inner_own))],
        7,
    )
    grad_inner_qkv = flat(side_all)[:, : 3 * RANK]

    one_cut = cut(normed_one, 1, quarter)
    two_cut = cut(normed_two, 1, quarter)
    in_qkv = dot_rows(grad_inner_qkv, one_cut)
    in_gu = dot_rows(grad_inner_gu, two_cut)
    o_a = dot_rows(grad_inner_o, attn_b)
    d_a = dot_rows(grad_inner_d, hidden)
    all_b = ADAPTER_SCALE * dot_rows(inner_qkv, grad_qkv)
    q_b = unpad_turned(all_b[:RANK, : 4 * PAD_HEAD])
    k_b = unpad_turned(all_b[RANK : 2 * RANK, 4 * PAD_HEAD : 6 * PAD_HEAD])
    v_b = unpad_plain(all_b[2 * RANK :, 6 * PAD_HEAD :])
    o_b = ADAPTER_SCALE * dot_rows(inner_o, cut(grad_low, 1, quarter))
    g_b = ADAPTER_SCALE * dot_rows(inner_gu[:, :RANK], grad_gate)
    u_b = ADAPTER_SCALE * dot_rows(inner_gu[:, RANK:], grad_up)
    d_b = ADAPTER_SCALE * dot_rows(inner_d, cut(grad_out, 1, quarter))
    parts = [
        in_qkv[:RANK],
        in_qkv[RANK : 2 * RANK],
        in_qkv[2 * RANK :],
        in_gu[:RANK],
        in_gu[RANK:],
        o_a,
        d_a,
        q_b,
        k_b,
        v_b,
        o_b,
        g_b,
        u_b,
        d_b,
    ]
    gathered = gather_all(jnp.concatenate(parts, axis=1).astype(BF16), 8)
    group_slot = [cc // 2 + 4 * (cc % 2) for cc in range(8)]
    group_adapter = slot_adapter_index[jnp.array(group_slot, dtype=jnp.int32)]
    onehot = (
        group_adapter[:, None] == jnp.arange(adapter_input_first.shape[0], dtype=jnp.int32)[None, :]
    ).astype(BF16)
    tables = jnp.einsum("sa,sfrn->arfn", onehot, gathered, preferred_element_type=F32)
    full = []
    start = 0
    for part in parts:
        n = part.shape[1]
        full.append(tables[..., start : start + n].reshape(tables.shape[0], RANK, 4 * n))
        start += n
    turn = lambda t: jnp.swapaxes(t, 1, 2)
    return (
        out_tokens,
        grad_tokens.astype(F32),
        jnp.stack([turn(t) for t in full[:5]], axis=1),
        turn(full[5]),
        turn(full[6]),
        full[7],
        jnp.stack([full[8], full[9]], axis=1),
        full[10],
        jnp.stack([full[11], full[12]], axis=1),
        full[13],
    )


def solution(mesh):
    one_slot = mesh.shape["ctx"] == 8 and mesh.shape["fsdp"] == 4
    return jax.shard_map(
        slot_local if one_slot else local,
        mesh=mesh,
        in_specs=(
            P("fsdp", "ctx", None),
            P("fsdp", "ctx", None),
            P(),
            P(),
            P(),
            P(),
            P(None, "fsdp"),
            P(None, "fsdp"),
            P(None, "fsdp"),
            P("fsdp", None),
            P(None, "fsdp"),
            P(None, "fsdp"),
            P("fsdp", None),
            P(),
            P(),
            P(),
            P(),
            P(),
            P(),
            P(),
            P(),
        ),
        out_specs=(
            P("fsdp", "ctx", None),
            P("fsdp", "ctx", None),
            P(),
            P(),
            P(),
            P(),
            P(),
            P(),
            P(),
            P(),
        ),
        check_vma=False,
    )
```

```python
import math

import jax
import jax.numpy as jnp
from jax import lax
from jax.experimental import pallas as pl
from jax.experimental.pallas import tpu as pltpu
from jax.sharding import PartitionSpec as P

QUERY_HEADS = 16
KEY_VALUE_HEADS = 8
HEAD_DIM = 96


EPSILON = 1e-05
NEGATIVE = -1e30
ADAPTER_SCALE = 0.5
ROPE_BASE = 100000.0


def from_behind(x, axis, by):
    size = lax.axis_size(axis)
    return lax.ppermute(x, axis, [(i, (i + by) % size) for i in range(size)])


def rope_tables(positions, head_size):
    half_size = head_size // 2
    freqs = ROPE_BASE ** (-(jnp.arange(half_size, dtype=jnp.float32) * 2.0 / head_size))
    angles = positions.astype(jnp.float32)[:, None] * freqs[None, :]
    return (jnp.cos(angles)[:, None, :], jnp.sin(angles)[:, None, :])


def apply_rotation(values, cosine_table, sine_table):
    half_size = values.shape[-1] // 2
    first_half = values[..., :half_size]
    second_half = values[..., half_size:]
    return jnp.concatenate(
        [
            first_half * cosine_table - second_half * sine_table,
            second_half * cosine_table + first_half * sine_table,
        ],
        axis=-1,
    )


def rotate_back(gradient_tree, cosine_table, sine_table):
    half_size = gradient_tree.shape[-1] // 2
    first_half = gradient_tree[..., :half_size]
    second_half = gradient_tree[..., half_size:]
    return jnp.concatenate(
        [
            first_half * cosine_table + second_half * sine_table,
            second_half * cosine_table - first_half * sine_table,
        ],
        axis=-1,
    )


def rms_factor(values):
    return lax.rsqrt(jnp.mean(values * values, axis=-1, keepdims=True) + EPSILON)


def norm_back(values, factor, gain, grad_norm):
    scaled = grad_norm * gain
    return factor * scaled - values * factor**3 * jnp.mean(scaled * values, axis=-1, keepdims=True)


def pick_rows(onehot, table):
    return jnp.einsum("sa,a...->s...", onehot, table, preferred_element_type=jnp.float32).astype(
        jnp.bfloat16
    )


def spread_rows(onehot, gradient_tree):
    return jnp.einsum("sa,s...->a...", onehot, gradient_tree, precision=lax.Precision.HIGHEST)


def direct_product(input_rows, weight_matrix):
    return jnp.einsum("std,do->sto", input_rows, weight_matrix, preferred_element_type=jnp.float32)


def direct_back(gradient_tree, weight_matrix):
    return jnp.einsum(
        "sto,do->std", gradient_tree, weight_matrix, preferred_element_type=jnp.float32
    )


def inner_product_part(input_rows, down):
    return jnp.einsum("std,sdr->str", input_rows, down, preferred_element_type=jnp.float32)


def inner_back(gradient_tree, upward_rows):
    return ADAPTER_SCALE * jnp.einsum(
        "sto,sro->str", gradient_tree, upward_rows, preferred_element_type=jnp.float32
    )


def through_down(grad_inner, down):
    return jnp.einsum("str,sdr->std", grad_inner, down, preferred_element_type=jnp.float32)


def down_grad(input_rows, grad_inner):
    return jnp.einsum("std,str->sdr", input_rows, grad_inner, preferred_element_type=jnp.float32)


def upward_grad(inner_rows, gradient_tree):
    return ADAPTER_SCALE * jnp.einsum(
        "jvp,jvx->jpx", inner_rows, gradient_tree, preferred_element_type=jnp.float32
    )


def upward_apply(inner_rows, upward_rows):
    return ADAPTER_SCALE * jnp.einsum(
        "str,sro->sto", inner_rows, upward_rows, preferred_element_type=jnp.float32
    )


def project(input_rows, weight_matrix, down, upward_rows):
    inner_rows = inner_product_part(input_rows, down).astype(jnp.bfloat16)
    return (
        inner_rows,
        direct_product(input_rows, weight_matrix) + upward_apply(inner_rows, upward_rows),
    )


def project_back(input_rows, grad_output, weight_matrix, down, upward_rows, inner_rows):
    grad_upward = upward_grad(inner_rows, grad_output)
    grad_inner = inner_back(grad_output, upward_rows).astype(jnp.bfloat16)
    grad_down = down_grad(input_rows, grad_inner)
    grad_inputs = direct_back(grad_output, weight_matrix) + through_down(grad_inner, down)
    return (grad_inputs, grad_down, grad_upward)


def allowed_mask(key_start, key_count, query_pos, lengths):
    key_pos = key_start + jnp.arange(key_count, dtype=jnp.int32)
    causal = key_pos[None, :] <= query_pos[:, None]
    live = key_pos[None, :] < lengths[:, None]
    return (causal[None, :, :] & live[:, None, :])[:, None, None, :, :]


def attend_block(state, key_block, value_block, key_start, query_head_rows, query_pos, lengths):
    run_max, run_sum, run_acc = state
    scale = query_head_rows.shape[-1] ** (-0.5)
    scores = (
        jnp.einsum(
            "sqhgd,skhd->shgqk", query_head_rows, key_block, preferred_element_type=jnp.float32
        )
        * scale
    )
    allowed = allowed_mask(key_start, key_block.shape[1], query_pos, lengths)
    new_max = jnp.maximum(run_max, jnp.max(jnp.where(allowed, scores, NEGATIVE), axis=-1))
    weights = jnp.where(allowed, jnp.exp(scores - new_max[..., None]), 0.0)
    factor = jnp.exp(run_max - new_max)
    new_sum = run_sum * factor + jnp.sum(weights, axis=-1)
    update = jnp.einsum(
        "shgqk,skhd->shgqd",
        weights.astype(jnp.bfloat16),
        value_block,
        preferred_element_type=jnp.float32,
    )
    return (new_max, new_sum, run_acc * factor[..., None] + update)


def attend_back(
    key_block,
    value_block,
    key_start,
    query_head_rows,
    grad_heads,
    log_total,
    row_dot,
    query_pos,
    lengths,
):
    scale = query_head_rows.shape[-1] ** (-0.5)
    scores = (
        jnp.einsum(
            "sqhgd,skhd->shgqk", query_head_rows, key_block, preferred_element_type=jnp.float32
        )
        * scale
    )
    allowed = allowed_mask(key_start, key_block.shape[1], query_pos, lengths)
    probs = jnp.where(allowed, jnp.exp(scores - log_total[..., None]), 0.0)
    grad_probs = jnp.einsum(
        "sqhgd,skhd->shgqk", grad_heads, value_block, preferred_element_type=jnp.float32
    )
    grad_scores = (probs * (grad_probs - row_dot[..., None])).astype(jnp.bfloat16)
    grad_query = scale * jnp.einsum(
        "shgqk,skhd->sqhgd", grad_scores, key_block, preferred_element_type=jnp.float32
    )
    grad_key = scale * jnp.einsum(
        "shgqk,sqhgd->skhd", grad_scores, query_head_rows, preferred_element_type=jnp.float32
    )
    grad_value = jnp.einsum(
        "shgqk,sqhgd->skhd",
        probs.astype(jnp.bfloat16),
        grad_heads,
        preferred_element_type=jnp.float32,
    )
    return (grad_query, grad_key, grad_value)


def attend_forward(query_head_rows, key_head_rows, value_head_rows, lengths_used, query_pos):
    slots, rows, kv_heads, group_size, head_size = query_head_rows.shape
    key_flat = key_head_rows.reshape(slots, rows, kv_heads * head_size)
    value_flat = value_head_rows.reshape(slots, rows, kv_heads * head_size)
    stat_shape = (slots, kv_heads, group_size, rows)
    initial = (
        jnp.full(stat_shape, NEGATIVE, jnp.float32),
        jnp.zeros(stat_shape, jnp.float32),
        jnp.zeros(stat_shape + (head_size,), jnp.float32),
    )
    part_keys = lax.all_gather(key_flat, "ctx", axis=1, tiled=True)
    part_values = lax.all_gather(value_flat, "ctx", axis=1, tiled=True)
    piece_rows = part_keys.shape[1]
    part_keys = part_keys.reshape(slots, piece_rows, kv_heads, head_size)
    part_values = part_values.reshape(slots, piece_rows, kv_heads, head_size)
    span_rows = math.gcd(piece_rows, 4 * rows)

    def inner_step(block_index, inner_state):
        sub_keys = lax.dynamic_slice_in_dim(part_keys, block_index * span_rows, span_rows, 1)
        sub_values = lax.dynamic_slice_in_dim(part_values, block_index * span_rows, span_rows, 1)
        return attend_block(
            inner_state,
            sub_keys,
            sub_values,
            block_index * span_rows,
            query_head_rows,
            query_pos,
            lengths_used,
        )

    run_max, run_sum, run_acc = lax.fori_loop(0, piece_rows // span_rows, inner_step, initial)
    log_total = run_max + jnp.log(run_sum)
    attended = jnp.transpose(run_acc / run_sum[..., None], (0, 3, 1, 2, 4))
    return (attended, log_total)


def attend_backward(
    query_head_rows,
    key_head_rows,
    value_head_rows,
    grad_heads,
    attended,
    log_total,
    lengths_used,
    query_pos,
):
    ctx_count = lax.axis_size("ctx")
    own_index = lax.axis_index("ctx")
    rows = query_head_rows.shape[1]
    row_dot = jnp.transpose(
        jnp.sum(grad_heads.astype(jnp.float32) * attended, axis=-1), (0, 2, 3, 1)
    )

    def cycle_step(step_index, carried):
        carried_keys, carried_values, grad_query, grad_key, grad_value = carried
        block_id = (own_index + step_index) % ctx_count
        query_part, key_part, value_part = attend_back(
            carried_keys,
            carried_values,
            block_id * rows,
            query_head_rows,
            grad_heads,
            log_total,
            row_dot,
            query_pos,
            lengths_used,
        )
        grad_key, grad_value = (
            from_behind((grad_key + key_part).astype(jnp.bfloat16), "ctx", -1).astype(jnp.float32),
            from_behind((grad_value + value_part).astype(jnp.bfloat16), "ctx", -1).astype(
                jnp.float32
            ),
        )
        carried_keys, carried_values = from_behind((carried_keys, carried_values), "ctx", -1)
        return (carried_keys, carried_values, grad_query + query_part, grad_key, grad_value)

    key_zeros = jnp.zeros(key_head_rows.shape, jnp.float32)
    start_state = (
        key_head_rows,
        value_head_rows,
        jnp.zeros(query_head_rows.shape, jnp.float32),
        key_zeros,
        key_zeros,
    )
    carried = lax.fori_loop(0, ctx_count, cycle_step, start_state)
    return (carried[2], carried[3], carried[4])


def table_total(rotation_tables):
    return lax.psum(rotation_tables, ("ctx", "fsdp"))


def local(
    tokens,
    cotangent,
    lengths,
    slot_adapter_index,
    attention_norm_gain,
    feedforward_norm_gain,
    query_weight,
    key_weight,
    value_weight,
    output_weight,
    gate_weight,
    up_weight,
    down_weight,
    adapter_input_first,
    adapter_output_first,
    adapter_down_first,
    adapter_query_second,
    adapter_key_value_second,
    adapter_output_second,
    adapter_gate_up_second,
    adapter_down_second,
):
    slot_count, tok_rows, model_width = tokens.shape
    head_groups = QUERY_HEADS // KEY_VALUE_HEADS
    own_index = lax.axis_index("ctx")
    fsdp_index = lax.axis_index("fsdp")
    query_pos = own_index * tok_rows + jnp.arange(tok_rows, dtype=jnp.int32)
    cosine_table, sine_table = rope_tables(query_pos, HEAD_DIM)
    own_lengths = lax.dynamic_slice_in_dim(lengths, fsdp_index * slot_count, slot_count, 0)
    own_adapters = lax.dynamic_slice_in_dim(
        slot_adapter_index, fsdp_index * slot_count, slot_count, 0
    )
    valid = query_pos[None, :] < own_lengths[:, None]
    adapter_labels = jnp.arange(adapter_input_first.shape[0], dtype=jnp.int32)
    onehot_own = own_adapters[:, None] == adapter_labels[None, :]
    owned_low_rank = onehot_own.astype(jnp.bfloat16)
    own_full = onehot_own.astype(jnp.float32)
    tokens_f = tokens.astype(jnp.float32)
    factor_one = rms_factor(tokens_f)
    normed_one = (tokens_f * factor_one * attention_norm_gain).astype(jnp.bfloat16)
    grad_out = jnp.where(valid[..., None], cotangent, jnp.zeros((), jnp.bfloat16))
    input_first = pick_rows(owned_low_rank, adapter_input_first)
    output_second = pick_rows(owned_low_rank, adapter_output_second)
    down_second = pick_rows(owned_low_rank, adapter_down_second)
    output_first = pick_rows(owned_low_rank, adapter_output_first)
    down_first = pick_rows(owned_low_rank, adapter_down_first)
    query_second = pick_rows(owned_low_rank, adapter_query_second)
    key_value_second = pick_rows(owned_low_rank, adapter_key_value_second)
    gate_up_second = pick_rows(owned_low_rank, adapter_gate_up_second)
    weight_q, weight_k, weight_v, weight_gate, weight_up, weight_o, weight_down = (
        lax.all_gather(query_weight, "fsdp", axis=1, tiled=True),
        lax.all_gather(key_weight, "fsdp", axis=1, tiled=True),
        lax.all_gather(value_weight, "fsdp", axis=1, tiled=True),
        lax.all_gather(gate_weight, "fsdp", axis=1, tiled=True),
        lax.all_gather(up_weight, "fsdp", axis=1, tiled=True),
        lax.all_gather(output_weight, "fsdp", axis=0, tiled=True),
        lax.all_gather(down_weight, "fsdp", axis=0, tiled=True),
    )
    inner_q, projected_queries = project(normed_one, weight_q, input_first[:, 0], query_second)
    inner_k, projected_keys = project(
        normed_one, weight_k, input_first[:, 1], key_value_second[:, 0]
    )
    inner_v, projected_values = project(
        normed_one, weight_v, input_first[:, 2], key_value_second[:, 1]
    )
    query_head_rows = apply_rotation(
        projected_queries.reshape(slot_count, tok_rows, -1, HEAD_DIM), cosine_table, sine_table
    ).astype(jnp.bfloat16)
    query_head_rows = query_head_rows.reshape(slot_count, tok_rows, -1, head_groups, HEAD_DIM)
    key_head_rows = apply_rotation(
        projected_keys.reshape(slot_count, tok_rows, -1, HEAD_DIM), cosine_table, sine_table
    ).astype(jnp.bfloat16)
    value_head_rows = projected_values.astype(jnp.bfloat16).reshape(
        slot_count, tok_rows, -1, HEAD_DIM
    )
    attended, log_total = attend_forward(
        query_head_rows, key_head_rows, value_head_rows, own_lengths, query_pos
    )
    attn_b = attended.reshape(slot_count, tok_rows, -1).astype(jnp.bfloat16)
    inner_o, proj_o = project(attn_b, weight_o, output_first, output_second)
    resid = tokens_f + proj_o
    factor_two = rms_factor(resid)
    normed_two = (resid * factor_two * feedforward_norm_gain).astype(jnp.bfloat16)
    inner_gate, gate = project(normed_two, weight_gate, input_first[:, 3], gate_up_second[:, 0])
    inner_up, up_proj = project(normed_two, weight_up, input_first[:, 4], gate_up_second[:, 1])
    sigmoid_gate = jax.nn.sigmoid(gate)
    hidden = (gate * sigmoid_gate * up_proj).astype(jnp.bfloat16)
    inner_down, proj_down = project(hidden, weight_down, down_first, down_second)
    out_tokens = jnp.where(valid[..., None], resid + proj_down, 0.0).astype(jnp.bfloat16)
    grad_hidden, grad_da, grad_db = project_back(
        hidden, grad_out, weight_down, down_first, down_second, inner_down
    )
    grad_gate = (grad_hidden * up_proj * sigmoid_gate * (1.0 + gate * (1.0 - sigmoid_gate))).astype(
        jnp.bfloat16
    )
    grad_up = (grad_hidden * gate * sigmoid_gate).astype(jnp.bfloat16)
    from_gate, grad_ga, grad_gb = project_back(
        normed_two, grad_gate, weight_gate, input_first[:, 3], gate_up_second[:, 0], inner_gate
    )
    from_up, grad_ua, grad_ub = project_back(
        normed_two, grad_up, weight_up, input_first[:, 4], gate_up_second[:, 1], inner_up
    )
    grad_normed_two = (from_gate + from_up).astype(jnp.bfloat16).astype(jnp.float32)
    grad_resid = grad_out.astype(jnp.float32) + norm_back(
        resid, factor_two, feedforward_norm_gain, grad_normed_two
    )
    grad_resid_low = grad_resid.astype(jnp.bfloat16)
    from_attn, grad_oa, grad_ob = project_back(
        attn_b, grad_resid_low, weight_o, output_first, output_second, inner_o
    )
    grad_heads = from_attn.astype(jnp.bfloat16).reshape(attended.shape)
    grad_query, grad_key, grad_value = attend_backward(
        query_head_rows,
        key_head_rows,
        value_head_rows,
        grad_heads,
        attended,
        log_total,
        own_lengths,
        query_pos,
    )
    grad_proj_q = (
        rotate_back(
            grad_query.reshape(slot_count, tok_rows, -1, HEAD_DIM), cosine_table, sine_table
        )
        .astype(jnp.bfloat16)
        .reshape(slot_count, tok_rows, -1)
    )
    grad_proj_k = (
        rotate_back(grad_key, cosine_table, sine_table)
        .astype(jnp.bfloat16)
        .reshape(slot_count, tok_rows, -1)
    )
    grad_proj_v = grad_value.astype(jnp.bfloat16).reshape(slot_count, tok_rows, -1)
    from_query, grad_qa, grad_qb = project_back(
        normed_one, grad_proj_q, weight_q, input_first[:, 0], query_second, inner_q
    )
    from_key, grad_ka, grad_kb = project_back(
        normed_one, grad_proj_k, weight_k, input_first[:, 1], key_value_second[:, 0], inner_k
    )
    from_value, grad_va, grad_vb = project_back(
        normed_one, grad_proj_v, weight_v, input_first[:, 2], key_value_second[:, 1], inner_v
    )
    grad_normed_one = (from_query + from_key + from_value).astype(jnp.bfloat16).astype(jnp.float32)
    grad_tokens = grad_resid + norm_back(tokens_f, factor_one, attention_norm_gain, grad_normed_one)
    slot_grads = (
        jnp.stack([grad_qa, grad_ka, grad_va, grad_ga, grad_ua], axis=1),
        grad_oa,
        grad_da,
        grad_qb,
        jnp.stack([grad_kb, grad_vb], axis=1),
        grad_ob,
        jnp.stack([grad_gb, grad_ub], axis=1),
        grad_db,
    )
    summed = table_total(tuple((spread_rows(own_full, entry_item) for entry_item in slot_grads)))
    return (
        out_tokens,
        grad_tokens,
        summed[0],
        summed[1],
        summed[2],
        summed[3],
        summed[4],
        summed[5],
        summed[6],
        summed[7],
    )


BF16 = jnp.bfloat16
F32 = jnp.float32
MESH_ID = pl.DeviceIdType.MESH
RANK = 16
SIDE = 128
PAD_HEAD = 128
HALF_PAD = 64


def _sem(count):
    return pltpu.SemaphoreType.DMA((count,))


def _place():
    c = lax.axis_index("ctx")
    f = lax.axis_index("fsdp")
    x = f // 2
    core = f % 2
    return c, f, x, core, (c, 2 * x + 1 - core), (c, 2 * (1 - x) + core)


def _greet(targets):
    barrier = pltpu.get_barrier_semaphore()
    for target in targets:
        pl.semaphore_signal(barrier, inc=1, device_id=target, device_id_type=MESH_ID)
    pl.semaphore_wait(barrier, len(targets))


def _remote(src, dst, send, recv, target):
    return pltpu.make_async_remote_copy(
        src_ref=src, dst_ref=dst, send_sem=send, recv_sem=recv, device_id=target, device_id_type=MESH_ID
    )


def _comm_call(kernel, ins, outs, scratch, cid, name, in_space=pl.ANY, out_space=pl.ANY, vmem=None):
    return pl.pallas_call(
        kernel,
        out_shape=outs,
        in_specs=[pl.BlockSpec(memory_space=in_space)] * len(ins),
        out_specs=jax.tree.map(lambda _: pl.BlockSpec(memory_space=out_space), outs),
        scratch_shapes=scratch,
        compiler_params=pltpu.CompilerParams(
            collective_id=cid, has_side_effects=True, vmem_limit_bytes=vmem
        ),
        name=name,
    )(*ins)


def _gather_steps(ins, outs, own_sem, send_sem, recv_sem, place):
    c, f, x, core, core_peer, x_peer = place
    h = 1 - core
    count = len(ins)
    local = []
    sends = []

    def first():
        for base, target in ((0, x_peer), (2 * count, core_peer)):
            for i in range(count):
                for j in range(2):
                    k = base + i * 2 + j
                    cp = _remote(
                        ins[i].at[j], outs[i].at[h, j, x], send_sem.at[k], recv_sem.at[k], target
                    )
                    cp.start()
                    sends.append(cp)
        for i in range(count):
            for j in range(2):
                lc = pltpu.make_async_copy(
                    ins[i].at[j], outs[i].at[h, j, x], own_sem.at[i * 2 + j]
                )
                lc.start()
                local.append(lc)

    def last():
        forwards = []
        for i in range(count):
            for j in range(2):
                k = i * 2 + j
                sends[k].wait_recv()
                cp = _remote(
                    outs[i].at[h, j, 1 - x],
                    outs[i].at[h, j, 1 - x],
                    send_sem.at[4 * count + k],
                    recv_sem.at[4 * count + k],
                    core_peer,
                )
                cp.start()
                forwards.append(cp)
        for k in range(2 * count):
            sends[2 * count + k].wait_recv()
            forwards[k].wait_recv()
        for cp in sends + forwards:
            cp.wait_send()
        for lc in local:
            lc.wait()

    return first, last


def _gather_body(*args):
    first, last = _gather_steps(*args)
    first()
    last()


def _ctx_body(piece, out, own_sem, send_sem, recv_sem, place):
    c, f, x, core, core_peer, x_peer = place
    z, y = c // 2, c % 2
    lc = pltpu.make_async_copy(piece, out.at[c, x, core], own_sem)
    lc.start()
    cross = _remote(piece, out.at[c, x, core], send_sem.at[0], recv_sem.at[0], x_peer)
    cross.start()

    def start():
        lc.wait()
        cross.wait_recv()
        sends = []
        for step in range(1, 4):
            cp = _remote(
                out.at[c, :, core],
                out.at[c, :, core],
                send_sem.at[step],
                recv_sem.at[step],
                (2 * ((z + step) % 4) + y, f),
            )
            cp.start()
            sends.append(cp)
        cp = _remote(
            out.at[c, :, core],
            out.at[c, :, core],
            send_sem.at[4],
            recv_sem.at[4],
            (2 * z + 1 - y, f),
        )
        cp.start()
        ys = [cp]
        return sends, ys

    def forward(state):
        sends, ys = state
        for step in range(1, 4):
            sends[step - 1].wait_recv()
            origin = 2 * ((z + 4 - step) % 4) + y
            cp = _remote(
                out.at[origin, :, core],
                out.at[origin, :, core],
                send_sem.at[4 + step],
                recv_sem.at[4 + step],
                (2 * z + 1 - y, f),
            )
            cp.start()
            ys.append(cp)
        return sends, ys

    def finish(state):
        sends, ys = state
        last = []

        def share(k, origin):
            cp = _remote(
                out.at[origin, :, core],
                out.at[origin, :, core],
                send_sem.at[8 + k],
                recv_sem.at[8 + k],
                core_peer,
            )
            cp.start()
            last.append(cp)

        share(0, c)
        for step in range(1, 4):
            share(step, 2 * ((z + 4 - step) % 4) + y)
        for step in range(4):
            ys[step].wait_recv()
            share(4 + step, 2 * ((z + 4 - step) % 4) + 1 - y)
        for cp in last:
            cp.wait_recv()
        for cp in [cross] + sends + ys + last:
            cp.wait_send()

    return start, forward, finish


def _ctx_peers(place):
    c, f, x, core, core_peer, x_peer = place
    z, y = c // 2, c % 2
    return [(2 * ((z + step) % 4) + y, f) for step in range(1, 4)] + [(2 * z + 1 - y, f)]


def _ctx_out(piece):
    return jax.ShapeDtypeStruct((8, 2, 2) + piece.shape, piece.dtype)


CTX_SEMS = [pltpu.SemaphoreType.DMA(()), _sem(16), _sem(16)]


def group_gather(array, piece, cid, name):
    def kernel(own, piece_in, whole, spread, own_sem, send_sem, recv_sem, *ctx_sems):
        place = _place()
        _greet([place[4], place[5]] + _ctx_peers(place))
        start, forward, finish = _ctx_body(piece_in, spread, *ctx_sems, place)
        first, last = _gather_steps([own], [whole], own_sem, send_sem, recv_sem, place)
        first()
        state = forward(start())
        last()
        finish(state)

    outs = [jax.ShapeDtypeStruct((2, 2, 2) + array.shape[1:], array.dtype), _ctx_out(piece)]
    return _comm_call(
        kernel, [array, piece], outs, [_sem(2), _sem(6), _sem(6)] + CTX_SEMS, cid, name
    )


def plain_gather(array, cid, name):
    def kernel(own, whole, own_sem, send_sem, recv_sem):
        place = _place()
        _greet([place[4], place[5]])
        _gather_body([own], [whole], own_sem, send_sem, recv_sem, place)

    outs = [jax.ShapeDtypeStruct((2, 2, 2) + array.shape[1:], array.dtype)]
    return _comm_call(kernel, [array], outs, [_sem(2), _sem(6), _sem(6)], cid, name)[0]


def group_scatter(main, side, cid, name, piece=None):
    spread = piece is not None

    def kernel(*refs):
        main_in, side_in = refs[:2]
        refs = refs[2:]
        if spread:
            piece_in, refs = refs[0], refs[1:]
        sums, side_all = refs[:2]
        refs = refs[2:]
        if spread:
            spread_out, refs = refs[0], refs[1:]
        first, staged, second, side_first, side_staged, side_second, side_own = refs[:7]
        send_sem, recv_sem, gsend_sem, grecv_sem, gown_sem = refs[7:12]
        place = _place()
        c, f, x, core, core_peer, x_peer = place
        h = 1 - core
        _greet([core_peer, x_peer] + (_ctx_peers(place) if spread else []))
        if spread:
            start, forward, finish = _ctx_body(piece_in, spread_out, *refs[12:], place)
        group = (
            (side_in, side_first, side_staged, side_second),
            (main_in, first, staged, second),
        )
        one, two = {}, {}
        for i, (src, land, _, _) in enumerate(group):
            for far in (1, 0):
                for j in range(2):
                    k = (i * 2 + j) * 2 + far
                    cp = _remote(
                        src.at[1 - h, j, 1 - x if far else x],
                        land.at[far, j],
                        send_sem.at[k],
                        recv_sem.at[k],
                        core_peer,
                    )
                    cp.start()
                    one[(i, j, far)] = cp
        for i, (src, land, stage, land_two) in enumerate(group):
            for j in range(2):
                one[(i, j, 1)].wait_recv()
                stage[j] = (src[h, j, 1 - x].astype(F32) + land[1, j].astype(F32)).astype(BF16)
                k = 8 + i * 2 + j
                cp = _remote(stage.at[j], land_two.at[j], send_sem.at[k], recv_sem.at[k], x_peer)
                cp.start()
                two[(i, j)] = cp
        if spread:
            state = start()
        for j in range(2):
            one[(0, j, 0)].wait_recv()
            two[(0, j)].wait_recv()
            side_own[j] = (
                side_in[h, j, x].astype(F32)
                + side_first[0, j].astype(F32)
                + side_second[j].astype(F32)
            ).astype(BF16)
        gfirst, glast = _gather_steps([side_own], [side_all], gown_sem, gsend_sem, grecv_sem, place)
        gfirst()
        for j in range(2):
            one[(1, j, 0)].wait_recv()
            sums[j] = main_in[h, j, x].astype(F32) + first[0, j].astype(F32)
        if spread:
            state = forward(state)
        glast()
        for j in range(2):
            two[(1, j)].wait_recv()
            sums[j] = sums[j] + second[j].astype(F32)
        if spread:
            finish(state)
        for cp in list(one.values()) + list(two.values()):
            cp.wait_send()

    vmem, hbm = pl.BlockSpec(memory_space=pltpu.VMEM), pl.BlockSpec(memory_space=pl.ANY)
    outs = [
        jax.ShapeDtypeStruct((2,) + main.shape[3:], F32),
        jax.ShapeDtypeStruct(side.shape, BF16),
    ]
    scratch = []
    for rows in (main.shape[3:], side.shape[3:]):
        scratch += [
            pltpu.VMEM((2, 2) + rows, BF16),
            pltpu.VMEM((2,) + rows, BF16),
            pltpu.VMEM((2,) + rows, BF16),
        ]
    scratch += [pltpu.VMEM((2,) + side.shape[3:], BF16)]
    scratch += [_sem(12), _sem(12), _sem(6), _sem(6), _sem(2)]
    ins, in_specs, out_specs = [main, side], [vmem, vmem], [vmem, vmem]
    if spread:
        ins += [piece]
        in_specs += [hbm]
        out_specs += [hbm]
        outs += [_ctx_out(piece)]
        scratch += CTX_SEMS
    return pl.pallas_call(
        kernel,
        out_shape=outs,
        in_specs=in_specs,
        out_specs=out_specs,
        scratch_shapes=scratch,
        compiler_params=pltpu.CompilerParams(
            collective_id=cid, has_side_effects=True, vmem_limit_bytes=40 * 1024 * 1024
        ),
        name=name,
    )(*ins)


def take_in(tokens, cotangent, cid):
    def kernel(tok, cot, tok_own, cot_own, tok_all, land_s, land_r, own_sem, send_sem, recv_sem):
        place = _place()
        c, f, x, core, core_peer, x_peer = place
        h = 1 - core
        slot = c // 2 + 4 * (c % 2)
        barrier = pltpu.get_barrier_semaphore()
        for j in range(2):
            pl.semaphore_signal(
                barrier, inc=1, device_id=(x + 2 * j + 4 * h, slot // 2), device_id_type=MESH_ID
            )
        for target in (core_peer, x_peer):
            pl.semaphore_signal(barrier, inc=1, device_id=target, device_id_type=MESH_ID)
        pl.semaphore_wait(barrier, 4)
        to_f = 2 * (c % 2) + 1 - c // 4
        to_j = (c // 2) % 2
        moves = []
        for a, (src, dst) in enumerate(((tok, tok_own), (cot, cot_own))):
            for half in range(2):
                s = 2 * f + half
                to_c = (s % 4) * 2 + s // 4
                cp = _remote(
                    src.at[half],
                    dst.at[to_j],
                    land_s.at[2 * a + half],
                    land_r.at[2 * a + to_j],
                    (to_c, to_f),
                )
                cp.start()
                moves.append(cp)
        for j in range(2):
            pltpu.make_async_copy(tok_own.at[j], tok_own.at[j], land_r.at[j]).wait()
        _gather_body([tok_own], [tok_all], own_sem, send_sem, recv_sem, place)
        for j in range(2):
            pltpu.make_async_copy(cot_own.at[j], cot_own.at[j], land_r.at[2 + j]).wait()
        for cp in moves:
            cp.wait_send()

    own = jax.ShapeDtypeStruct(tokens.shape, tokens.dtype)
    whole = jax.ShapeDtypeStruct((2, 2, 2) + tokens.shape[1:], tokens.dtype)
    return _comm_call(
        kernel,
        [tokens, cotangent],
        [own, own, whole],
        [_sem(4), _sem(4), _sem(2), _sem(6), _sem(6)],
        cid,
        "take_in",
    )


def _back_steps(src, dst, out_s, out_r, place):
    c, f, x, core, core_peer, x_peer = place
    h = 1 - core
    slot = c // 2 + 4 * (c % 2)
    place_in = slot % 2
    moves = []

    def first():
        for j in range(2):
            cp = _remote(
                src.at[j],
                dst.at[place_in],
                out_s.at[j],
                out_r.at[place_in],
                (x + 2 * j + 4 * h, slot // 2),
            )
            cp.start()
            moves.append(cp)

    def last():
        for half in range(2):
            pltpu.make_async_copy(dst.at[half], dst.at[half], out_r.at[half]).wait()
        for cp in moves:
            cp.wait_send()

    return first, last


def _back_sources(place):
    c, f = place[:2]
    from_f = 2 * (c % 2) + 1 - c // 4
    return [(((2 * f + half) % 4) * 2 + (2 * f + half) // 4, from_f) for half in range(2)]


def give_back(array, piece, cid):
    def kernel(own, piece_in, out, spread, out_s, out_r, *ctx_sems):
        place = _place()
        _greet(_back_sources(place) + [place[4], place[5]] + _ctx_peers(place))
        start, forward, finish = _ctx_body(piece_in, spread, *ctx_sems, place)
        first, last = _back_steps(own, out, out_s, out_r, place)
        state = start()
        first()
        finish(forward(state))
        last()

    outs = [jax.ShapeDtypeStruct(array.shape, array.dtype), _ctx_out(piece)]
    return _comm_call(
        kernel, [array, piece], outs, [_sem(2), _sem(2)] + CTX_SEMS, cid, "give_back"
    )


def attend_call(proj, cosine, sine, length, behind, cid):
    rows = proj.shape[0]
    step = 256
    scale = HEAD_DIM ** (-0.5)
    lane = PAD_HEAD

    def kernel(
        len_ref,
        proj_ref,
        cos_ref,
        sin_ref,
        behind_ref,
        att_ref,
        qkv_ref,
        lse_ref,
        whole_ref,
        own_sem,
        send_sem,
        recv_sem,
    ):
        place = _place()
        _greet([place[4], place[5]])
        first, last = _gather_steps([behind_ref], [whole_ref], own_sem, send_sem, recv_sem, place)
        first()
        live = len_ref[0]
        for part in range(6):
            cols = slice(part * lane, (part + 1) * lane)
            v = proj_ref[:, cols]
            v = v * cos_ref[...] + pltpu.roll(v, HALF_PAD, 1) * sin_ref[...]
            qkv_ref[:, cols] = v.astype(BF16)
        qkv_ref[:, 6 * lane :] = proj_ref[:, 6 * lane :].astype(BF16)
        for block in range(rows // step):
            keys = (block + 1) * step
            row = pl.ds(block * step, step)
            qpos = block * step + lax.broadcasted_iota(jnp.int32, (step, keys), 0)
            kpos = lax.broadcasted_iota(jnp.int32, (step, keys), 1)
            allowed = (kpos <= qpos) & (kpos < live)
            pieces = []
            stats = jnp.zeros((step, lane), F32)
            lanes = lax.broadcasted_iota(jnp.int32, (step, lane), 1)
            for head in range(4):
                q = qkv_ref[row, head * lane : (head + 1) * lane]
                kv = head // 2
                k = qkv_ref[:keys, (4 + kv) * lane : (5 + kv) * lane]
                v = qkv_ref[:keys, (6 + kv) * lane : (7 + kv) * lane]
                s = lax.dot_general(q, k, (((1,), (1,)), ((), ())), preferred_element_type=F32)
                s = jnp.where(allowed, s * scale, NEGATIVE)
                top = jnp.max(s, axis=1, keepdims=True)
                p = jnp.where(allowed, jnp.exp(s - top), 0.0)
                total = jnp.sum(p, axis=1, keepdims=True)
                o = jnp.dot(p.astype(BF16), v, preferred_element_type=F32) / total
                pieces.append(o[:, :HEAD_DIM])
                stats = jnp.where(lanes == head, top + jnp.log(total), stats)
            att_ref[row, :] = jnp.concatenate(pieces, axis=1).astype(BF16)
            lse_ref[row, :] = stats
        last()

    vmem, hbm = pl.BlockSpec(memory_space=pltpu.VMEM), pl.BlockSpec(memory_space=pl.ANY)
    return pl.pallas_call(
        kernel,
        out_shape=(
            jax.ShapeDtypeStruct((rows, 4 * HEAD_DIM), BF16),
            jax.ShapeDtypeStruct(proj.shape, BF16),
            jax.ShapeDtypeStruct((rows, lane), F32),
            jax.ShapeDtypeStruct((2, 2, 2) + behind.shape[1:], behind.dtype),
        ),
        in_specs=[pl.BlockSpec(memory_space=pltpu.SMEM), vmem, vmem, vmem, hbm],
        out_specs=(vmem, vmem, vmem, hbm),
        scratch_shapes=[_sem(2), _sem(6), _sem(6)],
        compiler_params=pltpu.CompilerParams(
            collective_id=cid, has_side_effects=True, vmem_limit_bytes=40 * 1024 * 1024
        ),
        name="attend",
    )(length, proj, cosine, sine, behind)


def attend_back_call(qkv, stats, grad_att, cosine, sine, length, behind, cid):
    rows = qkv.shape[0]
    step = 256
    scale = HEAD_DIM ** (-0.5)
    lane = PAD_HEAD

    def kernel(
        len_ref,
        qkv_ref,
        lse_ref,
        g_ref,
        cos_ref,
        sin_ref,
        behind_ref,
        out_ref,
        back_ref,
        dk_ref,
        dv_ref,
        do_ref,
        out_s,
        out_r,
    ):
        place = _place()
        _greet(_back_sources(place))
        first, last = _back_steps(behind_ref, back_ref, out_s, out_r, place)
        first()
        live = len_ref[0]
        pad = jnp.zeros((rows, lane - HEAD_DIM), BF16)
        for head in range(4):
            do_ref[head] = jnp.concatenate(
                [g_ref[:, head * HEAD_DIM : (head + 1) * HEAD_DIM], pad], axis=1
            )
        dk_ref[...] = jnp.zeros_like(dk_ref)
        dv_ref[...] = jnp.zeros_like(dv_ref)
        for block in range(rows // step):
            keys = (block + 1) * step
            row = pl.ds(block * step, step)
            qpos = block * step + lax.broadcasted_iota(jnp.int32, (step, keys), 0)
            kpos = lax.broadcasted_iota(jnp.int32, (step, keys), 1)
            allowed = (kpos <= qpos) & (kpos < live)
            cos, sin = cos_ref[row, :], sin_ref[row, :]
            for head in range(4):
                kv = head // 2
                q = qkv_ref[row, head * lane : (head + 1) * lane]
                k = qkv_ref[:keys, (4 + kv) * lane : (5 + kv) * lane]
                v = qkv_ref[:keys, (6 + kv) * lane : (7 + kv) * lane]
                do = do_ref[head, row, :]
                s = lax.dot_general(q, k, (((1,), (1,)), ((), ())), preferred_element_type=F32)
                p = jnp.where(allowed, jnp.exp(s * scale - lse_ref[row, head : head + 1]), 0.0)
                dp = lax.dot_general(do, v, (((1,), (1,)), ((), ())), preferred_element_type=F32)
                dot = jnp.sum(p * dp, axis=1, keepdims=True)
                ds = (p * (dp - dot)).astype(BF16)
                dq = scale * jnp.dot(ds, k, preferred_element_type=F32)
                dq = dq * cos - pltpu.roll(dq, HALF_PAD, 1) * sin
                out_ref[row, head * lane : (head + 1) * lane] = dq.astype(BF16)
                dk_ref[kv, :keys] += lax.dot_general(
                    ds, q, (((0,), (0,)), ((), ())), preferred_element_type=F32
                )
                dv_ref[kv, :keys] += lax.dot_general(
                    p.astype(BF16), do, (((0,), (0,)), ((), ())), preferred_element_type=F32
                )
        for kv in range(2):
            dk = scale * dk_ref[kv]
            dk = dk * cos_ref[...] - pltpu.roll(dk, HALF_PAD, 1) * sin_ref[...]
            out_ref[:, (4 + kv) * lane : (5 + kv) * lane] = dk.astype(BF16)
            out_ref[:, (6 + kv) * lane : (7 + kv) * lane] = dv_ref[kv].astype(BF16)
        last()

    vmem, hbm = pl.BlockSpec(memory_space=pltpu.VMEM), pl.BlockSpec(memory_space=pl.ANY)
    return pl.pallas_call(
        kernel,
        out_shape=[
            jax.ShapeDtypeStruct(qkv.shape, BF16),
            jax.ShapeDtypeStruct(behind.shape, behind.dtype),
        ],
        in_specs=[pl.BlockSpec(memory_space=pltpu.SMEM)] + [vmem] * 5 + [hbm],
        out_specs=[vmem, hbm],
        scratch_shapes=[
            pltpu.VMEM((2, rows, lane), F32),
            pltpu.VMEM((2, rows, lane), F32),
            pltpu.VMEM((4, rows, lane), BF16),
            _sem(2),
            _sem(2),
        ],
        compiler_params=pltpu.CompilerParams(
            collective_id=cid, has_side_effects=True, vmem_limit_bytes=40 * 1024 * 1024
        ),
        name="attend_back",
    )(length, qkv, stats, grad_att, cosine, sine, behind)


def table_call(early, middle, late, adapters):
    f32 = lambda *shape: jax.ShapeDtypeStruct(shape, F32)
    choices = 8
    outs = [
        f32(choices, 5, RANK, 1536),
        f32(choices, RANK, 1536),
        f32(choices, RANK, 4096),
        f32(choices, RANK, 1536),
        f32(choices, 2, RANK, 768),
        f32(choices, RANK, 1536),
        f32(choices, 2, RANK, 4096),
        f32(choices, RANK, 1536),
    ]
    plan = (
        ((6, 0, 1024), (6, 1, 1024), (2, None, 1024), (0, 3, 384), (0, 4, 384), (7, None, 384)),
        ((1, None, 384), (5, None, 384), (3, None, 384), (4, 0, 192), (4, 1, 192)),
        ((0, 0, 384), (0, 1, 384), (0, 2, 384)),
    )

    def kernel(which, early_ref, middle_ref, late_ref, *refs):
        outs, acc, sems = refs[:8], refs[8:16], refs[16]

        def add(piece, ref):
            def one_slot(origin, carry):
                row = which[origin]
                for f in range(4):
                    at = 0
                    for out, table, n in plan[piece]:
                        value = ref[origin, f, :, at : at + n].astype(F32)
                        cols = slice(f * n, (f + 1) * n)
                        if table is None:
                            acc[out][row, :, cols] += value
                        else:
                            acc[out][row, table, :, cols] += value
                        at += n
                return carry

            lax.fori_loop(0, 8, one_slot, 0)

        def send(out):
            cp = pltpu.make_async_copy(acc[out], outs[out], sems.at[out])
            cp.start()
            return cp

        for out in (2, 6, 7):
            acc[out][...] = jnp.zeros_like(acc[out])
        acc[0][...] = jnp.zeros_like(acc[0])
        add(0, early_ref)
        copies = [send(out) for out in (2, 6, 7)]
        for out in (1, 3, 4, 5):
            acc[out][...] = jnp.zeros_like(acc[out])
        add(1, middle_ref)
        copies += [send(out) for out in (1, 3, 4, 5)]
        add(2, late_ref)
        copies += [send(0)]
        for cp in copies:
            cp.wait()

    vmem, hbm = pl.BlockSpec(memory_space=pltpu.VMEM), pl.BlockSpec(memory_space=pl.ANY)
    return pl.pallas_call(
        kernel,
        out_shape=outs,
        in_specs=[pl.BlockSpec(memory_space=pltpu.SMEM), vmem, vmem, vmem],
        out_specs=[hbm] * 8,
        scratch_shapes=[pltpu.VMEM(o.shape, F32) for o in outs] + [_sem(8)],
        compiler_params=pltpu.CompilerParams(vmem_limit_bytes=40 * 1024 * 1024),
        name="tables",
    )(adapters, early, middle, late)


def dot(left, right):
    return jnp.dot(left, right, preferred_element_type=F32)


def dot_t(left, right):
    return lax.dot_general(left, right, (((1,), (1,)), ((), ())), preferred_element_type=F32)


def dot_rows(left, right):
    return lax.dot_general(left, right, (((0,), (0,)), ((), ())), preferred_element_type=F32)


def side_pad(value):
    return jnp.pad(value, ((0, 0), (0, SIDE - value.shape[1])))


def blocks(value):
    return value.reshape(2, 2, 2, 128, value.shape[-1])


def own_blocks(value):
    return value.reshape(2, 128, value.shape[-1])


def flat(value):
    return value.reshape(-1, value.shape[-1])


def slot_local(
    tokens,
    cotangent,
    lengths,
    slot_adapter_index,
    attention_norm_gain,
    feedforward_norm_gain,
    query_weight,
    key_weight,
    value_weight,
    output_weight,
    gate_weight,
    up_weight,
    down_weight,
    adapter_input_first,
    adapter_output_first,
    adapter_down_first,
    adapter_query_second,
    adapter_key_value_second,
    adapter_output_second,
    adapter_gate_up_second,
    adapter_down_second,
):
    width = tokens.shape[-1]
    hidden_units = gate_weight.shape[1]
    quarter = width // 4
    c = lax.axis_index("ctx")
    f = lax.axis_index("fsdp")
    x, core = f // 2, f % 2
    slot = c // 2 + 4 * (c % 2)
    length = lax.dynamic_slice_in_dim(lengths, slot, 1, 0)
    adapter = slot_adapter_index[slot]

    def pick(table):
        return lax.dynamic_index_in_dim(table, adapter, 0, keepdims=False)

    def cut(value, axis, size):
        return lax.dynamic_slice_in_dim(value, f * size, size, axis)

    first_in = pick(adapter_input_first)
    first_out = pick(adapter_output_first)
    first_down = pick(adapter_down_first)
    second_q = cut(pick(adapter_query_second), 1, query_weight.shape[1])
    second_kv = cut(pick(adapter_key_value_second), 2, key_weight.shape[1])
    second_o = pick(adapter_output_second)
    second_gu = cut(pick(adapter_gate_up_second), 2, hidden_units)
    second_d = pick(adapter_down_second)
    first_o_own = cut(first_out, 0, output_weight.shape[0])
    first_d_own = cut(first_down, 0, hidden_units)

    def pad_turned(w):
        rows = w.shape[0]
        w = w.reshape(rows, -1, 2, HEAD_DIM // 2)
        w = jnp.pad(w, ((0, 0), (0, 0), (0, 0), (0, HALF_PAD - HEAD_DIM // 2)))
        return w.reshape(rows, -1)

    def pad_plain(w):
        rows = w.shape[0]
        w = w.reshape(rows, -1, HEAD_DIM)
        w = jnp.pad(w, ((0, 0), (0, 0), (0, PAD_HEAD - HEAD_DIM)))
        return w.reshape(rows, -1)

    def unpad_turned(g):
        rows = g.shape[0]
        return g.reshape(rows, -1, 2, HALF_PAD)[..., : HEAD_DIM // 2].reshape(rows, -1)

    def unpad_plain(g):
        rows = g.shape[0]
        return g.reshape(rows, -1, PAD_HEAD)[..., :HEAD_DIM].reshape(rows, -1)

    weight_all = jnp.concatenate(
        [pad_turned(query_weight), pad_turned(key_weight), pad_plain(value_weight)], axis=1
    )
    zero_q = jnp.zeros((RANK, 4 * PAD_HEAD), BF16)
    zero_k = jnp.zeros((RANK, 2 * PAD_HEAD), BF16)
    second_all = jnp.concatenate(
        [
            jnp.concatenate([pad_turned(second_q), zero_k, zero_k], axis=1),
            jnp.concatenate([zero_q, pad_turned(second_kv[0]), zero_k], axis=1),
            jnp.concatenate([zero_q, zero_k, pad_plain(second_kv[1])], axis=1),
        ],
        axis=0,
    )
    first_all = jnp.concatenate([first_in[0], first_in[1], first_in[2]], axis=1)
    first_gu = jnp.concatenate([first_in[3], first_in[4]], axis=1)

    half = HEAD_DIM // 2
    rows = 4 * 2 * tokens.shape[1]
    freqs = ROPE_BASE ** (-(jnp.arange(half, dtype=F32) * 2.0 / HEAD_DIM))
    angles = jnp.arange(rows, dtype=jnp.int32).astype(F32)[:, None] * freqs[None, :]
    gap = jnp.zeros((rows, HALF_PAD - half), F32)
    cos, sin = jnp.cos(angles), jnp.sin(angles)
    cosine = jnp.concatenate([cos, gap, cos, gap], axis=1)
    sine = jnp.concatenate([-sin, gap, sin, gap], axis=1)

    tok_own, cot_own, tok_all = take_in(tokens, cotangent, 0)
    live_rows = (jnp.arange(rows, dtype=jnp.int32) < length[0])[:, None]
    block_of = x + 4 * (1 - core) + 2 * jnp.arange(2, dtype=jnp.int32)
    own_pos = (block_of[:, None] * 128 + jnp.arange(128, dtype=jnp.int32)[None, :]).reshape(-1)
    own_live = (own_pos < length[0])[:, None]

    def own_rows(whole):
        part = lax.dynamic_slice(
            whole, (1 - core, 0, x, 0, 0), (1, 2, 1, whole.shape[3], whole.shape[4])
        )
        return part.reshape(-1, whole.shape[4])

    tokens_f = flat(tok_all).astype(F32)
    normed_one = (tokens_f * rms_factor(tokens_f) * attention_norm_gain).astype(BF16)
    inner_qkv = dot(normed_one, first_all).astype(BF16)
    proj = dot(normed_one, weight_all) + ADAPTER_SCALE * dot(inner_qkv, second_all)
    attn_b, qkv, stats, cot_all = attend_call(proj, cosine, sine, length, cot_own, 9)
    grad_out = jnp.where(live_rows, flat(cot_all), jnp.zeros((), BF16))
    grad_out_own = jnp.where(own_live, flat(cot_own), jnp.zeros((), BF16))

    sums, side_all = group_scatter(
        blocks(dot(attn_b, output_weight).astype(BF16)),
        blocks(side_pad(dot(attn_b, first_o_own)).astype(BF16)),
        1,
        "scatter_o",
    )
    inner_o = flat(side_all)[:, :RANK]
    inner_o_own = own_rows(side_all)[:, :RANK]
    own_f = flat(tok_own).astype(F32)
    resid = own_f + flat(sums) + ADAPTER_SCALE * dot(inner_o_own, second_o)
    factor_two = rms_factor(resid)
    normed_two_own = (resid * factor_two * feedforward_norm_gain).astype(BF16)
    normed_two = flat(plain_gather(own_blocks(normed_two_own), 2, "gather_two"))

    inner_gu = dot(normed_two, first_gu).astype(BF16)
    gate = dot(normed_two, gate_weight) + ADAPTER_SCALE * dot(inner_gu[:, :RANK], second_gu[0])
    up_proj = dot(normed_two, up_weight) + ADAPTER_SCALE * dot(inner_gu[:, RANK:], second_gu[1])
    sigmoid_gate = jax.nn.sigmoid(gate)
    hidden = (gate * sigmoid_gate * up_proj).astype(BF16)
    grad_inner_d = (ADAPTER_SCALE * dot_t(grad_out, second_d)).astype(BF16)
    grad_hidden = dot_t(grad_out, down_weight) + dot_t(grad_inner_d, first_d_own)
    grad_gate = (grad_hidden * up_proj * sigmoid_gate * (1.0 + gate * (1.0 - sigmoid_gate))).astype(
        BF16
    )
    grad_up = (grad_hidden * gate * sigmoid_gate).astype(BF16)
    grad_two = (dot_t(grad_gate, gate_weight) + dot_t(grad_up, up_weight)).astype(BF16)
    side_gu = ADAPTER_SCALE * jnp.concatenate(
        [dot_t(grad_gate, second_gu[0]), dot_t(grad_up, second_gu[1])], axis=1
    )
    sums, side_all = group_scatter(
        blocks(grad_two), blocks(side_pad(side_gu).astype(BF16)), 3, "scatter_two"
    )
    grad_inner_gu = flat(side_all)[:, : 2 * RANK]
    grad_inner_gu_own = own_rows(side_all)[:, : 2 * RANK]
    grad_normed_two = (
        (flat(sums) + dot_t(grad_inner_gu_own, first_gu)).astype(BF16).astype(F32)
    )
    grad_resid = grad_out_own.astype(F32) + norm_back(
        resid, factor_two, feedforward_norm_gain, grad_normed_two
    )
    grad_low_own = grad_resid.astype(BF16)

    sums, side_all = group_scatter(
        blocks(dot(hidden, down_weight).astype(BF16)),
        blocks(side_pad(dot(hidden, first_d_own)).astype(BF16)),
        4,
        "scatter_out",
    )
    inner_d = flat(side_all)[:, :RANK]
    inner_d_own = own_rows(side_all)[:, :RANK]
    out_own = jnp.where(
        own_live, resid + flat(sums) + ADAPTER_SCALE * dot(inner_d_own, second_d), 0.0
    ).astype(BF16)

    def pack(parts):
        return jnp.concatenate(parts, axis=1).astype(BF16)

    two_cut = cut(normed_two, 1, quarter)
    in_gu = dot_rows(grad_inner_gu, two_cut)
    early = pack(
        [
            ADAPTER_SCALE * dot_rows(inner_gu[:, :RANK], grad_gate),
            ADAPTER_SCALE * dot_rows(inner_gu[:, RANK:], grad_up),
            dot_rows(grad_inner_d, hidden),
            in_gu[:RANK],
            in_gu[RANK:],
            ADAPTER_SCALE * dot_rows(inner_d, cut(grad_out, 1, quarter)),
        ]
    )
    grad_low, early = group_gather(own_blocks(grad_low_own), early, 5, "gather_resid")
    grad_low = flat(grad_low)
    grad_inner_o = (ADAPTER_SCALE * dot_t(grad_low, second_o)).astype(BF16)
    grad_att = (dot_t(grad_low, output_weight) + dot_t(grad_inner_o, first_o_own)).astype(BF16)
    grad_qkv, out_tokens = attend_back_call(
        qkv, stats, grad_att, cosine, sine, length, own_blocks(out_own), 10
    )
    grad_one = dot_t(grad_qkv, weight_all).astype(BF16)
    side_qkv = ADAPTER_SCALE * dot_t(grad_qkv, second_all)
    all_b = ADAPTER_SCALE * dot_rows(inner_qkv, grad_qkv)
    middle = pack(
        [
            dot_rows(grad_inner_o, attn_b),
            ADAPTER_SCALE * dot_rows(inner_o, cut(grad_low, 1, quarter)),
            unpad_turned(all_b[:RANK, : 4 * PAD_HEAD]),
            unpad_turned(all_b[RANK : 2 * RANK, 4 * PAD_HEAD : 6 * PAD_HEAD]),
            unpad_plain(all_b[2 * RANK :, 6 * PAD_HEAD :]),
        ]
    )
    sums, side_all, middle = group_scatter(
        blocks(grad_one), blocks(side_pad(side_qkv).astype(BF16)), 6, "scatter_one", middle
    )
    grad_inner_qkv = flat(side_all)[:, : 3 * RANK]
    grad_inner_own = own_rows(side_all)[:, : 3 * RANK]
    grad_normed_one = (flat(sums) + dot_t(grad_inner_own, first_all)).astype(BF16).astype(F32)
    grad_tok_own = grad_resid + norm_back(
        own_f, rms_factor(own_f), attention_norm_gain, grad_normed_one
    )
    one_cut = cut(normed_one, 1, quarter)
    in_qkv = dot_rows(grad_inner_qkv, one_cut)
    late = pack([in_qkv[:RANK], in_qkv[RANK : 2 * RANK], in_qkv[2 * RANK :]])
    grad_tokens, late = give_back(own_blocks(grad_tok_own.astype(BF16)), late, 7)

    group_slot = [cc // 2 + 4 * (cc % 2) for cc in range(8)]
    group_adapter = slot_adapter_index[jnp.array(group_slot, dtype=jnp.int32)]
    as_devices = lambda piece: piece.reshape((8, 4) + piece.shape[3:])
    full = table_call(as_devices(early), as_devices(middle), as_devices(late), group_adapter)
    turn = lambda t: jnp.swapaxes(t, -1, -2)
    return (
        out_tokens,
        grad_tokens.astype(F32),
        turn(full[0]),
        turn(full[1]),
        turn(full[2]),
        full[3],
        full[4],
        full[5],
        full[6],
        full[7],
    )


def solution(mesh):
    one_slot = mesh.shape["ctx"] == 8 and mesh.shape["fsdp"] == 4
    return jax.shard_map(
        slot_local if one_slot else local,
        mesh=mesh,
        in_specs=(
            P("fsdp", "ctx", None),
            P("fsdp", "ctx", None),
            P(),
            P(),
            P(),
            P(),
            P(None, "fsdp"),
            P(None, "fsdp"),
            P(None, "fsdp"),
            P("fsdp", None),
            P(None, "fsdp"),
            P(None, "fsdp"),
            P("fsdp", None),
            P(),
            P(),
            P(),
            P(),
            P(),
            P(),
            P(),
            P(),
        ),
        out_specs=(
            P("fsdp", "ctx", None),
            P("fsdp", "ctx", None),
            P(),
            P(),
            P(),
            P(),
            P(),
            P(),
            P(),
            P(),
        ),
        check_vma=False,
    )
```

```python
import math

import jax
import jax.numpy as jnp
from jax import lax
from jax.experimental import pallas as pl
from jax.experimental.pallas import tpu as pltpu
from jax.sharding import PartitionSpec as P

QUERY_HEADS = 16
KEY_VALUE_HEADS = 8
HEAD_DIM = 96


EPSILON = 1e-05
NEGATIVE = -1e30
ADAPTER_SCALE = 0.5
ROPE_BASE = 100000.0


def from_behind(x, axis, by):
    size = lax.axis_size(axis)
    return lax.ppermute(x, axis, [(i, (i + by) % size) for i in range(size)])


def rope_tables(positions, head_size):
    half_size = head_size // 2
    freqs = ROPE_BASE ** (-(jnp.arange(half_size, dtype=jnp.float32) * 2.0 / head_size))
    angles = positions.astype(jnp.float32)[:, None] * freqs[None, :]
    return (jnp.cos(angles)[:, None, :], jnp.sin(angles)[:, None, :])


def apply_rotation(values, cosine_table, sine_table):
    half_size = values.shape[-1] // 2
    first_half = values[..., :half_size]
    second_half = values[..., half_size:]
    return jnp.concatenate(
        [
            first_half * cosine_table - second_half * sine_table,
            second_half * cosine_table + first_half * sine_table,
        ],
        axis=-1,
    )


def rotate_back(gradient_tree, cosine_table, sine_table):
    half_size = gradient_tree.shape[-1] // 2
    first_half = gradient_tree[..., :half_size]
    second_half = gradient_tree[..., half_size:]
    return jnp.concatenate(
        [
            first_half * cosine_table + second_half * sine_table,
            second_half * cosine_table - first_half * sine_table,
        ],
        axis=-1,
    )


def rms_factor(values):
    return lax.rsqrt(jnp.mean(values * values, axis=-1, keepdims=True) + EPSILON)


def norm_back(values, factor, gain, grad_norm):
    scaled = grad_norm * gain
    return factor * scaled - values * factor**3 * jnp.mean(scaled * values, axis=-1, keepdims=True)


def pick_rows(onehot, table):
    return jnp.einsum("sa,a...->s...", onehot, table, preferred_element_type=jnp.float32).astype(
        jnp.bfloat16
    )


def spread_rows(onehot, gradient_tree):
    return jnp.einsum("sa,s...->a...", onehot, gradient_tree, precision=lax.Precision.HIGHEST)


def direct_product(input_rows, weight_matrix):
    return jnp.einsum("std,do->sto", input_rows, weight_matrix, preferred_element_type=jnp.float32)


def direct_back(gradient_tree, weight_matrix):
    return jnp.einsum(
        "sto,do->std", gradient_tree, weight_matrix, preferred_element_type=jnp.float32
    )


def inner_product_part(input_rows, down):
    return jnp.einsum("std,sdr->str", input_rows, down, preferred_element_type=jnp.float32)


def inner_back(gradient_tree, upward_rows):
    return ADAPTER_SCALE * jnp.einsum(
        "sto,sro->str", gradient_tree, upward_rows, preferred_element_type=jnp.float32
    )


def through_down(grad_inner, down):
    return jnp.einsum("str,sdr->std", grad_inner, down, preferred_element_type=jnp.float32)


def down_grad(input_rows, grad_inner):
    return jnp.einsum("std,str->sdr", input_rows, grad_inner, preferred_element_type=jnp.float32)


def upward_grad(inner_rows, gradient_tree):
    return ADAPTER_SCALE * jnp.einsum(
        "jvp,jvx->jpx", inner_rows, gradient_tree, preferred_element_type=jnp.float32
    )


def upward_apply(inner_rows, upward_rows):
    return ADAPTER_SCALE * jnp.einsum(
        "str,sro->sto", inner_rows, upward_rows, preferred_element_type=jnp.float32
    )


def project(input_rows, weight_matrix, down, upward_rows):
    inner_rows = inner_product_part(input_rows, down).astype(jnp.bfloat16)
    return (
        inner_rows,
        direct_product(input_rows, weight_matrix) + upward_apply(inner_rows, upward_rows),
    )


def project_back(input_rows, grad_output, weight_matrix, down, upward_rows, inner_rows):
    grad_upward = upward_grad(inner_rows, grad_output)
    grad_inner = inner_back(grad_output, upward_rows).astype(jnp.bfloat16)
    grad_down = down_grad(input_rows, grad_inner)
    grad_inputs = direct_back(grad_output, weight_matrix) + through_down(grad_inner, down)
    return (grad_inputs, grad_down, grad_upward)


def allowed_mask(key_start, key_count, query_pos, lengths):
    key_pos = key_start + jnp.arange(key_count, dtype=jnp.int32)
    causal = key_pos[None, :] <= query_pos[:, None]
    live = key_pos[None, :] < lengths[:, None]
    return (causal[None, :, :] & live[:, None, :])[:, None, None, :, :]


def attend_block(state, key_block, value_block, key_start, query_head_rows, query_pos, lengths):
    run_max, run_sum, run_acc = state
    scale = query_head_rows.shape[-1] ** (-0.5)
    scores = (
        jnp.einsum(
            "sqhgd,skhd->shgqk", query_head_rows, key_block, preferred_element_type=jnp.float32
        )
        * scale
    )
    allowed = allowed_mask(key_start, key_block.shape[1], query_pos, lengths)
    new_max = jnp.maximum(run_max, jnp.max(jnp.where(allowed, scores, NEGATIVE), axis=-1))
    weights = jnp.where(allowed, jnp.exp(scores - new_max[..., None]), 0.0)
    factor = jnp.exp(run_max - new_max)
    new_sum = run_sum * factor + jnp.sum(weights, axis=-1)
    update = jnp.einsum(
        "shgqk,skhd->shgqd",
        weights.astype(jnp.bfloat16),
        value_block,
        preferred_element_type=jnp.float32,
    )
    return (new_max, new_sum, run_acc * factor[..., None] + update)


def attend_back(
    key_block,
    value_block,
    key_start,
    query_head_rows,
    grad_heads,
    log_total,
    row_dot,
    query_pos,
    lengths,
):
    scale = query_head_rows.shape[-1] ** (-0.5)
    scores = (
        jnp.einsum(
            "sqhgd,skhd->shgqk", query_head_rows, key_block, preferred_element_type=jnp.float32
        )
        * scale
    )
    allowed = allowed_mask(key_start, key_block.shape[1], query_pos, lengths)
    probs = jnp.where(allowed, jnp.exp(scores - log_total[..., None]), 0.0)
    grad_probs = jnp.einsum(
        "sqhgd,skhd->shgqk", grad_heads, value_block, preferred_element_type=jnp.float32
    )
    grad_scores = (probs * (grad_probs - row_dot[..., None])).astype(jnp.bfloat16)
    grad_query = scale * jnp.einsum(
        "shgqk,skhd->sqhgd", grad_scores, key_block, preferred_element_type=jnp.float32
    )
    grad_key = scale * jnp.einsum(
        "shgqk,sqhgd->skhd", grad_scores, query_head_rows, preferred_element_type=jnp.float32
    )
    grad_value = jnp.einsum(
        "shgqk,sqhgd->skhd",
        probs.astype(jnp.bfloat16),
        grad_heads,
        preferred_element_type=jnp.float32,
    )
    return (grad_query, grad_key, grad_value)


def attend_forward(query_head_rows, key_head_rows, value_head_rows, lengths_used, query_pos):
    slots, rows, kv_heads, group_size, head_size = query_head_rows.shape
    key_flat = key_head_rows.reshape(slots, rows, kv_heads * head_size)
    value_flat = value_head_rows.reshape(slots, rows, kv_heads * head_size)
    stat_shape = (slots, kv_heads, group_size, rows)
    initial = (
        jnp.full(stat_shape, NEGATIVE, jnp.float32),
        jnp.zeros(stat_shape, jnp.float32),
        jnp.zeros(stat_shape + (head_size,), jnp.float32),
    )
    part_keys = lax.all_gather(key_flat, "ctx", axis=1, tiled=True)
    part_values = lax.all_gather(value_flat, "ctx", axis=1, tiled=True)
    piece_rows = part_keys.shape[1]
    part_keys = part_keys.reshape(slots, piece_rows, kv_heads, head_size)
    part_values = part_values.reshape(slots, piece_rows, kv_heads, head_size)
    span_rows = math.gcd(piece_rows, 4 * rows)

    def inner_step(block_index, inner_state):
        sub_keys = lax.dynamic_slice_in_dim(part_keys, block_index * span_rows, span_rows, 1)
        sub_values = lax.dynamic_slice_in_dim(part_values, block_index * span_rows, span_rows, 1)
        return attend_block(
            inner_state,
            sub_keys,
            sub_values,
            block_index * span_rows,
            query_head_rows,
            query_pos,
            lengths_used,
        )

    run_max, run_sum, run_acc = lax.fori_loop(0, piece_rows // span_rows, inner_step, initial)
    log_total = run_max + jnp.log(run_sum)
    attended = jnp.transpose(run_acc / run_sum[..., None], (0, 3, 1, 2, 4))
    return (attended, log_total)


def attend_backward(
    query_head_rows,
    key_head_rows,
    value_head_rows,
    grad_heads,
    attended,
    log_total,
    lengths_used,
    query_pos,
):
    ctx_count = lax.axis_size("ctx")
    own_index = lax.axis_index("ctx")
    rows = query_head_rows.shape[1]
    row_dot = jnp.transpose(
        jnp.sum(grad_heads.astype(jnp.float32) * attended, axis=-1), (0, 2, 3, 1)
    )

    def cycle_step(step_index, carried):
        carried_keys, carried_values, grad_query, grad_key, grad_value = carried
        block_id = (own_index + step_index) % ctx_count
        query_part, key_part, value_part = attend_back(
            carried_keys,
            carried_values,
            block_id * rows,
            query_head_rows,
            grad_heads,
            log_total,
            row_dot,
            query_pos,
            lengths_used,
        )
        grad_key, grad_value = (
            from_behind((grad_key + key_part).astype(jnp.bfloat16), "ctx", -1).astype(jnp.float32),
            from_behind((grad_value + value_part).astype(jnp.bfloat16), "ctx", -1).astype(
                jnp.float32
            ),
        )
        carried_keys, carried_values = from_behind((carried_keys, carried_values), "ctx", -1)
        return (carried_keys, carried_values, grad_query + query_part, grad_key, grad_value)

    key_zeros = jnp.zeros(key_head_rows.shape, jnp.float32)
    start_state = (
        key_head_rows,
        value_head_rows,
        jnp.zeros(query_head_rows.shape, jnp.float32),
        key_zeros,
        key_zeros,
    )
    carried = lax.fori_loop(0, ctx_count, cycle_step, start_state)
    return (carried[2], carried[3], carried[4])


def table_total(rotation_tables):
    return lax.psum(rotation_tables, ("ctx", "fsdp"))


def local(
    tokens,
    cotangent,
    lengths,
    slot_adapter_index,
    attention_norm_gain,
    feedforward_norm_gain,
    query_weight,
    key_weight,
    value_weight,
    output_weight,
    gate_weight,
    up_weight,
    down_weight,
    adapter_input_first,
    adapter_output_first,
    adapter_down_first,
    adapter_query_second,
    adapter_key_value_second,
    adapter_output_second,
    adapter_gate_up_second,
    adapter_down_second,
):
    slot_count, tok_rows, model_width = tokens.shape
    head_groups = QUERY_HEADS // KEY_VALUE_HEADS
    own_index = lax.axis_index("ctx")
    fsdp_index = lax.axis_index("fsdp")
    query_pos = own_index * tok_rows + jnp.arange(tok_rows, dtype=jnp.int32)
    cosine_table, sine_table = rope_tables(query_pos, HEAD_DIM)
    own_lengths = lax.dynamic_slice_in_dim(lengths, fsdp_index * slot_count, slot_count, 0)
    own_adapters = lax.dynamic_slice_in_dim(
        slot_adapter_index, fsdp_index * slot_count, slot_count, 0
    )
    valid = query_pos[None, :] < own_lengths[:, None]
    adapter_labels = jnp.arange(adapter_input_first.shape[0], dtype=jnp.int32)
    onehot_own = own_adapters[:, None] == adapter_labels[None, :]
    owned_low_rank = onehot_own.astype(jnp.bfloat16)
    own_full = onehot_own.astype(jnp.float32)
    tokens_f = tokens.astype(jnp.float32)
    factor_one = rms_factor(tokens_f)
    normed_one = (tokens_f * factor_one * attention_norm_gain).astype(jnp.bfloat16)
    grad_out = jnp.where(valid[..., None], cotangent, jnp.zeros((), jnp.bfloat16))
    input_first = pick_rows(owned_low_rank, adapter_input_first)
    output_second = pick_rows(owned_low_rank, adapter_output_second)
    down_second = pick_rows(owned_low_rank, adapter_down_second)
    output_first = pick_rows(owned_low_rank, adapter_output_first)
    down_first = pick_rows(owned_low_rank, adapter_down_first)
    query_second = pick_rows(owned_low_rank, adapter_query_second)
    key_value_second = pick_rows(owned_low_rank, adapter_key_value_second)
    gate_up_second = pick_rows(owned_low_rank, adapter_gate_up_second)
    weight_q, weight_k, weight_v, weight_gate, weight_up, weight_o, weight_down = (
        lax.all_gather(query_weight, "fsdp", axis=1, tiled=True),
        lax.all_gather(key_weight, "fsdp", axis=1, tiled=True),
        lax.all_gather(value_weight, "fsdp", axis=1, tiled=True),
        lax.all_gather(gate_weight, "fsdp", axis=1, tiled=True),
        lax.all_gather(up_weight, "fsdp", axis=1, tiled=True),
        lax.all_gather(output_weight, "fsdp", axis=0, tiled=True),
        lax.all_gather(down_weight, "fsdp", axis=0, tiled=True),
    )
    inner_q, projected_queries = project(normed_one, weight_q, input_first[:, 0], query_second)
    inner_k, projected_keys = project(
        normed_one, weight_k, input_first[:, 1], key_value_second[:, 0]
    )
    inner_v, projected_values = project(
        normed_one, weight_v, input_first[:, 2], key_value_second[:, 1]
    )
    query_head_rows = apply_rotation(
        projected_queries.reshape(slot_count, tok_rows, -1, HEAD_DIM), cosine_table, sine_table
    ).astype(jnp.bfloat16)
    query_head_rows = query_head_rows.reshape(slot_count, tok_rows, -1, head_groups, HEAD_DIM)
    key_head_rows = apply_rotation(
        projected_keys.reshape(slot_count, tok_rows, -1, HEAD_DIM), cosine_table, sine_table
    ).astype(jnp.bfloat16)
    value_head_rows = projected_values.astype(jnp.bfloat16).reshape(
        slot_count, tok_rows, -1, HEAD_DIM
    )
    attended, log_total = attend_forward(
        query_head_rows, key_head_rows, value_head_rows, own_lengths, query_pos
    )
    attn_b = attended.reshape(slot_count, tok_rows, -1).astype(jnp.bfloat16)
    inner_o, proj_o = project(attn_b, weight_o, output_first, output_second)
    resid = tokens_f + proj_o
    factor_two = rms_factor(resid)
    normed_two = (resid * factor_two * feedforward_norm_gain).astype(jnp.bfloat16)
    inner_gate, gate = project(normed_two, weight_gate, input_first[:, 3], gate_up_second[:, 0])
    inner_up, up_proj = project(normed_two, weight_up, input_first[:, 4], gate_up_second[:, 1])
    sigmoid_gate = jax.nn.sigmoid(gate)
    hidden = (gate * sigmoid_gate * up_proj).astype(jnp.bfloat16)
    inner_down, proj_down = project(hidden, weight_down, down_first, down_second)
    out_tokens = jnp.where(valid[..., None], resid + proj_down, 0.0).astype(jnp.bfloat16)
    grad_hidden, grad_da, grad_db = project_back(
        hidden, grad_out, weight_down, down_first, down_second, inner_down
    )
    grad_gate = (grad_hidden * up_proj * sigmoid_gate * (1.0 + gate * (1.0 - sigmoid_gate))).astype(
        jnp.bfloat16
    )
    grad_up = (grad_hidden * gate * sigmoid_gate).astype(jnp.bfloat16)
    from_gate, grad_ga, grad_gb = project_back(
        normed_two, grad_gate, weight_gate, input_first[:, 3], gate_up_second[:, 0], inner_gate
    )
    from_up, grad_ua, grad_ub = project_back(
        normed_two, grad_up, weight_up, input_first[:, 4], gate_up_second[:, 1], inner_up
    )
    grad_normed_two = (from_gate + from_up).astype(jnp.bfloat16).astype(jnp.float32)
    grad_resid = grad_out.astype(jnp.float32) + norm_back(
        resid, factor_two, feedforward_norm_gain, grad_normed_two
    )
    grad_resid_low = grad_resid.astype(jnp.bfloat16)
    from_attn, grad_oa, grad_ob = project_back(
        attn_b, grad_resid_low, weight_o, output_first, output_second, inner_o
    )
    grad_heads = from_attn.astype(jnp.bfloat16).reshape(attended.shape)
    grad_query, grad_key, grad_value = attend_backward(
        query_head_rows,
        key_head_rows,
        value_head_rows,
        grad_heads,
        attended,
        log_total,
        own_lengths,
        query_pos,
    )
    grad_proj_q = (
        rotate_back(
            grad_query.reshape(slot_count, tok_rows, -1, HEAD_DIM), cosine_table, sine_table
        )
        .astype(jnp.bfloat16)
        .reshape(slot_count, tok_rows, -1)
    )
    grad_proj_k = (
        rotate_back(grad_key, cosine_table, sine_table)
        .astype(jnp.bfloat16)
        .reshape(slot_count, tok_rows, -1)
    )
    grad_proj_v = grad_value.astype(jnp.bfloat16).reshape(slot_count, tok_rows, -1)
    from_query, grad_qa, grad_qb = project_back(
        normed_one, grad_proj_q, weight_q, input_first[:, 0], query_second, inner_q
    )
    from_key, grad_ka, grad_kb = project_back(
        normed_one, grad_proj_k, weight_k, input_first[:, 1], key_value_second[:, 0], inner_k
    )
    from_value, grad_va, grad_vb = project_back(
        normed_one, grad_proj_v, weight_v, input_first[:, 2], key_value_second[:, 1], inner_v
    )
    grad_normed_one = (from_query + from_key + from_value).astype(jnp.bfloat16).astype(jnp.float32)
    grad_tokens = grad_resid + norm_back(tokens_f, factor_one, attention_norm_gain, grad_normed_one)
    slot_grads = (
        jnp.stack([grad_qa, grad_ka, grad_va, grad_ga, grad_ua], axis=1),
        grad_oa,
        grad_da,
        grad_qb,
        jnp.stack([grad_kb, grad_vb], axis=1),
        grad_ob,
        jnp.stack([grad_gb, grad_ub], axis=1),
        grad_db,
    )
    summed = table_total(tuple((spread_rows(own_full, entry_item) for entry_item in slot_grads)))
    return (
        out_tokens,
        grad_tokens,
        summed[0],
        summed[1],
        summed[2],
        summed[3],
        summed[4],
        summed[5],
        summed[6],
        summed[7],
    )


BF16 = jnp.bfloat16
F32 = jnp.float32
MESH_ID = pl.DeviceIdType.MESH
RANK = 16
SIDE = 128
PAD_HEAD = 128
HALF_PAD = 64


def _sem(count):
    return pltpu.SemaphoreType.DMA((count,))


def _place():
    c = lax.axis_index("ctx")
    f = lax.axis_index("fsdp")
    x = f // 2
    core = f % 2
    return c, f, x, core, (c, 2 * x + 1 - core), (c, 2 * (1 - x) + core)


def _greet(targets):
    barrier = pltpu.get_barrier_semaphore()
    for target in targets:
        pl.semaphore_signal(barrier, inc=1, device_id=target, device_id_type=MESH_ID)
    pl.semaphore_wait(barrier, len(targets))


def _remote(src, dst, send, recv, target):
    return pltpu.make_async_remote_copy(
        src_ref=src, dst_ref=dst, send_sem=send, recv_sem=recv, device_id=target, device_id_type=MESH_ID
    )


def _comm_call(kernel, ins, outs, scratch, cid, name, in_space=pl.ANY, out_space=pl.ANY, vmem=None):
    return pl.pallas_call(
        kernel,
        out_shape=outs,
        in_specs=[pl.BlockSpec(memory_space=in_space)] * len(ins),
        out_specs=jax.tree.map(lambda _: pl.BlockSpec(memory_space=out_space), outs),
        scratch_shapes=scratch,
        compiler_params=pltpu.CompilerParams(
            collective_id=cid, has_side_effects=True, vmem_limit_bytes=vmem
        ),
        name=name,
    )(*ins)


def _gather_steps(ins, outs, own_sem, send_sem, recv_sem, place):
    c, f, x, core, core_peer, x_peer = place
    h = 1 - core
    count = len(ins)
    local = []
    sends = []

    def first():
        for base, target in ((0, x_peer), (2 * count, core_peer)):
            for i in range(count):
                for j in range(2):
                    k = base + i * 2 + j
                    cp = _remote(
                        ins[i].at[j], outs[i].at[h, j, x], send_sem.at[k], recv_sem.at[k], target
                    )
                    cp.start()
                    sends.append(cp)
        for i in range(count):
            for j in range(2):
                lc = pltpu.make_async_copy(
                    ins[i].at[j], outs[i].at[h, j, x], own_sem.at[i * 2 + j]
                )
                lc.start()
                local.append(lc)

    def last():
        forwards = []
        for i in range(count):
            for j in range(2):
                k = i * 2 + j
                sends[k].wait_recv()
                cp = _remote(
                    outs[i].at[h, j, 1 - x],
                    outs[i].at[h, j, 1 - x],
                    send_sem.at[4 * count + k],
                    recv_sem.at[4 * count + k],
                    core_peer,
                )
                cp.start()
                forwards.append(cp)
        for k in range(2 * count):
            sends[2 * count + k].wait_recv()
            forwards[k].wait_recv()
        for cp in sends + forwards:
            cp.wait_send()
        for lc in local:
            lc.wait()

    return first, last


def _gather_body(*args):
    first, last = _gather_steps(*args)
    first()
    last()


def _ctx_first(piece, lines, own_sem, send_sem, recv_sem, place):
    c, f, x, core, core_peer, x_peer = place
    z, y = c // 2, c % 2
    sends = []
    local = []

    def start():
        lc = pltpu.make_async_copy(piece, lines.at[z, x], own_sem)
        lc.start()
        local.append(lc)
        cp = _remote(piece, lines.at[z, x], send_sem.at[0], recv_sem.at[0], x_peer)
        cp.start()
        sends.append(cp)

    def spread():
        local[0].wait()
        sends[0].wait_recv()
        for step in range(1, 4):
            cp = _remote(
                lines.at[z],
                lines.at[z],
                send_sem.at[step],
                recv_sem.at[step],
                (2 * ((z + step) % 4) + y, f),
            )
            cp.start()
            sends.append(cp)

    def finish():
        for cp in sends[1:]:
            cp.wait_recv()
        for cp in sends:
            cp.wait_send()

    return start, spread, finish


def _ctx_second(lines, out, own_sem, send_sem, recv_sem, place):
    c, f, x, core, core_peer, x_peer = place
    z, y = c // 2, c % 2
    y_peer = (2 * z + 1 - y, f)
    sends = []
    local = []

    def start():
        lc = pltpu.make_async_copy(lines, out.at[y, core], own_sem)
        lc.start()
        local.append(lc)
        for k, target in ((0, y_peer), (1, core_peer)):
            cp = _remote(lines, out.at[y, core], send_sem.at[k], recv_sem.at[k], target)
            cp.start()
            sends.append(cp)

    def share():
        sends[0].wait_recv()
        cp = _remote(
            out.at[1 - y, core], out.at[1 - y, core], send_sem.at[2], recv_sem.at[2], core_peer
        )
        cp.start()
        sends.append(cp)

    def finish():
        sends[1].wait_recv()
        sends[2].wait_recv()
        for cp in sends:
            cp.wait_send()
        local[0].wait()

    return start, share, finish


def _z_peers(place):
    c, f = place[:2]
    return [(2 * ((c // 2 + step) % 4) + c % 2, f) for step in range(1, 4)]


def _y_peer(place):
    c, f = place[:2]
    return (2 * (c // 2) + 1 - c % 2, f)


def _lines_of(n):
    return (4, 2, RANK, n)


def _spread_of(n):
    return jax.ShapeDtypeStruct((2, 2, 4, 2, RANK, n), BF16)


FIRST_SEMS = [pltpu.SemaphoreType.DMA(()), _sem(4), _sem(4)]
SECOND_SEMS = [pltpu.SemaphoreType.DMA(()), _sem(3), _sem(3)]


def _order_steps(own, order, own_sem, send_sem, recv_sem, place):
    core_peer, x_peer = place[4:]
    sends, local, forwards = [], [], []

    def first():
        for j in range(2):
            cp = _remote(own.at[j], order.at[1 + j, 1], send_sem.at[j], recv_sem.at[j], x_peer)
            cp.start()
            sends.append(cp)
        for j in range(2):
            cp = _remote(
                own.at[j], order.at[3, j], send_sem.at[2 + j], recv_sem.at[2 + j], core_peer
            )
            cp.start()
            sends.append(cp)
        for j in range(2):
            lc = pltpu.make_async_copy(own.at[j], order.at[0, j], own_sem.at[j])
            lc.start()
            local.append(lc)

    def forward(j):
        sends[j].wait_recv()
        cp = _remote(
            order.at[1 + j, 1],
            order.at[1 + j, 0],
            send_sem.at[4 + j],
            recv_sem.at[4 + j],
            core_peer,
        )
        cp.start()
        forwards.append(cp)

    def own_here():
        for lc in local:
            lc.wait()

    def core_here():
        for j in range(2):
            sends[2 + j].wait_recv()

    def far_here(j):
        forwards[j].wait_recv()

    def last():
        for cp in sends + forwards:
            cp.wait_send()

    return first, forward, own_here, core_here, far_here, last


def _order_all(own, order, sems, place):
    first, forward, own_here, core_here, far_here, last = _order_steps(own, order, *sems, place)
    first()
    own_here()
    for j in range(2):
        forward(j)
    core_here()
    for j in range(2):
        far_here(j)
    last()


def feed_forward(own, grad_out, gate_w, up_w, down_w, first_gu, second_g, second_u, first_d, second_d, cid):
    width, units = gate_w.shape
    wide = width + SIDE
    tile = 256

    def kernel(
        own_ref,
        go_ref,
        gate_ref,
        up_ref,
        down_ref,
        first_ref,
        sg_ref,
        su_ref,
        fd_ref,
        sd_ref,
        sums,
        out_own,
        out_far,
        order,
        gate_b,
        up_b,
        down_a,
        hid_s,
        gg_s,
        gu_s,
        in_s,
        gid_s,
        part,
        out_part,
        near,
        out_near,
        far,
        out_land,
        staged,
        landed,
        own_sem,
        send_sem,
        recv_sem,
        s_sem,
        r_sem,
    ):
        place = _place()
        core_peer, x_peer = place[4:]
        _greet([core_peer, x_peer])
        first, forward, own_here, core_here, far_here, last = _order_steps(
            own_ref, order, own_sem, send_sem, recv_sem, place
        )
        first()
        copies = []

        def work(step):
            rows = order[step].reshape(2 * 128, width)
            go = go_ref[step]
            inner = dot(rows, first_ref[...]).astype(BF16)
            gid = dot_t(go, sd_ref[...]).astype(BF16)
            in_s[step] = inner
            gid_s[step] = gid
            for at in range(0, units, tile):
                cols = slice(at, at + tile)
                gate = dot(rows, gate_ref[:, cols]) + dot(inner, sg_ref[:, cols])
                up = dot(rows, up_ref[:, cols]) + dot(inner, su_ref[:, cols])
                grad = dot_t(go, down_ref[cols, :]) + dot_t(gid, fd_ref[cols, :])
                sig = 1.0 / (1.0 + jnp.exp(-gate))
                silu = gate * sig
                hid_s[step, :, cols] = (silu * up).astype(BF16)
                gg_s[step, :, cols] = (grad * up * sig * (1.0 + gate * (1.0 - sig))).astype(BF16)
                gu_s[step, :, cols] = (grad * silu).astype(BF16)
            gg, gu, hid = gg_s[step], gu_s[step], hid_s[step]
            for at in range(0, width, tile):
                cols = slice(at, at + tile)
                value = dot_t(gg, gate_ref[cols, :]) + dot_t(gu, up_ref[cols, :])
                out = dot(hid, down_ref[:, cols])
                if step == 0:
                    sums[:, :, cols] = value.reshape(2, 128, tile)
                    out_own[:, :, cols] = out.reshape(2, 128, tile)
                else:
                    part[step - 1, :, :, cols] = value.astype(BF16).reshape(2, 128, tile)
                    out_part[step - 1, :, :, cols] = out.astype(BF16).reshape(2, 128, tile)
            value = dot_t(gg, sg_ref[...]) + dot_t(gu, su_ref[...])
            out = dot(hid, fd_ref[...])
            if step == 0:
                sums[:, :, width:] = value.reshape(2, 128, SIDE)
                out_own[:, :, width:] = out.reshape(2, 128, SIDE)
            else:
                part[step - 1, :, :, width:] = value.astype(BF16).reshape(2, 128, SIDE)
                out_part[step - 1, :, :, width:] = out.astype(BF16).reshape(2, 128, SIDE)

        def send(src, dst, k, target):
            cp = _remote(src, dst, s_sem.at[k], r_sem.at[k], target)
            cp.start()
            copies.append(cp)
            return cp

        own_here()
        work(0)
        core_here()
        forward(0)
        work(3)
        near_cp = [
            send(part.at[2], near, 0, core_peer),
            send(out_part.at[2], out_near, 1, core_peer),
        ]
        across, out_cps = [], []
        for j in range(2):
            if j:
                forward(j)
            far_here(j)
            work(1 + j)
            cp = send(part.at[j, 0], far.at[j], 2 + j, core_peer)
            out_cps.append(send(out_part.at[j, 0], out_land.at[j], 4 + j, core_peer))
            cp.wait_recv()
            staged[j] = (part[j, 1].astype(F32) + far[j].astype(F32)).astype(BF16)
            across.append(send(staged.at[j], landed.at[j], 6 + j, x_peer))
        for j in range(2):
            out_cps[j].wait_recv()
            out_far[j] = (out_part[j, 1].astype(F32) + out_land[j].astype(F32)).astype(BF16)
        for cp in near_cp:
            cp.wait_recv()
        sums[...] = sums[...] + near[...].astype(F32)
        out_own[...] = out_own[...] + out_near[...].astype(F32)
        for at in range(0, units, 512):
            cols = slice(at, at + 512)
            g = jnp.zeros((SIDE, 512), F32)
            u = jnp.zeros((SIDE, 512), F32)
            d = jnp.zeros((SIDE, 512), F32)
            for step in range(4):
                g += dot_rows(in_s[step], gg_s[step, :, cols])
                u += dot_rows(in_s[step], gu_s[step, :, cols])
                d += dot_rows(gid_s[step], hid_s[step, :, cols])
            gate_b[:, cols] = ADAPTER_SCALE * g[:RANK]
            up_b[:, cols] = ADAPTER_SCALE * u[RANK : 2 * RANK]
            down_a[:, cols] = d[3 * RANK : 4 * RANK]
        for j in range(2):
            across[j].wait_recv()
            sums[j] = sums[j] + landed[j].astype(F32)
        last()
        for cp in copies:
            cp.wait_send()

    vmem = pl.BlockSpec(memory_space=pltpu.VMEM)
    rows = (2, 128, wide)
    f32 = lambda *shape: jax.ShapeDtypeStruct(shape, F32)
    ins = (own, grad_out, gate_w, up_w, down_w, first_gu, second_g, second_u, first_d, second_d)
    outs = [
        f32(*rows),
        f32(*rows),
        jax.ShapeDtypeStruct(rows, BF16),
        jax.ShapeDtypeStruct((4, 2, 128, width), BF16),
        f32(RANK, units),
        f32(RANK, units),
        f32(RANK, units),
    ]
    return pl.pallas_call(
        kernel,
        out_shape=outs,
        in_specs=[vmem] * len(ins),
        out_specs=[vmem] * len(outs),
        scratch_shapes=[pltpu.VMEM((4, 256, units), BF16)] * 3
        + [pltpu.VMEM((4, 256, SIDE), BF16)] * 2
        + [pltpu.VMEM((3,) + rows, BF16)] * 2
        + [pltpu.VMEM(rows, BF16)] * 6
        + [_sem(2), _sem(6), _sem(6), _sem(8), _sem(8)],
        compiler_params=pltpu.CompilerParams(
            collective_id=cid, has_side_effects=True, vmem_limit_bytes=56 * 1024 * 1024
        ),
        name="feed_forward",
    )(*ins)


def group_scatter(main, side, cid, name):
    def kernel(
        main_in,
        side_in,
        sums,
        side_all,
        first,
        staged,
        second,
        side_first,
        side_staged,
        side_second,
        side_own,
        send_sem,
        recv_sem,
        gown_sem,
        gsend_sem,
        grecv_sem,
    ):
        place = _place()
        c, f, x, core, core_peer, x_peer = place
        h = 1 - core
        _greet([core_peer, x_peer])
        group = (
            (side_in, side_first, side_staged, side_second),
            (main_in, first, staged, second),
        )
        one, two = {}, {}
        for i, (src, land, _, _) in enumerate(group):
            for far in (1, 0):
                for j in range(2):
                    k = (i * 2 + j) * 2 + far
                    cp = _remote(
                        src.at[1 - h, j, 1 - x if far else x],
                        land.at[far, j],
                        send_sem.at[k],
                        recv_sem.at[k],
                        core_peer,
                    )
                    cp.start()
                    one[(i, j, far)] = cp
        for i, (src, land, stage, land_two) in enumerate(group):
            for j in range(2):
                one[(i, j, 1)].wait_recv()
                stage[j] = (src[h, j, 1 - x].astype(F32) + land[1, j].astype(F32)).astype(BF16)
                k = 8 + i * 2 + j
                cp = _remote(stage.at[j], land_two.at[j], send_sem.at[k], recv_sem.at[k], x_peer)
                cp.start()
                two[(i, j)] = cp
        for j in range(2):
            one[(0, j, 0)].wait_recv()
            two[(0, j)].wait_recv()
            side_own[j] = (
                side_in[h, j, x].astype(F32)
                + side_first[0, j].astype(F32)
                + side_second[j].astype(F32)
            ).astype(BF16)
        gfirst, glast = _gather_steps([side_own], [side_all], gown_sem, gsend_sem, grecv_sem, place)
        gfirst()
        for j in range(2):
            one[(1, j, 0)].wait_recv()
            sums[j] = main_in[h, j, x].astype(F32) + first[0, j].astype(F32)
        glast()
        for j in range(2):
            two[(1, j)].wait_recv()
            sums[j] = sums[j] + second[j].astype(F32)
        for cp in list(one.values()) + list(two.values()):
            cp.wait_send()

    vmem = pl.BlockSpec(memory_space=pltpu.VMEM)
    outs = [
        jax.ShapeDtypeStruct((2,) + main.shape[3:], F32),
        jax.ShapeDtypeStruct(side.shape, BF16),
    ]
    scratch = []
    for rows in (main.shape[3:], side.shape[3:]):
        scratch += [
            pltpu.VMEM((2, 2) + rows, BF16),
            pltpu.VMEM((2,) + rows, BF16),
            pltpu.VMEM((2,) + rows, BF16),
        ]
    scratch += [pltpu.VMEM((2,) + side.shape[3:], BF16)]
    scratch += [_sem(12), _sem(12), _sem(2), _sem(6), _sem(6)]
    return pl.pallas_call(
        kernel,
        out_shape=outs,
        in_specs=[vmem, vmem],
        out_specs=[vmem, vmem],
        scratch_shapes=scratch,
        compiler_params=pltpu.CompilerParams(
            collective_id=cid, has_side_effects=True, vmem_limit_bytes=40 * 1024 * 1024
        ),
        name=name,
    )(main, side)


def take_in(tokens, cotangent, cid):
    def kernel(tok, cot, tok_own, cot_own, tok_all, land_s, land_r, own_sem, send_sem, recv_sem):
        place = _place()
        c, f, x, core, core_peer, x_peer = place
        h = 1 - core
        slot = c // 2 + 4 * (c % 2)
        barrier = pltpu.get_barrier_semaphore()
        for j in range(2):
            pl.semaphore_signal(
                barrier, inc=1, device_id=(x + 2 * j + 4 * h, slot // 2), device_id_type=MESH_ID
            )
        for target in (core_peer, x_peer):
            pl.semaphore_signal(barrier, inc=1, device_id=target, device_id_type=MESH_ID)
        pl.semaphore_wait(barrier, 4)
        to_f = 2 * (c % 2) + 1 - c // 4
        to_j = (c // 2) % 2
        moves = []
        for a, (src, dst) in enumerate(((tok, tok_own), (cot, cot_own))):
            for half in range(2):
                s = 2 * f + half
                to_c = (s % 4) * 2 + s // 4
                cp = _remote(
                    src.at[half],
                    dst.at[to_j],
                    land_s.at[2 * a + half],
                    land_r.at[2 * a + to_j],
                    (to_c, to_f),
                )
                cp.start()
                moves.append(cp)
        for j in range(2):
            pltpu.make_async_copy(tok_own.at[j], tok_own.at[j], land_r.at[j]).wait()
        _gather_body([tok_own], [tok_all], own_sem, send_sem, recv_sem, place)
        for j in range(2):
            pltpu.make_async_copy(cot_own.at[j], cot_own.at[j], land_r.at[2 + j]).wait()
        for cp in moves:
            cp.wait_send()

    own = jax.ShapeDtypeStruct(tokens.shape, tokens.dtype)
    whole = jax.ShapeDtypeStruct((2, 2, 2) + tokens.shape[1:], tokens.dtype)
    return _comm_call(
        kernel,
        [tokens, cotangent],
        [own, own, whole],
        [_sem(4), _sem(4), _sem(2), _sem(6), _sem(6)],
        cid,
        "take_in",
    )


def _back_steps(src, dst, out_s, out_r, place):
    c, f, x, core, core_peer, x_peer = place
    h = 1 - core
    slot = c // 2 + 4 * (c % 2)
    place_in = slot % 2
    moves = []

    def first():
        for j in range(2):
            cp = _remote(
                src.at[j],
                dst.at[place_in],
                out_s.at[j],
                out_r.at[place_in],
                (x + 2 * j + 4 * h, slot // 2),
            )
            cp.start()
            moves.append(cp)

    def last():
        for half in range(2):
            pltpu.make_async_copy(dst.at[half], dst.at[half], out_r.at[half]).wait()
        for cp in moves:
            cp.wait_send()

    return first, last


def _back_sources(place):
    c, f = place[:2]
    from_f = 2 * (c % 2) + 1 - c // 4
    return [(((2 * f + half) % 4) * 2 + (2 * f + half) // 4, from_f) for half in range(2)]


def give_back(arrays, piece, lines, cid):
    count = len(arrays)
    n = piece.shape[1]

    def kernel(*refs):
        owns, (piece_in, lines_in) = refs[:count], refs[count : count + 2]
        backs = refs[count + 2 : 2 * count + 2]
        spread, lines_out, late = refs[2 * count + 2 : 2 * count + 5]
        sems = refs[2 * count + 5 :]
        place = _place()
        _greet(
            _back_sources(place) + [place[4], place[5], _y_peer(place)] + _z_peers(place)
        )
        start, across, finish = _ctx_first(piece_in, late, *sems[2 * count : 2 * count + 3], place)
        second = _ctx_second(late, spread, *sems[2 * count + 3 : 2 * count + 6], place)
        other = _ctx_second(lines_in, lines_out, *sems[2 * count + 6 :], place)
        steps = [
            _back_steps(owns[i], backs[i], sems[2 * i], sems[2 * i + 1], place)
            for i in range(count)
        ]
        start()
        other[0]()
        across()
        for first, _ in steps:
            first()
        finish()
        second[0]()
        other[1]()
        second[1]()
        other[2]()
        second[2]()
        for _, last in steps:
            last()

    outs = [jax.ShapeDtypeStruct(a.shape, a.dtype) for a in arrays]
    outs += [_spread_of(n), _spread_of(lines.shape[-1]), jax.ShapeDtypeStruct(_lines_of(n), BF16)]
    return _comm_call(
        kernel,
        list(arrays) + [piece, lines],
        outs,
        [_sem(2)] * (2 * count) + FIRST_SEMS + SECOND_SEMS + SECOND_SEMS,
        cid,
        "give_back",
    )[:-1]


def attend_call(proj, cosine, sine, length, behind, cid):
    rows = proj.shape[0]
    step = 256
    scale = HEAD_DIM ** (-0.5)
    lane = PAD_HEAD

    def kernel(
        len_ref,
        proj_ref,
        cos_ref,
        sin_ref,
        behind_ref,
        att_ref,
        qkv_ref,
        lse_ref,
        whole_ref,
        own_sem,
        send_sem,
        recv_sem,
    ):
        place = _place()
        _greet([place[4], place[5]])
        first, forward, own_here, core_here, far_here, last = _order_steps(
            behind_ref, whole_ref, own_sem, send_sem, recv_sem, place
        )
        first()
        live = len_ref[0]
        for part in range(6):
            cols = slice(part * lane, (part + 1) * lane)
            v = proj_ref[:, cols]
            v = v * cos_ref[...] + pltpu.roll(v, HALF_PAD, 1) * sin_ref[...]
            qkv_ref[:, cols] = v.astype(BF16)
        qkv_ref[:, 6 * lane :] = proj_ref[:, 6 * lane :].astype(BF16)
        for block in range(rows // step):
            keys = (block + 1) * step
            row = pl.ds(block * step, step)
            qpos = block * step + lax.broadcasted_iota(jnp.int32, (step, keys), 0)
            kpos = lax.broadcasted_iota(jnp.int32, (step, keys), 1)
            allowed = (kpos <= qpos) & (kpos < live)
            stats = jnp.zeros((step, lane), F32)
            lanes = lax.broadcasted_iota(jnp.int32, (step, lane), 1)
            for head in range(4):
                q = qkv_ref[row, head * lane : (head + 1) * lane]
                kv = head // 2
                k = qkv_ref[:keys, (4 + kv) * lane : (5 + kv) * lane]
                v = qkv_ref[:keys, (6 + kv) * lane : (7 + kv) * lane]
                s = lax.dot_general(q, k, (((1,), (1,)), ((), ())), preferred_element_type=F32)
                s = jnp.where(allowed, s * scale, NEGATIVE)
                top = jnp.max(s, axis=1, keepdims=True)
                p = jnp.where(allowed, jnp.exp(s - top), 0.0)
                total = jnp.sum(p, axis=1, keepdims=True)
                o = jnp.dot(p.astype(BF16), v, preferred_element_type=F32) / total
                att_ref[row, head * lane : (head + 1) * lane] = o.astype(BF16)
                stats = jnp.where(lanes == head, top + jnp.log(total), stats)
            lse_ref[row, :] = stats
        own_here()
        core_here()
        for j in range(2):
            forward(j)
        for j in range(2):
            far_here(j)
        last()

    vmem, hbm = pl.BlockSpec(memory_space=pltpu.VMEM), pl.BlockSpec(memory_space=pl.ANY)
    return pl.pallas_call(
        kernel,
        out_shape=(
            jax.ShapeDtypeStruct((rows, 4 * lane), BF16),
            jax.ShapeDtypeStruct(proj.shape, BF16),
            jax.ShapeDtypeStruct((rows, lane), F32),
            jax.ShapeDtypeStruct((4,) + behind.shape, behind.dtype),
        ),
        in_specs=[pl.BlockSpec(memory_space=pltpu.SMEM), vmem, vmem, vmem, hbm],
        out_specs=(vmem, vmem, vmem, hbm),
        scratch_shapes=[_sem(2), _sem(6), _sem(6)],
        compiler_params=pltpu.CompilerParams(
            collective_id=cid, has_side_effects=True, vmem_limit_bytes=40 * 1024 * 1024
        ),
        name="attend",
    )(length, proj, cosine, sine, behind)


def attend_back_call(
    low_own,
    small_own,
    early,
    out_far,
    out_side,
    qkv,
    stats,
    att,
    inner_o,
    order,
    cosine,
    sine,
    length,
    out_w,
    first_o,
    second_o,
    weight_all,
    second_all,
    cid,
):
    width = low_own.shape[-1]
    rows = qkv.shape[0]
    wide = width + SIDE
    step_rows = 256
    scale = HEAD_DIM ** (-0.5)
    lane = PAD_HEAD
    quarter = width // 4
    middle_n = 4 * quarter
    early_n = early.shape[1]
    big = (qkv, stats, att, inner_o, order, cosine, sine, out_w, first_o, second_o, weight_all, second_all)
    count = len(big)

    def kernel(*refs):
        len_ref, low_ref, small_ref, early_ref, out_ref, out_side_ref = refs[:6]
        big_in = refs[6 : 6 + count]
        sums, side_all, grad_ref, landed_out, early_out, middle_lines, early_lines, small_out = refs[
            6 + count : 14 + count
        ]
        refs = refs[14 + count :]
        (
            qkv_ref,
            lse_ref,
            att_ref,
            inner_ref,
            order_ref,
            cos_ref,
            sin_ref,
            ow_ref,
            fo_ref,
            so_ref,
            wa_ref,
            sa_ref,
        ) = refs[:count]
        (
            low,
            do_ref,
            gio_ref,
            dk_ref,
            dv_ref,
            part,
            land,
            staged,
            landed,
            side_own,
            middle_ref,
            load_sem,
            own_sem,
            send_sem,
            recv_sem,
            s_sem,
            r_sem,
        ) = refs[count : count + 17]
        sems = refs[count + 17 :]
        place = _place()
        c, f, x, core, core_peer, x_peer = place
        _greet([core_peer, x_peer, _y_peer(place)] + _z_peers(place))
        loads = [
            pltpu.make_async_copy(big_in[i], refs[i], load_sem.at[i]) for i in range(count)
        ]
        small_first, small_forward, small_own_here, small_core, small_far, small_last = _order_steps(
            small_ref, small_out, *sems[0:3], place
        )
        early_start, early_across, early_finish = _ctx_first(early_ref, early_lines, *sems[3:6], place)
        early_two = _ctx_second(early_lines, early_out, *sems[6:9], place)
        mid_start, mid_across, mid_finish = _ctx_first(middle_ref, middle_lines, *sems[9:12], place)
        side_first, side_last = _gather_steps([side_own], [side_all], *sems[12:15], place)
        live = len_ref[0]

        sends = {}
        hh = 1 - core
        local = []
        small_first()
        early_start()
        for k, target in ((0, x_peer), (2, core_peer)):
            for j in (1, 0):
                cp = _remote(
                    low_ref.at[j], low.at[hh, j, x], send_sem.at[k + j], recv_sem.at[k + j], target
                )
                cp.start()
                sends[(k, j)] = cp
        for j in range(2):
            lc = pltpu.make_async_copy(low_ref.at[j], low.at[hh, j, x], own_sem.at[j])
            lc.start()
            local.append(lc)
        for cp in loads:
            cp.start()
        swaps = [
            _remote(out_ref.at[j], landed_out.at[j], s_sem.at[8 + j], r_sem.at[8 + j], x_peer)
            for j in range(2)
        ]
        dk_ref[...] = jnp.zeros_like(dk_ref)
        dv_ref[...] = jnp.zeros_like(dv_ref)
        early_across()
        small_own_here()
        for j in range(2):
            small_forward(j)
        for cp in loads:
            cp.wait()
        for lc in local:
            lc.wait()

        def arrive(j):
            sends[(0, j)].wait_recv()
            cp = _remote(
                low.at[hh, j, 1 - x],
                low.at[hh, j, 1 - x],
                send_sem.at[4 + j],
                recv_sem.at[4 + j],
                core_peer,
            )
            cp.start()
            sends[(4, j)] = cp
            sends[(2, j)].wait_recv()
            cp.wait_recv()

        def through_output(t):
            g = low[t // 2, t % 2].reshape(step_rows, width)
            gio = dot_t(g, so_ref[...]).astype(BF16)
            row = pl.ds(t * step_rows, step_rows)
            gio_ref[row, :] = gio
            do_ref[row, :] = (dot_t(g, ow_ref[...]) + dot_t(gio, fo_ref[...])).astype(BF16)

        def attention(t, hook):
            keys = (t + 1) * step_rows
            row = pl.ds(t * step_rows, step_rows)
            qpos = t * step_rows + lax.broadcasted_iota(jnp.int32, (step_rows, keys), 0)
            kpos = lax.broadcasted_iota(jnp.int32, (step_rows, keys), 1)
            allowed = (kpos <= qpos) & (kpos < live)
            cos, sin = cos_ref[row, :], sin_ref[row, :]
            for head in range(4):
                kv = head // 2
                at = slice(head * lane, (head + 1) * lane)
                q = qkv_ref[row, at]
                k = qkv_ref[:keys, (4 + kv) * lane : (5 + kv) * lane]
                v = qkv_ref[:keys, (6 + kv) * lane : (7 + kv) * lane]
                do = do_ref[row, at]
                s = dot_t(q, k)
                p = jnp.where(allowed, jnp.exp(s * scale - lse_ref[row, head : head + 1]), 0.0)
                dp = dot_t(do, v)
                total = jnp.sum(p * dp, axis=1, keepdims=True)
                ds = (p * (dp - total)).astype(BF16)
                dq = scale * dot(ds, k)
                dq = dq * cos - pltpu.roll(dq, HALF_PAD, 1) * sin
                grad_ref[row, at] = dq.astype(BF16)
                dk_ref[kv, :keys] += dot_rows(ds, q)
                dv_ref[kv, :keys] += dot_rows(p.astype(BF16), do)
                if head == 1 and hook is not None:
                    hook()
            for kv in range(2):
                dk = scale * dk_ref[kv, row, :]
                dk = dk * cos - pltpu.roll(dk, HALF_PAD, 1) * sin
                grad_ref[row, (4 + kv) * lane : (5 + kv) * lane] = dk.astype(BF16)
                grad_ref[row, (6 + kv) * lane : (7 + kv) * lane] = dv_ref[kv, row, :].astype(BF16)
            g = grad_ref[row, :]
            for at in range(0, width, 256):
                value = dot_t(g, wa_ref[at : at + 256, :])
                part[t, :, :, at : at + 256] = value.astype(BF16).reshape(2, 128, 256)
            part[t, :, :, width:] = dot_t(g, sa_ref[...]).astype(BF16).reshape(2, 128, SIDE)

        def to_core(t):
            h, j = t // 2, t % 2
            return _remote(part.at[t], land.at[j], s_sem.at[j], r_sem.at[j], core_peer)

        def to_x(j):
            return _remote(staged.at[j], landed.at[j], s_sem.at[2 + j], r_sem.at[2 + j], x_peer)

        def leave(t):
            @pl.when(core == t // 2)
            def _():
                to_core(t).start()

        def combine(t):
            j = t % 2

            @pl.when(core == 1 - t // 2)
            def _():
                to_core(t).wait_recv()
                staged[j] = (part[t, 1 - x].astype(F32) + land[j, 1 - x].astype(F32)).astype(BF16)
                to_x(j).start()
                sums[j] = part[t, x].astype(F32) + land[j, x].astype(F32)

        arrive(1)
        through_output(3)
        through_output(1)
        for cp in swaps:
            cp.start()
        attention(3, None)
        leave(3)
        arrive(0)
        through_output(2)
        through_output(0)
        o_a = dot_rows(gio_ref[...], att_ref[...])[:RANK]
        o_a = jnp.concatenate(
            [o_a[:, head * lane : head * lane + HEAD_DIM] for head in range(4)], axis=1
        )
        middle_ref[:, :quarter] = o_a.astype(BF16)
        own_cols = pl.ds(pl.multiple_of(f * quarter, 128), quarter)
        g = low[:, :, :, :, own_cols].reshape(rows, quarter)
        middle_ref[:, quarter : 2 * quarter] = (ADAPTER_SCALE * dot_rows(inner_ref[...], g)[:RANK]).astype(BF16)
        for j in range(2):
            small_far(j)
        small_core()
        in_gu = jnp.zeros((SIDE, quarter), F32)
        for k in range(4):
            u = order_ref[k, :, :, own_cols].reshape(step_rows, quarter)
            in_gu += dot_rows(small_out[k].reshape(step_rows, SIDE), u)
        middle_ref[:, 2 * quarter : 3 * quarter] = in_gu[:RANK].astype(BF16)
        middle_ref[:, 3 * quarter :] = in_gu[RANK : 2 * RANK].astype(BF16)
        mid_start()
        early_finish()
        early_two[0]()
        mid_across()
        attention(2, lambda: combine(3))
        leave(2)
        attention(1, lambda: combine(2))
        leave(1)
        early_two[1]()
        attention(0, lambda: combine(1))
        leave(0)
        combine(0)
        for t in range(4):

            @pl.when(core == t // 2)
            def _():
                to_core(t).wait_send()

        for j in range(2):
            swaps[j].wait()
            cp = to_x(j)
            cp.wait_recv()
            sums[j] = sums[j] + landed[j].astype(F32)
            cp.wait_send()
            side_own[j] = (
                sums[j, :, width:] + out_side_ref[j] + landed_out[j, :, width:].astype(F32)
            ).astype(BF16)
        side_first()
        small_last()
        early_two[2]()
        mid_finish()
        side_last()
        for cp in sends.values():
            cp.wait_send()

    vmem, hbm = pl.BlockSpec(memory_space=pltpu.VMEM), pl.BlockSpec(memory_space=pl.ANY)
    shape = jax.ShapeDtypeStruct
    return pl.pallas_call(
        kernel,
        out_shape=[
            shape((2, 128, wide), F32),
            shape((2, 2, 2, 128, SIDE), BF16),
            shape(qkv.shape, BF16),
            shape(out_far.shape, BF16),
            _spread_of(early_n),
            shape(_lines_of(middle_n), BF16),
            shape(_lines_of(early_n), BF16),
            shape((4, 2, 128, SIDE), BF16),
        ],
        in_specs=[pl.BlockSpec(memory_space=pltpu.SMEM)] + [hbm] * 4 + [vmem] + [hbm] * count,
        out_specs=[vmem, hbm, vmem, vmem, hbm, hbm, hbm, vmem],
        scratch_shapes=[pltpu.VMEM(a.shape, a.dtype) for a in big]
        + [
            pltpu.VMEM((2, 2, 2, 128, width), BF16),
            pltpu.VMEM((rows, 4 * lane), BF16),
            pltpu.VMEM((rows, SIDE), BF16),
            pltpu.VMEM((2, rows, lane), F32),
            pltpu.VMEM((2, rows, lane), F32),
            pltpu.VMEM((4, 2, 128, wide), BF16),
            pltpu.VMEM((2, 2, 128, wide), BF16),
            pltpu.VMEM((2, 128, wide), BF16),
            pltpu.VMEM((2, 128, wide), BF16),
            pltpu.VMEM((2, 128, SIDE), BF16),
            pltpu.VMEM((RANK, middle_n), BF16),
            _sem(count),
            _sem(2),
            _sem(6),
            _sem(6),
            _sem(10),
            _sem(10),
        ]
        + [_sem(2), _sem(6), _sem(6)]
        + FIRST_SEMS
        + SECOND_SEMS
        + FIRST_SEMS
        + [_sem(2), _sem(6), _sem(6)],
        compiler_params=pltpu.CompilerParams(
            collective_id=cid, has_side_effects=True, vmem_limit_bytes=58 * 1024 * 1024
        ),
        name="attend_back",
    )(length, low_own, small_own, early, out_far, out_side, *big)


def table_call(early, middle, late, adapters):
    f32 = lambda *shape: jax.ShapeDtypeStruct(shape, F32)
    choices = 8
    outs = [
        f32(choices, 5, RANK, 1536),
        f32(choices, RANK, 1536),
        f32(choices, RANK, 4096),
        f32(choices, RANK, 1536),
        f32(choices, 2, RANK, 768),
        f32(choices, RANK, 1536),
        f32(choices, 2, RANK, 4096),
        f32(choices, RANK, 1536),
    ]
    plan = (
        ((6, 0, 1024), (6, 1, 1024), (2, None, 1024)),
        ((1, None, 384), (5, None, 384), (0, 3, 384), (0, 4, 384)),
        (
            (0, 0, 384),
            (0, 1, 384),
            (0, 2, 384),
            (3, None, 384),
            (4, 0, 192),
            (4, 1, 192),
            (7, None, 384),
        ),
    )

    def kernel(which, early_ref, middle_ref, late_ref, *refs):
        outs, acc, sems = refs[:8], refs[8:16], refs[16]

        def add(piece, ref):
            def one_slot(origin, carry):
                row = which[origin]
                for f in range(4):
                    at = 0
                    for out, table, n in plan[piece]:
                        value = ref[origin // 4, f % 2, origin % 4, f // 2, :, at : at + n].astype(F32)
                        cols = slice(f * n, (f + 1) * n)
                        if table is None:
                            acc[out][row, :, cols] += value
                        else:
                            acc[out][row, table, :, cols] += value
                        at += n
                return carry

            lax.fori_loop(0, 8, one_slot, 0)

        def send(out):
            cp = pltpu.make_async_copy(acc[out], outs[out], sems.at[out])
            cp.start()
            return cp

        for out in (2, 6):
            acc[out][...] = jnp.zeros_like(acc[out])
        add(0, early_ref)
        copies = [send(out) for out in (2, 6)]
        for out in (0, 1, 3, 4, 5, 7):
            acc[out][...] = jnp.zeros_like(acc[out])
        add(1, middle_ref)
        copies += [send(out) for out in (1, 5)]
        add(2, late_ref)
        copies += [send(out) for out in (0, 3, 4, 7)]
        for cp in copies:
            cp.wait()

    vmem, hbm = pl.BlockSpec(memory_space=pltpu.VMEM), pl.BlockSpec(memory_space=pl.ANY)
    return pl.pallas_call(
        kernel,
        out_shape=outs,
        in_specs=[pl.BlockSpec(memory_space=pltpu.SMEM), vmem, vmem, vmem],
        out_specs=[hbm] * 8,
        scratch_shapes=[pltpu.VMEM(o.shape, F32) for o in outs] + [_sem(8)],
        compiler_params=pltpu.CompilerParams(vmem_limit_bytes=40 * 1024 * 1024),
        name="tables",
    )(adapters, early, middle, late)


def dot(left, right):
    return jnp.dot(left, right, preferred_element_type=F32)


def dot_t(left, right):
    return lax.dot_general(left, right, (((1,), (1,)), ((), ())), preferred_element_type=F32)


def dot_rows(left, right):
    return lax.dot_general(left, right, (((0,), (0,)), ((), ())), preferred_element_type=F32)


def side_pad(value, before=0):
    return jnp.pad(value, ((0, 0), (before, SIDE - before - value.shape[1])))


def blocks(value):
    return value.reshape(2, 2, 2, 128, value.shape[-1])


def own_blocks(value):
    return value.reshape(2, 128, value.shape[-1])


def flat(value):
    return value.reshape(-1, value.shape[-1])


def slot_local(
    tokens,
    cotangent,
    lengths,
    slot_adapter_index,
    attention_norm_gain,
    feedforward_norm_gain,
    query_weight,
    key_weight,
    value_weight,
    output_weight,
    gate_weight,
    up_weight,
    down_weight,
    adapter_input_first,
    adapter_output_first,
    adapter_down_first,
    adapter_query_second,
    adapter_key_value_second,
    adapter_output_second,
    adapter_gate_up_second,
    adapter_down_second,
):
    width = tokens.shape[-1]
    hidden_units = gate_weight.shape[1]
    quarter = width // 4
    c = lax.axis_index("ctx")
    f = lax.axis_index("fsdp")
    x, core = f // 2, f % 2
    slot = c // 2 + 4 * (c % 2)
    length = lax.dynamic_slice_in_dim(lengths, slot, 1, 0)
    adapter = slot_adapter_index[slot]

    def pick(table):
        return lax.dynamic_index_in_dim(table, adapter, 0, keepdims=False)

    def cut(value, axis, size):
        return lax.dynamic_slice_in_dim(value, f * size, size, axis)

    first_in = pick(adapter_input_first)
    first_out = pick(adapter_output_first)
    first_down = pick(adapter_down_first)
    second_q = cut(pick(adapter_query_second), 1, query_weight.shape[1])
    second_kv = cut(pick(adapter_key_value_second), 2, key_weight.shape[1])
    second_o = pick(adapter_output_second)
    second_gu = cut(pick(adapter_gate_up_second), 2, hidden_units)
    second_d = pick(adapter_down_second)
    first_o_own = cut(first_out, 0, output_weight.shape[0])
    first_d_own = cut(first_down, 0, hidden_units)

    def pad_turned(w):
        rows = w.shape[0]
        w = w.reshape(rows, -1, 2, HEAD_DIM // 2)
        w = jnp.pad(w, ((0, 0), (0, 0), (0, 0), (0, HALF_PAD - HEAD_DIM // 2)))
        return w.reshape(rows, -1)

    def pad_plain(w):
        rows = w.shape[0]
        w = w.reshape(rows, -1, HEAD_DIM)
        w = jnp.pad(w, ((0, 0), (0, 0), (0, PAD_HEAD - HEAD_DIM)))
        return w.reshape(rows, -1)

    def unpad_turned(g):
        rows = g.shape[0]
        return g.reshape(rows, -1, 2, HALF_PAD)[..., : HEAD_DIM // 2].reshape(rows, -1)

    def unpad_plain(g):
        rows = g.shape[0]
        return g.reshape(rows, -1, PAD_HEAD)[..., :HEAD_DIM].reshape(rows, -1)

    def pad_heads(w):
        w = w.reshape(-1, HEAD_DIM, w.shape[1])
        w = jnp.pad(w, ((0, 0), (0, PAD_HEAD - HEAD_DIM), (0, 0)))
        return w.reshape(-1, w.shape[2])

    out_w = pad_heads(output_weight)
    first_o_pad = pad_heads(side_pad(first_o_own))
    weight_all = jnp.concatenate(
        [pad_turned(query_weight), pad_turned(key_weight), pad_plain(value_weight)], axis=1
    )
    zero_q = jnp.zeros((RANK, 4 * PAD_HEAD), BF16)
    zero_k = jnp.zeros((RANK, 2 * PAD_HEAD), BF16)
    second_all = jnp.concatenate(
        [
            jnp.concatenate([pad_turned(second_q), zero_k, zero_k], axis=1),
            jnp.concatenate([zero_q, pad_turned(second_kv[0]), zero_k], axis=1),
            jnp.concatenate([zero_q, zero_k, pad_plain(second_kv[1])], axis=1),
        ],
        axis=0,
    )
    first_all = jnp.concatenate([first_in[0], first_in[1], first_in[2]], axis=1)
    first_gu = jnp.concatenate([first_in[3], first_in[4]], axis=1)

    half = HEAD_DIM // 2
    rows = 4 * 2 * tokens.shape[1]
    freqs = ROPE_BASE ** (-(jnp.arange(half, dtype=F32) * 2.0 / HEAD_DIM))
    angles = jnp.arange(rows, dtype=jnp.int32).astype(F32)[:, None] * freqs[None, :]
    gap = jnp.zeros((rows, HALF_PAD - half), F32)
    cos, sin = jnp.cos(angles), jnp.sin(angles)
    cosine = jnp.concatenate([cos, gap, cos, gap], axis=1)
    sine = jnp.concatenate([-sin, gap, sin, gap], axis=1)

    tok_own, cot_own, tok_all = take_in(tokens, cotangent, 0)
    live_rows = (jnp.arange(rows, dtype=jnp.int32) < length[0])[:, None]
    block_of = x + 4 * (1 - core) + 2 * jnp.arange(2, dtype=jnp.int32)
    own_pos = (block_of[:, None] * 128 + jnp.arange(128, dtype=jnp.int32)[None, :]).reshape(-1)
    own_live = (own_pos < length[0])[:, None]

    def own_rows(whole):
        part = lax.dynamic_slice(
            whole, (1 - core, 0, x, 0, 0), (1, 2, 1, whole.shape[3], whole.shape[4])
        )
        return part.reshape(-1, whole.shape[4])

    tokens_f = flat(tok_all).astype(F32)
    normed_one = (tokens_f * rms_factor(tokens_f) * attention_norm_gain).astype(BF16)
    inner_qkv = dot(normed_one, first_all).astype(BF16)
    proj = dot(normed_one, weight_all) + ADAPTER_SCALE * dot(inner_qkv, second_all)
    attn_b, qkv, stats, cot_order = attend_call(proj, cosine, sine, length, cot_own, 9)
    block_x = x + jnp.array([[0, 0], [1, 1], [1, 1], [0, 0]]) * (1 - 2 * x)
    block_core = core + jnp.array([[0, 0], [1, 0], [1, 0], [1, 1]]) * (1 - 2 * core)
    block_j = jnp.array([[0, 1], [0, 0], [1, 1], [0, 1]])
    order_block = (block_x + 2 * block_j + 4 * (1 - block_core)).reshape(8)
    order_pos = 128 * order_block.reshape(4, 2, 1) + jnp.arange(128, dtype=jnp.int32)
    order_live = (order_pos < length[0])[..., None]
    grad_out = jnp.where(order_live, cot_order, jnp.zeros((), BF16)).reshape(4, 256, width)
    grad_out_own = jnp.where(own_live, flat(cot_own), jnp.zeros((), BF16))

    sums, side_all = group_scatter(
        blocks(dot(attn_b, out_w).astype(BF16)),
        blocks(dot(attn_b, first_o_pad).astype(BF16)),
        1,
        "scatter_o",
    )
    inner_o = flat(side_all)[:, :RANK]
    inner_o_own = own_rows(side_all)[:, :RANK]
    own_f = flat(tok_own).astype(F32)
    resid = own_f + flat(sums) + ADAPTER_SCALE * dot(inner_o_own, second_o)
    factor_two = rms_factor(resid)
    normed_two_own = (resid * factor_two * feedforward_norm_gain).astype(BF16)

    def pad_rank(table, before=0):
        return jnp.pad(table, ((before, SIDE - before - table.shape[0]), (0, 0)))

    sums, out_sums, out_far, order, gate_b, up_b, down_a = feed_forward(
        own_blocks(normed_two_own),
        grad_out,
        gate_weight,
        up_weight,
        down_weight,
        side_pad(first_gu),
        pad_rank((ADAPTER_SCALE * second_gu[0]).astype(BF16)),
        pad_rank((ADAPTER_SCALE * second_gu[1]).astype(BF16), RANK),
        side_pad(first_d_own, 3 * RANK),
        pad_rank((ADAPTER_SCALE * second_d).astype(BF16), 3 * RANK),
        3,
    )
    sums = flat(sums)
    grad_inner_gu_own = sums[:, width : width + 2 * RANK].astype(BF16)
    sums = sums[:, :width]
    grad_normed_two = (
        (sums + dot_t(grad_inner_gu_own, first_gu)).astype(BF16).astype(F32)
    )
    grad_resid = grad_out_own.astype(F32) + norm_back(
        resid, factor_two, feedforward_norm_gain, grad_normed_two
    )
    grad_low_own = grad_resid.astype(BF16)

    def pack(parts):
        return jnp.concatenate(parts, axis=1).astype(BF16)

    early = pack([gate_b, up_b, down_a])
    second_scaled = (ADAPTER_SCALE * second_all).astype(BF16)
    sums, side_all, grad_qkv, out_landed, early, middle = attend_back_call(
        own_blocks(grad_low_own),
        own_blocks(side_pad(grad_inner_gu_own)),
        early,
        out_far,
        out_sums[..., width:],
        qkv,
        stats,
        attn_b,
        flat(side_all),
        order,
        cosine,
        sine,
        length,
        out_w,
        first_o_pad,
        pad_rank((ADAPTER_SCALE * second_o).astype(BF16)),
        weight_all,
        jnp.pad(second_scaled, ((0, SIDE - 3 * RANK), (0, 0))),
        10,
    )[:6]
    out_sums = flat(out_sums) + flat(out_landed).astype(F32)
    inner_d_own = out_sums[:, width + 3 * RANK : width + 4 * RANK].astype(BF16)
    out_own = jnp.where(
        own_live, resid + out_sums[:, :width] + ADAPTER_SCALE * dot(inner_d_own, second_d), 0.0
    ).astype(BF16)
    all_b = ADAPTER_SCALE * dot_rows(inner_qkv, grad_qkv)
    sums = flat(sums)
    grad_inner_qkv = flat(side_all)[:, : 3 * RANK]
    grad_inner_own = sums[:, width : width + 3 * RANK].astype(BF16)
    grad_normed_one = (sums[:, :width] + dot_t(grad_inner_own, first_all)).astype(BF16).astype(F32)
    grad_tok_own = grad_resid + norm_back(
        own_f, rms_factor(own_f), attention_norm_gain, grad_normed_one
    )
    one_cut = cut(normed_one, 1, quarter)
    in_qkv = dot_rows(grad_inner_qkv, one_cut)
    inner_d = flat(side_all.reshape(8, 128, SIDE)[order_block])[:, 3 * RANK : 4 * RANK]
    d_b = ADAPTER_SCALE * dot_rows(inner_d, cut(flat(grad_out), 1, quarter))
    late = pack(
        [
            in_qkv[:RANK],
            in_qkv[RANK : 2 * RANK],
            in_qkv[2 * RANK :],
            unpad_turned(all_b[:RANK, : 4 * PAD_HEAD]),
            unpad_turned(all_b[RANK : 2 * RANK, 4 * PAD_HEAD : 6 * PAD_HEAD]),
            unpad_plain(all_b[2 * RANK :, 6 * PAD_HEAD :]),
            d_b,
        ]
    )
    out_tokens, grad_tokens, late, middle = give_back(
        [own_blocks(out_own), own_blocks(grad_tok_own.astype(BF16))], late, middle, 7
    )

    full = table_call(early, middle, late, slot_adapter_index)
    turn = lambda t: jnp.swapaxes(t, -1, -2)
    return (
        out_tokens,
        grad_tokens.astype(F32),
        turn(full[0]),
        turn(full[1]),
        turn(full[2]),
        full[3],
        full[4],
        full[5],
        full[6],
        full[7],
    )


def solution(mesh):
    one_slot = mesh.shape["ctx"] == 8 and mesh.shape["fsdp"] == 4
    return jax.shard_map(
        slot_local if one_slot else local,
        mesh=mesh,
        in_specs=(
            P("fsdp", "ctx", None),
            P("fsdp", "ctx", None),
            P(),
            P(),
            P(),
            P(),
            P(None, "fsdp"),
            P(None, "fsdp"),
            P(None, "fsdp"),
            P("fsdp", None),
            P(None, "fsdp"),
            P(None, "fsdp"),
            P("fsdp", None),
            P(),
            P(),
            P(),
            P(),
            P(),
            P(),
            P(),
            P(),
        ),
        out_specs=(
            P("fsdp", "ctx", None),
            P("fsdp", "ctx", None),
            P(),
            P(),
            P(),
            P(),
            P(),
            P(),
            P(),
            P(),
        ),
        check_vma=False,
    )
```

```python
import math

import jax
import jax.numpy as jnp
import numpy as np
from jax import lax
from jax.experimental import pallas as pl
from jax.experimental.pallas import tpu as pltpu
from jax.sharding import PartitionSpec as P

QUERY_HEADS = 16
KEY_VALUE_HEADS = 8
HEAD_DIM = 96


EPSILON = 1e-05
NEGATIVE = -1e30
ADAPTER_SCALE = 0.5
ROPE_BASE = 100000.0


def from_behind(x, axis, by):
    size = lax.axis_size(axis)
    return lax.ppermute(x, axis, [(i, (i + by) % size) for i in range(size)])


def rope_tables(positions, head_size):
    half_size = head_size // 2
    freqs = ROPE_BASE ** (-(jnp.arange(half_size, dtype=jnp.float32) * 2.0 / head_size))
    angles = positions.astype(jnp.float32)[:, None] * freqs[None, :]
    return (jnp.cos(angles)[:, None, :], jnp.sin(angles)[:, None, :])


def apply_rotation(values, cosine_table, sine_table):
    half_size = values.shape[-1] // 2
    first_half = values[..., :half_size]
    second_half = values[..., half_size:]
    return jnp.concatenate(
        [
            first_half * cosine_table - second_half * sine_table,
            second_half * cosine_table + first_half * sine_table,
        ],
        axis=-1,
    )


def rotate_back(gradient_tree, cosine_table, sine_table):
    half_size = gradient_tree.shape[-1] // 2
    first_half = gradient_tree[..., :half_size]
    second_half = gradient_tree[..., half_size:]
    return jnp.concatenate(
        [
            first_half * cosine_table + second_half * sine_table,
            second_half * cosine_table - first_half * sine_table,
        ],
        axis=-1,
    )


def rms_factor(values):
    return lax.rsqrt(jnp.mean(values * values, axis=-1, keepdims=True) + EPSILON)


def norm_back(values, factor, gain, grad_norm):
    scaled = grad_norm * gain
    return factor * scaled - values * factor**3 * jnp.mean(scaled * values, axis=-1, keepdims=True)


def pick_rows(onehot, table):
    return jnp.einsum("sa,a...->s...", onehot, table, preferred_element_type=jnp.float32).astype(
        jnp.bfloat16
    )


def spread_rows(onehot, gradient_tree):
    return jnp.einsum("sa,s...->a...", onehot, gradient_tree, precision=lax.Precision.HIGHEST)


def direct_product(input_rows, weight_matrix):
    return jnp.einsum("std,do->sto", input_rows, weight_matrix, preferred_element_type=jnp.float32)


def direct_back(gradient_tree, weight_matrix):
    return jnp.einsum(
        "sto,do->std", gradient_tree, weight_matrix, preferred_element_type=jnp.float32
    )


def inner_product_part(input_rows, down):
    return jnp.einsum("std,sdr->str", input_rows, down, preferred_element_type=jnp.float32)


def inner_back(gradient_tree, upward_rows):
    return ADAPTER_SCALE * jnp.einsum(
        "sto,sro->str", gradient_tree, upward_rows, preferred_element_type=jnp.float32
    )


def through_down(grad_inner, down):
    return jnp.einsum("str,sdr->std", grad_inner, down, preferred_element_type=jnp.float32)


def down_grad(input_rows, grad_inner):
    return jnp.einsum("std,str->sdr", input_rows, grad_inner, preferred_element_type=jnp.float32)


def upward_grad(inner_rows, gradient_tree):
    return ADAPTER_SCALE * jnp.einsum(
        "jvp,jvx->jpx", inner_rows, gradient_tree, preferred_element_type=jnp.float32
    )


def upward_apply(inner_rows, upward_rows):
    return ADAPTER_SCALE * jnp.einsum(
        "str,sro->sto", inner_rows, upward_rows, preferred_element_type=jnp.float32
    )


def project(input_rows, weight_matrix, down, upward_rows):
    inner_rows = inner_product_part(input_rows, down).astype(jnp.bfloat16)
    return (
        inner_rows,
        direct_product(input_rows, weight_matrix) + upward_apply(inner_rows, upward_rows),
    )


def project_back(input_rows, grad_output, weight_matrix, down, upward_rows, inner_rows):
    grad_upward = upward_grad(inner_rows, grad_output)
    grad_inner = inner_back(grad_output, upward_rows).astype(jnp.bfloat16)
    grad_down = down_grad(input_rows, grad_inner)
    grad_inputs = direct_back(grad_output, weight_matrix) + through_down(grad_inner, down)
    return (grad_inputs, grad_down, grad_upward)


def allowed_mask(key_start, key_count, query_pos, lengths):
    key_pos = key_start + jnp.arange(key_count, dtype=jnp.int32)
    causal = key_pos[None, :] <= query_pos[:, None]
    live = key_pos[None, :] < lengths[:, None]
    return (causal[None, :, :] & live[:, None, :])[:, None, None, :, :]


def attend_block(state, key_block, value_block, key_start, query_head_rows, query_pos, lengths):
    run_max, run_sum, run_acc = state
    scale = query_head_rows.shape[-1] ** (-0.5)
    scores = (
        jnp.einsum(
            "sqhgd,skhd->shgqk", query_head_rows, key_block, preferred_element_type=jnp.float32
        )
        * scale
    )
    allowed = allowed_mask(key_start, key_block.shape[1], query_pos, lengths)
    new_max = jnp.maximum(run_max, jnp.max(jnp.where(allowed, scores, NEGATIVE), axis=-1))
    weights = jnp.where(allowed, jnp.exp(scores - new_max[..., None]), 0.0)
    factor = jnp.exp(run_max - new_max)
    new_sum = run_sum * factor + jnp.sum(weights, axis=-1)
    update = jnp.einsum(
        "shgqk,skhd->shgqd",
        weights.astype(jnp.bfloat16),
        value_block,
        preferred_element_type=jnp.float32,
    )
    return (new_max, new_sum, run_acc * factor[..., None] + update)


def attend_back(
    key_block,
    value_block,
    key_start,
    query_head_rows,
    grad_heads,
    log_total,
    row_dot,
    query_pos,
    lengths,
):
    scale = query_head_rows.shape[-1] ** (-0.5)
    scores = (
        jnp.einsum(
            "sqhgd,skhd->shgqk", query_head_rows, key_block, preferred_element_type=jnp.float32
        )
        * scale
    )
    allowed = allowed_mask(key_start, key_block.shape[1], query_pos, lengths)
    probs = jnp.where(allowed, jnp.exp(scores - log_total[..., None]), 0.0)
    grad_probs = jnp.einsum(
        "sqhgd,skhd->shgqk", grad_heads, value_block, preferred_element_type=jnp.float32
    )
    grad_scores = (probs * (grad_probs - row_dot[..., None])).astype(jnp.bfloat16)
    grad_query = scale * jnp.einsum(
        "shgqk,skhd->sqhgd", grad_scores, key_block, preferred_element_type=jnp.float32
    )
    grad_key = scale * jnp.einsum(
        "shgqk,sqhgd->skhd", grad_scores, query_head_rows, preferred_element_type=jnp.float32
    )
    grad_value = jnp.einsum(
        "shgqk,sqhgd->skhd",
        probs.astype(jnp.bfloat16),
        grad_heads,
        preferred_element_type=jnp.float32,
    )
    return (grad_query, grad_key, grad_value)


def attend_forward(query_head_rows, key_head_rows, value_head_rows, lengths_used, query_pos):
    slots, rows, kv_heads, group_size, head_size = query_head_rows.shape
    key_flat = key_head_rows.reshape(slots, rows, kv_heads * head_size)
    value_flat = value_head_rows.reshape(slots, rows, kv_heads * head_size)
    stat_shape = (slots, kv_heads, group_size, rows)
    initial = (
        jnp.full(stat_shape, NEGATIVE, jnp.float32),
        jnp.zeros(stat_shape, jnp.float32),
        jnp.zeros(stat_shape + (head_size,), jnp.float32),
    )
    part_keys = lax.all_gather(key_flat, "ctx", axis=1, tiled=True)
    part_values = lax.all_gather(value_flat, "ctx", axis=1, tiled=True)
    piece_rows = part_keys.shape[1]
    part_keys = part_keys.reshape(slots, piece_rows, kv_heads, head_size)
    part_values = part_values.reshape(slots, piece_rows, kv_heads, head_size)
    span_rows = math.gcd(piece_rows, 4 * rows)

    def inner_step(block_index, inner_state):
        sub_keys = lax.dynamic_slice_in_dim(part_keys, block_index * span_rows, span_rows, 1)
        sub_values = lax.dynamic_slice_in_dim(part_values, block_index * span_rows, span_rows, 1)
        return attend_block(
            inner_state,
            sub_keys,
            sub_values,
            block_index * span_rows,
            query_head_rows,
            query_pos,
            lengths_used,
        )

    run_max, run_sum, run_acc = lax.fori_loop(0, piece_rows // span_rows, inner_step, initial)
    log_total = run_max + jnp.log(run_sum)
    attended = jnp.transpose(run_acc / run_sum[..., None], (0, 3, 1, 2, 4))
    return (attended, log_total)


def attend_backward(
    query_head_rows,
    key_head_rows,
    value_head_rows,
    grad_heads,
    attended,
    log_total,
    lengths_used,
    query_pos,
):
    ctx_count = lax.axis_size("ctx")
    own_index = lax.axis_index("ctx")
    rows = query_head_rows.shape[1]
    row_dot = jnp.transpose(
        jnp.sum(grad_heads.astype(jnp.float32) * attended, axis=-1), (0, 2, 3, 1)
    )

    def cycle_step(step_index, carried):
        carried_keys, carried_values, grad_query, grad_key, grad_value = carried
        block_id = (own_index + step_index) % ctx_count
        query_part, key_part, value_part = attend_back(
            carried_keys,
            carried_values,
            block_id * rows,
            query_head_rows,
            grad_heads,
            log_total,
            row_dot,
            query_pos,
            lengths_used,
        )
        grad_key, grad_value = (
            from_behind((grad_key + key_part).astype(jnp.bfloat16), "ctx", -1).astype(jnp.float32),
            from_behind((grad_value + value_part).astype(jnp.bfloat16), "ctx", -1).astype(
                jnp.float32
            ),
        )
        carried_keys, carried_values = from_behind((carried_keys, carried_values), "ctx", -1)
        return (carried_keys, carried_values, grad_query + query_part, grad_key, grad_value)

    key_zeros = jnp.zeros(key_head_rows.shape, jnp.float32)
    start_state = (
        key_head_rows,
        value_head_rows,
        jnp.zeros(query_head_rows.shape, jnp.float32),
        key_zeros,
        key_zeros,
    )
    carried = lax.fori_loop(0, ctx_count, cycle_step, start_state)
    return (carried[2], carried[3], carried[4])


def table_total(rotation_tables):
    return lax.psum(rotation_tables, ("ctx", "fsdp"))


def local(
    tokens,
    cotangent,
    lengths,
    slot_adapter_index,
    attention_norm_gain,
    feedforward_norm_gain,
    query_weight,
    key_weight,
    value_weight,
    output_weight,
    gate_weight,
    up_weight,
    down_weight,
    adapter_input_first,
    adapter_output_first,
    adapter_down_first,
    adapter_query_second,
    adapter_key_value_second,
    adapter_output_second,
    adapter_gate_up_second,
    adapter_down_second,
):
    slot_count, tok_rows, model_width = tokens.shape
    head_groups = QUERY_HEADS // KEY_VALUE_HEADS
    own_index = lax.axis_index("ctx")
    fsdp_index = lax.axis_index("fsdp")
    query_pos = own_index * tok_rows + jnp.arange(tok_rows, dtype=jnp.int32)
    cosine_table, sine_table = rope_tables(query_pos, HEAD_DIM)
    own_lengths = lax.dynamic_slice_in_dim(lengths, fsdp_index * slot_count, slot_count, 0)
    own_adapters = lax.dynamic_slice_in_dim(
        slot_adapter_index, fsdp_index * slot_count, slot_count, 0
    )
    valid = query_pos[None, :] < own_lengths[:, None]
    adapter_labels = jnp.arange(adapter_input_first.shape[0], dtype=jnp.int32)
    onehot_own = own_adapters[:, None] == adapter_labels[None, :]
    owned_low_rank = onehot_own.astype(jnp.bfloat16)
    own_full = onehot_own.astype(jnp.float32)
    tokens_f = tokens.astype(jnp.float32)
    factor_one = rms_factor(tokens_f)
    normed_one = (tokens_f * factor_one * attention_norm_gain).astype(jnp.bfloat16)
    grad_out = jnp.where(valid[..., None], cotangent, jnp.zeros((), jnp.bfloat16))
    input_first = pick_rows(owned_low_rank, adapter_input_first)
    output_second = pick_rows(owned_low_rank, adapter_output_second)
    down_second = pick_rows(owned_low_rank, adapter_down_second)
    output_first = pick_rows(owned_low_rank, adapter_output_first)
    down_first = pick_rows(owned_low_rank, adapter_down_first)
    query_second = pick_rows(owned_low_rank, adapter_query_second)
    key_value_second = pick_rows(owned_low_rank, adapter_key_value_second)
    gate_up_second = pick_rows(owned_low_rank, adapter_gate_up_second)
    weight_q, weight_k, weight_v, weight_gate, weight_up, weight_o, weight_down = (
        lax.all_gather(query_weight, "fsdp", axis=1, tiled=True),
        lax.all_gather(key_weight, "fsdp", axis=1, tiled=True),
        lax.all_gather(value_weight, "fsdp", axis=1, tiled=True),
        lax.all_gather(gate_weight, "fsdp", axis=1, tiled=True),
        lax.all_gather(up_weight, "fsdp", axis=1, tiled=True),
        lax.all_gather(output_weight, "fsdp", axis=0, tiled=True),
        lax.all_gather(down_weight, "fsdp", axis=0, tiled=True),
    )
    inner_q, projected_queries = project(normed_one, weight_q, input_first[:, 0], query_second)
    inner_k, projected_keys = project(
        normed_one, weight_k, input_first[:, 1], key_value_second[:, 0]
    )
    inner_v, projected_values = project(
        normed_one, weight_v, input_first[:, 2], key_value_second[:, 1]
    )
    query_head_rows = apply_rotation(
        projected_queries.reshape(slot_count, tok_rows, -1, HEAD_DIM), cosine_table, sine_table
    ).astype(jnp.bfloat16)
    query_head_rows = query_head_rows.reshape(slot_count, tok_rows, -1, head_groups, HEAD_DIM)
    key_head_rows = apply_rotation(
        projected_keys.reshape(slot_count, tok_rows, -1, HEAD_DIM), cosine_table, sine_table
    ).astype(jnp.bfloat16)
    value_head_rows = projected_values.astype(jnp.bfloat16).reshape(
        slot_count, tok_rows, -1, HEAD_DIM
    )
    attended, log_total = attend_forward(
        query_head_rows, key_head_rows, value_head_rows, own_lengths, query_pos
    )
    attn_b = attended.reshape(slot_count, tok_rows, -1).astype(jnp.bfloat16)
    inner_o, proj_o = project(attn_b, weight_o, output_first, output_second)
    resid = tokens_f + proj_o
    factor_two = rms_factor(resid)
    normed_two = (resid * factor_two * feedforward_norm_gain).astype(jnp.bfloat16)
    inner_gate, gate = project(normed_two, weight_gate, input_first[:, 3], gate_up_second[:, 0])
    inner_up, up_proj = project(normed_two, weight_up, input_first[:, 4], gate_up_second[:, 1])
    sigmoid_gate = jax.nn.sigmoid(gate)
    hidden = (gate * sigmoid_gate * up_proj).astype(jnp.bfloat16)
    inner_down, proj_down = project(hidden, weight_down, down_first, down_second)
    out_tokens = jnp.where(valid[..., None], resid + proj_down, 0.0).astype(jnp.bfloat16)
    grad_hidden, grad_da, grad_db = project_back(
        hidden, grad_out, weight_down, down_first, down_second, inner_down
    )
    grad_gate = (grad_hidden * up_proj * sigmoid_gate * (1.0 + gate * (1.0 - sigmoid_gate))).astype(
        jnp.bfloat16
    )
    grad_up = (grad_hidden * gate * sigmoid_gate).astype(jnp.bfloat16)
    from_gate, grad_ga, grad_gb = project_back(
        normed_two, grad_gate, weight_gate, input_first[:, 3], gate_up_second[:, 0], inner_gate
    )
    from_up, grad_ua, grad_ub = project_back(
        normed_two, grad_up, weight_up, input_first[:, 4], gate_up_second[:, 1], inner_up
    )
    grad_normed_two = (from_gate + from_up).astype(jnp.bfloat16).astype(jnp.float32)
    grad_resid = grad_out.astype(jnp.float32) + norm_back(
        resid, factor_two, feedforward_norm_gain, grad_normed_two
    )
    grad_resid_low = grad_resid.astype(jnp.bfloat16)
    from_attn, grad_oa, grad_ob = project_back(
        attn_b, grad_resid_low, weight_o, output_first, output_second, inner_o
    )
    grad_heads = from_attn.astype(jnp.bfloat16).reshape(attended.shape)
    grad_query, grad_key, grad_value = attend_backward(
        query_head_rows,
        key_head_rows,
        value_head_rows,
        grad_heads,
        attended,
        log_total,
        own_lengths,
        query_pos,
    )
    grad_proj_q = (
        rotate_back(
            grad_query.reshape(slot_count, tok_rows, -1, HEAD_DIM), cosine_table, sine_table
        )
        .astype(jnp.bfloat16)
        .reshape(slot_count, tok_rows, -1)
    )
    grad_proj_k = (
        rotate_back(grad_key, cosine_table, sine_table)
        .astype(jnp.bfloat16)
        .reshape(slot_count, tok_rows, -1)
    )
    grad_proj_v = grad_value.astype(jnp.bfloat16).reshape(slot_count, tok_rows, -1)
    from_query, grad_qa, grad_qb = project_back(
        normed_one, grad_proj_q, weight_q, input_first[:, 0], query_second, inner_q
    )
    from_key, grad_ka, grad_kb = project_back(
        normed_one, grad_proj_k, weight_k, input_first[:, 1], key_value_second[:, 0], inner_k
    )
    from_value, grad_va, grad_vb = project_back(
        normed_one, grad_proj_v, weight_v, input_first[:, 2], key_value_second[:, 1], inner_v
    )
    grad_normed_one = (from_query + from_key + from_value).astype(jnp.bfloat16).astype(jnp.float32)
    grad_tokens = grad_resid + norm_back(tokens_f, factor_one, attention_norm_gain, grad_normed_one)
    slot_grads = (
        jnp.stack([grad_qa, grad_ka, grad_va, grad_ga, grad_ua], axis=1),
        grad_oa,
        grad_da,
        grad_qb,
        jnp.stack([grad_kb, grad_vb], axis=1),
        grad_ob,
        jnp.stack([grad_gb, grad_ub], axis=1),
        grad_db,
    )
    summed = table_total(tuple((spread_rows(own_full, entry_item) for entry_item in slot_grads)))
    return (
        out_tokens,
        grad_tokens,
        summed[0],
        summed[1],
        summed[2],
        summed[3],
        summed[4],
        summed[5],
        summed[6],
        summed[7],
    )


BF16 = jnp.bfloat16
F32 = jnp.float32
MESH_ID = pl.DeviceIdType.MESH
RANK = 16
SIDE = 128
PAD_HEAD = 128
HALF_PAD = 64


def _sem(count):
    return pltpu.SemaphoreType.DMA((count,))


def _place():
    c = lax.axis_index("ctx")
    f = lax.axis_index("fsdp")
    x = f // 2
    core = f % 2
    return c, f, x, core, (c, 2 * x + 1 - core), (c, 2 * (1 - x) + core)


def _greet(targets):
    barrier = pltpu.get_barrier_semaphore()
    for target in targets:
        pl.semaphore_signal(barrier, inc=1, device_id=target, device_id_type=MESH_ID)
    pl.semaphore_wait(barrier, len(targets))


def _remote(src, dst, send, recv, target):
    return pltpu.make_async_remote_copy(
        src_ref=src, dst_ref=dst, send_sem=send, recv_sem=recv, device_id=target, device_id_type=MESH_ID
    )


def _comm_call(kernel, ins, outs, scratch, cid, name, in_space=pl.ANY, out_space=pl.ANY, vmem=None):
    return pl.pallas_call(
        kernel,
        out_shape=outs,
        in_specs=[pl.BlockSpec(memory_space=in_space)] * len(ins),
        out_specs=jax.tree.map(lambda _: pl.BlockSpec(memory_space=out_space), outs),
        scratch_shapes=scratch,
        compiler_params=pltpu.CompilerParams(
            collective_id=cid, has_side_effects=True, vmem_limit_bytes=vmem
        ),
        name=name,
    )(*ins)


def _gather_steps(ins, outs, own_sem, send_sem, recv_sem, place):
    c, f, x, core, core_peer, x_peer = place
    h = 1 - core
    count = len(ins)
    local = []
    sends = []

    def first():
        for base, target in ((0, x_peer), (2 * count, core_peer)):
            for i in range(count):
                for j in range(2):
                    k = base + i * 2 + j
                    cp = _remote(
                        ins[i].at[j], outs[i].at[h, j, x], send_sem.at[k], recv_sem.at[k], target
                    )
                    cp.start()
                    sends.append(cp)
        for i in range(count):
            for j in range(2):
                lc = pltpu.make_async_copy(
                    ins[i].at[j], outs[i].at[h, j, x], own_sem.at[i * 2 + j]
                )
                lc.start()
                local.append(lc)

    def last():
        forwards = []
        for i in range(count):
            for j in range(2):
                k = i * 2 + j
                sends[k].wait_recv()
                cp = _remote(
                    outs[i].at[h, j, 1 - x],
                    outs[i].at[h, j, 1 - x],
                    send_sem.at[4 * count + k],
                    recv_sem.at[4 * count + k],
                    core_peer,
                )
                cp.start()
                forwards.append(cp)
        for k in range(2 * count):
            sends[2 * count + k].wait_recv()
            forwards[k].wait_recv()
        for cp in sends + forwards:
            cp.wait_send()
        for lc in local:
            lc.wait()

    return first, last


def _gather_body(*args):
    first, last = _gather_steps(*args)
    first()
    last()


def _ctx_first(piece, lines, own_sem, send_sem, recv_sem, place):
    c, f, x, core, core_peer, x_peer = place
    z, y = c // 2, c % 2
    sends = []
    local = []

    def start():
        lc = pltpu.make_async_copy(piece, lines.at[z, x], own_sem)
        lc.start()
        local.append(lc)
        cp = _remote(piece, lines.at[z, x], send_sem.at[0], recv_sem.at[0], x_peer)
        cp.start()
        sends.append(cp)

    def spread():
        local[0].wait()
        sends[0].wait_recv()
        for step in range(1, 4):
            cp = _remote(
                lines.at[z],
                lines.at[z],
                send_sem.at[step],
                recv_sem.at[step],
                (2 * ((z + step) % 4) + y, f),
            )
            cp.start()
            sends.append(cp)

    def finish():
        for cp in sends[1:]:
            cp.wait_recv()
        for cp in sends:
            cp.wait_send()

    return start, spread, finish


def _ctx_second(lines, out, own_sem, send_sem, recv_sem, place):
    c, f, x, core, core_peer, x_peer = place
    z, y = c // 2, c % 2
    y_peer = (2 * z + 1 - y, f)
    sends = []
    local = []

    def start():
        lc = pltpu.make_async_copy(lines, out.at[y, core], own_sem)
        lc.start()
        local.append(lc)
        for k, target in ((0, y_peer), (1, core_peer)):
            cp = _remote(lines, out.at[y, core], send_sem.at[k], recv_sem.at[k], target)
            cp.start()
            sends.append(cp)

    def share():
        sends[0].wait_recv()
        cp = _remote(
            out.at[1 - y, core], out.at[1 - y, core], send_sem.at[2], recv_sem.at[2], core_peer
        )
        cp.start()
        sends.append(cp)

    def finish():
        sends[1].wait_recv()
        sends[2].wait_recv()
        for cp in sends:
            cp.wait_send()
        local[0].wait()

    return start, share, finish


def _z_peers(place):
    c, f = place[:2]
    return [(2 * ((c // 2 + step) % 4) + c % 2, f) for step in range(1, 4)]


def _y_peer(place):
    c, f = place[:2]
    return (2 * (c // 2) + 1 - c % 2, f)


def _lines_of(n):
    return (4, 2, RANK, n)


def _spread_of(n):
    return jax.ShapeDtypeStruct((2, 2, 4, 2, RANK, n), BF16)


FIRST_SEMS = [pltpu.SemaphoreType.DMA(()), _sem(4), _sem(4)]
SECOND_SEMS = [pltpu.SemaphoreType.DMA(()), _sem(3), _sem(3)]


def _order_steps(own, order, own_sem, send_sem, recv_sem, place):
    core_peer, x_peer = place[4:]
    sends, local, forwards = [], [], []

    def first():
        for j in range(2):
            cp = _remote(own.at[j], order.at[1 + j, 1], send_sem.at[j], recv_sem.at[j], x_peer)
            cp.start()
            sends.append(cp)
        for j in range(2):
            cp = _remote(
                own.at[j], order.at[3, j], send_sem.at[2 + j], recv_sem.at[2 + j], core_peer
            )
            cp.start()
            sends.append(cp)
        for j in range(2):
            lc = pltpu.make_async_copy(own.at[j], order.at[0, j], own_sem.at[j])
            lc.start()
            local.append(lc)

    def forward(j):
        sends[j].wait_recv()
        cp = _remote(
            order.at[1 + j, 1],
            order.at[1 + j, 0],
            send_sem.at[4 + j],
            recv_sem.at[4 + j],
            core_peer,
        )
        cp.start()
        forwards.append(cp)

    def own_here():
        for lc in local:
            lc.wait()

    def core_here():
        for j in range(2):
            sends[2 + j].wait_recv()

    def far_here(j):
        forwards[j].wait_recv()

    def last():
        for cp in sends + forwards:
            cp.wait_send()

    return first, forward, own_here, core_here, far_here, last


def _order_all(own, order, sems, place):
    first, forward, own_here, core_here, far_here, last = _order_steps(own, order, *sems, place)
    first()
    own_here()
    for j in range(2):
        forward(j)
    core_here()
    for j in range(2):
        far_here(j)
    last()


def feed_forward(own, cot, resid, gain, length, weights, adapters, cid):
    gate_w, up_w, down_w = weights
    width, units = gate_w.shape
    wide = width + SIDE
    tile = 256

    loads_in = tuple(weights) + tuple(adapters) + (cot,)
    count = len(loads_in)

    def kernel(*refs):
        len_ref, own_ref, resid_ref, gain_ref = refs[:4]
        loads_hbm = refs[4 : 4 + count]
        grad_resid, grad_low, small, out_own, out_far, order, early = refs[4 + count : 11 + count]
        refs = refs[11 + count :]
        gate_ref, up_ref, down_ref, first_ref, sg_ref, su_ref, fd_ref, sd_ref, go_ref = refs[:count]
        (
            sums,
            hid_s,
            gg_s,
            gu_s,
            in_s,
            gid_s,
            part,
            out_part,
            near,
            out_near,
            far,
            out_land,
            staged,
            landed,
            load_sem,
            own_sem,
            send_sem,
            recv_sem,
            s_sem,
            r_sem,
        ) = refs[count:]
        place = _place()
        core_peer, x_peer = place[4:]
        _greet([core_peer, x_peer])
        first, forward, own_here, core_here, far_here, last = _order_steps(
            own_ref, order, own_sem, send_sem, recv_sem, place
        )
        first()
        copies = []
        loads = []
        for i in range(count):
            cp = pltpu.make_async_copy(loads_hbm[i], refs[i], load_sem.at[i])
            cp.start()
            loads.append(cp)
        c, f, x, core = place[:4]
        live = len_ref[0]

        def masked(step):
            other_x = x if step in (0, 3) else 1 - x
            pieces = []
            for k in range(2):
                other_core = (core, 1 - core)[step == 3 or (step in (1, 2) and k == 0)]
                j = k if step in (0, 3) else step - 1
                block = other_x + 2 * j + 4 * (1 - other_core)
                pos = 128 * block + lax.broadcasted_iota(jnp.int32, (128, width), 0)
                pieces.append(jnp.where(pos < live, go_ref[step, k].astype(F32), 0.0).astype(BF16))
            return pieces

        def work(step):
            rows = order[step].reshape(2 * 128, width)
            pieces = masked(step)
            for k in range(2):
                go_ref[step, k] = pieces[k]
            go = go_ref[step].reshape(2 * 128, width)
            inner = dot_t(rows, first_ref[...]).astype(BF16)
            gid = dot_t(go, sd_ref[...]).astype(BF16)
            in_s[step] = inner
            gid_s[step] = gid
            for at in range(0, units, tile):
                cols = slice(at, at + tile)
                gate = dot(rows, gate_ref[:, cols]) + dot(inner, sg_ref[:, cols])
                up = dot(rows, up_ref[:, cols]) + dot(inner, su_ref[:, cols])
                grad = dot_t(go, down_ref[cols, :]) + dot(gid, fd_ref[:, cols])
                sig = 1.0 / (1.0 + jnp.exp(-gate))
                silu = gate * sig
                hid_s[step, :, cols] = (silu * up).astype(BF16)
                gg_s[step, :, cols] = (grad * up * sig * (1.0 + gate * (1.0 - sig))).astype(BF16)
                gu_s[step, :, cols] = (grad * silu).astype(BF16)
            gg, gu, hid = gg_s[step], gu_s[step], hid_s[step]
            for at in range(0, width, tile):
                cols = slice(at, at + tile)
                value = dot_t(gg, gate_ref[cols, :]) + dot_t(gu, up_ref[cols, :])
                out = dot(hid, down_ref[:, cols])
                if step == 0:
                    sums[:, :, cols] = value.reshape(2, 128, tile)
                    out_own[:, :, cols] = out.reshape(2, 128, tile)
                else:
                    part[step - 1, :, :, cols] = value.astype(BF16).reshape(2, 128, tile)
                    out_part[step - 1, :, :, cols] = out.astype(BF16).reshape(2, 128, tile)
            value = dot_t(gg, sg_ref[...]) + dot_t(gu, su_ref[...])
            out = dot_t(hid, fd_ref[...])
            if step == 0:
                sums[:, :, width:] = value.reshape(2, 128, SIDE)
                out_own[:, :, width:] = out.reshape(2, 128, SIDE)
            else:
                part[step - 1, :, :, width:] = value.astype(BF16).reshape(2, 128, SIDE)
                out_part[step - 1, :, :, width:] = out.astype(BF16).reshape(2, 128, SIDE)

        def send(src, dst, k, target):
            cp = _remote(src, dst, s_sem.at[k], r_sem.at[k], target)
            cp.start()
            copies.append(cp)
            return cp

        own_here()
        for cp in loads:
            cp.wait()
        work(0)
        core_here()
        forward(0)
        work(3)
        near_cp = [
            send(part.at[2], near, 0, core_peer),
            send(out_part.at[2], out_near, 1, core_peer),
        ]
        across, out_cps = [], []
        for j in range(2):
            if j:
                forward(j)
            far_here(j)
            work(1 + j)
            cp = send(part.at[j, 0], far.at[j], 2 + j, core_peer)
            out_cps.append(send(out_part.at[j, 0], out_land.at[j], 4 + j, core_peer))
            cp.wait_recv()
            staged[j] = (part[j, 1].astype(F32) + far[j].astype(F32)).astype(BF16)
            across.append(send(staged.at[j], landed.at[j], 6 + j, x_peer))
        for j in range(2):
            out_cps[j].wait_recv()
            out_far[j] = (out_part[j, 1].astype(F32) + out_land[j].astype(F32)).astype(BF16)
        for cp in near_cp:
            cp.wait_recv()
        sums[...] = sums[...] + near[...].astype(F32)
        out_own[...] = out_own[...] + out_near[...].astype(F32)
        for at in range(0, units, 512):
            cols = slice(at, at + 512)
            g = jnp.zeros((SIDE, 512), F32)
            u = jnp.zeros((SIDE, 512), F32)
            d = jnp.zeros((SIDE, 512), F32)
            for step in range(4):
                g += dot_rows(in_s[step], gg_s[step, :, cols])
                u += dot_rows(in_s[step], gu_s[step, :, cols])
                d += dot_rows(gid_s[step], hid_s[step, :, cols])
            early[:, at : at + 512] = (ADAPTER_SCALE * g[:RANK]).astype(BF16)
            early[:, units + at : units + at + 512] = (ADAPTER_SCALE * u[RANK : 2 * RANK]).astype(BF16)
            early[:, 2 * units + at : 2 * units + at + 512] = d[3 * RANK : 4 * RANK].astype(BF16)
        for j in range(2):
            across[j].wait_recv()
            total = sums[j] + landed[j].astype(F32)
            gi = total[:, width:].astype(BF16)
            small[j] = gi
            gn = (total[:, :width] + dot(gi, first_ref[...])).astype(BF16).astype(F32)
            v = resid_ref[j]
            factor = lax.rsqrt(jnp.mean(v * v, axis=1, keepdims=True) + EPSILON)
            scaled = gn * gain_ref[...]
            mean = jnp.mean(scaled * v, axis=1, keepdims=True)
            grad = go_ref[0, j].astype(F32) + factor * scaled - v * (factor * factor * factor) * mean
            grad_resid[j] = grad
            grad_low[j] = grad.astype(BF16)
        last()
        for cp in copies:
            cp.wait_send()

    vmem = pl.BlockSpec(memory_space=pltpu.VMEM)
    rows = (2, 128, wide)
    f32 = lambda *shape: jax.ShapeDtypeStruct(shape, F32)
    outs = [
        f32(2, 128, width),
        jax.ShapeDtypeStruct((2, 128, width), BF16),
        jax.ShapeDtypeStruct((2, 128, SIDE), BF16),
        f32(*rows),
        jax.ShapeDtypeStruct(rows, BF16),
        jax.ShapeDtypeStruct((4, 2, 128, width), BF16),
        jax.ShapeDtypeStruct((RANK, 3 * units), BF16),
    ]
    hbm = pl.BlockSpec(memory_space=pl.ANY)
    return pl.pallas_call(
        kernel,
        out_shape=outs,
        in_specs=[pl.BlockSpec(memory_space=pltpu.SMEM), vmem, vmem, vmem] + [hbm] * count,
        out_specs=[vmem] * len(outs),
        scratch_shapes=[pltpu.VMEM(a.shape, a.dtype) for a in loads_in]
        + [pltpu.VMEM(rows, F32)]
        + [pltpu.VMEM((4, 256, units), BF16)] * 3
        + [pltpu.VMEM((4, 256, SIDE), BF16)] * 2
        + [pltpu.VMEM((3,) + rows, BF16)] * 2
        + [pltpu.VMEM(rows, BF16)] * 6
        + [_sem(count), _sem(2), _sem(6), _sem(6), _sem(8), _sem(8)],
        compiler_params=pltpu.CompilerParams(
            collective_id=cid, has_side_effects=True, vmem_limit_bytes=58 * 1024 * 1024
        ),
        name="feed_forward",
    )(length, own, resid, gain, *loads_in)


def _back_steps(src, dst, out_s, out_r, place):
    c, f, x, core, core_peer, x_peer = place
    h = 1 - core
    slot = c // 2 + 4 * (c % 2)
    place_in = slot % 2
    moves = []

    def first():
        for j in range(2):
            cp = _remote(
                src.at[j],
                dst.at[place_in],
                out_s.at[j],
                out_r.at[place_in],
                (x + 2 * j + 4 * h, slot // 2),
            )
            cp.start()
            moves.append(cp)

    def last():
        for half in range(2):
            pltpu.make_async_copy(dst.at[half], dst.at[half], out_r.at[half]).wait()
        for cp in moves:
            cp.wait_send()

    return first, last


def _back_sources(place):
    c, f = place[:2]
    from_f = 2 * (c % 2) + 1 - c // 4
    return [(((2 * f + half) % 4) * 2 + (2 * f + half) // 4, from_f) for half in range(2)]


def give_back(arrays, piece, lines, cid):
    count = len(arrays)
    n = piece.shape[1]

    def kernel(*refs):
        owns, (piece_in, lines_in) = refs[:count], refs[count : count + 2]
        backs = refs[count + 2 : 2 * count + 2]
        spread, lines_out, late = refs[2 * count + 2 : 2 * count + 5]
        sems = refs[2 * count + 5 :]
        place = _place()
        _greet(
            _back_sources(place) + [place[4], place[5], _y_peer(place)] + _z_peers(place)
        )
        start, across, finish = _ctx_first(piece_in, late, *sems[2 * count : 2 * count + 3], place)
        second = _ctx_second(late, spread, *sems[2 * count + 3 : 2 * count + 6], place)
        other = _ctx_second(lines_in, lines_out, *sems[2 * count + 6 :], place)
        steps = [
            _back_steps(owns[i], backs[i], sems[2 * i], sems[2 * i + 1], place)
            for i in range(count)
        ]
        start()
        other[0]()
        across()
        for first, _ in steps:
            first()
        finish()
        second[0]()
        other[1]()
        second[1]()
        other[2]()
        second[2]()
        for _, last in steps:
            last()

    outs = [jax.ShapeDtypeStruct(a.shape, a.dtype) for a in arrays]
    outs += [_spread_of(n), _spread_of(lines.shape[-1]), jax.ShapeDtypeStruct(_lines_of(n), BF16)]
    return _comm_call(
        kernel,
        list(arrays) + [piece, lines],
        outs,
        [_sem(2)] * (2 * count) + FIRST_SEMS + SECOND_SEMS + SECOND_SEMS,
        cid,
        "give_back",
    )[:-1]


def front_call(
    tokens,
    cotangent,
    length,
    adapter,
    gains,
    wq,
    wk,
    wv,
    wo,
    tables,
    cosine,
    sine,
    cid,
):
    width = tokens.shape[-1]
    rows = cosine.shape[0]
    wide = width + SIDE
    block = 256
    scale = HEAD_DIM ** (-0.5)
    lane = PAD_HEAD
    units = tables[6].shape[-1] // 4
    quarter = width // 4
    loads_in = (gains, wq, wk, wv, wo) + tables + (cosine, sine)
    count = len(loads_in)

    def kernel(*refs):
        len_ref, adapter_ref, tok_ref, cot_ref = refs[:4]
        loads_hbm = refs[4 : 4 + count]
        (
            sums_resid,
            normed_two,
            side_all,
            tok_own,
            cot_own,
            cot_order,
            qkv_ref,
            lse_ref,
            att_ref,
            one_cut,
            inner_ref,
            wa_ref,
            ow_ref,
            sa_ref,
            fa_ref,
            fgu_ref,
            sg_ref,
            su_ref,
            fd_ref,
            sd_ref,
            fo_ref,
            so_ref,
        ) = refs[4 + count : 26 + count]
        refs = refs[26 + count :]
        gain_v, wq_v, wk_v, wv_v, wo_v = refs[:5]
        in_first, out_first, down_first, q_second, kv_second, o_second, gu_second, d_second = refs[5:13]
        cos_ref, sin_ref = refs[13:15]
        (
            tok_all,
            one_ref,
            part,
            land,
            staged,
            landed,
            sums,
            side_own,
            load_sem,
            land_s,
            land_r,
            cot_s,
            cot_r,
            send_sem,
            recv_sem,
            s_sem,
            r_sem,
        ) = refs[15:32]
        order_sems, side_sems = refs[32:35], refs[35:38]
        place = _place()
        c, f, x, core, core_peer, x_peer = place
        hh = 1 - core
        slot = c // 2 + 4 * (c % 2)
        live = len_ref[0]
        which = adapter_ref[0]

        barrier = pltpu.get_barrier_semaphore()
        for j in range(2):
            pl.semaphore_signal(
                barrier, inc=1, device_id=(x + 2 * j + 4 * hh, slot // 2), device_id_type=MESH_ID
            )
        for target in (core_peer, x_peer):
            pl.semaphore_signal(barrier, inc=1, device_id=target, device_id_type=MESH_ID)
        pl.semaphore_wait(barrier, 4)
        to_x_index = c % 2
        to_h = c // 4
        to_j = (c // 2) % 2
        moves = []
        for part_row in range(2):
            span = pl.ds(64 * part_row, 64)
            for half in range(2):
                s = 2 * f + half
                cp = _remote(
                    tok_ref.at[half, span],
                    tok_all.at[to_h, to_j, to_x_index, span],
                    land_s.at[2 * part_row + half],
                    land_r.at[2 * part_row + to_j],
                    ((s % 4) * 2 + s // 4, 2 * to_x_index + 1 - to_h),
                )
                cp.start()
                moves.append(cp)
        cot_moves = []
        for half in range(2):
            s = 2 * f + half
            cot_moves.append(
                _remote(
                    cot_ref.at[half],
                    cot_own.at[to_j],
                    cot_s.at[half],
                    cot_r.at[to_j],
                    ((s % 4) * 2 + s // 4, 2 * to_x_index + 1 - to_h),
                )
            )
        loads = []
        for i in range(count):
            cp = pltpu.make_async_copy(loads_hbm[i], refs[i], load_sem.at[i])
            cp.start()
            loads.append(cp)
        for cp in loads:
            cp.wait()

        def group_sends(part_row):
            span = pl.ds(64 * part_row, 64)
            for j in range(2):
                pltpu.make_async_copy(
                    tok_all.at[hh, j, x, span],
                    tok_all.at[hh, j, x, span],
                    land_r.at[2 * part_row + j],
                ).wait()
                k = 2 * part_row + j
                here = tok_all.at[hh, j, x, span]
                for base, target in ((0, x_peer), (4, core_peer)):
                    cp = _remote(
                        here, here, send_sem.at[base + k], recv_sem.at[base + k], target
                    )
                    cp.start()
                    sends[base + k] = cp

        sends = {}

        def prepare_first():
            half = HEAD_DIM // 2
            wa_ref[...] = jnp.zeros_like(wa_ref)
            sa_ref[...] = jnp.zeros_like(sa_ref)
            for head in range(4):
                for side in range(2):
                    at = head * HEAD_DIM + side * half
                    to = head * lane + side * HALF_PAD
                    wa_ref[:, to : to + half] = wq_v[:, at : at + half]
            for head in range(2):
                for side in range(2):
                    at = head * HEAD_DIM + side * half
                    to = (4 + head) * lane + side * HALF_PAD
                    wa_ref[:, to : to + half] = wk_v[:, at : at + half]
                at, to = head * HEAD_DIM, (6 + head) * lane
                wa_ref[:, to : to + HEAD_DIM] = wv_v[:, at : at + HEAD_DIM]

        def prepare_second():
            half = HEAD_DIM // 2
            own_cols = pl.ds(pl.multiple_of(f * quarter, 128), quarter)
            own_units = pl.ds(pl.multiple_of(f * units, 128), units)
            low = lambda v: (ADAPTER_SCALE * v.astype(F32)).astype(BF16)
            for ref in (fa_ref, fgu_ref, sg_ref, su_ref, fd_ref, sd_ref, fo_ref, so_ref, ow_ref):
                ref[...] = jnp.zeros_like(ref)
            for i in range(3):
                fa_ref[i * RANK : (i + 1) * RANK, :] = in_first[which, i]
            for i in range(2):
                fgu_ref[i * RANK : (i + 1) * RANK, :] = in_first[which, 3 + i]
            all_gu = gu_second.at[:, :, :, own_units]
            sg_ref[:RANK, :] = low(all_gu[which, 0])
            su_ref[RANK : 2 * RANK, :] = low(all_gu[which, 1])
            fd_ref[3 * RANK : 4 * RANK, :] = down_first.at[:, :, own_units][which]
            sd_ref[3 * RANK : 4 * RANK, :] = low(d_second[which])
            so_ref[:RANK, :] = low(o_second[which])
            own_first = out_first.at[:, :, own_cols][which]
            own_q = low(q_second.at[:, :, own_cols][which])
            for head in range(4):
                at = head * HEAD_DIM
                fo_ref[:RANK, head * lane : head * lane + HEAD_DIM] = own_first[:, at : at + HEAD_DIM]
                ow_ref[head * lane : head * lane + HEAD_DIM, :] = wo_v[at : at + HEAD_DIM, :]
                for side in range(2):
                    to = head * lane + side * HALF_PAD
                    sa_ref[:RANK, to : to + half] = own_q[:, at + side * half : at + (side + 1) * half]
            for i in range(2):
                own_kv = low(kv_second[which, i])
                for head in range(2):
                    at = head * HEAD_DIM
                    if i:
                        to = (6 + head) * lane
                        sa_ref[2 * RANK : 3 * RANK, to : to + HEAD_DIM] = own_kv[:, at : at + HEAD_DIM]
                    else:
                        for side in range(2):
                            to = (4 + head) * lane + side * HALF_PAD
                            sa_ref[RANK : 2 * RANK, to : to + half] = own_kv[
                                :, at + side * half : at + (side + 1) * half
                            ]

        prepare_first()
        group_sends(0)
        prepare_second()
        group_sends(1)
        for cp in cot_moves:
            cp.start()

        def forward(j):
            for part_row in range(2):
                k = 2 * part_row + j
                span = pl.ds(64 * part_row, 64)
                sends[k].wait_recv()
                there = tok_all.at[hh, j, 1 - x, span]
                cp = _remote(there, there, send_sem.at[8 + k], recv_sem.at[8 + k], core_peer)
                cp.start()
                sends[8 + k] = cp
            for part_row in range(2):
                k = 2 * part_row + j
                sends[4 + k].wait_recv()
                sends[8 + k].wait_recv()

        def project_rows(t):
            row = pl.ds(t * block, block)
            v = tok_all[t // 2, t % 2].reshape(block, width).astype(F32)
            factor = lax.rsqrt(jnp.mean(v * v, axis=1, keepdims=True) + EPSILON)
            u = (v * factor * gain_v[0:1, :]).astype(BF16)
            one_ref[row, :] = u
            inner = dot_t(u, fa_ref[...]).astype(BF16)
            inner_ref[row, :] = inner
            cos, sin = cos_ref[row, :], sin_ref[row, :]
            for pair in range(4):
                cols = slice(pair * 2 * lane, (pair + 1) * 2 * lane)
                both = dot(u, wa_ref[:, cols]) + dot(inner, sa_ref[:, cols])
                for k in range(2):
                    p = both[:, k * lane : (k + 1) * lane]
                    if pair < 3:
                        p = p * cos + pltpu.roll(p, HALF_PAD, 1) * sin
                    qkv_ref[row, (2 * pair + k) * lane : (2 * pair + k + 1) * lane] = p.astype(BF16)

        def attention(t, hook):
            keys = (t + 1) * block
            row = pl.ds(t * block, block)
            qpos = t * block + lax.broadcasted_iota(jnp.int32, (block, keys), 0)
            kpos = lax.broadcasted_iota(jnp.int32, (block, keys), 1)
            allowed = (kpos <= qpos) & (kpos < live)
            stats = jnp.zeros((block, lane), F32)
            lanes = lax.broadcasted_iota(jnp.int32, (block, lane), 1)
            for head in range(4):
                q = qkv_ref[row, head * lane : (head + 1) * lane]
                kv = head // 2
                k = qkv_ref[:keys, (4 + kv) * lane : (5 + kv) * lane]
                v = qkv_ref[:keys, (6 + kv) * lane : (7 + kv) * lane]
                s = jnp.where(allowed, dot_t(q, k) * scale, NEGATIVE)
                top = jnp.max(s, axis=1, keepdims=True)
                p = jnp.where(allowed, jnp.exp(s - top), 0.0)
                total = jnp.sum(p, axis=1, keepdims=True)
                o = dot(p.astype(BF16), v) / total
                att_ref[row, head * lane : (head + 1) * lane] = o.astype(BF16)
                stats = jnp.where(lanes == head, top + jnp.log(total), stats)
                if head == 1 and hook is not None:
                    hook()
            lse_ref[row, :] = stats
            a = att_ref[row, :]
            for at in range(0, width, 256):
                value = dot(a, ow_ref[:, at : at + 256])
                part[t, :, :, at : at + 256] = value.astype(BF16).reshape(2, 128, 256)
            part[t, :, :, width:] = dot_t(a, fo_ref[...]).astype(BF16).reshape(2, 128, SIDE)

        def to_core(t):
            return _remote(part.at[t], land.at[t % 2], s_sem.at[t % 2], r_sem.at[t % 2], core_peer)

        def to_x(j):
            return _remote(staged.at[j], landed.at[j], s_sem.at[2 + j], r_sem.at[2 + j], x_peer)

        def leave(t):
            @pl.when(core == t // 2)
            def _():
                to_core(t).start()

        def combine(t):
            j = t % 2

            @pl.when(core == 1 - t // 2)
            def _():
                to_core(t).wait_recv()
                staged[j] = (part[t, 1 - x].astype(F32) + land[j, 1 - x].astype(F32)).astype(BF16)
                to_x(j).start()
                sums[j] = part[t, x].astype(F32) + land[j, x].astype(F32)

        forward(0)
        project_rows(0)
        project_rows(2)
        attention(0, None)
        leave(0)
        forward(1)
        project_rows(1)
        project_rows(3)
        attention(1, lambda: combine(0))
        leave(1)
        for half in range(2):
            pltpu.make_async_copy(cot_own.at[half], cot_own.at[half], cot_r.at[half]).wait()
        c_first, c_forward, c_own, c_core, c_far, c_last = _order_steps(
            cot_own, cot_order, *order_sems, place
        )
        attention(2, lambda: combine(1))
        leave(2)
        c_first()
        attention(3, lambda: combine(2))
        leave(3)
        combine(3)
        for t in range(4):

            @pl.when(core == t // 2)
            def _():
                to_core(t).wait_send()

        tok_own[...] = tok_all[hh, :, x]
        one_cut[...] = one_ref[:, pl.ds(pl.multiple_of(f * quarter, 128), quarter)]
        for j in range(2):
            cp = to_x(j)
            cp.wait_recv()
            sums[j] = sums[j] + landed[j].astype(F32)
            cp.wait_send()
            side_own[j] = sums[j, :, width:].astype(BF16)
        side_first, side_last = _gather_steps([side_own], [side_all], *side_sems, place)
        side_first()
        for j in range(2):
            v = (
                tok_own[j].astype(F32)
                + sums[j, :, :width]
                + dot(side_own[j], so_ref[...])
            )
            sums_resid[j] = v
            factor = lax.rsqrt(jnp.mean(v * v, axis=1, keepdims=True) + EPSILON)
            normed_two[j] = (v * factor * gain_v[1:2, :]).astype(BF16)
        c_own()
        c_core()
        for j in range(2):
            c_forward(j)
        for j in range(2):
            c_far(j)
        c_last()
        side_last()
        for cp in moves + cot_moves + list(sends.values()):
            cp.wait_send()

    vmem, hbm = pl.BlockSpec(memory_space=pltpu.VMEM), pl.BlockSpec(memory_space=pl.ANY)
    smem = pl.BlockSpec(memory_space=pltpu.SMEM)
    low = lambda *shape: jax.ShapeDtypeStruct(shape, BF16)
    outs = [
        (jax.ShapeDtypeStruct((2, 128, width), F32), vmem),
        (low(2, 128, width), vmem),
        (low(2, 2, 2, 128, SIDE), hbm),
        (low(2, 128, width), vmem),
        (low(2, 128, width), hbm),
        (low(4, 2, 128, width), hbm),
        (low(rows, 8 * lane), vmem),
        (jax.ShapeDtypeStruct((rows, lane), F32), vmem),
        (low(rows, 4 * lane), vmem),
        (low(rows, quarter), vmem),
        (low(rows, SIDE), vmem),
        (low(width, 8 * lane), vmem),
        (low(4 * lane, width), vmem),
        (low(SIDE, 8 * lane), vmem),
        (low(SIDE, width), vmem),
        (low(SIDE, width), vmem),
        (low(SIDE, units), vmem),
        (low(SIDE, units), vmem),
        (low(SIDE, units), vmem),
        (low(SIDE, width), vmem),
        (low(SIDE, 4 * lane), vmem),
        (low(SIDE, width), vmem),
    ]
    own = (2, 128, wide)
    return pl.pallas_call(
        kernel,
        out_shape=[o[0] for o in outs],
        in_specs=[smem, smem] + [hbm] * (2 + count),
        out_specs=[o[1] for o in outs],
        scratch_shapes=[pltpu.VMEM(a.shape, a.dtype) for a in loads_in]
        + [
            pltpu.VMEM((2, 2, 2, 128, width), BF16),
            pltpu.VMEM((rows, width), BF16),
            pltpu.VMEM((4,) + own, BF16),
            pltpu.VMEM((2,) + own, BF16),
            pltpu.VMEM(own, BF16),
            pltpu.VMEM(own, BF16),
            pltpu.VMEM(own, F32),
            pltpu.VMEM((2, 128, SIDE), BF16),
            _sem(count),
            _sem(4),
            _sem(4),
            _sem(2),
            _sem(2),
            _sem(12),
            _sem(12),
            _sem(4),
            _sem(4),
        ]
        + [_sem(2), _sem(6), _sem(6)] * 2,
        compiler_params=pltpu.CompilerParams(
            collective_id=cid, has_side_effects=True, vmem_limit_bytes=58 * 1024 * 1024
        ),
        name="front",
    )(length, adapter, tokens, cotangent, *loads_in)


def attend_back_call(
    low_own,
    small_own,
    early,
    out_far,
    out_side,
    qkv,
    stats,
    att,
    inner_o,
    order,
    cosine,
    sine,
    length,
    out_w,
    first_o,
    second_o,
    weight_all,
    second_all,
    cid,
):
    width = low_own.shape[-1]
    rows = qkv.shape[0]
    wide = width + SIDE
    step_rows = 256
    scale = HEAD_DIM ** (-0.5)
    lane = PAD_HEAD
    quarter = width // 4
    middle_n = 4 * quarter
    early_n = early.shape[1]
    big = (qkv, stats, att, inner_o, order, cosine, sine, out_w, first_o, second_o, weight_all, second_all)
    count = len(big)

    def kernel(*refs):
        len_ref, low_ref, small_ref, early_ref, out_ref, out_side_ref = refs[:6]
        big_in = refs[6 : 6 + count]
        sums, side_all, grad_ref, landed_out, early_out, middle_lines, early_lines, small_out = refs[
            6 + count : 14 + count
        ]
        refs = refs[14 + count :]
        (
            qkv_ref,
            lse_ref,
            att_ref,
            inner_ref,
            order_ref,
            cos_ref,
            sin_ref,
            ow_ref,
            fo_ref,
            so_ref,
            wa_ref,
            sa_ref,
        ) = refs[:count]
        (
            low,
            do_ref,
            gio_ref,
            dk_ref,
            dv_ref,
            part,
            land,
            staged,
            landed,
            side_own,
            middle_ref,
            load_sem,
            own_sem,
            send_sem,
            recv_sem,
            s_sem,
            r_sem,
        ) = refs[count : count + 17]
        sems = refs[count + 17 :]
        place = _place()
        c, f, x, core, core_peer, x_peer = place
        _greet([core_peer, x_peer, _y_peer(place)] + _z_peers(place))
        loads = [
            pltpu.make_async_copy(big_in[i], refs[i], load_sem.at[i]) for i in range(count)
        ]
        small_first, small_forward, small_own_here, small_core, small_far, small_last = _order_steps(
            small_ref, small_out, *sems[0:3], place
        )
        early_start, early_across, early_finish = _ctx_first(early_ref, early_lines, *sems[3:6], place)
        early_two = _ctx_second(early_lines, early_out, *sems[6:9], place)
        mid_start, mid_across, mid_finish = _ctx_first(middle_ref, middle_lines, *sems[9:12], place)
        side_first, side_last = _gather_steps([side_own], [side_all], *sems[12:15], place)
        live = len_ref[0]

        sends = {}
        hh = 1 - core
        local = []
        small_first()
        early_start()
        for k, target in ((0, x_peer), (2, core_peer)):
            for j in (1, 0):
                cp = _remote(
                    low_ref.at[j], low.at[hh, j, x], send_sem.at[k + j], recv_sem.at[k + j], target
                )
                cp.start()
                sends[(k, j)] = cp
        for j in range(2):
            lc = pltpu.make_async_copy(low_ref.at[j], low.at[hh, j, x], own_sem.at[j])
            lc.start()
            local.append(lc)
        for cp in loads:
            cp.start()
        swaps = [
            _remote(out_ref.at[j], landed_out.at[j], s_sem.at[8 + j], r_sem.at[8 + j], x_peer)
            for j in range(2)
        ]
        dk_ref[...] = jnp.zeros_like(dk_ref)
        dv_ref[...] = jnp.zeros_like(dv_ref)
        early_across()
        small_own_here()
        for j in range(2):
            small_forward(j)
        for cp in loads:
            cp.wait()
        for lc in local:
            lc.wait()

        def arrive(j):
            sends[(0, j)].wait_recv()
            cp = _remote(
                low.at[hh, j, 1 - x],
                low.at[hh, j, 1 - x],
                send_sem.at[4 + j],
                recv_sem.at[4 + j],
                core_peer,
            )
            cp.start()
            sends[(4, j)] = cp
            sends[(2, j)].wait_recv()
            cp.wait_recv()

        def through_output(t):
            g = low[t // 2, t % 2].reshape(step_rows, width)
            gio = dot_t(g, so_ref[...]).astype(BF16)
            row = pl.ds(t * step_rows, step_rows)
            gio_ref[row, :] = gio
            do_ref[row, :] = (dot_t(g, ow_ref[...]) + dot(gio, fo_ref[...])).astype(BF16)

        def attention(t, hook):
            keys = (t + 1) * step_rows
            row = pl.ds(t * step_rows, step_rows)
            qpos = t * step_rows + lax.broadcasted_iota(jnp.int32, (step_rows, keys), 0)
            kpos = lax.broadcasted_iota(jnp.int32, (step_rows, keys), 1)
            allowed = (kpos <= qpos) & (kpos < live)
            cos, sin = cos_ref[row, :], sin_ref[row, :]
            for head in range(4):
                kv = head // 2
                at = slice(head * lane, (head + 1) * lane)
                q = qkv_ref[row, at]
                k = qkv_ref[:keys, (4 + kv) * lane : (5 + kv) * lane]
                v = qkv_ref[:keys, (6 + kv) * lane : (7 + kv) * lane]
                do = do_ref[row, at]
                s = dot_t(q, k)
                p = jnp.where(allowed, jnp.exp(s * scale - lse_ref[row, head : head + 1]), 0.0)
                dp = dot_t(do, v)
                total = jnp.sum(p * dp, axis=1, keepdims=True)
                ds = (p * (dp - total)).astype(BF16)
                dq = scale * dot(ds, k)
                dq = dq * cos - pltpu.roll(dq, HALF_PAD, 1) * sin
                grad_ref[row, at] = dq.astype(BF16)
                dk_ref[kv, :keys] += dot_rows(ds, q)
                dv_ref[kv, :keys] += dot_rows(p.astype(BF16), do)
                if head == 1 and hook is not None:
                    hook()
            for kv in range(2):
                dk = scale * dk_ref[kv, row, :]
                dk = dk * cos - pltpu.roll(dk, HALF_PAD, 1) * sin
                grad_ref[row, (4 + kv) * lane : (5 + kv) * lane] = dk.astype(BF16)
                grad_ref[row, (6 + kv) * lane : (7 + kv) * lane] = dv_ref[kv, row, :].astype(BF16)
            g = grad_ref[row, :]
            for at in range(0, width, 256):
                value = dot_t(g, wa_ref[at : at + 256, :])
                part[t, :, :, at : at + 256] = value.astype(BF16).reshape(2, 128, 256)
            part[t, :, :, width:] = dot_t(g, sa_ref[...]).astype(BF16).reshape(2, 128, SIDE)

        def to_core(t):
            h, j = t // 2, t % 2
            return _remote(part.at[t], land.at[j], s_sem.at[j], r_sem.at[j], core_peer)

        def to_x(j):
            return _remote(staged.at[j], landed.at[j], s_sem.at[2 + j], r_sem.at[2 + j], x_peer)

        def leave(t):
            @pl.when(core == t // 2)
            def _():
                to_core(t).start()

        def combine(t):
            j = t % 2

            @pl.when(core == 1 - t // 2)
            def _():
                to_core(t).wait_recv()
                staged[j] = (part[t, 1 - x].astype(F32) + land[j, 1 - x].astype(F32)).astype(BF16)
                to_x(j).start()
                sums[j] = part[t, x].astype(F32) + land[j, x].astype(F32)

        arrive(1)
        through_output(3)
        through_output(1)
        for cp in swaps:
            cp.start()
        attention(3, None)
        leave(3)
        arrive(0)
        through_output(2)
        through_output(0)
        o_a = dot_rows(gio_ref[...], att_ref[...])[:RANK]
        o_a = jnp.concatenate(
            [o_a[:, head * lane : head * lane + HEAD_DIM] for head in range(4)], axis=1
        )
        middle_ref[:, :quarter] = o_a.astype(BF16)
        own_cols = pl.ds(pl.multiple_of(f * quarter, 128), quarter)
        g = low[:, :, :, :, own_cols].reshape(rows, quarter)
        middle_ref[:, quarter : 2 * quarter] = (ADAPTER_SCALE * dot_rows(inner_ref[...], g)[:RANK]).astype(BF16)
        for j in range(2):
            small_far(j)
        small_core()
        in_gu = jnp.zeros((SIDE, quarter), F32)
        for k in range(4):
            u = order_ref[k, :, :, own_cols].reshape(step_rows, quarter)
            in_gu += dot_rows(small_out[k].reshape(step_rows, SIDE), u)
        middle_ref[:, 2 * quarter : 3 * quarter] = in_gu[:RANK].astype(BF16)
        middle_ref[:, 3 * quarter :] = in_gu[RANK : 2 * RANK].astype(BF16)
        mid_start()
        early_finish()
        early_two[0]()
        mid_across()
        attention(2, lambda: combine(3))
        leave(2)
        attention(1, lambda: combine(2))
        leave(1)
        early_two[1]()
        attention(0, lambda: combine(1))
        leave(0)
        combine(0)
        for t in range(4):

            @pl.when(core == t // 2)
            def _():
                to_core(t).wait_send()

        for j in range(2):
            swaps[j].wait()
            cp = to_x(j)
            cp.wait_recv()
            sums[j] = sums[j] + landed[j].astype(F32)
            cp.wait_send()
            side_own[j] = (
                sums[j, :, width:] + out_side_ref[j] + landed_out[j, :, width:].astype(F32)
            ).astype(BF16)
        side_first()
        small_last()
        early_two[2]()
        mid_finish()
        side_last()
        for cp in sends.values():
            cp.wait_send()

    vmem, hbm = pl.BlockSpec(memory_space=pltpu.VMEM), pl.BlockSpec(memory_space=pl.ANY)
    shape = jax.ShapeDtypeStruct
    return pl.pallas_call(
        kernel,
        out_shape=[
            shape((2, 128, wide), F32),
            shape((2, 2, 2, 128, SIDE), BF16),
            shape(qkv.shape, BF16),
            shape(out_far.shape, BF16),
            _spread_of(early_n),
            shape(_lines_of(middle_n), BF16),
            shape(_lines_of(early_n), BF16),
            shape((4, 2, 128, SIDE), BF16),
        ],
        in_specs=[pl.BlockSpec(memory_space=pltpu.SMEM)] + [hbm] * 4 + [vmem] + [hbm] * count,
        out_specs=[vmem, hbm, vmem, vmem, hbm, hbm, hbm, vmem],
        scratch_shapes=[pltpu.VMEM(a.shape, a.dtype) for a in big]
        + [
            pltpu.VMEM((2, 2, 2, 128, width), BF16),
            pltpu.VMEM((rows, 4 * lane), BF16),
            pltpu.VMEM((rows, SIDE), BF16),
            pltpu.VMEM((2, rows, lane), F32),
            pltpu.VMEM((2, rows, lane), F32),
            pltpu.VMEM((4, 2, 128, wide), BF16),
            pltpu.VMEM((2, 2, 128, wide), BF16),
            pltpu.VMEM((2, 128, wide), BF16),
            pltpu.VMEM((2, 128, wide), BF16),
            pltpu.VMEM((2, 128, SIDE), BF16),
            pltpu.VMEM((RANK, middle_n), BF16),
            _sem(count),
            _sem(2),
            _sem(6),
            _sem(6),
            _sem(10),
            _sem(10),
        ]
        + [_sem(2), _sem(6), _sem(6)]
        + FIRST_SEMS
        + SECOND_SEMS
        + FIRST_SEMS
        + [_sem(2), _sem(6), _sem(6)],
        compiler_params=pltpu.CompilerParams(
            collective_id=cid, has_side_effects=True, vmem_limit_bytes=58 * 1024 * 1024
        ),
        name="attend_back",
    )(length, low_own, small_own, early, out_far, out_side, *big)


def table_call(early, middle, late, adapters):
    f32 = lambda *shape: jax.ShapeDtypeStruct(shape, F32)
    choices = 8
    outs = [
        f32(choices, 5, RANK, 1536),
        f32(choices, RANK, 1536),
        f32(choices, RANK, 4096),
        f32(choices, RANK, 1536),
        f32(choices, 2, RANK, 768),
        f32(choices, RANK, 1536),
        f32(choices, 2, RANK, 4096),
        f32(choices, RANK, 1536),
    ]
    plan = (
        ((6, 0, 1024), (6, 1, 1024), (2, None, 1024)),
        ((1, None, 384), (5, None, 384), (0, 3, 384), (0, 4, 384)),
        (
            (0, 0, 384),
            (0, 1, 384),
            (0, 2, 384),
            (3, None, 384),
            (4, 0, 192),
            (4, 1, 192),
            (7, None, 384),
        ),
    )

    def kernel(which, early_ref, middle_ref, late_ref, *refs):
        outs, acc, sems = refs[:8], refs[8:16], refs[16]

        def add(piece, ref):
            def one_slot(origin, carry):
                row = which[origin]
                for f in range(4):
                    at = 0
                    for out, table, n in plan[piece]:
                        value = ref[origin // 4, f % 2, origin % 4, f // 2, :, at : at + n].astype(F32)
                        cols = slice(f * n, (f + 1) * n)
                        if table is None:
                            acc[out][row, :, cols] += value
                        else:
                            acc[out][row, table, :, cols] += value
                        at += n
                return carry

            lax.fori_loop(0, 8, one_slot, 0)

        def send(out):
            cp = pltpu.make_async_copy(acc[out], outs[out], sems.at[out])
            cp.start()
            return cp

        for out in (2, 6):
            acc[out][...] = jnp.zeros_like(acc[out])
        add(0, early_ref)
        copies = [send(out) for out in (2, 6)]
        for out in (0, 1, 3, 4, 5, 7):
            acc[out][...] = jnp.zeros_like(acc[out])
        add(1, middle_ref)
        copies += [send(out) for out in (1, 5)]
        add(2, late_ref)
        copies += [send(out) for out in (0, 3, 4, 7)]
        for cp in copies:
            cp.wait()

    vmem, hbm = pl.BlockSpec(memory_space=pltpu.VMEM), pl.BlockSpec(memory_space=pl.ANY)
    return pl.pallas_call(
        kernel,
        out_shape=outs,
        in_specs=[pl.BlockSpec(memory_space=pltpu.SMEM), vmem, vmem, vmem],
        out_specs=[hbm] * 8,
        scratch_shapes=[pltpu.VMEM(o.shape, F32) for o in outs] + [_sem(8)],
        compiler_params=pltpu.CompilerParams(vmem_limit_bytes=40 * 1024 * 1024),
        name="tables",
    )(adapters, early, middle, late)


def rope_constants(rows):
    half = HEAD_DIM // 2
    freqs = np.float32(ROPE_BASE) ** (-(np.arange(half, dtype=np.float32) * 2.0 / HEAD_DIM))
    angles = np.arange(rows).astype(np.float32)[:, None] * freqs.astype(np.float32)[None, :]
    cos = np.cos(angles.astype(np.float64)).astype(np.float32)
    sin = np.sin(angles.astype(np.float64)).astype(np.float32)
    gap = np.zeros((rows, HALF_PAD - half), np.float32)
    cosine = np.concatenate([cos, gap, cos, gap], axis=1)
    sine = np.concatenate([-sin, gap, sin, gap], axis=1)
    return jnp.asarray(cosine), jnp.asarray(sine)


def dot(left, right):
    return jnp.dot(left, right, preferred_element_type=F32)


def dot_t(left, right):
    return lax.dot_general(left, right, (((1,), (1,)), ((), ())), preferred_element_type=F32)


def dot_rows(left, right):
    return lax.dot_general(left, right, (((0,), (0,)), ((), ())), preferred_element_type=F32)


def side_pad(value, before=0):
    return jnp.pad(value, ((0, 0), (before, SIDE - before - value.shape[1])))


def blocks(value):
    return value.reshape(2, 2, 2, 128, value.shape[-1])


def own_blocks(value):
    return value.reshape(2, 128, value.shape[-1])


def flat(value):
    return value.reshape(-1, value.shape[-1])


def slot_local(
    tokens,
    cotangent,
    lengths,
    slot_adapter_index,
    attention_norm_gain,
    feedforward_norm_gain,
    query_weight,
    key_weight,
    value_weight,
    output_weight,
    gate_weight,
    up_weight,
    down_weight,
    adapter_input_first,
    adapter_output_first,
    adapter_down_first,
    adapter_query_second,
    adapter_key_value_second,
    adapter_output_second,
    adapter_gate_up_second,
    adapter_down_second,
):
    width = tokens.shape[-1]
    quarter = width // 4
    c = lax.axis_index("ctx")
    f = lax.axis_index("fsdp")
    x, core = f // 2, f % 2
    slot = c // 2 + 4 * (c % 2)
    length = lax.dynamic_slice_in_dim(lengths, slot, 1, 0)
    adapter = slot_adapter_index[slot]

    def cut(value, axis, size):
        return lax.dynamic_slice_in_dim(value, f * size, size, axis)

    def unpad_turned(g):
        rows = g.shape[0]
        return g.reshape(rows, -1, 2, HALF_PAD)[..., : HEAD_DIM // 2].reshape(rows, -1)

    def unpad_plain(g):
        rows = g.shape[0]
        return g.reshape(rows, -1, PAD_HEAD)[..., :HEAD_DIM].reshape(rows, -1)

    rows = 4 * 2 * tokens.shape[1]
    cosine, sine = rope_constants(rows)
    turned = lambda t: jnp.swapaxes(t, -1, -2)
    second_kv = adapter_key_value_second
    second_kv = lax.dynamic_slice_in_dim(second_kv, f * key_weight.shape[1], key_weight.shape[1], 3)
    (
        resid,
        normed_two_own,
        inner_o,
        tok_own,
        cot_own,
        cot_order,
        qkv,
        stats,
        attn_b,
        one_cut,
        inner_qkv,
        weight_all,
        out_w,
        second_all,
        first_all,
        first_gu,
        second_g,
        second_u,
        first_d,
        second_d,
        first_o,
        second_o,
    ) = front_call(
        tokens,
        cotangent,
        length,
        adapter.reshape(1),
        jnp.stack([attention_norm_gain, feedforward_norm_gain]),
        query_weight,
        key_weight,
        value_weight,
        output_weight,
        (
            turned(adapter_input_first),
            turned(adapter_output_first),
            turned(adapter_down_first),
            adapter_query_second,
            second_kv,
            adapter_output_second,
            adapter_gate_up_second,
            adapter_down_second,
        ),
        cosine,
        sine,
        0,
    )
    block_x = x + jnp.array([[0, 0], [1, 1], [1, 1], [0, 0]]) * (1 - 2 * x)
    block_core = core + jnp.array([[0, 0], [1, 0], [1, 0], [1, 1]]) * (1 - 2 * core)
    block_j = jnp.array([[0, 1], [0, 0], [1, 1], [0, 1]])
    order_block = (block_x + 2 * block_j + 4 * (1 - block_core)).reshape(8)
    order_pos = (128 * order_block[:, None] + jnp.arange(128, dtype=jnp.int32)).reshape(-1)
    own_live = (order_pos[:256] < length[0])[:, None]
    own_f = flat(tok_own).astype(F32)

    grad_resid, grad_low_own, small, out_sums, out_far, order, early = feed_forward(
        normed_two_own,
        cot_order,
        resid,
        feedforward_norm_gain[None, :],
        length,
        (gate_weight, up_weight, down_weight),
        (first_gu, second_g, second_u, first_d, second_d),
        3,
    )
    grad_resid = flat(grad_resid)
    resid = flat(resid)

    def pack(parts):
        return jnp.concatenate(parts, axis=1).astype(BF16)

    sums, side_all, grad_qkv, out_landed, early, middle = attend_back_call(
        grad_low_own,
        small,
        early,
        out_far,
        out_sums[..., width:],
        qkv,
        stats,
        attn_b,
        flat(inner_o),
        order,
        cosine,
        sine,
        length,
        out_w,
        first_o,
        second_o,
        weight_all,
        second_all,
        10,
    )[:6]
    out_sums = flat(out_sums) + flat(out_landed).astype(F32)
    inner_d_own = out_sums[:, width + 3 * RANK : width + 4 * RANK].astype(BF16)
    out_own = jnp.where(
        own_live, resid + out_sums[:, :width] + dot(inner_d_own, second_d[3 * RANK : 4 * RANK]), 0.0
    ).astype(BF16)
    all_b = ADAPTER_SCALE * dot_rows(inner_qkv, grad_qkv)[: 3 * RANK]
    sums = flat(sums)
    grad_inner_qkv = flat(side_all)[:, : 3 * RANK]
    grad_inner_own = sums[:, width : width + 3 * RANK].astype(BF16)
    grad_normed_one = (sums[:, :width] + dot(grad_inner_own, first_all[: 3 * RANK])).astype(BF16).astype(F32)
    grad_tok_own = grad_resid + norm_back(
        own_f, rms_factor(own_f), attention_norm_gain, grad_normed_one
    )
    in_qkv = dot_rows(grad_inner_qkv, one_cut)
    inner_d = flat(side_all.reshape(8, 128, SIDE)[order_block])[:, 3 * RANK : 4 * RANK]
    out_cut = jnp.where(
        (order_pos < length[0])[:, None], cut(flat(cot_order), 1, quarter), jnp.zeros((), BF16)
    )
    d_b = ADAPTER_SCALE * dot_rows(inner_d, out_cut)
    late = pack(
        [
            in_qkv[:RANK],
            in_qkv[RANK : 2 * RANK],
            in_qkv[2 * RANK :],
            unpad_turned(all_b[:RANK, : 4 * PAD_HEAD]),
            unpad_turned(all_b[RANK : 2 * RANK, 4 * PAD_HEAD : 6 * PAD_HEAD]),
            unpad_plain(all_b[2 * RANK :, 6 * PAD_HEAD :]),
            d_b,
        ]
    )
    out_tokens, grad_tokens, late, middle = give_back(
        [own_blocks(out_own), own_blocks(grad_tok_own.astype(BF16))], late, middle, 7
    )

    full = table_call(early, middle, late, slot_adapter_index)
    turn = lambda t: jnp.swapaxes(t, -1, -2)
    return (
        out_tokens,
        grad_tokens.astype(F32),
        turn(full[0]),
        turn(full[1]),
        turn(full[2]),
        full[3],
        full[4],
        full[5],
        full[6],
        full[7],
    )


def solution(mesh):
    one_slot = mesh.shape["ctx"] == 8 and mesh.shape["fsdp"] == 4
    return jax.shard_map(
        slot_local if one_slot else local,
        mesh=mesh,
        in_specs=(
            P("fsdp", "ctx", None),
            P("fsdp", "ctx", None),
            P(),
            P(),
            P(),
            P(),
            P(None, "fsdp"),
            P(None, "fsdp"),
            P(None, "fsdp"),
            P("fsdp", None),
            P(None, "fsdp"),
            P(None, "fsdp"),
            P("fsdp", None),
            P(),
            P(),
            P(),
            P(),
            P(),
            P(),
            P(),
            P(),
        ),
        out_specs=(
            P("fsdp", "ctx", None),
            P("fsdp", "ctx", None),
            P(),
            P(),
            P(),
            P(),
            P(),
            P(),
            P(),
            P(),
        ),
        check_vma=False,
    )
```

```python
import math

import jax
import jax.numpy as jnp
import numpy as np
from jax import lax
from jax.experimental import pallas as pl
from jax.experimental.pallas import tpu as pltpu
from jax.sharding import PartitionSpec as P

QUERY_HEADS = 16
KEY_VALUE_HEADS = 8
HEAD_DIM = 96


EPSILON = 1e-05
NEGATIVE = -1e30
ADAPTER_SCALE = 0.5
ROPE_BASE = 100000.0


def from_behind(x, axis, by):
    size = lax.axis_size(axis)
    return lax.ppermute(x, axis, [(i, (i + by) % size) for i in range(size)])


def rope_tables(positions, head_size):
    half_size = head_size // 2
    freqs = ROPE_BASE ** (-(jnp.arange(half_size, dtype=jnp.float32) * 2.0 / head_size))
    angles = positions.astype(jnp.float32)[:, None] * freqs[None, :]
    return (jnp.cos(angles)[:, None, :], jnp.sin(angles)[:, None, :])


def apply_rotation(values, cosine_table, sine_table):
    half_size = values.shape[-1] // 2
    first_half = values[..., :half_size]
    second_half = values[..., half_size:]
    return jnp.concatenate(
        [
            first_half * cosine_table - second_half * sine_table,
            second_half * cosine_table + first_half * sine_table,
        ],
        axis=-1,
    )


def rotate_back(gradient_tree, cosine_table, sine_table):
    half_size = gradient_tree.shape[-1] // 2
    first_half = gradient_tree[..., :half_size]
    second_half = gradient_tree[..., half_size:]
    return jnp.concatenate(
        [
            first_half * cosine_table + second_half * sine_table,
            second_half * cosine_table - first_half * sine_table,
        ],
        axis=-1,
    )


def rms_factor(values):
    return lax.rsqrt(jnp.mean(values * values, axis=-1, keepdims=True) + EPSILON)


def norm_back(values, factor, gain, grad_norm):
    scaled = grad_norm * gain
    return factor * scaled - values * factor**3 * jnp.mean(scaled * values, axis=-1, keepdims=True)


def pick_rows(onehot, table):
    return jnp.einsum("sa,a...->s...", onehot, table, preferred_element_type=jnp.float32).astype(
        jnp.bfloat16
    )


def spread_rows(onehot, gradient_tree):
    return jnp.einsum("sa,s...->a...", onehot, gradient_tree, precision=lax.Precision.HIGHEST)


def direct_product(input_rows, weight_matrix):
    return jnp.einsum("std,do->sto", input_rows, weight_matrix, preferred_element_type=jnp.float32)


def direct_back(gradient_tree, weight_matrix):
    return jnp.einsum(
        "sto,do->std", gradient_tree, weight_matrix, preferred_element_type=jnp.float32
    )


def inner_product_part(input_rows, down):
    return jnp.einsum("std,sdr->str", input_rows, down, preferred_element_type=jnp.float32)


def inner_back(gradient_tree, upward_rows):
    return ADAPTER_SCALE * jnp.einsum(
        "sto,sro->str", gradient_tree, upward_rows, preferred_element_type=jnp.float32
    )


def through_down(grad_inner, down):
    return jnp.einsum("str,sdr->std", grad_inner, down, preferred_element_type=jnp.float32)


def down_grad(input_rows, grad_inner):
    return jnp.einsum("std,str->sdr", input_rows, grad_inner, preferred_element_type=jnp.float32)


def upward_grad(inner_rows, gradient_tree):
    return ADAPTER_SCALE * jnp.einsum(
        "jvp,jvx->jpx", inner_rows, gradient_tree, preferred_element_type=jnp.float32
    )


def upward_apply(inner_rows, upward_rows):
    return ADAPTER_SCALE * jnp.einsum(
        "str,sro->sto", inner_rows, upward_rows, preferred_element_type=jnp.float32
    )


def project(input_rows, weight_matrix, down, upward_rows):
    inner_rows = inner_product_part(input_rows, down).astype(jnp.bfloat16)
    return (
        inner_rows,
        direct_product(input_rows, weight_matrix) + upward_apply(inner_rows, upward_rows),
    )


def project_back(input_rows, grad_output, weight_matrix, down, upward_rows, inner_rows):
    grad_upward = upward_grad(inner_rows, grad_output)
    grad_inner = inner_back(grad_output, upward_rows).astype(jnp.bfloat16)
    grad_down = down_grad(input_rows, grad_inner)
    grad_inputs = direct_back(grad_output, weight_matrix) + through_down(grad_inner, down)
    return (grad_inputs, grad_down, grad_upward)


def allowed_mask(key_start, key_count, query_pos, lengths):
    key_pos = key_start + jnp.arange(key_count, dtype=jnp.int32)
    causal = key_pos[None, :] <= query_pos[:, None]
    live = key_pos[None, :] < lengths[:, None]
    return (causal[None, :, :] & live[:, None, :])[:, None, None, :, :]


def attend_block(state, key_block, value_block, key_start, query_head_rows, query_pos, lengths):
    run_max, run_sum, run_acc = state
    scale = query_head_rows.shape[-1] ** (-0.5)
    scores = (
        jnp.einsum(
            "sqhgd,skhd->shgqk", query_head_rows, key_block, preferred_element_type=jnp.float32
        )
        * scale
    )
    allowed = allowed_mask(key_start, key_block.shape[1], query_pos, lengths)
    new_max = jnp.maximum(run_max, jnp.max(jnp.where(allowed, scores, NEGATIVE), axis=-1))
    weights = jnp.where(allowed, jnp.exp(scores - new_max[..., None]), 0.0)
    factor = jnp.exp(run_max - new_max)
    new_sum = run_sum * factor + jnp.sum(weights, axis=-1)
    update = jnp.einsum(
        "shgqk,skhd->shgqd",
        weights.astype(jnp.bfloat16),
        value_block,
        preferred_element_type=jnp.float32,
    )
    return (new_max, new_sum, run_acc * factor[..., None] + update)


def attend_back(
    key_block,
    value_block,
    key_start,
    query_head_rows,
    grad_heads,
    log_total,
    row_dot,
    query_pos,
    lengths,
):
    scale = query_head_rows.shape[-1] ** (-0.5)
    scores = (
        jnp.einsum(
            "sqhgd,skhd->shgqk", query_head_rows, key_block, preferred_element_type=jnp.float32
        )
        * scale
    )
    allowed = allowed_mask(key_start, key_block.shape[1], query_pos, lengths)
    probs = jnp.where(allowed, jnp.exp(scores - log_total[..., None]), 0.0)
    grad_probs = jnp.einsum(
        "sqhgd,skhd->shgqk", grad_heads, value_block, preferred_element_type=jnp.float32
    )
    grad_scores = (probs * (grad_probs - row_dot[..., None])).astype(jnp.bfloat16)
    grad_query = scale * jnp.einsum(
        "shgqk,skhd->sqhgd", grad_scores, key_block, preferred_element_type=jnp.float32
    )
    grad_key = scale * jnp.einsum(
        "shgqk,sqhgd->skhd", grad_scores, query_head_rows, preferred_element_type=jnp.float32
    )
    grad_value = jnp.einsum(
        "shgqk,sqhgd->skhd",
        probs.astype(jnp.bfloat16),
        grad_heads,
        preferred_element_type=jnp.float32,
    )
    return (grad_query, grad_key, grad_value)


def attend_forward(query_head_rows, key_head_rows, value_head_rows, lengths_used, query_pos):
    slots, rows, kv_heads, group_size, head_size = query_head_rows.shape
    key_flat = key_head_rows.reshape(slots, rows, kv_heads * head_size)
    value_flat = value_head_rows.reshape(slots, rows, kv_heads * head_size)
    stat_shape = (slots, kv_heads, group_size, rows)
    initial = (
        jnp.full(stat_shape, NEGATIVE, jnp.float32),
        jnp.zeros(stat_shape, jnp.float32),
        jnp.zeros(stat_shape + (head_size,), jnp.float32),
    )
    part_keys = lax.all_gather(key_flat, "ctx", axis=1, tiled=True)
    part_values = lax.all_gather(value_flat, "ctx", axis=1, tiled=True)
    piece_rows = part_keys.shape[1]
    part_keys = part_keys.reshape(slots, piece_rows, kv_heads, head_size)
    part_values = part_values.reshape(slots, piece_rows, kv_heads, head_size)
    span_rows = math.gcd(piece_rows, 4 * rows)

    def inner_step(block_index, inner_state):
        sub_keys = lax.dynamic_slice_in_dim(part_keys, block_index * span_rows, span_rows, 1)
        sub_values = lax.dynamic_slice_in_dim(part_values, block_index * span_rows, span_rows, 1)
        return attend_block(
            inner_state,
            sub_keys,
            sub_values,
            block_index * span_rows,
            query_head_rows,
            query_pos,
            lengths_used,
        )

    run_max, run_sum, run_acc = lax.fori_loop(0, piece_rows // span_rows, inner_step, initial)
    log_total = run_max + jnp.log(run_sum)
    attended = jnp.transpose(run_acc / run_sum[..., None], (0, 3, 1, 2, 4))
    return (attended, log_total)


def attend_backward(
    query_head_rows,
    key_head_rows,
    value_head_rows,
    grad_heads,
    attended,
    log_total,
    lengths_used,
    query_pos,
):
    ctx_count = lax.axis_size("ctx")
    own_index = lax.axis_index("ctx")
    rows = query_head_rows.shape[1]
    row_dot = jnp.transpose(
        jnp.sum(grad_heads.astype(jnp.float32) * attended, axis=-1), (0, 2, 3, 1)
    )

    def cycle_step(step_index, carried):
        carried_keys, carried_values, grad_query, grad_key, grad_value = carried
        block_id = (own_index + step_index) % ctx_count
        query_part, key_part, value_part = attend_back(
            carried_keys,
            carried_values,
            block_id * rows,
            query_head_rows,
            grad_heads,
            log_total,
            row_dot,
            query_pos,
            lengths_used,
        )
        grad_key, grad_value = (
            from_behind((grad_key + key_part).astype(jnp.bfloat16), "ctx", -1).astype(jnp.float32),
            from_behind((grad_value + value_part).astype(jnp.bfloat16), "ctx", -1).astype(
                jnp.float32
            ),
        )
        carried_keys, carried_values = from_behind((carried_keys, carried_values), "ctx", -1)
        return (carried_keys, carried_values, grad_query + query_part, grad_key, grad_value)

    key_zeros = jnp.zeros(key_head_rows.shape, jnp.float32)
    start_state = (
        key_head_rows,
        value_head_rows,
        jnp.zeros(query_head_rows.shape, jnp.float32),
        key_zeros,
        key_zeros,
    )
    carried = lax.fori_loop(0, ctx_count, cycle_step, start_state)
    return (carried[2], carried[3], carried[4])


def table_total(rotation_tables):
    return lax.psum(rotation_tables, ("ctx", "fsdp"))


def local(
    tokens,
    cotangent,
    lengths,
    slot_adapter_index,
    attention_norm_gain,
    feedforward_norm_gain,
    query_weight,
    key_weight,
    value_weight,
    output_weight,
    gate_weight,
    up_weight,
    down_weight,
    adapter_input_first,
    adapter_output_first,
    adapter_down_first,
    adapter_query_second,
    adapter_key_value_second,
    adapter_output_second,
    adapter_gate_up_second,
    adapter_down_second,
):
    slot_count, tok_rows, model_width = tokens.shape
    head_groups = QUERY_HEADS // KEY_VALUE_HEADS
    own_index = lax.axis_index("ctx")
    fsdp_index = lax.axis_index("fsdp")
    query_pos = own_index * tok_rows + jnp.arange(tok_rows, dtype=jnp.int32)
    cosine_table, sine_table = rope_tables(query_pos, HEAD_DIM)
    own_lengths = lax.dynamic_slice_in_dim(lengths, fsdp_index * slot_count, slot_count, 0)
    own_adapters = lax.dynamic_slice_in_dim(
        slot_adapter_index, fsdp_index * slot_count, slot_count, 0
    )
    valid = query_pos[None, :] < own_lengths[:, None]
    adapter_labels = jnp.arange(adapter_input_first.shape[0], dtype=jnp.int32)
    onehot_own = own_adapters[:, None] == adapter_labels[None, :]
    owned_low_rank = onehot_own.astype(jnp.bfloat16)
    own_full = onehot_own.astype(jnp.float32)
    tokens_f = tokens.astype(jnp.float32)
    factor_one = rms_factor(tokens_f)
    normed_one = (tokens_f * factor_one * attention_norm_gain).astype(jnp.bfloat16)
    grad_out = jnp.where(valid[..., None], cotangent, jnp.zeros((), jnp.bfloat16))
    input_first = pick_rows(owned_low_rank, adapter_input_first)
    output_second = pick_rows(owned_low_rank, adapter_output_second)
    down_second = pick_rows(owned_low_rank, adapter_down_second)
    output_first = pick_rows(owned_low_rank, adapter_output_first)
    down_first = pick_rows(owned_low_rank, adapter_down_first)
    query_second = pick_rows(owned_low_rank, adapter_query_second)
    key_value_second = pick_rows(owned_low_rank, adapter_key_value_second)
    gate_up_second = pick_rows(owned_low_rank, adapter_gate_up_second)
    weight_q, weight_k, weight_v, weight_gate, weight_up, weight_o, weight_down = (
        lax.all_gather(query_weight, "fsdp", axis=1, tiled=True),
        lax.all_gather(key_weight, "fsdp", axis=1, tiled=True),
        lax.all_gather(value_weight, "fsdp", axis=1, tiled=True),
        lax.all_gather(gate_weight, "fsdp", axis=1, tiled=True),
        lax.all_gather(up_weight, "fsdp", axis=1, tiled=True),
        lax.all_gather(output_weight, "fsdp", axis=0, tiled=True),
        lax.all_gather(down_weight, "fsdp", axis=0, tiled=True),
    )
    inner_q, projected_queries = project(normed_one, weight_q, input_first[:, 0], query_second)
    inner_k, projected_keys = project(
        normed_one, weight_k, input_first[:, 1], key_value_second[:, 0]
    )
    inner_v, projected_values = project(
        normed_one, weight_v, input_first[:, 2], key_value_second[:, 1]
    )
    query_head_rows = apply_rotation(
        projected_queries.reshape(slot_count, tok_rows, -1, HEAD_DIM), cosine_table, sine_table
    ).astype(jnp.bfloat16)
    query_head_rows = query_head_rows.reshape(slot_count, tok_rows, -1, head_groups, HEAD_DIM)
    key_head_rows = apply_rotation(
        projected_keys.reshape(slot_count, tok_rows, -1, HEAD_DIM), cosine_table, sine_table
    ).astype(jnp.bfloat16)
    value_head_rows = projected_values.astype(jnp.bfloat16).reshape(
        slot_count, tok_rows, -1, HEAD_DIM
    )
    attended, log_total = attend_forward(
        query_head_rows, key_head_rows, value_head_rows, own_lengths, query_pos
    )
    attn_b = attended.reshape(slot_count, tok_rows, -1).astype(jnp.bfloat16)
    inner_o, proj_o = project(attn_b, weight_o, output_first, output_second)
    resid = tokens_f + proj_o
    factor_two = rms_factor(resid)
    normed_two = (resid * factor_two * feedforward_norm_gain).astype(jnp.bfloat16)
    inner_gate, gate = project(normed_two, weight_gate, input_first[:, 3], gate_up_second[:, 0])
    inner_up, up_proj = project(normed_two, weight_up, input_first[:, 4], gate_up_second[:, 1])
    sigmoid_gate = jax.nn.sigmoid(gate)
    hidden = (gate * sigmoid_gate * up_proj).astype(jnp.bfloat16)
    inner_down, proj_down = project(hidden, weight_down, down_first, down_second)
    out_tokens = jnp.where(valid[..., None], resid + proj_down, 0.0).astype(jnp.bfloat16)
    grad_hidden, grad_da, grad_db = project_back(
        hidden, grad_out, weight_down, down_first, down_second, inner_down
    )
    grad_gate = (grad_hidden * up_proj * sigmoid_gate * (1.0 + gate * (1.0 - sigmoid_gate))).astype(
        jnp.bfloat16
    )
    grad_up = (grad_hidden * gate * sigmoid_gate).astype(jnp.bfloat16)
    from_gate, grad_ga, grad_gb = project_back(
        normed_two, grad_gate, weight_gate, input_first[:, 3], gate_up_second[:, 0], inner_gate
    )
    from_up, grad_ua, grad_ub = project_back(
        normed_two, grad_up, weight_up, input_first[:, 4], gate_up_second[:, 1], inner_up
    )
    grad_normed_two = (from_gate + from_up).astype(jnp.bfloat16).astype(jnp.float32)
    grad_resid = grad_out.astype(jnp.float32) + norm_back(
        resid, factor_two, feedforward_norm_gain, grad_normed_two
    )
    grad_resid_low = grad_resid.astype(jnp.bfloat16)
    from_attn, grad_oa, grad_ob = project_back(
        attn_b, grad_resid_low, weight_o, output_first, output_second, inner_o
    )
    grad_heads = from_attn.astype(jnp.bfloat16).reshape(attended.shape)
    grad_query, grad_key, grad_value = attend_backward(
        query_head_rows,
        key_head_rows,
        value_head_rows,
        grad_heads,
        attended,
        log_total,
        own_lengths,
        query_pos,
    )
    grad_proj_q = (
        rotate_back(
            grad_query.reshape(slot_count, tok_rows, -1, HEAD_DIM), cosine_table, sine_table
        )
        .astype(jnp.bfloat16)
        .reshape(slot_count, tok_rows, -1)
    )
    grad_proj_k = (
        rotate_back(grad_key, cosine_table, sine_table)
        .astype(jnp.bfloat16)
        .reshape(slot_count, tok_rows, -1)
    )
    grad_proj_v = grad_value.astype(jnp.bfloat16).reshape(slot_count, tok_rows, -1)
    from_query, grad_qa, grad_qb = project_back(
        normed_one, grad_proj_q, weight_q, input_first[:, 0], query_second, inner_q
    )
    from_key, grad_ka, grad_kb = project_back(
        normed_one, grad_proj_k, weight_k, input_first[:, 1], key_value_second[:, 0], inner_k
    )
    from_value, grad_va, grad_vb = project_back(
        normed_one, grad_proj_v, weight_v, input_first[:, 2], key_value_second[:, 1], inner_v
    )
    grad_normed_one = (from_query + from_key + from_value).astype(jnp.bfloat16).astype(jnp.float32)
    grad_tokens = grad_resid + norm_back(tokens_f, factor_one, attention_norm_gain, grad_normed_one)
    slot_grads = (
        jnp.stack([grad_qa, grad_ka, grad_va, grad_ga, grad_ua], axis=1),
        grad_oa,
        grad_da,
        grad_qb,
        jnp.stack([grad_kb, grad_vb], axis=1),
        grad_ob,
        jnp.stack([grad_gb, grad_ub], axis=1),
        grad_db,
    )
    summed = table_total(tuple((spread_rows(own_full, entry_item) for entry_item in slot_grads)))
    return (
        out_tokens,
        grad_tokens,
        summed[0],
        summed[1],
        summed[2],
        summed[3],
        summed[4],
        summed[5],
        summed[6],
        summed[7],
    )


BF16 = jnp.bfloat16
F32 = jnp.float32
MESH_ID = pl.DeviceIdType.MESH
RANK = 16
SIDE = 128
PAD_HEAD = 128
HALF_PAD = 64


def _sem(count):
    return pltpu.SemaphoreType.DMA((count,))


def _place():
    c = lax.axis_index("ctx")
    f = lax.axis_index("fsdp")
    x = f // 2
    core = f % 2
    return c, f, x, core, (c, 2 * x + 1 - core), (c, 2 * (1 - x) + core)


def _slot_of(c):
    return c // 2 + 4 * ((c // 2 + c) % 2)


def _group_of(slot):
    return 2 * (slot % 4) + (slot // 4 + slot) % 2


def _block(x, core, j):
    return 4 * (1 - core) + 2 * j + (x + j) % 2


def _owner(b):
    return 2 * ((b // 2 + b) % 2) + 1 - b // 4


def _greet(targets):
    barrier = pltpu.get_barrier_semaphore()
    for target in targets:
        pl.semaphore_signal(barrier, inc=1, device_id=target, device_id_type=MESH_ID)
    pl.semaphore_wait(barrier, len(targets))


def _remote(src, dst, send, recv, target):
    return pltpu.make_async_remote_copy(
        src_ref=src, dst_ref=dst, send_sem=send, recv_sem=recv, device_id=target, device_id_type=MESH_ID
    )


def _comm_call(kernel, ins, outs, scratch, cid, name, in_space=pl.ANY, out_space=pl.ANY, vmem=None):
    return pl.pallas_call(
        kernel,
        out_shape=outs,
        in_specs=[pl.BlockSpec(memory_space=in_space)] * len(ins),
        out_specs=jax.tree.map(lambda _: pl.BlockSpec(memory_space=out_space), outs),
        scratch_shapes=scratch,
        compiler_params=pltpu.CompilerParams(
            collective_id=cid, has_side_effects=True, vmem_limit_bytes=vmem
        ),
        name=name,
    )(*ins)


def _gather_steps(ins, outs, own_sem, send_sem, recv_sem, place):
    c, f, x, core, core_peer, x_peer = place
    h = 1 - core
    count = len(ins)
    local = []
    sends = []

    def first():
        for base, target in ((0, x_peer), (2 * count, core_peer)):
            for i in range(count):
                for j in range(2):
                    k = base + i * 2 + j
                    cp = _remote(
                        ins[i].at[j], outs[i].at[h, j, (x + j) % 2], send_sem.at[k], recv_sem.at[k], target
                    )
                    cp.start()
                    sends.append(cp)
        for i in range(count):
            for j in range(2):
                lc = pltpu.make_async_copy(
                    ins[i].at[j], outs[i].at[h, j, (x + j) % 2], own_sem.at[i * 2 + j]
                )
                lc.start()
                local.append(lc)

    def last():
        forwards = []
        for i in range(count):
            for j in range(2):
                k = i * 2 + j
                sends[k].wait_recv()
                cp = _remote(
                    outs[i].at[h, j, (x + j + 1) % 2],
                    outs[i].at[h, j, (x + j + 1) % 2],
                    send_sem.at[4 * count + k],
                    recv_sem.at[4 * count + k],
                    core_peer,
                )
                cp.start()
                forwards.append(cp)
        for k in range(2 * count):
            sends[2 * count + k].wait_recv()
            forwards[k].wait_recv()
        for cp in sends + forwards:
            cp.wait_send()
        for lc in local:
            lc.wait()

    return first, last


def _ctx_first(piece, lines, own_sem, send_sem, recv_sem, place):
    c, f, x, core, core_peer, x_peer = place
    z, y = c // 2, c % 2
    sends = []
    local = []

    def start():
        lc = pltpu.make_async_copy(piece, lines.at[z, x], own_sem)
        lc.start()
        local.append(lc)
        cp = _remote(piece, lines.at[z, x], send_sem.at[0], recv_sem.at[0], x_peer)
        cp.start()
        sends.append(cp)

    def spread():
        local[0].wait()
        sends[0].wait_recv()
        for step in range(1, 4):
            cp = _remote(
                lines.at[z],
                lines.at[z],
                send_sem.at[step],
                recv_sem.at[step],
                (2 * ((z + step) % 4) + y, f),
            )
            cp.start()
            sends.append(cp)

    def finish():
        for cp in sends[1:]:
            cp.wait_recv()
        for cp in sends:
            cp.wait_send()

    return start, spread, finish


def _ctx_second(lines, out, own_sem, send_sem, recv_sem, place):
    c, f, x, core, core_peer, x_peer = place
    z, y = c // 2, c % 2
    y_peer = (2 * z + 1 - y, f)
    sends = []
    local = []

    def start():
        lc = pltpu.make_async_copy(lines, out.at[y, core], own_sem)
        lc.start()
        local.append(lc)
        for k, target in ((0, y_peer), (1, core_peer)):
            cp = _remote(lines, out.at[y, core], send_sem.at[k], recv_sem.at[k], target)
            cp.start()
            sends.append(cp)

    def share():
        sends[0].wait_recv()
        cp = _remote(
            out.at[1 - y, core], out.at[1 - y, core], send_sem.at[2], recv_sem.at[2], core_peer
        )
        cp.start()
        sends.append(cp)

    def finish():
        sends[1].wait_recv()
        sends[2].wait_recv()
        for cp in sends:
            cp.wait_send()
        local[0].wait()

    return start, share, finish


def _z_peers(place):
    c, f = place[:2]
    return [(2 * ((c // 2 + step) % 4) + c % 2, f) for step in range(1, 4)]


def _y_peer(place):
    c, f = place[:2]
    return (2 * (c // 2) + 1 - c % 2, f)


def _lines_of(n):
    return (4, 2, RANK, n)


def _spread_of(n):
    return jax.ShapeDtypeStruct((2, 2, 4, 2, RANK, n), BF16)


FIRST_SEMS = [pltpu.SemaphoreType.DMA(()), _sem(4), _sem(4)]
SECOND_SEMS = [pltpu.SemaphoreType.DMA(()), _sem(3), _sem(3)]


def _order_steps(own, order, own_sem, send_sem, recv_sem, place):
    core_peer, x_peer = place[4:]
    sends, local, forwards = [], [], []

    def first():
        for j in range(2):
            cp = _remote(own.at[j], order.at[1 + j, 1], send_sem.at[j], recv_sem.at[j], x_peer)
            cp.start()
            sends.append(cp)
        for j in range(2):
            cp = _remote(
                own.at[j], order.at[3, j], send_sem.at[2 + j], recv_sem.at[2 + j], core_peer
            )
            cp.start()
            sends.append(cp)
        for j in range(2):
            lc = pltpu.make_async_copy(own.at[j], order.at[0, j], own_sem.at[j])
            lc.start()
            local.append(lc)

    def forward(j):
        sends[j].wait_recv()
        cp = _remote(
            order.at[1 + j, 1],
            order.at[1 + j, 0],
            send_sem.at[4 + j],
            recv_sem.at[4 + j],
            core_peer,
        )
        cp.start()
        forwards.append(cp)

    def own_here():
        for lc in local:
            lc.wait()

    def core_here():
        for j in range(2):
            sends[2 + j].wait_recv()

    def far_here(j):
        forwards[j].wait_recv()

    def last():
        for cp in sends + forwards:
            cp.wait_send()

    return first, forward, own_here, core_here, far_here, last


def _order_all(own, order, sems, place):
    first, forward, own_here, core_here, far_here, last = _order_steps(own, order, *sems, place)
    first()
    own_here()
    for j in range(2):
        forward(j)
    core_here()
    for j in range(2):
        far_here(j)
    last()


def feed_forward(own, cot, resid, gain, length, weights, adapters, cid):
    gate_w, up_w, down_w = weights
    width, units = gate_w.shape
    wide = width + SIDE
    tile = 256

    loads_in = tuple(weights) + tuple(adapters) + (cot,)
    count = len(loads_in)

    def kernel(*refs):
        len_ref, own_ref, resid_ref, gain_ref = refs[:4]
        loads_hbm = refs[4 : 4 + count]
        grad_resid, grad_low, small, out_own, out_far, order, early = refs[4 + count : 11 + count]
        refs = refs[11 + count :]
        gate_ref, up_ref, down_ref, first_ref, sg_ref, su_ref, fd_ref, sd_ref, go_ref = refs[:count]
        (
            sums,
            hid_s,
            gg_s,
            gu_s,
            in_s,
            gid_s,
            part,
            out_part,
            near,
            out_near,
            far,
            out_land,
            staged,
            landed,
            load_sem,
            own_sem,
            send_sem,
            recv_sem,
            s_sem,
            r_sem,
        ) = refs[count:]
        place = _place()
        core_peer, x_peer = place[4:]
        loads = []
        for i in range(count):
            cp = pltpu.make_async_copy(loads_hbm[i], refs[i], load_sem.at[i])
            cp.start()
            loads.append(cp)
        _greet([core_peer, x_peer])
        first, forward, own_here, core_here, far_here, last = _order_steps(
            own_ref, order, own_sem, send_sem, recv_sem, place
        )
        first()
        copies = []
        c, f, x, core = place[:4]
        live = len_ref[0]

        def masked(step):
            other_x = x if step in (0, 3) else 1 - x
            pieces = []
            for k in range(2):
                other_core = (core, 1 - core)[step == 3 or (step in (1, 2) and k == 0)]
                j = k if step in (0, 3) else step - 1
                pos = 128 * _block(other_x, other_core, j) + lax.broadcasted_iota(jnp.int32, (128, width), 0)
                pieces.append(jnp.where(pos < live, go_ref[step, k].astype(F32), 0.0).astype(BF16))
            return pieces

        def work(step):
            rows = order[step].reshape(2 * 128, width)
            pieces = masked(step)
            for k in range(2):
                go_ref[step, k] = pieces[k]
            go = go_ref[step].reshape(2 * 128, width)
            inner = dot_t(rows, first_ref[...]).astype(BF16)
            gid = dot_t(go, sd_ref[...]).astype(BF16)
            in_s[step] = inner
            gid_s[step] = gid
            for at in range(0, units, tile):
                cols = slice(at, at + tile)
                gate = dot(rows, gate_ref[:, cols]) + dot(inner, sg_ref[:, cols])
                up = dot(rows, up_ref[:, cols]) + dot(inner, su_ref[:, cols])
                grad = dot_t(go, down_ref[cols, :]) + dot(gid, fd_ref[:, cols])
                sig = 1.0 / (1.0 + jnp.exp(-gate))
                silu = gate * sig
                hid_s[step, :, cols] = (silu * up).astype(BF16)
                gg_s[step, :, cols] = (grad * up * sig * (1.0 + gate * (1.0 - sig))).astype(BF16)
                gu_s[step, :, cols] = (grad * silu).astype(BF16)
            gg, gu, hid = gg_s[step], gu_s[step], hid_s[step]
            for at in range(0, width, tile):
                cols = slice(at, at + tile)
                value = dot_t(gg, gate_ref[cols, :]) + dot_t(gu, up_ref[cols, :])
                out = dot(hid, down_ref[:, cols])
                if step == 0:
                    sums[:, :, cols] = value.reshape(2, 128, tile)
                    out_own[:, :, cols] = out.reshape(2, 128, tile)
                else:
                    part[step - 1, :, :, cols] = value.astype(BF16).reshape(2, 128, tile)
                    out_part[step - 1, :, :, cols] = out.astype(BF16).reshape(2, 128, tile)
            value = dot_t(gg, sg_ref[...]) + dot_t(gu, su_ref[...])
            out = dot_t(hid, fd_ref[...])
            if step == 0:
                sums[:, :, width:] = value.reshape(2, 128, SIDE)
                out_own[:, :, width:] = out.reshape(2, 128, SIDE)
            else:
                part[step - 1, :, :, width:] = value.astype(BF16).reshape(2, 128, SIDE)
                out_part[step - 1, :, :, width:] = out.astype(BF16).reshape(2, 128, SIDE)

        def send(src, dst, k, target):
            cp = _remote(src, dst, s_sem.at[k], r_sem.at[k], target)
            cp.start()
            copies.append(cp)
            return cp

        own_here()
        for cp in loads:
            cp.wait()
        work(0)
        core_here()
        forward(0)
        work(3)
        near_cp = [
            send(part.at[2], near, 0, core_peer),
            send(out_part.at[2], out_near, 1, core_peer),
        ]
        across, out_cps = [], []
        for j in range(2):
            if j:
                forward(j)
            far_here(j)
            work(1 + j)
            cp = send(part.at[j, 0], far.at[j], 2 + j, core_peer)
            out_cps.append(send(out_part.at[j, 0], out_land.at[j], 4 + j, core_peer))
            cp.wait_recv()
            staged[j] = (part[j, 1].astype(F32) + far[j].astype(F32)).astype(BF16)
            across.append(send(staged.at[j], landed.at[j], 6 + j, x_peer))
        for j in range(2):
            out_cps[j].wait_recv()
            out_far[j] = (out_part[j, 1].astype(F32) + out_land[j].astype(F32)).astype(BF16)
        for cp in near_cp:
            cp.wait_recv()
        sums[...] = sums[...] + near[...].astype(F32)
        out_own[...] = out_own[...] + out_near[...].astype(F32)
        for at in range(0, units, 512):
            cols = slice(at, at + 512)
            g = jnp.zeros((SIDE, 512), F32)
            u = jnp.zeros((SIDE, 512), F32)
            d = jnp.zeros((SIDE, 512), F32)
            for step in range(4):
                g += dot_rows(in_s[step], gg_s[step, :, cols])
                u += dot_rows(in_s[step], gu_s[step, :, cols])
                d += dot_rows(gid_s[step], hid_s[step, :, cols])
            early[:, at : at + 512] = (ADAPTER_SCALE * g[:RANK]).astype(BF16)
            early[:, units + at : units + at + 512] = (ADAPTER_SCALE * u[RANK : 2 * RANK]).astype(BF16)
            early[:, 2 * units + at : 2 * units + at + 512] = d[3 * RANK : 4 * RANK].astype(BF16)
        for j in range(2):
            across[j].wait_recv()
            total = sums[j] + landed[j].astype(F32)
            gi = total[:, width:].astype(BF16)
            small[j] = gi
            gn = (total[:, :width] + dot(gi, first_ref[...])).astype(BF16).astype(F32)
            v = resid_ref[j]
            factor = lax.rsqrt(jnp.mean(v * v, axis=1, keepdims=True) + EPSILON)
            scaled = gn * gain_ref[...]
            mean = jnp.mean(scaled * v, axis=1, keepdims=True)
            grad = go_ref[0, j].astype(F32) + factor * scaled - v * (factor * factor * factor) * mean
            grad_resid[j] = grad
            grad_low[j] = grad.astype(BF16)
        last()
        for cp in copies:
            cp.wait_send()

    vmem = pl.BlockSpec(memory_space=pltpu.VMEM)
    rows = (2, 128, wide)
    f32 = lambda *shape: jax.ShapeDtypeStruct(shape, F32)
    outs = [
        f32(2, 128, width),
        jax.ShapeDtypeStruct((2, 128, width), BF16),
        jax.ShapeDtypeStruct((2, 128, SIDE), BF16),
        f32(*rows),
        jax.ShapeDtypeStruct(rows, BF16),
        jax.ShapeDtypeStruct((4, 2, 128, width), BF16),
        jax.ShapeDtypeStruct((RANK, 3 * units), BF16),
    ]
    hbm = pl.BlockSpec(memory_space=pl.ANY)
    return pl.pallas_call(
        kernel,
        out_shape=outs,
        in_specs=[pl.BlockSpec(memory_space=pltpu.SMEM), vmem, vmem, vmem] + [hbm] * count,
        out_specs=[vmem] * len(outs),
        scratch_shapes=[pltpu.VMEM(a.shape, a.dtype) for a in loads_in]
        + [pltpu.VMEM(rows, F32)]
        + [pltpu.VMEM((4, 256, units), BF16)] * 3
        + [pltpu.VMEM((4, 256, SIDE), BF16)] * 2
        + [pltpu.VMEM((3,) + rows, BF16)] * 2
        + [pltpu.VMEM(rows, BF16)] * 6
        + [_sem(count), _sem(2), _sem(6), _sem(6), _sem(8), _sem(8)],
        compiler_params=pltpu.CompilerParams(
            collective_id=cid, has_side_effects=True, vmem_limit_bytes=58 * 1024 * 1024
        ),
        name="feed_forward",
    )(length, own, resid, gain, *loads_in)


def _back_steps(src, dst, out_s, out_r, place):
    c, f, x, core = place[:4]
    slot = _slot_of(c)
    place_in = slot % 2
    moves = []

    def first(j):
        cp = _remote(
            src.at[j],
            dst.at[place_in],
            out_s.at[j],
            out_r.at[place_in],
            (_block(x, core, j), slot // 2),
        )
        cp.start()
        moves.append(cp)

    def last():
        for half in range(2):
            pltpu.make_async_copy(dst.at[half], dst.at[half], out_r.at[half]).wait()
        for cp in moves:
            cp.wait_send()

    return first, last


def _back_sources(place):
    c, f = place[:2]
    return [(_group_of(2 * f + half), _owner(c)) for half in range(2)]


def front_call(
    tokens,
    cotangent,
    length,
    adapter,
    gains,
    wq,
    wk,
    wv,
    wo,
    tables,
    cosine,
    sine,
    cid,
):
    width = tokens.shape[-1]
    rows = cosine.shape[0]
    wide = width + SIDE
    block = 256
    scale = HEAD_DIM ** (-0.5)
    lane = PAD_HEAD
    units = tables[6].shape[-1] // 4
    quarter = width // 4
    loads_in = (gains, wq, wk, wv, wo) + tables + (cosine, sine)
    count = len(loads_in)

    def kernel(*refs):
        len_ref, adapter_ref, tok_ref, cot_ref = refs[:4]
        loads_hbm = refs[4 : 4 + count]
        (
            sums_resid,
            normed_two,
            side_all,
            tok_own,
            cot_own,
            cot_order,
            qkv_ref,
            lse_ref,
            att_ref,
            one_cut,
            inner_ref,
            wa_ref,
            ow_ref,
            sa_ref,
            fa_ref,
            fgu_ref,
            sg_ref,
            su_ref,
            fd_ref,
            sd_ref,
            fo_ref,
            so_ref,
        ) = refs[4 + count : 26 + count]
        refs = refs[26 + count :]
        gain_v, wq_v, wk_v, wv_v, wo_v = refs[:5]
        in_first, out_first, down_first, q_second, kv_second, o_second, gu_second, d_second = refs[5:13]
        cos_ref, sin_ref = refs[13:15]
        (
            tok_all,
            one_ref,
            part,
            land,
            staged,
            landed,
            sums,
            side_own,
            load_sem,
            land_s,
            land_r,
            cot_s,
            cot_r,
            send_sem,
            recv_sem,
            s_sem,
            r_sem,
        ) = refs[15:32]
        order_sems, side_sems = refs[32:35], refs[35:38]
        place = _place()
        c, f, x, core, core_peer, x_peer = place
        hh = 1 - core
        slot = _slot_of(c)
        live = len_ref[0]
        which = adapter_ref[0]
        loads = []
        for i in range(count):
            cp = pltpu.make_async_copy(loads_hbm[i], refs[i], load_sem.at[i])
            cp.start()
            loads.append(cp)

        barrier = pltpu.get_barrier_semaphore()
        for j in range(2):
            pl.semaphore_signal(
                barrier, inc=1, device_id=(_block(x, core, j), slot // 2), device_id_type=MESH_ID
            )
        for target in (core_peer, x_peer):
            pl.semaphore_signal(barrier, inc=1, device_id=target, device_id_type=MESH_ID)
        pl.semaphore_wait(barrier, 4)
        to_f = _owner(c)
        to_h = c // 4
        to_j = (c // 2) % 2
        to_i = c % 2
        moves = []
        for part_row in range(2):
            span = pl.ds(64 * part_row, 64)
            for half in range(2):
                s = 2 * f + half
                cp = _remote(
                    tok_ref.at[half, span],
                    tok_all.at[to_h, to_j, to_i, span],
                    land_s.at[2 * part_row + half],
                    land_r.at[2 * part_row + to_j],
                    (_group_of(s), to_f),
                )
                cp.start()
                moves.append(cp)
        cot_moves = []
        for half in range(2):
            s = 2 * f + half
            cot_moves.append(
                _remote(
                    cot_ref.at[half],
                    cot_own.at[to_j],
                    cot_s.at[half],
                    cot_r.at[to_j],
                    (_group_of(s), to_f),
                )
            )
        for cp in loads:
            cp.wait()

        def group_sends(part_row):
            span = pl.ds(64 * part_row, 64)
            for j in range(2):
                pltpu.make_async_copy(
                    tok_all.at[hh, j, (x + j) % 2, span],
                    tok_all.at[hh, j, (x + j) % 2, span],
                    land_r.at[2 * part_row + j],
                ).wait()
                k = 2 * part_row + j
                here = tok_all.at[hh, j, (x + j) % 2, span]
                for base, target in ((0, x_peer), (4, core_peer)):
                    cp = _remote(
                        here, here, send_sem.at[base + k], recv_sem.at[base + k], target
                    )
                    cp.start()
                    sends[base + k] = cp

        sends = {}

        def prepare_first():
            half = HEAD_DIM // 2
            wa_ref[...] = jnp.zeros_like(wa_ref)
            sa_ref[...] = jnp.zeros_like(sa_ref)
            for head in range(4):
                for side in range(2):
                    at = head * HEAD_DIM + side * half
                    to = head * lane + side * HALF_PAD
                    wa_ref[:, to : to + half] = wq_v[:, at : at + half]
            for head in range(2):
                for side in range(2):
                    at = head * HEAD_DIM + side * half
                    to = (4 + head) * lane + side * HALF_PAD
                    wa_ref[:, to : to + half] = wk_v[:, at : at + half]
                at, to = head * HEAD_DIM, (6 + head) * lane
                wa_ref[:, to : to + HEAD_DIM] = wv_v[:, at : at + HEAD_DIM]

        def prepare_second():
            half = HEAD_DIM // 2
            own_cols = pl.ds(pl.multiple_of(f * quarter, 128), quarter)
            own_units = pl.ds(pl.multiple_of(f * units, 128), units)
            low = lambda v: (ADAPTER_SCALE * v.astype(F32)).astype(BF16)
            for ref in (fa_ref, fgu_ref, sg_ref, su_ref, fd_ref, sd_ref, fo_ref, so_ref, ow_ref):
                ref[...] = jnp.zeros_like(ref)
            for i in range(3):
                fa_ref[i * RANK : (i + 1) * RANK, :] = in_first[which, i]
            for i in range(2):
                fgu_ref[i * RANK : (i + 1) * RANK, :] = in_first[which, 3 + i]
            all_gu = gu_second.at[:, :, :, own_units]
            sg_ref[:RANK, :] = low(all_gu[which, 0])
            su_ref[RANK : 2 * RANK, :] = low(all_gu[which, 1])
            fd_ref[3 * RANK : 4 * RANK, :] = down_first.at[:, :, own_units][which]
            sd_ref[3 * RANK : 4 * RANK, :] = low(d_second[which])
            so_ref[:RANK, :] = low(o_second[which])
            own_first = out_first.at[:, :, own_cols][which]
            own_q = low(q_second.at[:, :, own_cols][which])
            for head in range(4):
                at = head * HEAD_DIM
                fo_ref[:RANK, head * lane : head * lane + HEAD_DIM] = own_first[:, at : at + HEAD_DIM]
                ow_ref[head * lane : head * lane + HEAD_DIM, :] = wo_v[at : at + HEAD_DIM, :]
                for side in range(2):
                    to = head * lane + side * HALF_PAD
                    sa_ref[:RANK, to : to + half] = own_q[:, at + side * half : at + (side + 1) * half]
            for i in range(2):
                own_kv = low(kv_second[which, i])
                for head in range(2):
                    at = head * HEAD_DIM
                    if i:
                        to = (6 + head) * lane
                        sa_ref[2 * RANK : 3 * RANK, to : to + HEAD_DIM] = own_kv[:, at : at + HEAD_DIM]
                    else:
                        for side in range(2):
                            to = (4 + head) * lane + side * HALF_PAD
                            sa_ref[RANK : 2 * RANK, to : to + half] = own_kv[
                                :, at + side * half : at + (side + 1) * half
                            ]

        prepare_first()
        group_sends(0)
        prepare_second()
        group_sends(1)
        for cp in cot_moves:
            cp.start()

        def forward(j):
            for part_row in range(2):
                k = 2 * part_row + j
                span = pl.ds(64 * part_row, 64)
                sends[k].wait_recv()
                there = tok_all.at[hh, j, (x + j + 1) % 2, span]
                cp = _remote(there, there, send_sem.at[8 + k], recv_sem.at[8 + k], core_peer)
                cp.start()
                sends[8 + k] = cp
            for part_row in range(2):
                k = 2 * part_row + j
                sends[4 + k].wait_recv()
                sends[8 + k].wait_recv()

        def project_rows(t):
            row = pl.ds(t * block, block)
            v = tok_all[t // 2, t % 2].reshape(block, width).astype(F32)
            factor = lax.rsqrt(jnp.mean(v * v, axis=1, keepdims=True) + EPSILON)
            u = (v * factor * gain_v[0:1, :]).astype(BF16)
            one_ref[row, :] = u
            inner = dot_t(u, fa_ref[...]).astype(BF16)
            inner_ref[row, :] = inner
            cos, sin = cos_ref[row, :], sin_ref[row, :]
            for pair in range(4):
                cols = slice(pair * 2 * lane, (pair + 1) * 2 * lane)
                both = dot(u, wa_ref[:, cols]) + dot(inner, sa_ref[:, cols])
                for k in range(2):
                    p = both[:, k * lane : (k + 1) * lane]
                    if pair < 3:
                        p = p * cos + pltpu.roll(p, HALF_PAD, 1) * sin
                    qkv_ref[row, (2 * pair + k) * lane : (2 * pair + k + 1) * lane] = p.astype(BF16)

        def attention(t, hook):
            keys = (t + 1) * block
            row = pl.ds(t * block, block)
            qpos = t * block + lax.broadcasted_iota(jnp.int32, (block, keys), 0)
            kpos = lax.broadcasted_iota(jnp.int32, (block, keys), 1)
            allowed = (kpos <= qpos) & (kpos < live)
            stats = jnp.zeros((block, lane), F32)
            lanes = lax.broadcasted_iota(jnp.int32, (block, lane), 1)
            for head in range(4):
                q = qkv_ref[row, head * lane : (head + 1) * lane]
                kv = head // 2
                k = qkv_ref[:keys, (4 + kv) * lane : (5 + kv) * lane]
                v = qkv_ref[:keys, (6 + kv) * lane : (7 + kv) * lane]
                s = jnp.where(allowed, dot_t(q, k) * scale, NEGATIVE)
                top = jnp.max(s, axis=1, keepdims=True)
                p = jnp.where(allowed, jnp.exp(s - top), 0.0)
                total = jnp.sum(p, axis=1, keepdims=True)
                o = dot(p.astype(BF16), v) / total
                att_ref[row, head * lane : (head + 1) * lane] = o.astype(BF16)
                stats = jnp.where(lanes == head, top + jnp.log(total), stats)
                if head == 1 and hook is not None:
                    hook()
            lse_ref[row, :] = stats
            a = att_ref[row, :]
            for at in range(0, width, 256):
                value = dot(a, ow_ref[:, at : at + 256])
                part[t, :, :, at : at + 256] = value.astype(BF16).reshape(2, 128, 256)
            part[t, :, :, width:] = dot_t(a, fo_ref[...]).astype(BF16).reshape(2, 128, SIDE)

        def to_core(t):
            return _remote(part.at[t], land.at[t % 2], s_sem.at[t % 2], r_sem.at[t % 2], core_peer)

        def to_x(j):
            return _remote(staged.at[j], landed.at[j], s_sem.at[2 + j], r_sem.at[2 + j], x_peer)

        def leave(t):
            @pl.when(core == t // 2)
            def _():
                to_core(t).start()

        def combine(t):
            j = t % 2

            @pl.when(core == 1 - t // 2)
            def _():
                to_core(t).wait_recv()
                mine, other = (x + j) % 2, (x + j + 1) % 2
                staged[j] = (part[t, other].astype(F32) + land[j, other].astype(F32)).astype(BF16)
                to_x(j).start()
                sums[j] = part[t, mine].astype(F32) + land[j, mine].astype(F32)

        forward(0)
        project_rows(0)
        project_rows(2)
        attention(0, None)
        leave(0)
        forward(1)
        for half in range(2):
            pltpu.make_async_copy(cot_own.at[half], cot_own.at[half], cot_r.at[half]).wait()
        c_first, c_forward, c_own, c_core, c_far, c_last = _order_steps(
            cot_own, cot_order, *order_sems, place
        )
        c_first()
        project_rows(1)
        project_rows(3)
        attention(1, lambda: combine(0))
        leave(1)
        attention(2, lambda: combine(1))
        leave(2)
        c_own()
        c_core()
        c_forward(0)
        attention(3, lambda: combine(2))
        leave(3)
        combine(3)
        for t in range(4):

            @pl.when(core == t // 2)
            def _():
                to_core(t).wait_send()

        for j in range(2):
            tok_own[j] = tok_all[hh, j, (x + j) % 2]
        one_cut[...] = one_ref[:, pl.ds(pl.multiple_of(f * quarter, 128), quarter)]
        for j in range(2):
            cp = to_x(j)
            cp.wait_recv()
            sums[j] = sums[j] + landed[j].astype(F32)
            cp.wait_send()
            side_own[j] = sums[j, :, width:].astype(BF16)
        side_first, side_last = _gather_steps([side_own], [side_all], *side_sems, place)
        side_first()
        for j in range(2):
            v = (
                tok_own[j].astype(F32)
                + sums[j, :, :width]
                + dot(side_own[j], so_ref[...])
            )
            sums_resid[j] = v
            factor = lax.rsqrt(jnp.mean(v * v, axis=1, keepdims=True) + EPSILON)
            normed_two[j] = (v * factor * gain_v[1:2, :]).astype(BF16)
        c_forward(1)
        for j in range(2):
            c_far(j)
        c_last()
        side_last()
        for cp in moves + cot_moves + list(sends.values()):
            cp.wait_send()

    vmem, hbm = pl.BlockSpec(memory_space=pltpu.VMEM), pl.BlockSpec(memory_space=pl.ANY)
    smem = pl.BlockSpec(memory_space=pltpu.SMEM)
    low = lambda *shape: jax.ShapeDtypeStruct(shape, BF16)
    outs = [
        (jax.ShapeDtypeStruct((2, 128, width), F32), vmem),
        (low(2, 128, width), vmem),
        (low(2, 2, 2, 128, SIDE), hbm),
        (low(2, 128, width), vmem),
        (low(2, 128, width), hbm),
        (low(4, 2, 128, width), hbm),
        (low(rows, 8 * lane), vmem),
        (jax.ShapeDtypeStruct((rows, lane), F32), vmem),
        (low(rows, 4 * lane), vmem),
        (low(rows, quarter), vmem),
        (low(rows, SIDE), vmem),
        (low(width, 8 * lane), vmem),
        (low(4 * lane, width), vmem),
        (low(SIDE, 8 * lane), vmem),
        (low(SIDE, width), vmem),
        (low(SIDE, width), vmem),
        (low(SIDE, units), vmem),
        (low(SIDE, units), vmem),
        (low(SIDE, units), vmem),
        (low(SIDE, width), vmem),
        (low(SIDE, 4 * lane), vmem),
        (low(SIDE, width), vmem),
    ]
    own = (2, 128, wide)
    return pl.pallas_call(
        kernel,
        out_shape=[o[0] for o in outs],
        in_specs=[smem, smem] + [hbm] * (2 + count),
        out_specs=[o[1] for o in outs],
        scratch_shapes=[pltpu.VMEM(a.shape, a.dtype) for a in loads_in]
        + [
            pltpu.VMEM((2, 2, 2, 128, width), BF16),
            pltpu.VMEM((rows, width), BF16),
            pltpu.VMEM((4,) + own, BF16),
            pltpu.VMEM((2,) + own, BF16),
            pltpu.VMEM(own, BF16),
            pltpu.VMEM(own, BF16),
            pltpu.VMEM(own, F32),
            pltpu.VMEM((2, 128, SIDE), BF16),
            _sem(count),
            _sem(4),
            _sem(4),
            _sem(2),
            _sem(2),
            _sem(12),
            _sem(12),
            _sem(4),
            _sem(4),
        ]
        + [_sem(2), _sem(6), _sem(6)] * 2,
        compiler_params=pltpu.CompilerParams(
            collective_id=cid, has_side_effects=True, vmem_limit_bytes=58 * 1024 * 1024
        ),
        name="front",
    )(length, adapter, tokens, cotangent, *loads_in)


def attend_back_call(
    low_own,
    small_own,
    early,
    out_far,
    length,
    own_arrays,
    arrays,
    cid,
):
    (qkv, stats, att, inner_o, order, cosine, sine, out_w, first_o, second_o, weight_all) = arrays[:11]
    width = low_own.shape[-1]
    rows = qkv.shape[0]
    wide = width + SIDE
    step_rows = 256
    scale = HEAD_DIM ** (-0.5)
    lane = PAD_HEAD
    quarter = width // 4
    middle_n = 4 * quarter
    early_n = early.shape[1]
    big = tuple(arrays) + tuple(own_arrays)
    late_n = 6 * quarter
    count = len(big)

    def kernel(*refs):
        len_ref, low_ref, small_ref, early_ref, out_ref = refs[:5]
        big_in = refs[5 : 5 + count]
        (
            out_back,
            grad_back,
            early_out,
            middle_out,
            late_out,
            early_lines,
            middle_lines,
            late_lines,
        ) = refs[5 + count : 13 + count]
        refs = refs[13 + count :]
        (
            qkv_ref,
            lse_ref,
            att_ref,
            inner_ref,
            order_ref,
            cos_ref,
            sin_ref,
            ow_ref,
            fo_ref,
            so_ref,
            wa_ref,
            sa_ref,
            fa_ref,
            sd_ref,
            cut_ref,
            inner_qkv_ref,
            cot_ref,
            out_own,
            resid_ref,
            tok_ref,
            grad_resid_ref,
            gain_ref,
        ) = refs[:count]
        (
            low,
            do_ref,
            gio_ref,
            dk_ref,
            dv_ref,
            part,
            land,
            staged,
            landed,
            side_own,
            middle_ref,
            sums,
            side_all,
            grad_ref,
            landed_out,
            small_out,
            late_ref,
            out_tok,
            grad_tok,
            load_sem,
            own_sem,
            send_sem,
            recv_sem,
            s_sem,
            r_sem,
        ) = refs[count : count + 25]
        sems = refs[count + 25 :]
        place = _place()
        c, f, x, core, core_peer, x_peer = place
        loads = [
            pltpu.make_async_copy(big_in[i], refs[i], load_sem.at[i]) for i in range(count)
        ]
        for cp in loads:
            cp.start()
        _greet(
            _back_sources(place) + [core_peer, x_peer, _y_peer(place)] + _z_peers(place)
        )
        small_first, small_forward, small_own_here, small_core, small_far, small_last = _order_steps(
            small_ref, small_out, *sems[0:3], place
        )
        early_start, early_across, early_finish = _ctx_first(early_ref, early_lines, *sems[3:6], place)
        early_two = _ctx_second(early_lines, early_out, *sems[6:9], place)
        mid_start, mid_across, mid_finish = _ctx_first(middle_ref, middle_lines, *sems[9:12], place)
        mid_two = _ctx_second(middle_lines, middle_out, *sems[12:15], place)
        late_one = _ctx_first(late_ref, late_lines, *sems[15:18], place)
        late_two = _ctx_second(late_lines, late_out, *sems[18:21], place)
        side_first, side_last = _gather_steps([side_own], [side_all], *sems[21:24], place)
        out_first, out_last = _back_steps(out_tok, out_back, *sems[24:26], place)
        grad_first, grad_last = _back_steps(grad_tok, grad_back, *sems[26:28], place)
        live = len_ref[0]

        sends = {}
        hh = 1 - core
        local = []
        small_first()
        early_start()
        for k, target in ((0, x_peer), (2, core_peer)):
            for j in (1, 0):
                cp = _remote(
                    low_ref.at[j],
                    low.at[hh, j, (x + j) % 2],
                    send_sem.at[k + j],
                    recv_sem.at[k + j],
                    target,
                )
                cp.start()
                sends[(k, j)] = cp
        for j in range(2):
            lc = pltpu.make_async_copy(low_ref.at[j], low.at[hh, j, (x + j) % 2], own_sem.at[j])
            lc.start()
            local.append(lc)
        swaps = [
            _remote(out_ref.at[j], landed_out.at[j], s_sem.at[8 + j], r_sem.at[8 + j], x_peer)
            for j in range(2)
        ]
        dk_ref[...] = jnp.zeros_like(dk_ref)
        dv_ref[...] = jnp.zeros_like(dv_ref)
        early_across()
        small_own_here()
        for j in range(2):
            small_forward(j)
        for cp in loads:
            cp.wait()
        for lc in local:
            lc.wait()

        def arrive(j):
            sends[(0, j)].wait_recv()
            cp = _remote(
                low.at[hh, j, (x + j + 1) % 2],
                low.at[hh, j, (x + j + 1) % 2],
                send_sem.at[4 + j],
                recv_sem.at[4 + j],
                core_peer,
            )
            cp.start()
            sends[(4, j)] = cp
            sends[(2, j)].wait_recv()
            cp.wait_recv()

        def through_output(t):
            g = low[t // 2, t % 2].reshape(step_rows, width)
            gio = dot_t(g, so_ref[...]).astype(BF16)
            row = pl.ds(t * step_rows, step_rows)
            gio_ref[row, :] = gio
            do_ref[row, :] = (dot_t(g, ow_ref[...]) + dot(gio, fo_ref[...])).astype(BF16)

        def attention(t, hook):
            keys = (t + 1) * step_rows
            row = pl.ds(t * step_rows, step_rows)
            qpos = t * step_rows + lax.broadcasted_iota(jnp.int32, (step_rows, keys), 0)
            kpos = lax.broadcasted_iota(jnp.int32, (step_rows, keys), 1)
            allowed = (kpos <= qpos) & (kpos < live)
            cos, sin = cos_ref[row, :], sin_ref[row, :]
            for head in range(4):
                kv = head // 2
                at = slice(head * lane, (head + 1) * lane)
                q = qkv_ref[row, at]
                k = qkv_ref[:keys, (4 + kv) * lane : (5 + kv) * lane]
                v = qkv_ref[:keys, (6 + kv) * lane : (7 + kv) * lane]
                do = do_ref[row, at]
                s = dot_t(q, k)
                p = jnp.where(allowed, jnp.exp(s * scale - lse_ref[row, head : head + 1]), 0.0)
                dp = dot_t(do, v)
                total = jnp.sum(p * dp, axis=1, keepdims=True)
                ds = (p * (dp - total)).astype(BF16)
                dq = scale * dot(ds, k)
                dq = dq * cos - pltpu.roll(dq, HALF_PAD, 1) * sin
                grad_ref[row, at] = dq.astype(BF16)
                dk_ref[kv, :keys] += dot_rows(ds, q)
                dv_ref[kv, :keys] += dot_rows(p.astype(BF16), do)
                if head == 1 and hook is not None:
                    hook()
            for kv in range(2):
                dk = scale * dk_ref[kv, row, :]
                dk = dk * cos - pltpu.roll(dk, HALF_PAD, 1) * sin
                grad_ref[row, (4 + kv) * lane : (5 + kv) * lane] = dk.astype(BF16)
                grad_ref[row, (6 + kv) * lane : (7 + kv) * lane] = dv_ref[kv, row, :].astype(BF16)
            g = grad_ref[row, :]
            for at in range(0, width, 256):
                value = dot_t(g, wa_ref[at : at + 256, :])
                part[t, :, :, at : at + 256] = value.astype(BF16).reshape(2, 128, 256)
            part[t, :, :, width:] = dot_t(g, sa_ref[...]).astype(BF16).reshape(2, 128, SIDE)

        def to_core(t):
            h, j = t // 2, t % 2
            return _remote(part.at[t], land.at[j], s_sem.at[j], r_sem.at[j], core_peer)

        def to_x(j):
            return _remote(staged.at[j], landed.at[j], s_sem.at[2 + j], r_sem.at[2 + j], x_peer)

        def leave(t):
            @pl.when(core == t // 2)
            def _():
                to_core(t).start()

        def combine(t):
            j = t % 2

            @pl.when(core == 1 - t // 2)
            def _():
                to_core(t).wait_recv()
                mine, other = (x + j) % 2, (x + j + 1) % 2
                staged[j] = (part[t, other].astype(F32) + land[j, other].astype(F32)).astype(BF16)
                to_x(j).start()
                sums[j] = part[t, mine].astype(F32) + land[j, mine].astype(F32)

        arrive(1)
        through_output(3)
        through_output(1)
        for cp in swaps:
            cp.start()
        attention(3, None)
        leave(3)
        arrive(0)
        through_output(2)
        through_output(0)
        o_a = dot_rows(gio_ref[...], att_ref[...])[:RANK]
        o_a = jnp.concatenate(
            [o_a[:, head * lane : head * lane + HEAD_DIM] for head in range(4)], axis=1
        )
        middle_ref[:, :quarter] = o_a.astype(BF16)
        own_cols = pl.ds(pl.multiple_of(f * quarter, 128), quarter)
        g = low[:, :, :, :, own_cols].reshape(rows, quarter)
        middle_ref[:, quarter : 2 * quarter] = (ADAPTER_SCALE * dot_rows(inner_ref[...], g)[:RANK]).astype(BF16)
        for j in range(2):
            small_far(j)
        small_core()
        in_gu = jnp.zeros((SIDE, quarter), F32)
        for k in range(4):
            u = order_ref[k, :, :, own_cols].reshape(step_rows, quarter)
            in_gu += dot_rows(small_out[k].reshape(step_rows, SIDE), u)
        middle_ref[:, 2 * quarter : 3 * quarter] = in_gu[:RANK].astype(BF16)
        middle_ref[:, 3 * quarter :] = in_gu[RANK : 2 * RANK].astype(BF16)
        mid_start()
        early_finish()
        early_two[0]()
        mid_across()
        def outputs():
            for j in range(2):
                swaps[j].wait()
                total = out_own[j] + landed_out[j].astype(F32)
                side = total[:, width:]
                out_own[j, :, width:] = side
                pos = 128 * _block(x, core, j) + lax.broadcasted_iota(jnp.int32, (128, width), 0)
                value = resid_ref[j] + total[:, :width] + dot(side.astype(BF16), sd_ref[...])
                out_tok[j] = jnp.where(pos < live, value, 0.0).astype(BF16)
                out_first(j)

        attention(2, lambda: combine(3))
        leave(2)
        mid_finish()
        attention(1, lambda: combine(2))
        leave(1)
        early_two[1]()
        mid_two[0]()
        outputs()
        attention(0, lambda: combine(1))
        leave(0)
        combine(0)
        all_b = ADAPTER_SCALE * dot_rows(inner_qkv_ref[...], grad_ref[...])
        half = HEAD_DIM // 2
        pieces = []
        for head in range(6):
            r = slice(0, RANK) if head < 4 else slice(RANK, 2 * RANK)
            for side in range(2):
                to = head * lane + side * HALF_PAD
                pieces.append(all_b[r, to : to + half])
        for head in range(2):
            to = (6 + head) * lane
            pieces.append(all_b[2 * RANK : 3 * RANK, to : to + HEAD_DIM])
        late_ref[:, 3 * quarter : 5 * quarter] = jnp.concatenate(pieces, axis=1).astype(BF16)
        for t in range(4):

            @pl.when(core == t // 2)
            def _():
                to_core(t).wait_send()

        for j in range(2):
            cp = to_x(j)
            cp.wait_recv()
            sums[j] = sums[j] + landed[j].astype(F32)
            cp.wait_send()
            side_own[j] = (sums[j, :, width:] + out_own[j, :, width:]).astype(BF16)
        side_first()
        for j in range(2):
            gi = sums[j, :, width:].astype(BF16)
            gn = (sums[j, :, :width] + dot(gi, fa_ref[...])).astype(BF16).astype(F32)
            v = tok_ref[j].astype(F32)
            factor = lax.rsqrt(jnp.mean(v * v, axis=1, keepdims=True) + EPSILON)
            scaled = gn * gain_ref[...]
            mean = jnp.mean(scaled * v, axis=1, keepdims=True)
            grad = grad_resid_ref[j] + factor * scaled - v * (factor * factor * factor) * mean
            grad_tok[j] = grad.astype(BF16)
            if j == 0:
                side_last()
                in_qkv = dot_rows(side_all[...].reshape(rows, SIDE), cut_ref[...])
                for i in range(3):
                    late_ref[:, i * quarter : (i + 1) * quarter] = in_qkv[
                        i * RANK : (i + 1) * RANK
                    ].astype(BF16)
                d_b = jnp.zeros((SIDE, quarter), F32)
                for step in range(4):
                    other_x = x if step in (0, 3) else 1 - x
                    for i in range(2):
                        other_core = (core, 1 - core)[step == 3 or (step in (1, 2) and i == 0)]
                        jj = i if step in (0, 3) else step - 1
                        pos = 128 * _block(other_x, other_core, jj) + lax.broadcasted_iota(
                            jnp.int32, (128, quarter), 0
                        )
                        go = cot_ref[step, i, :, own_cols].astype(F32)
                        go = jnp.where(pos < live, go, 0.0).astype(BF16)
                        d_b += dot_rows(side_all[1 - other_core, jj, (other_x + jj) % 2], go)
                d_b = ADAPTER_SCALE * d_b[3 * RANK : 4 * RANK]
                late_ref[:, 5 * quarter :] = d_b.astype(BF16)
                late_one[0]()
            grad_first(j)
        late_one[1]()
        mid_two[1]()
        late_one[2]()
        late_two[0]()
        small_last()
        early_two[2]()
        mid_two[2]()
        late_two[1]()
        late_two[2]()
        out_last()
        grad_last()
        for cp in sends.values():
            cp.wait_send()

    vmem, hbm = pl.BlockSpec(memory_space=pltpu.VMEM), pl.BlockSpec(memory_space=pl.ANY)
    shape = jax.ShapeDtypeStruct
    own = (2, 128, wide)
    return pl.pallas_call(
        kernel,
        out_shape=[
            shape((2, 128, width), BF16),
            shape((2, 128, width), BF16),
            _spread_of(early_n),
            _spread_of(middle_n),
            _spread_of(late_n),
            shape(_lines_of(early_n), BF16),
            shape(_lines_of(middle_n), BF16),
            shape(_lines_of(late_n), BF16),
        ],
        in_specs=[pl.BlockSpec(memory_space=pltpu.SMEM)] + [hbm] * (4 + count),
        out_specs=[hbm] * 8,
        scratch_shapes=[pltpu.VMEM(a.shape, a.dtype) for a in big]
        + [
            pltpu.VMEM((2, 2, 2, 128, width), BF16),
            pltpu.VMEM((rows, 4 * lane), BF16),
            pltpu.VMEM((rows, SIDE), BF16),
            pltpu.VMEM((2, rows, lane), F32),
            pltpu.VMEM((2, rows, lane), F32),
            pltpu.VMEM((4,) + own, BF16),
            pltpu.VMEM((2,) + own, BF16),
            pltpu.VMEM(own, BF16),
            pltpu.VMEM(own, BF16),
            pltpu.VMEM((2, 128, SIDE), BF16),
            pltpu.VMEM((RANK, middle_n), BF16),
            pltpu.VMEM(own, F32),
            pltpu.VMEM((2, 2, 2, 128, SIDE), BF16),
            pltpu.VMEM((rows, 8 * lane), BF16),
            pltpu.VMEM(own, BF16),
            pltpu.VMEM((4, 2, 128, SIDE), BF16),
            pltpu.VMEM((RANK, late_n), BF16),
            pltpu.VMEM((2, 128, width), BF16),
            pltpu.VMEM((2, 128, width), BF16),
            _sem(count),
            _sem(2),
            _sem(6),
            _sem(6),
            _sem(10),
            _sem(10),
        ]
        + [_sem(2), _sem(6), _sem(6)]
        + FIRST_SEMS
        + SECOND_SEMS
        + FIRST_SEMS
        + SECOND_SEMS
        + FIRST_SEMS
        + SECOND_SEMS
        + [_sem(2), _sem(6), _sem(6)]
        + [_sem(2), _sem(2), _sem(2), _sem(2)],
        compiler_params=pltpu.CompilerParams(
            collective_id=cid, has_side_effects=True, vmem_limit_bytes=62 * 1024 * 1024
        ),
        name="attend_back",
    )(length, low_own, small_own, early, out_far, *big)


def table_call(early, middle, late, adapters):
    f32 = lambda *shape: jax.ShapeDtypeStruct(shape, F32)
    choices = 8
    outs = [
        f32(choices, 5, RANK, 1536),
        f32(choices, RANK, 1536),
        f32(choices, RANK, 4096),
        f32(choices, RANK, 1536),
        f32(choices, 2, RANK, 768),
        f32(choices, RANK, 1536),
        f32(choices, 2, RANK, 4096),
        f32(choices, RANK, 1536),
    ]
    plan = (
        ((6, 0, 1024), (6, 1, 1024), (2, None, 1024)),
        ((1, None, 384), (5, None, 384), (0, 3, 384), (0, 4, 384)),
        (
            (0, 0, 384),
            (0, 1, 384),
            (0, 2, 384),
            (3, None, 384),
            (4, 0, 192),
            (4, 1, 192),
            (7, None, 384),
        ),
    )

    def kernel(which, early_ref, middle_ref, late_ref, *refs):
        outs, acc, sems = refs[:8], refs[8:16], refs[16]

        def add(piece, ref):
            def one_slot(origin, carry):
                row = which[origin % 4 + 4 * ((origin // 4 + origin) % 2)]
                for f in range(4):
                    at = 0
                    for out, table, n in plan[piece]:
                        value = ref[origin // 4, f % 2, origin % 4, f // 2, :, at : at + n].astype(F32)
                        cols = slice(f * n, (f + 1) * n)
                        if table is None:
                            acc[out][row, :, cols] += value
                        else:
                            acc[out][row, table, :, cols] += value
                        at += n
                return carry

            lax.fori_loop(0, 8, one_slot, 0)

        def send(out):
            cp = pltpu.make_async_copy(acc[out], outs[out], sems.at[out])
            cp.start()
            return cp

        for out in (2, 6):
            acc[out][...] = jnp.zeros_like(acc[out])
        add(0, early_ref)
        copies = [send(out) for out in (2, 6)]
        for out in (0, 1, 3, 4, 5, 7):
            acc[out][...] = jnp.zeros_like(acc[out])
        add(1, middle_ref)
        copies += [send(out) for out in (1, 5)]
        add(2, late_ref)
        copies += [send(out) for out in (0, 3, 4, 7)]
        for cp in copies:
            cp.wait()

    vmem, hbm = pl.BlockSpec(memory_space=pltpu.VMEM), pl.BlockSpec(memory_space=pl.ANY)
    return pl.pallas_call(
        kernel,
        out_shape=outs,
        in_specs=[pl.BlockSpec(memory_space=pltpu.SMEM), vmem, vmem, vmem],
        out_specs=[hbm] * 8,
        scratch_shapes=[pltpu.VMEM(o.shape, F32) for o in outs] + [_sem(8)],
        compiler_params=pltpu.CompilerParams(vmem_limit_bytes=40 * 1024 * 1024),
        name="tables",
    )(adapters, early, middle, late)


def rope_constants(rows):
    half = HEAD_DIM // 2
    freqs = np.float32(ROPE_BASE) ** (-(np.arange(half, dtype=np.float32) * 2.0 / HEAD_DIM))
    angles = np.arange(rows).astype(np.float32)[:, None] * freqs.astype(np.float32)[None, :]
    cos = np.cos(angles.astype(np.float64)).astype(np.float32)
    sin = np.sin(angles.astype(np.float64)).astype(np.float32)
    gap = np.zeros((rows, HALF_PAD - half), np.float32)
    cosine = np.concatenate([cos, gap, cos, gap], axis=1)
    sine = np.concatenate([-sin, gap, sin, gap], axis=1)
    return jnp.asarray(cosine), jnp.asarray(sine)


def dot(left, right):
    return jnp.dot(left, right, preferred_element_type=F32)


def dot_t(left, right):
    return lax.dot_general(left, right, (((1,), (1,)), ((), ())), preferred_element_type=F32)


def dot_rows(left, right):
    return lax.dot_general(left, right, (((0,), (0,)), ((), ())), preferred_element_type=F32)


def side_pad(value, before=0):
    return jnp.pad(value, ((0, 0), (before, SIDE - before - value.shape[1])))


def blocks(value):
    return value.reshape(2, 2, 2, 128, value.shape[-1])


def own_blocks(value):
    return value.reshape(2, 128, value.shape[-1])


def flat(value):
    return value.reshape(-1, value.shape[-1])


def slot_local(
    tokens,
    cotangent,
    lengths,
    slot_adapter_index,
    attention_norm_gain,
    feedforward_norm_gain,
    query_weight,
    key_weight,
    value_weight,
    output_weight,
    gate_weight,
    up_weight,
    down_weight,
    adapter_input_first,
    adapter_output_first,
    adapter_down_first,
    adapter_query_second,
    adapter_key_value_second,
    adapter_output_second,
    adapter_gate_up_second,
    adapter_down_second,
):
    width = tokens.shape[-1]
    quarter = width // 4
    c = lax.axis_index("ctx")
    f = lax.axis_index("fsdp")
    slot = _slot_of(c)
    length = lax.dynamic_slice_in_dim(lengths, slot, 1, 0)
    adapter = slot_adapter_index[slot]

    def cut(value, axis, size):
        return lax.dynamic_slice_in_dim(value, f * size, size, axis)

    rows = 4 * 2 * tokens.shape[1]
    cosine, sine = rope_constants(rows)
    turned = lambda t: jnp.swapaxes(t, -1, -2)
    second_kv = adapter_key_value_second
    second_kv = lax.dynamic_slice_in_dim(second_kv, f * key_weight.shape[1], key_weight.shape[1], 3)
    (
        resid,
        normed_two_own,
        inner_o,
        tok_own,
        cot_own,
        cot_order,
        qkv,
        stats,
        attn_b,
        one_cut,
        inner_qkv,
        weight_all,
        out_w,
        second_all,
        first_all,
        first_gu,
        second_g,
        second_u,
        first_d,
        second_d,
        first_o,
        second_o,
    ) = front_call(
        tokens,
        cotangent,
        length,
        adapter.reshape(1),
        jnp.stack([attention_norm_gain, feedforward_norm_gain]),
        query_weight,
        key_weight,
        value_weight,
        output_weight,
        (
            turned(adapter_input_first),
            turned(adapter_output_first),
            turned(adapter_down_first),
            adapter_query_second,
            second_kv,
            adapter_output_second,
            adapter_gate_up_second,
            adapter_down_second,
        ),
        cosine,
        sine,
        0,
    )
    grad_resid, grad_low_own, small, out_sums, out_far, order, early = feed_forward(
        normed_two_own,
        cot_order,
        resid,
        feedforward_norm_gain[None, :],
        length,
        (gate_weight, up_weight, down_weight),
        (first_gu, second_g, second_u, first_d, second_d),
        3,
    )
    out_tokens, grad_tokens, early, middle, late = attend_back_call(
        grad_low_own,
        small,
        early,
        out_far,
        length,
        (out_sums, resid, tok_own, grad_resid, attention_norm_gain[None, :]),
        (
            qkv,
            stats,
            attn_b,
            flat(inner_o),
            order,
            cosine,
            sine,
            out_w,
            first_o,
            second_o,
            weight_all,
            second_all,
            first_all,
            second_d,
            one_cut,
            inner_qkv,
            cot_order,
        ),
        10,
    )[:5]
    full = table_call(early, middle, late, slot_adapter_index)
    turn = lambda t: jnp.swapaxes(t, -1, -2)
    return (
        out_tokens,
        grad_tokens.astype(F32),
        turn(full[0]),
        turn(full[1]),
        turn(full[2]),
        full[3],
        full[4],
        full[5],
        full[6],
        full[7],
    )


def solution(mesh):
    one_slot = mesh.shape["ctx"] == 8 and mesh.shape["fsdp"] == 4
    return jax.shard_map(
        slot_local if one_slot else local,
        mesh=mesh,
        in_specs=(
            P("fsdp", "ctx", None),
            P("fsdp", "ctx", None),
            P(),
            P(),
            P(),
            P(),
            P(None, "fsdp"),
            P(None, "fsdp"),
            P(None, "fsdp"),
            P("fsdp", None),
            P(None, "fsdp"),
            P(None, "fsdp"),
            P("fsdp", None),
            P(),
            P(),
            P(),
            P(),
            P(),
            P(),
            P(),
            P(),
        ),
        out_specs=(
            P("fsdp", "ctx", None),
            P("fsdp", "ctx", None),
            P(),
            P(),
            P(),
            P(),
            P(),
            P(),
            P(),
            P(),
        ),
        check_vma=False,
    )
```

```python
import math

import jax
import jax.numpy as jnp
import numpy as np
from jax import lax
from jax.experimental import pallas as pl
from jax.experimental.pallas import tpu as pltpu
from jax.sharding import PartitionSpec as P

QUERY_HEADS = 16
KEY_VALUE_HEADS = 8
HEAD_DIM = 96


EPSILON = 1e-05
NEGATIVE = -1e30
ADAPTER_SCALE = 0.5
ROPE_BASE = 100000.0


def from_behind(x, axis, by):
    size = lax.axis_size(axis)
    return lax.ppermute(x, axis, [(i, (i + by) % size) for i in range(size)])


def rope_tables(positions, head_size):
    half_size = head_size // 2
    freqs = ROPE_BASE ** (-(jnp.arange(half_size, dtype=jnp.float32) * 2.0 / head_size))
    angles = positions.astype(jnp.float32)[:, None] * freqs[None, :]
    return (jnp.cos(angles)[:, None, :], jnp.sin(angles)[:, None, :])


def apply_rotation(values, cosine_table, sine_table):
    half_size = values.shape[-1] // 2
    first_half = values[..., :half_size]
    second_half = values[..., half_size:]
    return jnp.concatenate(
        [
            first_half * cosine_table - second_half * sine_table,
            second_half * cosine_table + first_half * sine_table,
        ],
        axis=-1,
    )


def rotate_back(gradient_tree, cosine_table, sine_table):
    half_size = gradient_tree.shape[-1] // 2
    first_half = gradient_tree[..., :half_size]
    second_half = gradient_tree[..., half_size:]
    return jnp.concatenate(
        [
            first_half * cosine_table + second_half * sine_table,
            second_half * cosine_table - first_half * sine_table,
        ],
        axis=-1,
    )


def rms_factor(values):
    return lax.rsqrt(jnp.mean(values * values, axis=-1, keepdims=True) + EPSILON)


def norm_back(values, factor, gain, grad_norm):
    scaled = grad_norm * gain
    return factor * scaled - values * factor**3 * jnp.mean(scaled * values, axis=-1, keepdims=True)


def pick_rows(onehot, table):
    return jnp.einsum("sa,a...->s...", onehot, table, preferred_element_type=jnp.float32).astype(
        jnp.bfloat16
    )


def spread_rows(onehot, gradient_tree):
    return jnp.einsum("sa,s...->a...", onehot, gradient_tree, precision=lax.Precision.HIGHEST)


def direct_product(input_rows, weight_matrix):
    return jnp.einsum("std,do->sto", input_rows, weight_matrix, preferred_element_type=jnp.float32)


def direct_back(gradient_tree, weight_matrix):
    return jnp.einsum(
        "sto,do->std", gradient_tree, weight_matrix, preferred_element_type=jnp.float32
    )


def inner_product_part(input_rows, down):
    return jnp.einsum("std,sdr->str", input_rows, down, preferred_element_type=jnp.float32)


def inner_back(gradient_tree, upward_rows):
    return ADAPTER_SCALE * jnp.einsum(
        "sto,sro->str", gradient_tree, upward_rows, preferred_element_type=jnp.float32
    )


def through_down(grad_inner, down):
    return jnp.einsum("str,sdr->std", grad_inner, down, preferred_element_type=jnp.float32)


def down_grad(input_rows, grad_inner):
    return jnp.einsum("std,str->sdr", input_rows, grad_inner, preferred_element_type=jnp.float32)


def upward_grad(inner_rows, gradient_tree):
    return ADAPTER_SCALE * jnp.einsum(
        "jvp,jvx->jpx", inner_rows, gradient_tree, preferred_element_type=jnp.float32
    )


def upward_apply(inner_rows, upward_rows):
    return ADAPTER_SCALE * jnp.einsum(
        "str,sro->sto", inner_rows, upward_rows, preferred_element_type=jnp.float32
    )


def project(input_rows, weight_matrix, down, upward_rows):
    inner_rows = inner_product_part(input_rows, down).astype(jnp.bfloat16)
    return (
        inner_rows,
        direct_product(input_rows, weight_matrix) + upward_apply(inner_rows, upward_rows),
    )


def project_back(input_rows, grad_output, weight_matrix, down, upward_rows, inner_rows):
    grad_upward = upward_grad(inner_rows, grad_output)
    grad_inner = inner_back(grad_output, upward_rows).astype(jnp.bfloat16)
    grad_down = down_grad(input_rows, grad_inner)
    grad_inputs = direct_back(grad_output, weight_matrix) + through_down(grad_inner, down)
    return (grad_inputs, grad_down, grad_upward)


def allowed_mask(key_start, key_count, query_pos, lengths):
    key_pos = key_start + jnp.arange(key_count, dtype=jnp.int32)
    causal = key_pos[None, :] <= query_pos[:, None]
    live = key_pos[None, :] < lengths[:, None]
    return (causal[None, :, :] & live[:, None, :])[:, None, None, :, :]


def attend_block(state, key_block, value_block, key_start, query_head_rows, query_pos, lengths):
    run_max, run_sum, run_acc = state
    scale = query_head_rows.shape[-1] ** (-0.5)
    scores = (
        jnp.einsum(
            "sqhgd,skhd->shgqk", query_head_rows, key_block, preferred_element_type=jnp.float32
        )
        * scale
    )
    allowed = allowed_mask(key_start, key_block.shape[1], query_pos, lengths)
    new_max = jnp.maximum(run_max, jnp.max(jnp.where(allowed, scores, NEGATIVE), axis=-1))
    weights = jnp.where(allowed, jnp.exp(scores - new_max[..., None]), 0.0)
    factor = jnp.exp(run_max - new_max)
    new_sum = run_sum * factor + jnp.sum(weights, axis=-1)
    update = jnp.einsum(
        "shgqk,skhd->shgqd",
        weights.astype(jnp.bfloat16),
        value_block,
        preferred_element_type=jnp.float32,
    )
    return (new_max, new_sum, run_acc * factor[..., None] + update)


def attend_back(
    key_block,
    value_block,
    key_start,
    query_head_rows,
    grad_heads,
    log_total,
    row_dot,
    query_pos,
    lengths,
):
    scale = query_head_rows.shape[-1] ** (-0.5)
    scores = (
        jnp.einsum(
            "sqhgd,skhd->shgqk", query_head_rows, key_block, preferred_element_type=jnp.float32
        )
        * scale
    )
    allowed = allowed_mask(key_start, key_block.shape[1], query_pos, lengths)
    probs = jnp.where(allowed, jnp.exp(scores - log_total[..., None]), 0.0)
    grad_probs = jnp.einsum(
        "sqhgd,skhd->shgqk", grad_heads, value_block, preferred_element_type=jnp.float32
    )
    grad_scores = (probs * (grad_probs - row_dot[..., None])).astype(jnp.bfloat16)
    grad_query = scale * jnp.einsum(
        "shgqk,skhd->sqhgd", grad_scores, key_block, preferred_element_type=jnp.float32
    )
    grad_key = scale * jnp.einsum(
        "shgqk,sqhgd->skhd", grad_scores, query_head_rows, preferred_element_type=jnp.float32
    )
    grad_value = jnp.einsum(
        "shgqk,sqhgd->skhd",
        probs.astype(jnp.bfloat16),
        grad_heads,
        preferred_element_type=jnp.float32,
    )
    return (grad_query, grad_key, grad_value)


def attend_forward(query_head_rows, key_head_rows, value_head_rows, lengths_used, query_pos):
    slots, rows, kv_heads, group_size, head_size = query_head_rows.shape
    key_flat = key_head_rows.reshape(slots, rows, kv_heads * head_size)
    value_flat = value_head_rows.reshape(slots, rows, kv_heads * head_size)
    stat_shape = (slots, kv_heads, group_size, rows)
    initial = (
        jnp.full(stat_shape, NEGATIVE, jnp.float32),
        jnp.zeros(stat_shape, jnp.float32),
        jnp.zeros(stat_shape + (head_size,), jnp.float32),
    )
    part_keys = lax.all_gather(key_flat, "ctx", axis=1, tiled=True)
    part_values = lax.all_gather(value_flat, "ctx", axis=1, tiled=True)
    piece_rows = part_keys.shape[1]
    part_keys = part_keys.reshape(slots, piece_rows, kv_heads, head_size)
    part_values = part_values.reshape(slots, piece_rows, kv_heads, head_size)
    span_rows = math.gcd(piece_rows, 4 * rows)

    def inner_step(block_index, inner_state):
        sub_keys = lax.dynamic_slice_in_dim(part_keys, block_index * span_rows, span_rows, 1)
        sub_values = lax.dynamic_slice_in_dim(part_values, block_index * span_rows, span_rows, 1)
        return attend_block(
            inner_state,
            sub_keys,
            sub_values,
            block_index * span_rows,
            query_head_rows,
            query_pos,
            lengths_used,
        )

    run_max, run_sum, run_acc = lax.fori_loop(0, piece_rows // span_rows, inner_step, initial)
    log_total = run_max + jnp.log(run_sum)
    attended = jnp.transpose(run_acc / run_sum[..., None], (0, 3, 1, 2, 4))
    return (attended, log_total)


def attend_backward(
    query_head_rows,
    key_head_rows,
    value_head_rows,
    grad_heads,
    attended,
    log_total,
    lengths_used,
    query_pos,
):
    ctx_count = lax.axis_size("ctx")
    own_index = lax.axis_index("ctx")
    rows = query_head_rows.shape[1]
    row_dot = jnp.transpose(
        jnp.sum(grad_heads.astype(jnp.float32) * attended, axis=-1), (0, 2, 3, 1)
    )

    def cycle_step(step_index, carried):
        carried_keys, carried_values, grad_query, grad_key, grad_value = carried
        block_id = (own_index + step_index) % ctx_count
        query_part, key_part, value_part = attend_back(
            carried_keys,
            carried_values,
            block_id * rows,
            query_head_rows,
            grad_heads,
            log_total,
            row_dot,
            query_pos,
            lengths_used,
        )
        grad_key, grad_value = (
            from_behind((grad_key + key_part).astype(jnp.bfloat16), "ctx", -1).astype(jnp.float32),
            from_behind((grad_value + value_part).astype(jnp.bfloat16), "ctx", -1).astype(
                jnp.float32
            ),
        )
        carried_keys, carried_values = from_behind((carried_keys, carried_values), "ctx", -1)
        return (carried_keys, carried_values, grad_query + query_part, grad_key, grad_value)

    key_zeros = jnp.zeros(key_head_rows.shape, jnp.float32)
    start_state = (
        key_head_rows,
        value_head_rows,
        jnp.zeros(query_head_rows.shape, jnp.float32),
        key_zeros,
        key_zeros,
    )
    carried = lax.fori_loop(0, ctx_count, cycle_step, start_state)
    return (carried[2], carried[3], carried[4])


def table_total(rotation_tables):
    return lax.psum(rotation_tables, ("ctx", "fsdp"))


def local(
    tokens,
    cotangent,
    lengths,
    slot_adapter_index,
    attention_norm_gain,
    feedforward_norm_gain,
    query_weight,
    key_weight,
    value_weight,
    output_weight,
    gate_weight,
    up_weight,
    down_weight,
    adapter_input_first,
    adapter_output_first,
    adapter_down_first,
    adapter_query_second,
    adapter_key_value_second,
    adapter_output_second,
    adapter_gate_up_second,
    adapter_down_second,
):
    slot_count, tok_rows, model_width = tokens.shape
    head_groups = QUERY_HEADS // KEY_VALUE_HEADS
    own_index = lax.axis_index("ctx")
    fsdp_index = lax.axis_index("fsdp")
    query_pos = own_index * tok_rows + jnp.arange(tok_rows, dtype=jnp.int32)
    cosine_table, sine_table = rope_tables(query_pos, HEAD_DIM)
    own_lengths = lax.dynamic_slice_in_dim(lengths, fsdp_index * slot_count, slot_count, 0)
    own_adapters = lax.dynamic_slice_in_dim(
        slot_adapter_index, fsdp_index * slot_count, slot_count, 0
    )
    valid = query_pos[None, :] < own_lengths[:, None]
    adapter_labels = jnp.arange(adapter_input_first.shape[0], dtype=jnp.int32)
    onehot_own = own_adapters[:, None] == adapter_labels[None, :]
    owned_low_rank = onehot_own.astype(jnp.bfloat16)
    own_full = onehot_own.astype(jnp.float32)
    tokens_f = tokens.astype(jnp.float32)
    factor_one = rms_factor(tokens_f)
    normed_one = (tokens_f * factor_one * attention_norm_gain).astype(jnp.bfloat16)
    grad_out = jnp.where(valid[..., None], cotangent, jnp.zeros((), jnp.bfloat16))
    input_first = pick_rows(owned_low_rank, adapter_input_first)
    output_second = pick_rows(owned_low_rank, adapter_output_second)
    down_second = pick_rows(owned_low_rank, adapter_down_second)
    output_first = pick_rows(owned_low_rank, adapter_output_first)
    down_first = pick_rows(owned_low_rank, adapter_down_first)
    query_second = pick_rows(owned_low_rank, adapter_query_second)
    key_value_second = pick_rows(owned_low_rank, adapter_key_value_second)
    gate_up_second = pick_rows(owned_low_rank, adapter_gate_up_second)
    weight_q, weight_k, weight_v, weight_gate, weight_up, weight_o, weight_down = (
        lax.all_gather(query_weight, "fsdp", axis=1, tiled=True),
        lax.all_gather(key_weight, "fsdp", axis=1, tiled=True),
        lax.all_gather(value_weight, "fsdp", axis=1, tiled=True),
        lax.all_gather(gate_weight, "fsdp", axis=1, tiled=True),
        lax.all_gather(up_weight, "fsdp", axis=1, tiled=True),
        lax.all_gather(output_weight, "fsdp", axis=0, tiled=True),
        lax.all_gather(down_weight, "fsdp", axis=0, tiled=True),
    )
    inner_q, projected_queries = project(normed_one, weight_q, input_first[:, 0], query_second)
    inner_k, projected_keys = project(
        normed_one, weight_k, input_first[:, 1], key_value_second[:, 0]
    )
    inner_v, projected_values = project(
        normed_one, weight_v, input_first[:, 2], key_value_second[:, 1]
    )
    query_head_rows = apply_rotation(
        projected_queries.reshape(slot_count, tok_rows, -1, HEAD_DIM), cosine_table, sine_table
    ).astype(jnp.bfloat16)
    query_head_rows = query_head_rows.reshape(slot_count, tok_rows, -1, head_groups, HEAD_DIM)
    key_head_rows = apply_rotation(
        projected_keys.reshape(slot_count, tok_rows, -1, HEAD_DIM), cosine_table, sine_table
    ).astype(jnp.bfloat16)
    value_head_rows = projected_values.astype(jnp.bfloat16).reshape(
        slot_count, tok_rows, -1, HEAD_DIM
    )
    attended, log_total = attend_forward(
        query_head_rows, key_head_rows, value_head_rows, own_lengths, query_pos
    )
    attn_b = attended.reshape(slot_count, tok_rows, -1).astype(jnp.bfloat16)
    inner_o, proj_o = project(attn_b, weight_o, output_first, output_second)
    resid = tokens_f + proj_o
    factor_two = rms_factor(resid)
    normed_two = (resid * factor_two * feedforward_norm_gain).astype(jnp.bfloat16)
    inner_gate, gate = project(normed_two, weight_gate, input_first[:, 3], gate_up_second[:, 0])
    inner_up, up_proj = project(normed_two, weight_up, input_first[:, 4], gate_up_second[:, 1])
    sigmoid_gate = jax.nn.sigmoid(gate)
    hidden = (gate * sigmoid_gate * up_proj).astype(jnp.bfloat16)
    inner_down, proj_down = project(hidden, weight_down, down_first, down_second)
    out_tokens = jnp.where(valid[..., None], resid + proj_down, 0.0).astype(jnp.bfloat16)
    grad_hidden, grad_da, grad_db = project_back(
        hidden, grad_out, weight_down, down_first, down_second, inner_down
    )
    grad_gate = (grad_hidden * up_proj * sigmoid_gate * (1.0 + gate * (1.0 - sigmoid_gate))).astype(
        jnp.bfloat16
    )
    grad_up = (grad_hidden * gate * sigmoid_gate).astype(jnp.bfloat16)
    from_gate, grad_ga, grad_gb = project_back(
        normed_two, grad_gate, weight_gate, input_first[:, 3], gate_up_second[:, 0], inner_gate
    )
    from_up, grad_ua, grad_ub = project_back(
        normed_two, grad_up, weight_up, input_first[:, 4], gate_up_second[:, 1], inner_up
    )
    grad_normed_two = (from_gate + from_up).astype(jnp.bfloat16).astype(jnp.float32)
    grad_resid = grad_out.astype(jnp.float32) + norm_back(
        resid, factor_two, feedforward_norm_gain, grad_normed_two
    )
    grad_resid_low = grad_resid.astype(jnp.bfloat16)
    from_attn, grad_oa, grad_ob = project_back(
        attn_b, grad_resid_low, weight_o, output_first, output_second, inner_o
    )
    grad_heads = from_attn.astype(jnp.bfloat16).reshape(attended.shape)
    grad_query, grad_key, grad_value = attend_backward(
        query_head_rows,
        key_head_rows,
        value_head_rows,
        grad_heads,
        attended,
        log_total,
        own_lengths,
        query_pos,
    )
    grad_proj_q = (
        rotate_back(
            grad_query.reshape(slot_count, tok_rows, -1, HEAD_DIM), cosine_table, sine_table
        )
        .astype(jnp.bfloat16)
        .reshape(slot_count, tok_rows, -1)
    )
    grad_proj_k = (
        rotate_back(grad_key, cosine_table, sine_table)
        .astype(jnp.bfloat16)
        .reshape(slot_count, tok_rows, -1)
    )
    grad_proj_v = grad_value.astype(jnp.bfloat16).reshape(slot_count, tok_rows, -1)
    from_query, grad_qa, grad_qb = project_back(
        normed_one, grad_proj_q, weight_q, input_first[:, 0], query_second, inner_q
    )
    from_key, grad_ka, grad_kb = project_back(
        normed_one, grad_proj_k, weight_k, input_first[:, 1], key_value_second[:, 0], inner_k
    )
    from_value, grad_va, grad_vb = project_back(
        normed_one, grad_proj_v, weight_v, input_first[:, 2], key_value_second[:, 1], inner_v
    )
    grad_normed_one = (from_query + from_key + from_value).astype(jnp.bfloat16).astype(jnp.float32)
    grad_tokens = grad_resid + norm_back(tokens_f, factor_one, attention_norm_gain, grad_normed_one)
    slot_grads = (
        jnp.stack([grad_qa, grad_ka, grad_va, grad_ga, grad_ua], axis=1),
        grad_oa,
        grad_da,
        grad_qb,
        jnp.stack([grad_kb, grad_vb], axis=1),
        grad_ob,
        jnp.stack([grad_gb, grad_ub], axis=1),
        grad_db,
    )
    summed = table_total(tuple((spread_rows(own_full, entry_item) for entry_item in slot_grads)))
    return (
        out_tokens,
        grad_tokens,
        summed[0],
        summed[1],
        summed[2],
        summed[3],
        summed[4],
        summed[5],
        summed[6],
        summed[7],
    )


BF16 = jnp.bfloat16
F32 = jnp.float32
MESH_ID = pl.DeviceIdType.MESH
RANK = 16
SIDE = 128
PAD_HEAD = 128
HALF_PAD = 64


def _sem(count):
    return pltpu.SemaphoreType.DMA((count,))


def _place():
    c = lax.axis_index("ctx")
    f = lax.axis_index("fsdp")
    x = f // 2
    core = f % 2
    return c, f, x, core, (c, 2 * x + 1 - core), (c, 2 * (1 - x) + core)


def _slot_of(c):
    return c // 2 + 4 * ((c // 2 + c) % 2)


def _group_of(slot):
    return 2 * (slot % 4) + (slot // 4 + slot) % 2


def _block(x, core, j):
    return 4 * (1 - core) + 2 * j + (x + j) % 2


def _owner(b):
    return 2 * ((b // 2 + b) % 2) + 1 - b // 4


def _greet(targets):
    barrier = pltpu.get_barrier_semaphore()
    for target in targets:
        pl.semaphore_signal(barrier, inc=1, device_id=target, device_id_type=MESH_ID)
    pl.semaphore_wait(barrier, len(targets))


def _remote(src, dst, send, recv, target):
    return pltpu.make_async_remote_copy(
        src_ref=src, dst_ref=dst, send_sem=send, recv_sem=recv, device_id=target, device_id_type=MESH_ID
    )


def _comm_call(kernel, ins, outs, scratch, cid, name, in_space=pl.ANY, out_space=pl.ANY, vmem=None):
    return pl.pallas_call(
        kernel,
        out_shape=outs,
        in_specs=[pl.BlockSpec(memory_space=in_space)] * len(ins),
        out_specs=jax.tree.map(lambda _: pl.BlockSpec(memory_space=out_space), outs),
        scratch_shapes=scratch,
        compiler_params=pltpu.CompilerParams(
            collective_id=cid, has_side_effects=True, vmem_limit_bytes=vmem
        ),
        name=name,
    )(*ins)


def _gather_steps(ins, outs, own_sem, send_sem, recv_sem, place):
    c, f, x, core, core_peer, x_peer = place
    h = 1 - core
    count = len(ins)
    local = []
    sends = []

    def first():
        for base, target in ((0, x_peer), (2 * count, core_peer)):
            for i in range(count):
                for j in range(2):
                    k = base + i * 2 + j
                    cp = _remote(
                        ins[i].at[j], outs[i].at[h, j, (x + j) % 2], send_sem.at[k], recv_sem.at[k], target
                    )
                    cp.start()
                    sends.append(cp)
        for i in range(count):
            for j in range(2):
                lc = pltpu.make_async_copy(
                    ins[i].at[j], outs[i].at[h, j, (x + j) % 2], own_sem.at[i * 2 + j]
                )
                lc.start()
                local.append(lc)

    def last():
        forwards = []
        for i in range(count):
            for j in range(2):
                k = i * 2 + j
                sends[k].wait_recv()
                cp = _remote(
                    outs[i].at[h, j, (x + j + 1) % 2],
                    outs[i].at[h, j, (x + j + 1) % 2],
                    send_sem.at[4 * count + k],
                    recv_sem.at[4 * count + k],
                    core_peer,
                )
                cp.start()
                forwards.append(cp)
        for k in range(2 * count):
            sends[2 * count + k].wait_recv()
            forwards[k].wait_recv()
        for cp in sends + forwards:
            cp.wait_send()
        for lc in local:
            lc.wait()

    return first, last


def _ctx_first(piece, lines, own_sem, send_sem, recv_sem, place):
    c, f, x, core, core_peer, x_peer = place
    z, y = c // 2, c % 2
    sends = []
    local = []

    def start():
        lc = pltpu.make_async_copy(piece, lines.at[z, x], own_sem)
        lc.start()
        local.append(lc)
        cp = _remote(piece, lines.at[z, x], send_sem.at[0], recv_sem.at[0], x_peer)
        cp.start()
        sends.append(cp)

    def spread():
        local[0].wait()
        sends[0].wait_recv()
        for step in range(1, 4):
            cp = _remote(
                lines.at[z],
                lines.at[z],
                send_sem.at[step],
                recv_sem.at[step],
                (2 * ((z + step) % 4) + y, f),
            )
            cp.start()
            sends.append(cp)

    def finish():
        for cp in sends[1:]:
            cp.wait_recv()
        for cp in sends:
            cp.wait_send()

    return start, spread, finish


def _ctx_second(lines, out, own_sem, send_sem, recv_sem, place):
    c, f, x, core, core_peer, x_peer = place
    z, y = c // 2, c % 2
    y_peer = (2 * z + 1 - y, f)
    sends = []
    local = []

    def start():
        lc = pltpu.make_async_copy(lines, out.at[y, core], own_sem)
        lc.start()
        local.append(lc)
        for k, target in ((0, y_peer), (1, core_peer)):
            cp = _remote(lines, out.at[y, core], send_sem.at[k], recv_sem.at[k], target)
            cp.start()
            sends.append(cp)

    def share():
        sends[0].wait_recv()
        cp = _remote(
            out.at[1 - y, core], out.at[1 - y, core], send_sem.at[2], recv_sem.at[2], core_peer
        )
        cp.start()
        sends.append(cp)

    def finish():
        sends[1].wait_recv()
        sends[2].wait_recv()
        for cp in sends:
            cp.wait_send()
        local[0].wait()

    return start, share, finish


def _ctx_planes(piece, out, own_sem, send_sem, recv_sem, place):
    c, f, x, core, core_peer, x_peer = place
    z, y = c // 2, c % 2
    y_peer = (2 * z + 1 - y, f)
    sends = {}
    local = []

    def send(k, src, dst, target):
        cp = _remote(src, dst, send_sem.at[k], recv_sem.at[k], target)
        cp.start()
        sends[k] = cp

    def spot(yy, zz):
        return out.at[yy, core, zz, x]

    def start():
        lc = pltpu.make_async_copy(piece, spot(y, z), own_sem)
        lc.start()
        local.append(lc)
        for step in range(1, 4):
            send(step, piece, spot(y, z), (2 * ((z + step) % 4) + y, f))
        send(4, piece, spot(y, z), y_peer)
        send(8, piece, spot(y, z), x_peer)

    def forward():
        for step in range(1, 4):
            sends[step].wait_recv()
            at = spot(y, (z + 4 - step) % 4)
            send(4 + step, at, at, y_peer)
            send(8 + step, at, at, x_peer)
        for step in range(4):
            sends[4 + step].wait_recv()
            at = spot(1 - y, (z + 4 - step) % 4)
            send(12 + step, at, at, x_peer)

    def finish():
        local[0].wait()
        for half in range(2):
            for step in range(4):
                sends[8 + 4 * half + step].wait_recv()
            yy = 1 - y if half else y
            send(16 + half, out.at[yy, core], out.at[yy, core], core_peer)
        for half in range(2):
            sends[16 + half].wait_recv()
        for cp in sends.values():
            cp.wait_send()

    return start, forward, finish


def _z_peers(place):
    c, f = place[:2]
    return [(2 * ((c // 2 + step) % 4) + c % 2, f) for step in range(1, 4)]


def _y_peer(place):
    c, f = place[:2]
    return (2 * (c // 2) + 1 - c % 2, f)


def _lines_of(n):
    return (4, 2, RANK, n)


def _spread_of(n):
    return jax.ShapeDtypeStruct((2, 2, 4, 2, RANK, n), BF16)


FIRST_SEMS = [pltpu.SemaphoreType.DMA(()), _sem(4), _sem(4)]
SECOND_SEMS = [pltpu.SemaphoreType.DMA(()), _sem(3), _sem(3)]
PLANE_SEMS = [pltpu.SemaphoreType.DMA(()), _sem(18), _sem(18)]


def _order_steps(own, order, own_sem, send_sem, recv_sem, place):
    core_peer, x_peer = place[4:]
    sends, local, forwards = [], [], []

    def first():
        for j in range(2):
            cp = _remote(own.at[j], order.at[1 + j, 1], send_sem.at[j], recv_sem.at[j], x_peer)
            cp.start()
            sends.append(cp)
        for j in range(2):
            cp = _remote(
                own.at[j], order.at[3, j], send_sem.at[2 + j], recv_sem.at[2 + j], core_peer
            )
            cp.start()
            sends.append(cp)
        for j in range(2):
            lc = pltpu.make_async_copy(own.at[j], order.at[0, j], own_sem.at[j])
            lc.start()
            local.append(lc)

    def forward(j):
        sends[j].wait_recv()
        cp = _remote(
            order.at[1 + j, 1],
            order.at[1 + j, 0],
            send_sem.at[4 + j],
            recv_sem.at[4 + j],
            core_peer,
        )
        cp.start()
        forwards.append(cp)

    def own_here():
        for lc in local:
            lc.wait()

    def core_here():
        for j in range(2):
            sends[2 + j].wait_recv()

    def far_here(j):
        forwards[j].wait_recv()

    def last():
        for cp in sends + forwards:
            cp.wait_send()

    return first, forward, own_here, core_here, far_here, last


def _order_all(own, order, sems, place):
    first, forward, own_here, core_here, far_here, last = _order_steps(own, order, *sems, place)
    first()
    own_here()
    for j in range(2):
        forward(j)
    core_here()
    for j in range(2):
        far_here(j)
    last()


def feed_forward(own, cot, resid, gain, length, weights, adapters, cid):
    gate_w, up_w, down_w = weights
    width, units = gate_w.shape
    wide = width + SIDE
    tile = 256

    loads_in = tuple(weights) + tuple(adapters) + (cot,)
    count = len(loads_in)

    def kernel(*refs):
        len_ref, own_ref, resid_ref, gain_ref = refs[:4]
        loads_hbm = refs[4 : 4 + count]
        grad_resid, grad_low, small, out_own, out_far, order, early = refs[4 + count : 11 + count]
        refs = refs[11 + count :]
        gate_ref, up_ref, down_ref, first_ref, sg_ref, su_ref, fd_ref, sd_ref, go_ref = refs[:count]
        (
            sums,
            hid_s,
            gg_s,
            gu_s,
            in_s,
            gid_s,
            part,
            out_part,
            near,
            out_near,
            far,
            out_land,
            staged,
            landed,
            load_sem,
            own_sem,
            send_sem,
            recv_sem,
            s_sem,
            r_sem,
        ) = refs[count:]
        place = _place()
        core_peer, x_peer = place[4:]
        loads = []
        for i in range(count):
            cp = pltpu.make_async_copy(loads_hbm[i], refs[i], load_sem.at[i])
            cp.start()
            loads.append(cp)
        _greet([core_peer, x_peer])
        first, forward, own_here, core_here, far_here, last = _order_steps(
            own_ref, order, own_sem, send_sem, recv_sem, place
        )
        first()
        copies = []
        c, f, x, core = place[:4]
        live = len_ref[0]

        def masked(step):
            other_x = x if step in (0, 3) else 1 - x
            pieces = []
            for k in range(2):
                other_core = (core, 1 - core)[step == 3 or (step in (1, 2) and k == 0)]
                j = k if step in (0, 3) else step - 1
                pos = 128 * _block(other_x, other_core, j) + lax.broadcasted_iota(jnp.int32, (128, width), 0)
                pieces.append(jnp.where(pos < live, go_ref[step, k].astype(F32), 0.0).astype(BF16))
            return pieces

        def work(step):
            rows = order[step].reshape(2 * 128, width)
            pieces = masked(step)
            for k in range(2):
                go_ref[step, k] = pieces[k]
            go = go_ref[step].reshape(2 * 128, width)
            inner = dot_t(rows, first_ref[...]).astype(BF16)
            gid = dot_t(go, sd_ref[...]).astype(BF16)
            in_s[step] = inner
            gid_s[step] = gid
            for at in range(0, units, tile):
                cols = slice(at, at + tile)
                gate = dot(rows, gate_ref[:, cols]) + dot(inner, sg_ref[:, cols])
                up = dot(rows, up_ref[:, cols]) + dot(inner, su_ref[:, cols])
                grad = dot_t(go, down_ref[cols, :]) + dot(gid, fd_ref[:, cols])
                sig = 0.5 * jnp.tanh(0.5 * gate) + 0.5
                silu = gate * sig
                hid_s[step, :, cols] = (silu * up).astype(BF16)
                gg_s[step, :, cols] = (grad * up * sig * (1.0 + gate * (1.0 - sig))).astype(BF16)
                gu_s[step, :, cols] = (grad * silu).astype(BF16)
            gg, gu = gg_s[step], gu_s[step]
            for at in range(0, width, tile):
                cols = slice(at, at + tile)
                value = dot_t(gg, gate_ref[cols, :]) + dot_t(gu, up_ref[cols, :])
                if step == 0:
                    sums[:, :, cols] = value.reshape(2, 128, tile)
                else:
                    part[step - 1, :, :, cols] = value.astype(BF16).reshape(2, 128, tile)
            value = dot_t(gg, sg_ref[...]) + dot_t(gu, su_ref[...])
            if step == 0:
                sums[:, :, width:] = value.reshape(2, 128, SIDE)
            else:
                part[step - 1, :, :, width:] = value.astype(BF16).reshape(2, 128, SIDE)

        def down(step):
            hid = hid_s[step]
            for at in range(0, width, tile):
                cols = slice(at, at + tile)
                out = dot(hid, down_ref[:, cols])
                if step == 0:
                    out_own[:, :, cols] = out.reshape(2, 128, tile)
                else:
                    out_part[step - 1, :, :, cols] = out.astype(BF16).reshape(2, 128, tile)
            out = dot_t(hid, fd_ref[...])
            if step == 0:
                out_own[:, :, width:] = out.reshape(2, 128, SIDE)
            else:
                out_part[step - 1, :, :, width:] = out.astype(BF16).reshape(2, 128, SIDE)

        def send(src, dst, k, target):
            cp = _remote(src, dst, s_sem.at[k], r_sem.at[k], target)
            cp.start()
            copies.append(cp)
            return cp

        own_here()
        for cp in loads:
            cp.wait()
        work(0)
        across, out_cps = [], []

        def leave(j, cp):
            cp.wait_recv()
            staged[j] = (part[j, 1].astype(F32) + far[j].astype(F32)).astype(BF16)
            across.append(send(staged.at[j], landed.at[j], 6 + j, x_peer))

        for j in range(2):
            forward(j)
            far_here(j)
            work(1 + j)
            cp = send(part.at[j, 0], far.at[j], 2 + j, core_peer)
            down(1 + j)
            out_cps.append(send(out_part.at[j, 0], out_land.at[j], 4 + j, core_peer))
            leave(j, cp)
        core_here()
        work(3)
        near_cp = [send(part.at[2], near, 0, core_peer)]
        down(3)
        near_cp.append(send(out_part.at[2], out_near, 1, core_peer))
        down(0)
        for j in range(2):
            out_cps[j].wait_recv()
            out_far[j] = (out_part[j, 1].astype(F32) + out_land[j].astype(F32)).astype(BF16)
        for cp in near_cp:
            cp.wait_recv()
        sums[...] = sums[...] + near[...].astype(F32)
        out_own[...] = out_own[...] + out_near[...].astype(F32)
        for at in range(0, units, 512):
            cols = slice(at, at + 512)
            g = jnp.zeros((SIDE, 512), F32)
            u = jnp.zeros((SIDE, 512), F32)
            d = jnp.zeros((SIDE, 512), F32)
            for step in range(4):
                g += dot_rows(in_s[step], gg_s[step, :, cols])
                u += dot_rows(in_s[step], gu_s[step, :, cols])
                d += dot_rows(gid_s[step], hid_s[step, :, cols])
            early[:, at : at + 512] = (ADAPTER_SCALE * g[:RANK]).astype(BF16)
            early[:, units + at : units + at + 512] = (ADAPTER_SCALE * u[RANK : 2 * RANK]).astype(BF16)
            early[:, 2 * units + at : 2 * units + at + 512] = d[3 * RANK : 4 * RANK].astype(BF16)
        for j in range(2):
            across[j].wait_recv()
            total = sums[j] + landed[j].astype(F32)
            gi = total[:, width:].astype(BF16)
            small[j] = gi
            gn = (total[:, :width] + dot(gi, first_ref[...])).astype(BF16).astype(F32)
            v = resid_ref[j]
            factor = lax.rsqrt(jnp.mean(v * v, axis=1, keepdims=True) + EPSILON)
            scaled = gn * gain_ref[...]
            mean = jnp.mean(scaled * v, axis=1, keepdims=True)
            grad = go_ref[0, j].astype(F32) + factor * scaled - v * (factor * factor * factor) * mean
            grad_resid[j] = grad
            grad_low[j] = grad.astype(BF16)
        last()
        for cp in copies:
            cp.wait_send()

    vmem = pl.BlockSpec(memory_space=pltpu.VMEM)
    rows = (2, 128, wide)
    f32 = lambda *shape: jax.ShapeDtypeStruct(shape, F32)
    outs = [
        f32(2, 128, width),
        jax.ShapeDtypeStruct((2, 128, width), BF16),
        jax.ShapeDtypeStruct((2, 128, SIDE), BF16),
        f32(*rows),
        jax.ShapeDtypeStruct(rows, BF16),
        jax.ShapeDtypeStruct((4, 2, 128, width), BF16),
        jax.ShapeDtypeStruct((RANK, 3 * units), BF16),
    ]
    hbm = pl.BlockSpec(memory_space=pl.ANY)
    return pl.pallas_call(
        kernel,
        out_shape=outs,
        in_specs=[pl.BlockSpec(memory_space=pltpu.SMEM), vmem, vmem, vmem] + [hbm] * count,
        out_specs=[vmem] * len(outs),
        scratch_shapes=[pltpu.VMEM(a.shape, a.dtype) for a in loads_in]
        + [pltpu.VMEM(rows, F32)]
        + [pltpu.VMEM((4, 256, units), BF16)] * 3
        + [pltpu.VMEM((4, 256, SIDE), BF16)] * 2
        + [pltpu.VMEM((3,) + rows, BF16)] * 2
        + [pltpu.VMEM(rows, BF16)] * 6
        + [_sem(count), _sem(2), _sem(6), _sem(6), _sem(8), _sem(8)],
        compiler_params=pltpu.CompilerParams(
            collective_id=cid, has_side_effects=True, vmem_limit_bytes=58 * 1024 * 1024
        ),
        name="feed_forward",
    )(length, own, resid, gain, *loads_in)


def _back_steps(src, dst, out_s, out_r, place):
    c, f, x, core = place[:4]
    slot = _slot_of(c)
    place_in = slot % 2
    moves = []

    def first(j):
        cp = _remote(
            src.at[j],
            dst.at[place_in],
            out_s.at[j],
            out_r.at[place_in],
            (_block(x, core, j), slot // 2),
        )
        cp.start()
        moves.append(cp)

    def last():
        for half in range(2):
            pltpu.make_async_copy(dst.at[half], dst.at[half], out_r.at[half]).wait()
        for cp in moves:
            cp.wait_send()

    return first, last


def _back_sources(place):
    c, f = place[:2]
    return [(_group_of(2 * f + half), _owner(c)) for half in range(2)]


def front_call(
    tokens,
    cotangent,
    length,
    adapter,
    gains,
    wq,
    wk,
    wv,
    wo,
    tables,
    cosine,
    sine,
    cid,
):
    width = tokens.shape[-1]
    rows = cosine.shape[0]
    wide = width + SIDE
    block = 256
    scale = HEAD_DIM ** (-0.5)
    lane = PAD_HEAD
    units = tables[6].shape[-1] // 4
    quarter = width // 4
    loads_in = (gains, wq, wk, wv, wo) + tables + (cosine, sine)
    count = len(loads_in)

    def kernel(*refs):
        len_ref, adapter_ref, tok_ref, cot_ref = refs[:4]
        loads_hbm = refs[4 : 4 + count]
        (
            sums_resid,
            normed_two,
            side_all,
            tok_own,
            cot_order,
            cot_peer,
            qkv_ref,
            lse_ref,
            att_ref,
            one_cut,
            inner_ref,
            wa_ref,
            ow_ref,
            sa_ref,
            fa_ref,
            fgu_ref,
            sg_ref,
            su_ref,
            fd_ref,
            sd_ref,
            fo_ref,
            so_ref,
        ) = refs[4 + count : 26 + count]
        refs = refs[26 + count :]
        gain_v, wq_v, wk_v, wv_v, wo_v = refs[:5]
        in_first, out_first, down_first, q_second, kv_second, o_second, gu_second, d_second = refs[5:13]
        cos_ref, sin_ref = refs[13:15]
        (
            tok_all,
            one_ref,
            part,
            land,
            staged,
            landed,
            sums,
            side_own,
            load_sem,
            land_s,
            land_r,
            cot_s,
            cot_r,
            send_sem,
            recv_sem,
            s_sem,
            r_sem,
        ) = refs[15:32]
        side_sems = refs[32:35]
        place = _place()
        c, f, x, core, core_peer, x_peer = place
        hh = 1 - core
        slot = _slot_of(c)
        live = len_ref[0]
        which = adapter_ref[0]
        loads = []
        for i in range(count):
            cp = pltpu.make_async_copy(loads_hbm[i], refs[i], load_sem.at[i])
            cp.start()
            loads.append(cp)

        barrier = pltpu.get_barrier_semaphore()
        for j in range(2):
            pl.semaphore_signal(
                barrier, inc=1, device_id=(_block(x, core, j), slot // 2), device_id_type=MESH_ID
            )
        for target in (core_peer, x_peer):
            pl.semaphore_signal(barrier, inc=1, device_id=target, device_id_type=MESH_ID)
        for b in range(4):
            pl.semaphore_signal(
                barrier,
                inc=1,
                device_id=(4 * hh + b, 2 * x + (slot // 2) % 2),
                device_id_type=MESH_ID,
            )
        pl.semaphore_wait(barrier, 8)
        to_f = _owner(c)
        to_h = c // 4
        to_j = (c // 2) % 2
        to_i = c % 2
        moves = []
        for part_row in range(2):
            span = pl.ds(64 * part_row, 64)
            for half in range(2):
                s = 2 * f + half
                cp = _remote(
                    tok_ref.at[half, span],
                    tok_all.at[to_h, to_j, to_i, span],
                    land_s.at[2 * part_row + half],
                    land_r.at[2 * part_row + to_j],
                    (_group_of(s), to_f),
                )
                cp.start()
                moves.append(cp)
        cross = [
            _remote(cot_ref.at[half], cot_peer.at[half], cot_s.at[half], cot_r.at[half], x_peer)
            for half in range(2)
        ]
        for cp in cross:
            cp.start()
        cot_moves = []
        for relay in range(2):
            for half in range(2):
                s = 2 * (2 * ((x + relay) % 2) + core) + half
                away = ((c // 2 + c) % 2 + x) % 2
                cot_moves.append(
                    _remote(
                        (cot_peer if relay else cot_ref).at[half],
                        cot_order.at[away * (1 + to_j), (1 - away) * to_j + away],
                        cot_s.at[2 + 2 * relay + half],
                        cot_r.at[2 + 2 * away + to_j],
                        (_group_of(s), 2 * x + 1 - to_h),
                    )
                )
        for cp in loads:
            cp.wait()

        def group_sends(part_row):
            span = pl.ds(64 * part_row, 64)
            for j in range(2):
                pltpu.make_async_copy(
                    tok_all.at[hh, j, (x + j) % 2, span],
                    tok_all.at[hh, j, (x + j) % 2, span],
                    land_r.at[2 * part_row + j],
                ).wait()
                k = 2 * part_row + j
                here = tok_all.at[hh, j, (x + j) % 2, span]
                for base, target in ((0, x_peer), (4, core_peer)):
                    cp = _remote(
                        here, here, send_sem.at[base + k], recv_sem.at[base + k], target
                    )
                    cp.start()
                    sends[base + k] = cp

        sends = {}

        def prepare_first():
            half = HEAD_DIM // 2
            wa_ref[...] = jnp.zeros_like(wa_ref)
            sa_ref[...] = jnp.zeros_like(sa_ref)
            for head in range(4):
                for side in range(2):
                    at = head * HEAD_DIM + side * half
                    to = head * lane + side * HALF_PAD
                    wa_ref[:, to : to + half] = wq_v[:, at : at + half]
            for head in range(2):
                for side in range(2):
                    at = head * HEAD_DIM + side * half
                    to = (4 + head) * lane + side * HALF_PAD
                    wa_ref[:, to : to + half] = wk_v[:, at : at + half]
                at, to = head * HEAD_DIM, (6 + head) * lane
                wa_ref[:, to : to + HEAD_DIM] = wv_v[:, at : at + HEAD_DIM]

        def prepare_second():
            half = HEAD_DIM // 2
            own_cols = pl.ds(pl.multiple_of(f * quarter, 128), quarter)
            own_units = pl.ds(pl.multiple_of(f * units, 128), units)
            low = lambda v: (ADAPTER_SCALE * v.astype(F32)).astype(BF16)
            for ref in (fa_ref, fgu_ref, sg_ref, su_ref, fd_ref, sd_ref, fo_ref, so_ref, ow_ref):
                ref[...] = jnp.zeros_like(ref)
            for i in range(3):
                fa_ref[i * RANK : (i + 1) * RANK, :] = in_first[which, i]
            for i in range(2):
                fgu_ref[i * RANK : (i + 1) * RANK, :] = in_first[which, 3 + i]
            all_gu = gu_second.at[:, :, :, own_units]
            sg_ref[:RANK, :] = low(all_gu[which, 0])
            su_ref[RANK : 2 * RANK, :] = low(all_gu[which, 1])
            fd_ref[3 * RANK : 4 * RANK, :] = down_first.at[:, :, own_units][which]
            sd_ref[3 * RANK : 4 * RANK, :] = low(d_second[which])
            so_ref[:RANK, :] = low(o_second[which])
            own_first = out_first.at[:, :, own_cols][which]
            own_q = low(q_second.at[:, :, own_cols][which])
            for head in range(4):
                at = head * HEAD_DIM
                fo_ref[:RANK, head * lane : head * lane + HEAD_DIM] = own_first[:, at : at + HEAD_DIM]
                ow_ref[head * lane : head * lane + HEAD_DIM, :] = wo_v[at : at + HEAD_DIM, :]
                for side in range(2):
                    to = head * lane + side * HALF_PAD
                    sa_ref[:RANK, to : to + half] = own_q[:, at + side * half : at + (side + 1) * half]
            for i in range(2):
                own_kv = low(kv_second[which, i])
                for head in range(2):
                    at = head * HEAD_DIM
                    if i:
                        to = (6 + head) * lane
                        sa_ref[2 * RANK : 3 * RANK, to : to + HEAD_DIM] = own_kv[:, at : at + HEAD_DIM]
                    else:
                        for side in range(2):
                            to = (4 + head) * lane + side * HALF_PAD
                            sa_ref[RANK : 2 * RANK, to : to + half] = own_kv[
                                :, at + side * half : at + (side + 1) * half
                            ]

        prepare_first()
        group_sends(0)
        prepare_second()
        group_sends(1)
        for cp in cross:
            cp.wait_recv()
        for cp in cot_moves:
            cp.start()

        def cot_spot(away, j):
            return cot_order.at[(1 + j) if away else 0, 1 if away else j]

        def cot_share():
            for away in range(2):
                for j in range(2):
                    here = cot_spot(away, j)
                    pltpu.make_async_copy(here, here, cot_r.at[2 + 2 * away + j]).wait()
                    there = cot_order.at[1 + j, 0] if away else cot_order.at[3, j]
                    k = 6 + 2 * away + j
                    cp = _remote(here, there, cot_s.at[k], cot_r.at[k], core_peer)
                    cp.start()
                    shared.append(cp)

        shared = []

        def forward(j):
            for part_row in range(2):
                k = 2 * part_row + j
                span = pl.ds(64 * part_row, 64)
                sends[k].wait_recv()
                there = tok_all.at[hh, j, (x + j + 1) % 2, span]
                cp = _remote(there, there, send_sem.at[8 + k], recv_sem.at[8 + k], core_peer)
                cp.start()
                sends[8 + k] = cp
            for part_row in range(2):
                k = 2 * part_row + j
                sends[4 + k].wait_recv()
                sends[8 + k].wait_recv()

        def project_rows(t):
            row = pl.ds(t * block, block)
            v = tok_all[t // 2, t % 2].reshape(block, width).astype(F32)
            factor = lax.rsqrt(jnp.mean(v * v, axis=1, keepdims=True) + EPSILON)
            u = (v * factor * gain_v[0:1, :]).astype(BF16)
            one_ref[row, :] = u
            inner = dot_t(u, fa_ref[...]).astype(BF16)
            inner_ref[row, :] = inner
            cos, sin = cos_ref[row, :], sin_ref[row, :]
            for pair in range(4):
                cols = slice(pair * 2 * lane, (pair + 1) * 2 * lane)
                both = dot(u, wa_ref[:, cols]) + dot(inner, sa_ref[:, cols])
                for k in range(2):
                    p = both[:, k * lane : (k + 1) * lane]
                    if pair < 3:
                        p = p * cos + pltpu.roll(p, HALF_PAD, 1) * sin
                    qkv_ref[row, (2 * pair + k) * lane : (2 * pair + k + 1) * lane] = p.astype(BF16)

        def attention(t, hook):
            keys = (t + 1) * block
            row = pl.ds(t * block, block)
            qpos = t * block + lax.broadcasted_iota(jnp.int32, (block, keys), 0)
            kpos = lax.broadcasted_iota(jnp.int32, (block, keys), 1)
            allowed = (kpos <= qpos) & (kpos < live)
            stats = jnp.zeros((block, lane), F32)
            lanes = lax.broadcasted_iota(jnp.int32, (block, lane), 1)
            for head in range(4):
                q = qkv_ref[row, head * lane : (head + 1) * lane]
                kv = head // 2
                k = qkv_ref[:keys, (4 + kv) * lane : (5 + kv) * lane]
                v = qkv_ref[:keys, (6 + kv) * lane : (7 + kv) * lane]
                s = jnp.where(allowed, dot_t(q, k) * scale, NEGATIVE)
                top = jnp.max(s, axis=1, keepdims=True)
                p = jnp.where(allowed, jnp.exp(s - top), 0.0)
                total = jnp.sum(p, axis=1, keepdims=True)
                o = dot(p.astype(BF16), v) / total
                att_ref[row, head * lane : (head + 1) * lane] = o.astype(BF16)
                stats = jnp.where(lanes == head, top + jnp.log(total), stats)
                if head == 1 and hook is not None:
                    hook()
            lse_ref[row, :] = stats
            a = att_ref[row, :]
            for at in range(0, width, 256):
                value = dot(a, ow_ref[:, at : at + 256])
                part[t, :, :, at : at + 256] = value.astype(BF16).reshape(2, 128, 256)
            part[t, :, :, width:] = dot_t(a, fo_ref[...]).astype(BF16).reshape(2, 128, SIDE)

        def to_core(t):
            return _remote(part.at[t], land.at[t % 2], s_sem.at[t % 2], r_sem.at[t % 2], core_peer)

        def to_x(j):
            return _remote(staged.at[j], landed.at[j], s_sem.at[2 + j], r_sem.at[2 + j], x_peer)

        def leave(t):
            @pl.when(core == t // 2)
            def _():
                to_core(t).start()

        def combine(t):
            j = t % 2

            @pl.when(core == 1 - t // 2)
            def _():
                to_core(t).wait_recv()
                mine, other = (x + j) % 2, (x + j + 1) % 2
                staged[j] = (part[t, other].astype(F32) + land[j, other].astype(F32)).astype(BF16)
                to_x(j).start()
                sums[j] = part[t, mine].astype(F32) + land[j, mine].astype(F32)

        forward(0)
        project_rows(0)
        project_rows(2)
        attention(0, None)
        leave(0)
        forward(1)
        project_rows(1)
        project_rows(3)
        attention(1, lambda: combine(0))
        leave(1)
        attention(2, lambda: combine(1))
        leave(2)
        attention(3, lambda: combine(2))
        leave(3)
        combine(3)
        for t in range(4):

            @pl.when(core == t // 2)
            def _():
                to_core(t).wait_send()

        for j in range(2):
            tok_own[j] = tok_all[hh, j, (x + j) % 2]
        one_cut[...] = one_ref[:, pl.ds(pl.multiple_of(f * quarter, 128), quarter)]
        for j in range(2):
            cp = to_x(j)
            cp.wait_recv()
            sums[j] = sums[j] + landed[j].astype(F32)
            cp.wait_send()
            side_own[j] = sums[j, :, width:].astype(BF16)
        side_first, side_last = _gather_steps([side_own], [side_all], *side_sems, place)
        side_first()
        for j in range(2):
            v = (
                tok_own[j].astype(F32)
                + sums[j, :, :width]
                + dot(side_own[j], so_ref[...])
            )
            sums_resid[j] = v
            factor = lax.rsqrt(jnp.mean(v * v, axis=1, keepdims=True) + EPSILON)
            normed_two[j] = (v * factor * gain_v[1:2, :]).astype(BF16)
        cot_share()
        for cp in shared:
            cp.wait_recv()
        side_last()
        for cp in moves + cross + cot_moves + shared + list(sends.values()):
            cp.wait_send()

    vmem, hbm = pl.BlockSpec(memory_space=pltpu.VMEM), pl.BlockSpec(memory_space=pl.ANY)
    smem = pl.BlockSpec(memory_space=pltpu.SMEM)
    low = lambda *shape: jax.ShapeDtypeStruct(shape, BF16)
    outs = [
        (jax.ShapeDtypeStruct((2, 128, width), F32), vmem),
        (low(2, 128, width), vmem),
        (low(2, 2, 2, 128, SIDE), hbm),
        (low(2, 128, width), vmem),
        (low(4, 2, 128, width), hbm),
        (low(2, 128, width), hbm),
        (low(rows, 8 * lane), vmem),
        (jax.ShapeDtypeStruct((rows, lane), F32), vmem),
        (low(rows, 4 * lane), vmem),
        (low(rows, quarter), vmem),
        (low(rows, SIDE), vmem),
        (low(width, 8 * lane), vmem),
        (low(4 * lane, width), vmem),
        (low(SIDE, 8 * lane), vmem),
        (low(SIDE, width), vmem),
        (low(SIDE, width), vmem),
        (low(SIDE, units), vmem),
        (low(SIDE, units), vmem),
        (low(SIDE, units), vmem),
        (low(SIDE, width), vmem),
        (low(SIDE, 4 * lane), vmem),
        (low(SIDE, width), vmem),
    ]
    own = (2, 128, wide)
    return pl.pallas_call(
        kernel,
        out_shape=[o[0] for o in outs],
        in_specs=[smem, smem] + [hbm] * (2 + count),
        out_specs=[o[1] for o in outs],
        scratch_shapes=[pltpu.VMEM(a.shape, a.dtype) for a in loads_in]
        + [
            pltpu.VMEM((2, 2, 2, 128, width), BF16),
            pltpu.VMEM((rows, width), BF16),
            pltpu.VMEM((4,) + own, BF16),
            pltpu.VMEM((2,) + own, BF16),
            pltpu.VMEM(own, BF16),
            pltpu.VMEM(own, BF16),
            pltpu.VMEM(own, F32),
            pltpu.VMEM((2, 128, SIDE), BF16),
            _sem(count),
            _sem(4),
            _sem(4),
            _sem(10),
            _sem(10),
            _sem(12),
            _sem(12),
            _sem(4),
            _sem(4),
        ]
        + [_sem(2), _sem(6), _sem(6)],
        compiler_params=pltpu.CompilerParams(
            collective_id=cid, has_side_effects=True, vmem_limit_bytes=58 * 1024 * 1024
        ),
        name="front",
    )(length, adapter, tokens, cotangent, *loads_in)


def attend_back_call(
    low_own,
    small_own,
    early,
    out_far,
    length,
    own_arrays,
    arrays,
    cid,
):
    (qkv, stats, att, inner_o, order, cosine, sine, out_w, first_o, second_o, weight_all) = arrays[:11]
    width = low_own.shape[-1]
    rows = qkv.shape[0]
    wide = width + SIDE
    step_rows = 256
    scale = HEAD_DIM ** (-0.5)
    lane = PAD_HEAD
    quarter = width // 4
    middle_n = 4 * quarter
    early_n = early.shape[1]
    big = tuple(arrays) + tuple(own_arrays)
    late_n = 4 * quarter
    factor_n = 2 * quarter
    count = len(big)

    def kernel(*refs):
        len_ref, low_ref, small_ref, early_ref, out_ref = refs[:5]
        big_in = refs[5 : 5 + count]
        (
            out_back,
            grad_back,
            early_out,
            middle_out,
            late_out,
            factor_out,
            early_lines,
            middle_lines,
        ) = refs[5 + count : 13 + count]
        refs = refs[13 + count :]
        (
            qkv_ref,
            lse_ref,
            att_ref,
            inner_ref,
            order_ref,
            cos_ref,
            sin_ref,
            ow_ref,
            fo_ref,
            so_ref,
            wa_ref,
            sa_ref,
            fa_ref,
            sd_ref,
            cut_ref,
            inner_qkv_ref,
            cot_ref,
            out_own,
            resid_ref,
            tok_ref,
            grad_resid_ref,
            gain_ref,
        ) = refs[:count]
        (
            low,
            do_ref,
            gio_ref,
            dk_ref,
            dv_ref,
            part,
            land,
            staged,
            landed,
            side_own,
            middle_ref,
            sums,
            side_all,
            grad_ref,
            landed_out,
            small_out,
            late_ref,
            factor_ref,
            out_tok,
            grad_tok,
            load_sem,
            own_sem,
            send_sem,
            recv_sem,
            s_sem,
            r_sem,
        ) = refs[count : count + 26]
        sems = refs[count + 26 :]
        place = _place()
        c, f, x, core, core_peer, x_peer = place
        loads = [
            pltpu.make_async_copy(big_in[i], refs[i], load_sem.at[i]) for i in range(count)
        ]
        for cp in loads:
            cp.start()
        _greet(
            _back_sources(place) + [core_peer, x_peer, _y_peer(place)] + _z_peers(place)
        )
        small_first, small_forward, small_own_here, small_core, small_far, small_last = _order_steps(
            small_ref, small_out, *sems[0:3], place
        )
        early_start, early_across, early_finish = _ctx_first(early_ref, early_lines, *sems[3:6], place)
        early_two = _ctx_second(early_lines, early_out, *sems[6:9], place)
        mid_start, mid_across, mid_finish = _ctx_first(middle_ref, middle_lines, *sems[9:12], place)
        mid_two = _ctx_second(middle_lines, middle_out, *sems[12:15], place)
        late = _ctx_planes(late_ref, late_out, *sems[15:18], place)
        factor = _ctx_planes(factor_ref, factor_out, *sems[25:28], place)
        side_first, side_last = _gather_steps([side_own], [side_all], *sems[18:21], place)
        out_first, out_last = _back_steps(out_tok, out_back, *sems[21:23], place)
        grad_first, grad_last = _back_steps(grad_tok, grad_back, *sems[23:25], place)
        live = len_ref[0]

        sends = {}
        hh = 1 - core
        local = []
        for j in (1, 0):
            for k, target in ((0, x_peer), (2, core_peer)):
                cp = _remote(
                    low_ref.at[j],
                    low.at[hh, j, (x + j) % 2],
                    send_sem.at[k + j],
                    recv_sem.at[k + j],
                    target,
                )
                cp.start()
                sends[(k, j)] = cp
            if j:
                early_start()
                small_first()
        for j in range(2):
            lc = pltpu.make_async_copy(low_ref.at[j], low.at[hh, j, (x + j) % 2], own_sem.at[j])
            lc.start()
            local.append(lc)
        swaps = [
            _remote(out_ref.at[j], landed_out.at[j], s_sem.at[8 + j], r_sem.at[8 + j], x_peer)
            for j in range(2)
        ]
        dk_ref[...] = jnp.zeros_like(dk_ref)
        dv_ref[...] = jnp.zeros_like(dv_ref)
        for cp in loads:
            cp.wait()
        for lc in local:
            lc.wait()

        def arrive(j):
            sends[(0, j)].wait_recv()
            cp = _remote(
                low.at[hh, j, (x + j + 1) % 2],
                low.at[hh, j, (x + j + 1) % 2],
                send_sem.at[4 + j],
                recv_sem.at[4 + j],
                core_peer,
            )
            cp.start()
            sends[(4, j)] = cp
            sends[(2, j)].wait_recv()
            cp.wait_recv()

        def through_output(t):
            g = low[t // 2, t % 2].reshape(step_rows, width)
            gio = dot_t(g, so_ref[...]).astype(BF16)
            row = pl.ds(t * step_rows, step_rows)
            gio_ref[row, :] = gio
            do_ref[row, :] = (dot_t(g, ow_ref[...]) + dot(gio, fo_ref[...])).astype(BF16)

        def attention(t, hook):
            keys = (t + 1) * step_rows
            row = pl.ds(t * step_rows, step_rows)
            qpos = t * step_rows + lax.broadcasted_iota(jnp.int32, (step_rows, keys), 0)
            kpos = lax.broadcasted_iota(jnp.int32, (step_rows, keys), 1)
            allowed = (kpos <= qpos) & (kpos < live)
            cos, sin = cos_ref[row, :], sin_ref[row, :]
            for head in range(4):
                kv = head // 2
                at = slice(head * lane, (head + 1) * lane)
                q = qkv_ref[row, at]
                k = qkv_ref[:keys, (4 + kv) * lane : (5 + kv) * lane]
                v = qkv_ref[:keys, (6 + kv) * lane : (7 + kv) * lane]
                do = do_ref[row, at]
                s = dot_t(q, k)
                p = jnp.where(allowed, jnp.exp(s * scale - lse_ref[row, head : head + 1]), 0.0)
                dp = dot_t(do, v)
                total = jnp.sum(p * dp, axis=1, keepdims=True)
                ds = (p * (dp - total)).astype(BF16)
                dq = scale * dot(ds, k)
                dq = dq * cos - pltpu.roll(dq, HALF_PAD, 1) * sin
                grad_ref[row, at] = dq.astype(BF16)
                dk_ref[kv, :keys] += dot_rows(ds, q)
                dv_ref[kv, :keys] += dot_rows(p.astype(BF16), do)
                if head == 1 and hook is not None:
                    hook()
            for kv in range(2):
                dk = scale * dk_ref[kv, row, :]
                dk = dk * cos - pltpu.roll(dk, HALF_PAD, 1) * sin
                grad_ref[row, (4 + kv) * lane : (5 + kv) * lane] = dk.astype(BF16)
                grad_ref[row, (6 + kv) * lane : (7 + kv) * lane] = dv_ref[kv, row, :].astype(BF16)
            g = grad_ref[row, :]
            for at in range(0, width, 256):
                value = dot_t(g, wa_ref[at : at + 256, :])
                part[t, :, :, at : at + 256] = value.astype(BF16).reshape(2, 128, 256)
            part[t, :, :, width:] = dot_t(g, sa_ref[...]).astype(BF16).reshape(2, 128, SIDE)

        def to_core(t):
            h, j = t // 2, t % 2
            return _remote(part.at[t], land.at[j], s_sem.at[j], r_sem.at[j], core_peer)

        def to_x(j):
            return _remote(staged.at[j], landed.at[j], s_sem.at[2 + j], r_sem.at[2 + j], x_peer)

        def leave(t):
            @pl.when(core == t // 2)
            def _():
                to_core(t).start()

        def combine(t):
            j = t % 2

            @pl.when(core == 1 - t // 2)
            def _():
                to_core(t).wait_recv()
                mine, other = (x + j) % 2, (x + j + 1) % 2
                staged[j] = (part[t, other].astype(F32) + land[j, other].astype(F32)).astype(BF16)
                to_x(j).start()
                sums[j] = part[t, mine].astype(F32) + land[j, mine].astype(F32)

        arrive(1)
        early_across()
        through_output(3)
        through_output(1)
        small_own_here()
        for j in range(2):
            small_forward(j)
        def second():
            arrive(0)
            for cp in swaps:
                cp.start()

        attention(3, second)
        leave(3)
        through_output(2)
        through_output(0)
        o_a = dot_rows(gio_ref[...], att_ref[...])[:RANK]
        o_a = jnp.concatenate(
            [o_a[:, head * lane : head * lane + HEAD_DIM] for head in range(4)], axis=1
        )
        middle_ref[:, :quarter] = o_a.astype(BF16)
        own_cols = pl.ds(pl.multiple_of(f * quarter, 128), quarter)
        g = low[:, :, :, :, own_cols].reshape(rows, quarter)
        middle_ref[:, quarter : 2 * quarter] = (ADAPTER_SCALE * dot_rows(inner_ref[...], g)[:RANK]).astype(BF16)
        for j in range(2):
            small_far(j)
        small_core()
        in_gu = jnp.zeros((SIDE, quarter), F32)
        for k in range(4):
            u = order_ref[k, :, :, own_cols].reshape(step_rows, quarter)
            in_gu += dot_rows(small_out[k].reshape(step_rows, SIDE), u)
        middle_ref[:, 2 * quarter : 3 * quarter] = in_gu[:RANK].astype(BF16)
        middle_ref[:, 3 * quarter :] = in_gu[RANK : 2 * RANK].astype(BF16)
        mid_start()
        early_finish()
        early_two[0]()

        def outputs():
            for j in range(2):
                swaps[j].wait()
                total = out_own[j] + landed_out[j].astype(F32)
                side = total[:, width:]
                out_own[j, :, width:] = side
                pos = 128 * _block(x, core, j) + lax.broadcasted_iota(jnp.int32, (128, width), 0)
                value = resid_ref[j] + total[:, :width] + dot(side.astype(BF16), sd_ref[...])
                out_tok[j] = jnp.where(pos < live, value, 0.0).astype(BF16)
                out_first(j)

        def third():
            combine(3)
            mid_across()

        attention(2, third)
        leave(2)
        outputs()
        attention(1, lambda: combine(2))
        leave(1)
        mid_finish()
        mid_two[0]()
        early_two[1]()
        attention(0, lambda: combine(1))
        leave(0)
        combine(0)
        all_b = ADAPTER_SCALE * dot_rows(inner_qkv_ref[...], grad_ref[...])
        half = HEAD_DIM // 2
        pieces = []
        for head in range(6):
            r = slice(0, RANK) if head < 4 else slice(RANK, 2 * RANK)
            for side in range(2):
                to = head * lane + side * HALF_PAD
                pieces.append(all_b[r, to : to + half])
        for head in range(2):
            to = (6 + head) * lane
            pieces.append(all_b[2 * RANK : 3 * RANK, to : to + HEAD_DIM])
        factor_ref[...] = jnp.concatenate(pieces, axis=1).astype(BF16)
        factor[0]()
        mid_two[1]()
        for j in range(2):
            cp = to_x(j)
            cp.wait_recv()
            sums[j] = sums[j] + landed[j].astype(F32)
            side_own[j] = (sums[j, :, width:] + out_own[j, :, width:]).astype(BF16)
        side_first()
        for j in range(2):
            gi = sums[j, :, width:].astype(BF16)
            gn = (sums[j, :, :width] + dot(gi, fa_ref[...])).astype(BF16).astype(F32)
            v = tok_ref[j].astype(F32)
            rms = lax.rsqrt(jnp.mean(v * v, axis=1, keepdims=True) + EPSILON)
            scaled = gn * gain_ref[...]
            mean = jnp.mean(scaled * v, axis=1, keepdims=True)
            grad = grad_resid_ref[j] + rms * scaled - v * (rms * rms * rms) * mean
            grad_tok[j] = grad.astype(BF16)
            grad_first(j)
        factor[1]()
        side_last()
        in_qkv = dot_rows(side_all[...].reshape(rows, SIDE), cut_ref[...])
        for i in range(3):
            late_ref[:, i * quarter : (i + 1) * quarter] = in_qkv[i * RANK : (i + 1) * RANK].astype(
                BF16
            )
        d_b = jnp.zeros((SIDE, quarter), F32)
        for step in range(4):
            other_x = x if step in (0, 3) else 1 - x
            for i in range(2):
                other_core = (core, 1 - core)[step == 3 or (step in (1, 2) and i == 0)]
                jj = i if step in (0, 3) else step - 1
                pos = 128 * _block(other_x, other_core, jj) + lax.broadcasted_iota(
                    jnp.int32, (128, quarter), 0
                )
                go = cot_ref[step, i, :, own_cols].astype(F32)
                go = jnp.where(pos < live, go, 0.0).astype(BF16)
                d_b += dot_rows(side_all[1 - other_core, jj, (other_x + jj) % 2], go)
        late_ref[:, 3 * quarter :] = (ADAPTER_SCALE * d_b[3 * RANK : 4 * RANK]).astype(BF16)
        late[0]()
        late[1]()
        for t in range(4):

            @pl.when(core == t // 2)
            def _():
                to_core(t).wait_send()

        for j in range(2):
            to_x(j).wait_send()
        small_last()
        early_two[2]()
        mid_two[2]()
        factor[2]()
        late[2]()
        out_last()
        grad_last()
        for cp in sends.values():
            cp.wait_send()

    vmem, hbm = pl.BlockSpec(memory_space=pltpu.VMEM), pl.BlockSpec(memory_space=pl.ANY)
    shape = jax.ShapeDtypeStruct
    own = (2, 128, wide)
    return pl.pallas_call(
        kernel,
        out_shape=[
            shape((2, 128, width), BF16),
            shape((2, 128, width), BF16),
            _spread_of(early_n),
            _spread_of(middle_n),
            _spread_of(late_n),
            _spread_of(factor_n),
            shape(_lines_of(early_n), BF16),
            shape(_lines_of(middle_n), BF16),
        ],
        in_specs=[pl.BlockSpec(memory_space=pltpu.SMEM)] + [hbm] * (4 + count),
        out_specs=[hbm] * 8,
        scratch_shapes=[pltpu.VMEM(a.shape, a.dtype) for a in big]
        + [
            pltpu.VMEM((2, 2, 2, 128, width), BF16),
            pltpu.VMEM((rows, 4 * lane), BF16),
            pltpu.VMEM((rows, SIDE), BF16),
            pltpu.VMEM((2, rows, lane), F32),
            pltpu.VMEM((2, rows, lane), F32),
            pltpu.VMEM((4,) + own, BF16),
            pltpu.VMEM((2,) + own, BF16),
            pltpu.VMEM(own, BF16),
            pltpu.VMEM(own, BF16),
            pltpu.VMEM((2, 128, SIDE), BF16),
            pltpu.VMEM((RANK, middle_n), BF16),
            pltpu.VMEM(own, F32),
            pltpu.VMEM((2, 2, 2, 128, SIDE), BF16),
            pltpu.VMEM((rows, 8 * lane), BF16),
            pltpu.VMEM(own, BF16),
            pltpu.VMEM((4, 2, 128, SIDE), BF16),
            pltpu.VMEM((RANK, late_n), BF16),
            pltpu.VMEM((RANK, factor_n), BF16),
            pltpu.VMEM((2, 128, width), BF16),
            pltpu.VMEM((2, 128, width), BF16),
            _sem(count),
            _sem(2),
            _sem(6),
            _sem(6),
            _sem(10),
            _sem(10),
        ]
        + [_sem(2), _sem(6), _sem(6)]
        + FIRST_SEMS
        + SECOND_SEMS
        + FIRST_SEMS
        + SECOND_SEMS
        + PLANE_SEMS
        + [_sem(2), _sem(6), _sem(6)]
        + [_sem(2), _sem(2), _sem(2), _sem(2)]
        + PLANE_SEMS,
        compiler_params=pltpu.CompilerParams(
            collective_id=cid, has_side_effects=True, vmem_limit_bytes=62 * 1024 * 1024
        ),
        name="attend_back",
    )(length, low_own, small_own, early, out_far, *big)


def table_call(pieces, out_rows, grad_rows, adapters):
    f32 = lambda *shape: jax.ShapeDtypeStruct(shape, F32)
    choices = 8
    outs = [
        f32(choices, 5, RANK, 1536),
        f32(choices, RANK, 1536),
        f32(choices, RANK, 4096),
        f32(choices, RANK, 1536),
        f32(choices, 2, RANK, 768),
        f32(choices, RANK, 1536),
        f32(choices, 2, RANK, 4096),
        f32(choices, RANK, 1536),
    ]
    plan = (
        ((6, 0, 1024), (6, 1, 1024), (2, None, 1024)),
        ((1, None, 384), (5, None, 384), (0, 3, 384), (0, 4, 384)),
        (
            (0, 0, 384),
            (0, 1, 384),
            (0, 2, 384),
            (7, None, 384),
        ),
        ((3, None, 384), (4, 0, 192), (4, 1, 192)),
    )

    def kernel(which, early_in, middle_in, late_in, factor_in, rows_in, grad_in, *refs):
        outs, rows_out, grad_out = refs[:8], refs[8], refs[9]
        acc, held = refs[10:18], refs[18:22]
        grad_low, grad_full, sems, load_sem = refs[22:26]
        loads = []
        for i, src in enumerate((early_in, middle_in, factor_in, late_in)):
            loads.append(pltpu.make_async_copy(src, held[(0, 1, 3, 2)[i]], load_sem.at[i]))
        grad_load = pltpu.make_async_copy(grad_in, grad_low, load_sem.at[4])
        rows_copy = pltpu.make_async_copy(rows_in, rows_out, load_sem.at[5])
        for cp in loads + [grad_load, rows_copy]:
            cp.start()

        def add(piece, ref):
            def one_slot(origin, carry):
                row = which[origin % 4 + 4 * ((origin // 4 + origin) % 2)]
                for f in range(4):
                    at = 0
                    for out, table, n in plan[piece]:
                        value = ref[origin // 4, f % 2, origin % 4, f // 2, :, at : at + n].astype(F32)
                        cols = slice(f * n, (f + 1) * n)
                        if table is None:
                            acc[out][row, :, cols] += value
                        else:
                            acc[out][row, table, :, cols] += value
                        at += n
                return carry

            lax.fori_loop(0, 8, one_slot, 0)

        def send(out):
            cp = pltpu.make_async_copy(acc[out], outs[out], sems.at[out])
            cp.start()
            return cp

        for out in range(8):
            acc[out][...] = jnp.zeros_like(acc[out])
        loads[0].wait()
        add(0, held[0])
        copies = [send(out) for out in (2, 6)]
        loads[1].wait()
        add(1, held[1])
        copies += [send(out) for out in (1, 5)]
        loads[2].wait()
        add(3, held[3])
        copies += [send(out) for out in (3, 4)]
        loads[3].wait()
        add(2, held[2])
        copies += [send(out) for out in (0, 7)]
        grad_load.wait()
        grad_full[...] = grad_low[...].astype(F32)
        last = pltpu.make_async_copy(grad_full, grad_out, load_sem.at[6])
        last.start()
        copies += [last, rows_copy]
        for cp in copies:
            cp.wait()

    hbm = pl.BlockSpec(memory_space=pl.ANY)
    return pl.pallas_call(
        kernel,
        out_shape=outs + [jax.ShapeDtypeStruct(out_rows.shape, BF16), f32(*grad_rows.shape)],
        in_specs=[pl.BlockSpec(memory_space=pltpu.SMEM)] + [hbm] * 6,
        out_specs=[hbm] * 10,
        scratch_shapes=[pltpu.VMEM(o.shape, F32) for o in outs]
        + [pltpu.VMEM(p.shape, BF16) for p in pieces]
        + [pltpu.VMEM(grad_rows.shape, BF16), pltpu.VMEM(grad_rows.shape, F32)]
        + [_sem(8), _sem(7)],
        compiler_params=pltpu.CompilerParams(vmem_limit_bytes=62 * 1024 * 1024),
        name="tables",
    )(adapters, *pieces, out_rows, grad_rows)


def rope_constants(rows):
    half = HEAD_DIM // 2
    freqs = np.float32(ROPE_BASE) ** (-(np.arange(half, dtype=np.float32) * 2.0 / HEAD_DIM))
    angles = np.arange(rows).astype(np.float32)[:, None] * freqs.astype(np.float32)[None, :]
    cos = np.cos(angles.astype(np.float64)).astype(np.float32)
    sin = np.sin(angles.astype(np.float64)).astype(np.float32)
    gap = np.zeros((rows, HALF_PAD - half), np.float32)
    cosine = np.concatenate([cos, gap, cos, gap], axis=1)
    sine = np.concatenate([-sin, gap, sin, gap], axis=1)
    return jnp.asarray(cosine), jnp.asarray(sine)


def dot(left, right):
    return jnp.dot(left, right, preferred_element_type=F32)


def dot_t(left, right):
    return lax.dot_general(left, right, (((1,), (1,)), ((), ())), preferred_element_type=F32)


def dot_rows(left, right):
    return lax.dot_general(left, right, (((0,), (0,)), ((), ())), preferred_element_type=F32)


def side_pad(value, before=0):
    return jnp.pad(value, ((0, 0), (before, SIDE - before - value.shape[1])))


def blocks(value):
    return value.reshape(2, 2, 2, 128, value.shape[-1])


def own_blocks(value):
    return value.reshape(2, 128, value.shape[-1])


def flat(value):
    return value.reshape(-1, value.shape[-1])


def slot_local(
    tokens,
    cotangent,
    lengths,
    slot_adapter_index,
    attention_norm_gain,
    feedforward_norm_gain,
    query_weight,
    key_weight,
    value_weight,
    output_weight,
    gate_weight,
    up_weight,
    down_weight,
    adapter_input_first,
    adapter_output_first,
    adapter_down_first,
    adapter_query_second,
    adapter_key_value_second,
    adapter_output_second,
    adapter_gate_up_second,
    adapter_down_second,
):
    width = tokens.shape[-1]
    quarter = width // 4
    c = lax.axis_index("ctx")
    f = lax.axis_index("fsdp")
    slot = _slot_of(c)
    length = lax.dynamic_slice_in_dim(lengths, slot, 1, 0)
    adapter = slot_adapter_index[slot]

    def cut(value, axis, size):
        return lax.dynamic_slice_in_dim(value, f * size, size, axis)

    rows = 4 * 2 * tokens.shape[1]
    cosine, sine = rope_constants(rows)
    turned = lambda t: jnp.swapaxes(t, -1, -2)
    second_kv = adapter_key_value_second
    second_kv = lax.dynamic_slice_in_dim(second_kv, f * key_weight.shape[1], key_weight.shape[1], 3)
    (
        resid,
        normed_two_own,
        inner_o,
        tok_own,
        cot_order,
        _,
        qkv,
        stats,
        attn_b,
        one_cut,
        inner_qkv,
        weight_all,
        out_w,
        second_all,
        first_all,
        first_gu,
        second_g,
        second_u,
        first_d,
        second_d,
        first_o,
        second_o,
    ) = front_call(
        tokens,
        cotangent,
        length,
        adapter.reshape(1),
        jnp.stack([attention_norm_gain, feedforward_norm_gain]),
        query_weight,
        key_weight,
        value_weight,
        output_weight,
        (
            turned(adapter_input_first),
            turned(adapter_output_first),
            turned(adapter_down_first),
            adapter_query_second,
            second_kv,
            adapter_output_second,
            adapter_gate_up_second,
            adapter_down_second,
        ),
        cosine,
        sine,
        0,
    )
    grad_resid, grad_low_own, small, out_sums, out_far, order, early = feed_forward(
        normed_two_own,
        cot_order,
        resid,
        feedforward_norm_gain[None, :],
        length,
        (gate_weight, up_weight, down_weight),
        (first_gu, second_g, second_u, first_d, second_d),
        3,
    )
    out_rows, grad_rows, early, middle, late, factors = attend_back_call(
        grad_low_own,
        small,
        early,
        out_far,
        length,
        (out_sums, resid, tok_own, grad_resid, attention_norm_gain[None, :]),
        (
            qkv,
            stats,
            attn_b,
            flat(inner_o),
            order,
            cosine,
            sine,
            out_w,
            first_o,
            second_o,
            weight_all,
            second_all,
            first_all,
            second_d,
            one_cut,
            inner_qkv,
            cot_order,
        ),
        10,
    )[:6]
    full = table_call((early, middle, late, factors), out_rows, grad_rows, slot_adapter_index)
    turn = lambda t: jnp.swapaxes(t, -1, -2)
    return (
        full[8],
        full[9],
        turn(full[0]),
        turn(full[1]),
        turn(full[2]),
        full[3],
        full[4],
        full[5],
        full[6],
        full[7],
    )


def solution(mesh):
    one_slot = mesh.shape["ctx"] == 8 and mesh.shape["fsdp"] == 4
    return jax.shard_map(
        slot_local if one_slot else local,
        mesh=mesh,
        in_specs=(
            P("fsdp", "ctx", None),
            P("fsdp", "ctx", None),
            P(),
            P(),
            P(),
            P(),
            P(None, "fsdp"),
            P(None, "fsdp"),
            P(None, "fsdp"),
            P("fsdp", None),
            P(None, "fsdp"),
            P(None, "fsdp"),
            P("fsdp", None),
            P(),
            P(),
            P(),
            P(),
            P(),
            P(),
            P(),
            P(),
        ),
        out_specs=(
            P("fsdp", "ctx", None),
            P("fsdp", "ctx", None),
            P(),
            P(),
            P(),
            P(),
            P(),
            P(),
            P(),
            P(),
        ),
        check_vma=False,
    )
```

```python
import math

import jax
import jax.numpy as jnp
import numpy as np
from jax import lax
from jax.experimental import pallas as pl
from jax.experimental.pallas import tpu as pltpu
from jax.sharding import PartitionSpec as P

QUERY_HEADS = 16
KEY_VALUE_HEADS = 8
HEAD_DIM = 96


EPSILON = 1e-05
NEGATIVE = -1e30
ADAPTER_SCALE = 0.5
ROPE_BASE = 100000.0


def from_behind(x, axis, by):
    size = lax.axis_size(axis)
    return lax.ppermute(x, axis, [(i, (i + by) % size) for i in range(size)])


def rope_tables(positions, head_size):
    half_size = head_size // 2
    freqs = ROPE_BASE ** (-(jnp.arange(half_size, dtype=jnp.float32) * 2.0 / head_size))
    angles = positions.astype(jnp.float32)[:, None] * freqs[None, :]
    return (jnp.cos(angles)[:, None, :], jnp.sin(angles)[:, None, :])


def apply_rotation(values, cosine_table, sine_table):
    half_size = values.shape[-1] // 2
    first_half = values[..., :half_size]
    second_half = values[..., half_size:]
    return jnp.concatenate(
        [
            first_half * cosine_table - second_half * sine_table,
            second_half * cosine_table + first_half * sine_table,
        ],
        axis=-1,
    )


def rotate_back(gradient_tree, cosine_table, sine_table):
    half_size = gradient_tree.shape[-1] // 2
    first_half = gradient_tree[..., :half_size]
    second_half = gradient_tree[..., half_size:]
    return jnp.concatenate(
        [
            first_half * cosine_table + second_half * sine_table,
            second_half * cosine_table - first_half * sine_table,
        ],
        axis=-1,
    )


def rms_factor(values):
    return lax.rsqrt(jnp.mean(values * values, axis=-1, keepdims=True) + EPSILON)


def norm_back(values, factor, gain, grad_norm):
    scaled = grad_norm * gain
    return factor * scaled - values * factor**3 * jnp.mean(scaled * values, axis=-1, keepdims=True)


def pick_rows(onehot, table):
    return jnp.einsum("sa,a...->s...", onehot, table, preferred_element_type=jnp.float32).astype(
        jnp.bfloat16
    )


def spread_rows(onehot, gradient_tree):
    return jnp.einsum("sa,s...->a...", onehot, gradient_tree, precision=lax.Precision.HIGHEST)


def direct_product(input_rows, weight_matrix):
    return jnp.einsum("std,do->sto", input_rows, weight_matrix, preferred_element_type=jnp.float32)


def direct_back(gradient_tree, weight_matrix):
    return jnp.einsum(
        "sto,do->std", gradient_tree, weight_matrix, preferred_element_type=jnp.float32
    )


def inner_product_part(input_rows, down):
    return jnp.einsum("std,sdr->str", input_rows, down, preferred_element_type=jnp.float32)


def inner_back(gradient_tree, upward_rows):
    return ADAPTER_SCALE * jnp.einsum(
        "sto,sro->str", gradient_tree, upward_rows, preferred_element_type=jnp.float32
    )


def through_down(grad_inner, down):
    return jnp.einsum("str,sdr->std", grad_inner, down, preferred_element_type=jnp.float32)


def down_grad(input_rows, grad_inner):
    return jnp.einsum("std,str->sdr", input_rows, grad_inner, preferred_element_type=jnp.float32)


def upward_grad(inner_rows, gradient_tree):
    return ADAPTER_SCALE * jnp.einsum(
        "jvp,jvx->jpx", inner_rows, gradient_tree, preferred_element_type=jnp.float32
    )


def upward_apply(inner_rows, upward_rows):
    return ADAPTER_SCALE * jnp.einsum(
        "str,sro->sto", inner_rows, upward_rows, preferred_element_type=jnp.float32
    )


def project(input_rows, weight_matrix, down, upward_rows):
    inner_rows = inner_product_part(input_rows, down).astype(jnp.bfloat16)
    return (
        inner_rows,
        direct_product(input_rows, weight_matrix) + upward_apply(inner_rows, upward_rows),
    )


def project_back(input_rows, grad_output, weight_matrix, down, upward_rows, inner_rows):
    grad_upward = upward_grad(inner_rows, grad_output)
    grad_inner = inner_back(grad_output, upward_rows).astype(jnp.bfloat16)
    grad_down = down_grad(input_rows, grad_inner)
    grad_inputs = direct_back(grad_output, weight_matrix) + through_down(grad_inner, down)
    return (grad_inputs, grad_down, grad_upward)


def allowed_mask(key_start, key_count, query_pos, lengths):
    key_pos = key_start + jnp.arange(key_count, dtype=jnp.int32)
    causal = key_pos[None, :] <= query_pos[:, None]
    live = key_pos[None, :] < lengths[:, None]
    return (causal[None, :, :] & live[:, None, :])[:, None, None, :, :]


def attend_block(state, key_block, value_block, key_start, query_head_rows, query_pos, lengths):
    run_max, run_sum, run_acc = state
    scale = query_head_rows.shape[-1] ** (-0.5)
    scores = (
        jnp.einsum(
            "sqhgd,skhd->shgqk", query_head_rows, key_block, preferred_element_type=jnp.float32
        )
        * scale
    )
    allowed = allowed_mask(key_start, key_block.shape[1], query_pos, lengths)
    new_max = jnp.maximum(run_max, jnp.max(jnp.where(allowed, scores, NEGATIVE), axis=-1))
    weights = jnp.where(allowed, jnp.exp(scores - new_max[..., None]), 0.0)
    factor = jnp.exp(run_max - new_max)
    new_sum = run_sum * factor + jnp.sum(weights, axis=-1)
    update = jnp.einsum(
        "shgqk,skhd->shgqd",
        weights.astype(jnp.bfloat16),
        value_block,
        preferred_element_type=jnp.float32,
    )
    return (new_max, new_sum, run_acc * factor[..., None] + update)


def attend_back(
    key_block,
    value_block,
    key_start,
    query_head_rows,
    grad_heads,
    log_total,
    row_dot,
    query_pos,
    lengths,
):
    scale = query_head_rows.shape[-1] ** (-0.5)
    scores = (
        jnp.einsum(
            "sqhgd,skhd->shgqk", query_head_rows, key_block, preferred_element_type=jnp.float32
        )
        * scale
    )
    allowed = allowed_mask(key_start, key_block.shape[1], query_pos, lengths)
    probs = jnp.where(allowed, jnp.exp(scores - log_total[..., None]), 0.0)
    grad_probs = jnp.einsum(
        "sqhgd,skhd->shgqk", grad_heads, value_block, preferred_element_type=jnp.float32
    )
    grad_scores = (probs * (grad_probs - row_dot[..., None])).astype(jnp.bfloat16)
    grad_query = scale * jnp.einsum(
        "shgqk,skhd->sqhgd", grad_scores, key_block, preferred_element_type=jnp.float32
    )
    grad_key = scale * jnp.einsum(
        "shgqk,sqhgd->skhd", grad_scores, query_head_rows, preferred_element_type=jnp.float32
    )
    grad_value = jnp.einsum(
        "shgqk,sqhgd->skhd",
        probs.astype(jnp.bfloat16),
        grad_heads,
        preferred_element_type=jnp.float32,
    )
    return (grad_query, grad_key, grad_value)


def attend_forward(query_head_rows, key_head_rows, value_head_rows, lengths_used, query_pos):
    slots, rows, kv_heads, group_size, head_size = query_head_rows.shape
    key_flat = key_head_rows.reshape(slots, rows, kv_heads * head_size)
    value_flat = value_head_rows.reshape(slots, rows, kv_heads * head_size)
    stat_shape = (slots, kv_heads, group_size, rows)
    initial = (
        jnp.full(stat_shape, NEGATIVE, jnp.float32),
        jnp.zeros(stat_shape, jnp.float32),
        jnp.zeros(stat_shape + (head_size,), jnp.float32),
    )
    part_keys = lax.all_gather(key_flat, "ctx", axis=1, tiled=True)
    part_values = lax.all_gather(value_flat, "ctx", axis=1, tiled=True)
    piece_rows = part_keys.shape[1]
    part_keys = part_keys.reshape(slots, piece_rows, kv_heads, head_size)
    part_values = part_values.reshape(slots, piece_rows, kv_heads, head_size)
    span_rows = math.gcd(piece_rows, 4 * rows)

    def inner_step(block_index, inner_state):
        sub_keys = lax.dynamic_slice_in_dim(part_keys, block_index * span_rows, span_rows, 1)
        sub_values = lax.dynamic_slice_in_dim(part_values, block_index * span_rows, span_rows, 1)
        return attend_block(
            inner_state,
            sub_keys,
            sub_values,
            block_index * span_rows,
            query_head_rows,
            query_pos,
            lengths_used,
        )

    run_max, run_sum, run_acc = lax.fori_loop(0, piece_rows // span_rows, inner_step, initial)
    log_total = run_max + jnp.log(run_sum)
    attended = jnp.transpose(run_acc / run_sum[..., None], (0, 3, 1, 2, 4))
    return (attended, log_total)


def attend_backward(
    query_head_rows,
    key_head_rows,
    value_head_rows,
    grad_heads,
    attended,
    log_total,
    lengths_used,
    query_pos,
):
    ctx_count = lax.axis_size("ctx")
    own_index = lax.axis_index("ctx")
    rows = query_head_rows.shape[1]
    row_dot = jnp.transpose(
        jnp.sum(grad_heads.astype(jnp.float32) * attended, axis=-1), (0, 2, 3, 1)
    )

    def cycle_step(step_index, carried):
        carried_keys, carried_values, grad_query, grad_key, grad_value = carried
        block_id = (own_index + step_index) % ctx_count
        query_part, key_part, value_part = attend_back(
            carried_keys,
            carried_values,
            block_id * rows,
            query_head_rows,
            grad_heads,
            log_total,
            row_dot,
            query_pos,
            lengths_used,
        )
        grad_key, grad_value = (
            from_behind((grad_key + key_part).astype(jnp.bfloat16), "ctx", -1).astype(jnp.float32),
            from_behind((grad_value + value_part).astype(jnp.bfloat16), "ctx", -1).astype(
                jnp.float32
            ),
        )
        carried_keys, carried_values = from_behind((carried_keys, carried_values), "ctx", -1)
        return (carried_keys, carried_values, grad_query + query_part, grad_key, grad_value)

    key_zeros = jnp.zeros(key_head_rows.shape, jnp.float32)
    start_state = (
        key_head_rows,
        value_head_rows,
        jnp.zeros(query_head_rows.shape, jnp.float32),
        key_zeros,
        key_zeros,
    )
    carried = lax.fori_loop(0, ctx_count, cycle_step, start_state)
    return (carried[2], carried[3], carried[4])


def table_total(rotation_tables):
    return lax.psum(rotation_tables, ("ctx", "fsdp"))


def local(
    tokens,
    cotangent,
    lengths,
    slot_adapter_index,
    attention_norm_gain,
    feedforward_norm_gain,
    query_weight,
    key_weight,
    value_weight,
    output_weight,
    gate_weight,
    up_weight,
    down_weight,
    adapter_input_first,
    adapter_output_first,
    adapter_down_first,
    adapter_query_second,
    adapter_key_value_second,
    adapter_output_second,
    adapter_gate_up_second,
    adapter_down_second,
):
    slot_count, tok_rows, model_width = tokens.shape
    head_groups = QUERY_HEADS // KEY_VALUE_HEADS
    own_index = lax.axis_index("ctx")
    fsdp_index = lax.axis_index("fsdp")
    query_pos = own_index * tok_rows + jnp.arange(tok_rows, dtype=jnp.int32)
    cosine_table, sine_table = rope_tables(query_pos, HEAD_DIM)
    own_lengths = lax.dynamic_slice_in_dim(lengths, fsdp_index * slot_count, slot_count, 0)
    own_adapters = lax.dynamic_slice_in_dim(
        slot_adapter_index, fsdp_index * slot_count, slot_count, 0
    )
    valid = query_pos[None, :] < own_lengths[:, None]
    adapter_labels = jnp.arange(adapter_input_first.shape[0], dtype=jnp.int32)
    onehot_own = own_adapters[:, None] == adapter_labels[None, :]
    owned_low_rank = onehot_own.astype(jnp.bfloat16)
    own_full = onehot_own.astype(jnp.float32)
    tokens_f = tokens.astype(jnp.float32)
    factor_one = rms_factor(tokens_f)
    normed_one = (tokens_f * factor_one * attention_norm_gain).astype(jnp.bfloat16)
    grad_out = jnp.where(valid[..., None], cotangent, jnp.zeros((), jnp.bfloat16))
    input_first = pick_rows(owned_low_rank, adapter_input_first)
    output_second = pick_rows(owned_low_rank, adapter_output_second)
    down_second = pick_rows(owned_low_rank, adapter_down_second)
    output_first = pick_rows(owned_low_rank, adapter_output_first)
    down_first = pick_rows(owned_low_rank, adapter_down_first)
    query_second = pick_rows(owned_low_rank, adapter_query_second)
    key_value_second = pick_rows(owned_low_rank, adapter_key_value_second)
    gate_up_second = pick_rows(owned_low_rank, adapter_gate_up_second)
    weight_q, weight_k, weight_v, weight_gate, weight_up, weight_o, weight_down = (
        lax.all_gather(query_weight, "fsdp", axis=1, tiled=True),
        lax.all_gather(key_weight, "fsdp", axis=1, tiled=True),
        lax.all_gather(value_weight, "fsdp", axis=1, tiled=True),
        lax.all_gather(gate_weight, "fsdp", axis=1, tiled=True),
        lax.all_gather(up_weight, "fsdp", axis=1, tiled=True),
        lax.all_gather(output_weight, "fsdp", axis=0, tiled=True),
        lax.all_gather(down_weight, "fsdp", axis=0, tiled=True),
    )
    inner_q, projected_queries = project(normed_one, weight_q, input_first[:, 0], query_second)
    inner_k, projected_keys = project(
        normed_one, weight_k, input_first[:, 1], key_value_second[:, 0]
    )
    inner_v, projected_values = project(
        normed_one, weight_v, input_first[:, 2], key_value_second[:, 1]
    )
    query_head_rows = apply_rotation(
        projected_queries.reshape(slot_count, tok_rows, -1, HEAD_DIM), cosine_table, sine_table
    ).astype(jnp.bfloat16)
    query_head_rows = query_head_rows.reshape(slot_count, tok_rows, -1, head_groups, HEAD_DIM)
    key_head_rows = apply_rotation(
        projected_keys.reshape(slot_count, tok_rows, -1, HEAD_DIM), cosine_table, sine_table
    ).astype(jnp.bfloat16)
    value_head_rows = projected_values.astype(jnp.bfloat16).reshape(
        slot_count, tok_rows, -1, HEAD_DIM
    )
    attended, log_total = attend_forward(
        query_head_rows, key_head_rows, value_head_rows, own_lengths, query_pos
    )
    attn_b = attended.reshape(slot_count, tok_rows, -1).astype(jnp.bfloat16)
    inner_o, proj_o = project(attn_b, weight_o, output_first, output_second)
    resid = tokens_f + proj_o
    factor_two = rms_factor(resid)
    normed_two = (resid * factor_two * feedforward_norm_gain).astype(jnp.bfloat16)
    inner_gate, gate = project(normed_two, weight_gate, input_first[:, 3], gate_up_second[:, 0])
    inner_up, up_proj = project(normed_two, weight_up, input_first[:, 4], gate_up_second[:, 1])
    sigmoid_gate = jax.nn.sigmoid(gate)
    hidden = (gate * sigmoid_gate * up_proj).astype(jnp.bfloat16)
    inner_down, proj_down = project(hidden, weight_down, down_first, down_second)
    out_tokens = jnp.where(valid[..., None], resid + proj_down, 0.0).astype(jnp.bfloat16)
    grad_hidden, grad_da, grad_db = project_back(
        hidden, grad_out, weight_down, down_first, down_second, inner_down
    )
    grad_gate = (grad_hidden * up_proj * sigmoid_gate * (1.0 + gate * (1.0 - sigmoid_gate))).astype(
        jnp.bfloat16
    )
    grad_up = (grad_hidden * gate * sigmoid_gate).astype(jnp.bfloat16)
    from_gate, grad_ga, grad_gb = project_back(
        normed_two, grad_gate, weight_gate, input_first[:, 3], gate_up_second[:, 0], inner_gate
    )
    from_up, grad_ua, grad_ub = project_back(
        normed_two, grad_up, weight_up, input_first[:, 4], gate_up_second[:, 1], inner_up
    )
    grad_normed_two = (from_gate + from_up).astype(jnp.bfloat16).astype(jnp.float32)
    grad_resid = grad_out.astype(jnp.float32) + norm_back(
        resid, factor_two, feedforward_norm_gain, grad_normed_two
    )
    grad_resid_low = grad_resid.astype(jnp.bfloat16)
    from_attn, grad_oa, grad_ob = project_back(
        attn_b, grad_resid_low, weight_o, output_first, output_second, inner_o
    )
    grad_heads = from_attn.astype(jnp.bfloat16).reshape(attended.shape)
    grad_query, grad_key, grad_value = attend_backward(
        query_head_rows,
        key_head_rows,
        value_head_rows,
        grad_heads,
        attended,
        log_total,
        own_lengths,
        query_pos,
    )
    grad_proj_q = (
        rotate_back(
            grad_query.reshape(slot_count, tok_rows, -1, HEAD_DIM), cosine_table, sine_table
        )
        .astype(jnp.bfloat16)
        .reshape(slot_count, tok_rows, -1)
    )
    grad_proj_k = (
        rotate_back(grad_key, cosine_table, sine_table)
        .astype(jnp.bfloat16)
        .reshape(slot_count, tok_rows, -1)
    )
    grad_proj_v = grad_value.astype(jnp.bfloat16).reshape(slot_count, tok_rows, -1)
    from_query, grad_qa, grad_qb = project_back(
        normed_one, grad_proj_q, weight_q, input_first[:, 0], query_second, inner_q
    )
    from_key, grad_ka, grad_kb = project_back(
        normed_one, grad_proj_k, weight_k, input_first[:, 1], key_value_second[:, 0], inner_k
    )
    from_value, grad_va, grad_vb = project_back(
        normed_one, grad_proj_v, weight_v, input_first[:, 2], key_value_second[:, 1], inner_v
    )
    grad_normed_one = (from_query + from_key + from_value).astype(jnp.bfloat16).astype(jnp.float32)
    grad_tokens = grad_resid + norm_back(tokens_f, factor_one, attention_norm_gain, grad_normed_one)
    slot_grads = (
        jnp.stack([grad_qa, grad_ka, grad_va, grad_ga, grad_ua], axis=1),
        grad_oa,
        grad_da,
        grad_qb,
        jnp.stack([grad_kb, grad_vb], axis=1),
        grad_ob,
        jnp.stack([grad_gb, grad_ub], axis=1),
        grad_db,
    )
    summed = table_total(tuple((spread_rows(own_full, entry_item) for entry_item in slot_grads)))
    return (
        out_tokens,
        grad_tokens,
        summed[0],
        summed[1],
        summed[2],
        summed[3],
        summed[4],
        summed[5],
        summed[6],
        summed[7],
    )


BF16 = jnp.bfloat16
F32 = jnp.float32
MESH_ID = pl.DeviceIdType.MESH
RANK = 16
SIDE = 128
PAD_HEAD = 128
HALF_PAD = 64


def _sem(count):
    return pltpu.SemaphoreType.DMA((count,))


def _place():
    c = lax.axis_index("ctx")
    f = lax.axis_index("fsdp")
    x = f // 2
    core = f % 2
    return c, f, x, core, (c, 2 * x + 1 - core), (c, 2 * (1 - x) + core)


def _slot_of(c):
    return c // 2 + 4 * ((c // 2 + c) % 2)


def _group_of(slot):
    return 2 * (slot % 4) + (slot // 4 + slot) % 2


def _block(x, core, j):
    return 4 * (1 - core) + 2 * j + (x + j) % 2


def _owner(b):
    return 2 * ((b // 2 + b) % 2) + 1 - b // 4


def _greet(targets):
    barrier = pltpu.get_barrier_semaphore()
    for target in targets:
        pl.semaphore_signal(barrier, inc=1, device_id=target, device_id_type=MESH_ID)
    pl.semaphore_wait(barrier, len(targets))


def _remote(src, dst, send, recv, target):
    return pltpu.make_async_remote_copy(
        src_ref=src, dst_ref=dst, send_sem=send, recv_sem=recv, device_id=target, device_id_type=MESH_ID
    )


def _comm_call(kernel, ins, outs, scratch, cid, name, in_space=pl.ANY, out_space=pl.ANY, vmem=None):
    return pl.pallas_call(
        kernel,
        out_shape=outs,
        in_specs=[pl.BlockSpec(memory_space=in_space)] * len(ins),
        out_specs=jax.tree.map(lambda _: pl.BlockSpec(memory_space=out_space), outs),
        scratch_shapes=scratch,
        compiler_params=pltpu.CompilerParams(
            collective_id=cid, has_side_effects=True, vmem_limit_bytes=vmem
        ),
        name=name,
    )(*ins)


def _gather_steps(ins, outs, own_sem, send_sem, recv_sem, place):
    c, f, x, core, core_peer, x_peer = place
    h = 1 - core
    count = len(ins)
    local = []
    sends = []

    def first():
        for base, target in ((0, x_peer), (2 * count, core_peer)):
            for i in range(count):
                for j in range(2):
                    k = base + i * 2 + j
                    cp = _remote(
                        ins[i].at[j], outs[i].at[h, j, (x + j) % 2], send_sem.at[k], recv_sem.at[k], target
                    )
                    cp.start()
                    sends.append(cp)
        for i in range(count):
            for j in range(2):
                lc = pltpu.make_async_copy(
                    ins[i].at[j], outs[i].at[h, j, (x + j) % 2], own_sem.at[i * 2 + j]
                )
                lc.start()
                local.append(lc)

    def last():
        forwards = []
        for i in range(count):
            for j in range(2):
                k = i * 2 + j
                sends[k].wait_recv()
                cp = _remote(
                    outs[i].at[h, j, (x + j + 1) % 2],
                    outs[i].at[h, j, (x + j + 1) % 2],
                    send_sem.at[4 * count + k],
                    recv_sem.at[4 * count + k],
                    core_peer,
                )
                cp.start()
                forwards.append(cp)
        for k in range(2 * count):
            sends[2 * count + k].wait_recv()
            forwards[k].wait_recv()
        for cp in sends + forwards:
            cp.wait_send()
        for lc in local:
            lc.wait()

    return first, last


def _ctx_first(piece, lines, own_sem, send_sem, recv_sem, place):
    c, f, x, core, core_peer, x_peer = place
    z, y = c // 2, c % 2
    sends = []
    local = []

    def start():
        lc = pltpu.make_async_copy(piece, lines.at[z, x], own_sem)
        lc.start()
        local.append(lc)
        cp = _remote(piece, lines.at[z, x], send_sem.at[0], recv_sem.at[0], x_peer)
        cp.start()
        sends.append(cp)

    def spread():
        local[0].wait()
        sends[0].wait_recv()
        for step in range(1, 4):
            cp = _remote(
                lines.at[z],
                lines.at[z],
                send_sem.at[step],
                recv_sem.at[step],
                (2 * ((z + step) % 4) + y, f),
            )
            cp.start()
            sends.append(cp)

    def finish():
        for cp in sends[1:]:
            cp.wait_recv()
        for cp in sends:
            cp.wait_send()

    return start, spread, finish


def _ctx_second(lines, out, own_sem, send_sem, recv_sem, place):
    c, f, x, core, core_peer, x_peer = place
    z, y = c // 2, c % 2
    y_peer = (2 * z + 1 - y, f)
    sends = []
    local = []

    def start():
        lc = pltpu.make_async_copy(lines, out.at[y, core], own_sem)
        lc.start()
        local.append(lc)
        for k, target in ((0, y_peer), (1, core_peer)):
            cp = _remote(lines, out.at[y, core], send_sem.at[k], recv_sem.at[k], target)
            cp.start()
            sends.append(cp)

    def share():
        sends[0].wait_recv()
        cp = _remote(
            out.at[1 - y, core], out.at[1 - y, core], send_sem.at[2], recv_sem.at[2], core_peer
        )
        cp.start()
        sends.append(cp)

    def finish():
        sends[1].wait_recv()
        sends[2].wait_recv()
        for cp in sends:
            cp.wait_send()
        local[0].wait()

    return start, share, finish


def _ctx_planes(piece, out, own_sem, send_sem, recv_sem, place):
    c, f, x, core, core_peer, x_peer = place
    z, y = c // 2, c % 2
    y_peer = (2 * z + 1 - y, f)
    sends = {}
    local = []

    def send(k, src, dst, target):
        cp = _remote(src, dst, send_sem.at[k], recv_sem.at[k], target)
        cp.start()
        sends[k] = cp

    def spot(yy, zz):
        return out.at[yy, core, zz, x]

    def start():
        lc = pltpu.make_async_copy(piece, spot(y, z), own_sem)
        lc.start()
        local.append(lc)
        for step in range(1, 4):
            send(step, piece, spot(y, z), (2 * ((z + step) % 4) + y, f))
        send(4, piece, spot(y, z), y_peer)
        send(8, piece, spot(y, z), x_peer)

    def forward():
        for step in range(1, 4):
            sends[step].wait_recv()
            at = spot(y, (z + 4 - step) % 4)
            send(4 + step, at, at, y_peer)
            send(8 + step, at, at, x_peer)
        for step in range(4):
            sends[4 + step].wait_recv()
            at = spot(1 - y, (z + 4 - step) % 4)
            send(12 + step, at, at, x_peer)

    def finish():
        local[0].wait()
        for half in range(2):
            for step in range(4):
                sends[8 + 4 * half + step].wait_recv()
            yy = 1 - y if half else y
            send(16 + half, out.at[yy, core], out.at[yy, core], core_peer)
        for half in range(2):
            sends[16 + half].wait_recv()
        for cp in sends.values():
            cp.wait_send()

    return start, forward, finish


def _z_peers(place):
    c, f = place[:2]
    return [(2 * ((c // 2 + step) % 4) + c % 2, f) for step in range(1, 4)]


def _y_peer(place):
    c, f = place[:2]
    return (2 * (c // 2) + 1 - c % 2, f)


def _lines_of(n):
    return (4, 2, RANK, n)


def _spread_of(n):
    return jax.ShapeDtypeStruct((2, 2, 4, 2, RANK, n), BF16)


FIRST_SEMS = [pltpu.SemaphoreType.DMA(()), _sem(4), _sem(4)]
SECOND_SEMS = [pltpu.SemaphoreType.DMA(()), _sem(3), _sem(3)]
PLANE_SEMS = [pltpu.SemaphoreType.DMA(()), _sem(18), _sem(18)]


def _order_steps(own, order, own_sem, send_sem, recv_sem, place):
    core_peer, x_peer = place[4:]
    sends, local, forwards = [], [], []

    def first():
        for j in range(2):
            cp = _remote(own.at[j], order.at[1 + j, 1], send_sem.at[j], recv_sem.at[j], x_peer)
            cp.start()
            sends.append(cp)
        for j in range(2):
            cp = _remote(
                own.at[j], order.at[3, j], send_sem.at[2 + j], recv_sem.at[2 + j], core_peer
            )
            cp.start()
            sends.append(cp)
        for j in range(2):
            lc = pltpu.make_async_copy(own.at[j], order.at[0, j], own_sem.at[j])
            lc.start()
            local.append(lc)

    def forward(j):
        sends[j].wait_recv()
        cp = _remote(
            order.at[1 + j, 1],
            order.at[1 + j, 0],
            send_sem.at[4 + j],
            recv_sem.at[4 + j],
            core_peer,
        )
        cp.start()
        forwards.append(cp)

    def own_here():
        for lc in local:
            lc.wait()

    def core_here():
        for j in range(2):
            sends[2 + j].wait_recv()

    def far_here(j):
        forwards[j].wait_recv()

    def last():
        for cp in sends + forwards:
            cp.wait_send()

    return first, forward, own_here, core_here, far_here, last


def _order_all(own, order, sems, place):
    first, forward, own_here, core_here, far_here, last = _order_steps(own, order, *sems, place)
    first()
    own_here()
    for j in range(2):
        forward(j)
    core_here()
    for j in range(2):
        far_here(j)
    last()


def feed_forward(own, cot, resid, gain, length, weights, adapters, cid):
    gate_w, up_w, down_w = weights
    width, units = gate_w.shape
    wide = width + SIDE
    tile = 256

    loads_in = tuple(weights) + tuple(adapters) + (cot,)
    count = len(loads_in)

    def kernel(*refs):
        len_ref, own_ref, resid_ref, gain_ref = refs[:4]
        loads_hbm = refs[4 : 4 + count]
        grad_resid, grad_low, small, out_own, out_far, order, early = refs[4 + count : 11 + count]
        refs = refs[11 + count :]
        gate_ref, up_ref, down_ref, first_ref, sg_ref, su_ref, fd_ref, sd_ref, go_ref = refs[:count]
        (
            sums,
            hid_s,
            gg_s,
            gu_s,
            in_s,
            gid_s,
            part,
            out_part,
            near,
            out_near,
            far,
            out_land,
            staged,
            landed,
            load_sem,
            own_sem,
            send_sem,
            recv_sem,
            s_sem,
            r_sem,
        ) = refs[count:]
        place = _place()
        core_peer, x_peer = place[4:]
        loads = []
        for i in range(count):
            cp = pltpu.make_async_copy(loads_hbm[i], refs[i], load_sem.at[i])
            cp.start()
            loads.append(cp)
        _greet([core_peer, x_peer])
        first, forward, own_here, core_here, far_here, last = _order_steps(
            own_ref, order, own_sem, send_sem, recv_sem, place
        )
        first()
        copies = []
        c, f, x, core = place[:4]
        live = len_ref[_slot_of(c)]

        def masked(step):
            other_x = x if step in (0, 3) else 1 - x
            pieces = []
            for k in range(2):
                other_core = (core, 1 - core)[step == 3 or (step in (1, 2) and k == 0)]
                j = k if step in (0, 3) else step - 1
                pos = 128 * _block(other_x, other_core, j) + lax.broadcasted_iota(jnp.int32, (128, width), 0)
                pieces.append(jnp.where(pos < live, go_ref[step, k].astype(F32), 0.0).astype(BF16))
            return pieces

        def work(step):
            rows = order[step].reshape(2 * 128, width)
            pieces = masked(step)
            for k in range(2):
                go_ref[step, k] = pieces[k]
            go = go_ref[step].reshape(2 * 128, width)
            inner = dot_t(rows, first_ref[...]).astype(BF16)
            gid = dot_t(go, sd_ref[...]).astype(BF16)
            in_s[step] = inner
            gid_s[step] = gid
            for at in range(0, units, tile):
                cols = slice(at, at + tile)
                gate = dot(rows, gate_ref[:, cols]) + dot(inner, sg_ref[:, cols])
                up = dot(rows, up_ref[:, cols]) + dot(inner, su_ref[:, cols])
                grad = dot_t(go, down_ref[cols, :]) + dot(gid, fd_ref[:, cols])
                sig = 0.5 * jnp.tanh(0.5 * gate) + 0.5
                silu = gate * sig
                hid_s[step, :, cols] = (silu * up).astype(BF16)
                gg_s[step, :, cols] = (grad * up * sig * (1.0 + gate * (1.0 - sig))).astype(BF16)
                gu_s[step, :, cols] = (grad * silu).astype(BF16)
            gg, gu = gg_s[step], gu_s[step]
            for at in range(0, width, tile):
                cols = slice(at, at + tile)
                value = dot_t(gg, gate_ref[cols, :]) + dot_t(gu, up_ref[cols, :])
                if step == 0:
                    sums[:, :, cols] = value.reshape(2, 128, tile)
                else:
                    part[step - 1, :, :, cols] = value.astype(BF16).reshape(2, 128, tile)
            value = dot_t(gg, sg_ref[...]) + dot_t(gu, su_ref[...])
            if step == 0:
                sums[:, :, width:] = value.reshape(2, 128, SIDE)
            else:
                part[step - 1, :, :, width:] = value.astype(BF16).reshape(2, 128, SIDE)

        def down(step):
            hid = hid_s[step]
            for at in range(0, width, tile):
                cols = slice(at, at + tile)
                out = dot(hid, down_ref[:, cols])
                if step == 0:
                    out_own[:, :, cols] = out.reshape(2, 128, tile)
                else:
                    out_part[step - 1, :, :, cols] = out.astype(BF16).reshape(2, 128, tile)
            out = dot_t(hid, fd_ref[...])
            if step == 0:
                out_own[:, :, width:] = out.reshape(2, 128, SIDE)
            else:
                out_part[step - 1, :, :, width:] = out.astype(BF16).reshape(2, 128, SIDE)

        def send(src, dst, k, target):
            cp = _remote(src, dst, s_sem.at[k], r_sem.at[k], target)
            cp.start()
            copies.append(cp)
            return cp

        own_here()
        for cp in loads:
            cp.wait()
        work(0)
        across, out_cps = [], []

        def leave(j, cp):
            cp.wait_recv()
            staged[j] = (part[j, 1].astype(F32) + far[j].astype(F32)).astype(BF16)
            across.append(send(staged.at[j], landed.at[j], 6 + j, x_peer))

        for j in range(2):
            forward(j)
            far_here(j)
            work(1 + j)
            cp = send(part.at[j, 0], far.at[j], 2 + j, core_peer)
            down(1 + j)
            out_cps.append(send(out_part.at[j, 0], out_land.at[j], 4 + j, core_peer))
            leave(j, cp)
        core_here()
        work(3)
        near_cp = [send(part.at[2], near, 0, core_peer)]
        down(3)
        near_cp.append(send(out_part.at[2], out_near, 1, core_peer))
        down(0)
        for j in range(2):
            out_cps[j].wait_recv()
            out_far[j] = (out_part[j, 1].astype(F32) + out_land[j].astype(F32)).astype(BF16)
        for cp in near_cp:
            cp.wait_recv()
        sums[...] = sums[...] + near[...].astype(F32)
        out_own[...] = out_own[...] + out_near[...].astype(F32)
        for at in range(0, units, 512):
            cols = slice(at, at + 512)
            g = jnp.zeros((SIDE, 512), F32)
            u = jnp.zeros((SIDE, 512), F32)
            d = jnp.zeros((SIDE, 512), F32)
            for step in range(4):
                g += dot_rows(in_s[step], gg_s[step, :, cols])
                u += dot_rows(in_s[step], gu_s[step, :, cols])
                d += dot_rows(gid_s[step], hid_s[step, :, cols])
            early[:, at : at + 512] = (ADAPTER_SCALE * g[:RANK]).astype(BF16)
            early[:, units + at : units + at + 512] = (ADAPTER_SCALE * u[RANK : 2 * RANK]).astype(BF16)
            early[:, 2 * units + at : 2 * units + at + 512] = d[3 * RANK : 4 * RANK].astype(BF16)
        for j in range(2):
            across[j].wait_recv()
            total = sums[j] + landed[j].astype(F32)
            gi = total[:, width:].astype(BF16)
            small[j] = gi
            gn = (total[:, :width] + dot(gi, first_ref[...])).astype(BF16).astype(F32)
            v = resid_ref[j]
            factor = lax.rsqrt(jnp.mean(v * v, axis=1, keepdims=True) + EPSILON)
            scaled = gn * gain_ref[...]
            mean = jnp.mean(scaled * v, axis=1, keepdims=True)
            grad = go_ref[0, j].astype(F32) + factor * scaled - v * (factor * factor * factor) * mean
            grad_resid[j] = grad
            grad_low[j] = grad.astype(BF16)
        last()
        for cp in copies:
            cp.wait_send()

    vmem = pl.BlockSpec(memory_space=pltpu.VMEM)
    rows = (2, 128, wide)
    f32 = lambda *shape: jax.ShapeDtypeStruct(shape, F32)
    outs = [
        f32(2, 128, width),
        jax.ShapeDtypeStruct((2, 128, width), BF16),
        jax.ShapeDtypeStruct((2, 128, SIDE), BF16),
        f32(*rows),
        jax.ShapeDtypeStruct(rows, BF16),
        jax.ShapeDtypeStruct((4, 2, 128, width), BF16),
        jax.ShapeDtypeStruct((RANK, 3 * units), BF16),
    ]
    hbm = pl.BlockSpec(memory_space=pl.ANY)
    return pl.pallas_call(
        kernel,
        out_shape=outs,
        in_specs=[pl.BlockSpec(memory_space=pltpu.SMEM), vmem, vmem, vmem] + [hbm] * count,
        out_specs=[vmem] * len(outs),
        scratch_shapes=[pltpu.VMEM(a.shape, a.dtype) for a in loads_in]
        + [pltpu.VMEM(rows, F32)]
        + [pltpu.VMEM((4, 256, units), BF16)] * 3
        + [pltpu.VMEM((4, 256, SIDE), BF16)] * 2
        + [pltpu.VMEM((3,) + rows, BF16)] * 2
        + [pltpu.VMEM(rows, BF16)] * 6
        + [_sem(count), _sem(2), _sem(6), _sem(6), _sem(8), _sem(8)],
        compiler_params=pltpu.CompilerParams(
            collective_id=cid, has_side_effects=True, vmem_limit_bytes=58 * 1024 * 1024
        ),
        name="feed_forward",
    )(length, own, resid, gain, *loads_in)


def _back_steps(src, dst, out_s, out_r, place):
    c, f, x, core = place[:4]
    slot = _slot_of(c)
    place_in = slot % 2
    moves = []

    def first(j):
        cp = _remote(
            src.at[j],
            dst.at[place_in],
            out_s.at[j],
            out_r.at[place_in],
            (_block(x, core, j), slot // 2),
        )
        cp.start()
        moves.append(cp)

    def last():
        for half in range(2):
            pltpu.make_async_copy(dst.at[half], dst.at[half], out_r.at[half]).wait()
        for cp in moves:
            cp.wait_send()

    return first, last


def _back_sources(place):
    c, f = place[:2]
    return [(_group_of(2 * f + half), _owner(c)) for half in range(2)]


def front_call(
    tokens,
    cotangent,
    lengths,
    adapters,
    gains,
    wq,
    wk,
    wv,
    wo,
    tables,
    cosine,
    sine,
    cid,
):
    width = tokens.shape[-1]
    rows = cosine.shape[0]
    wide = width + SIDE
    block = 256
    scale = HEAD_DIM ** (-0.5)
    lane = PAD_HEAD
    units = tables[6].shape[-1] // 4
    quarter = width // 4
    loads_in = gains + (wq, wk, wv, wo) + tables + (cosine, sine)
    count = len(loads_in)

    def kernel(*refs):
        len_ref, adapter_ref, tok_ref, cot_ref = refs[:4]
        loads_hbm = refs[4 : 4 + count]
        (
            sums_resid,
            normed_two,
            side_all,
            tok_own,
            cot_order,
            cot_peer,
            qkv_ref,
            lse_ref,
            att_ref,
            one_cut,
            inner_ref,
            wa_ref,
            wkv_ref,
            ow_ref,
            sa_ref,
            fa_ref,
            fgu_ref,
            sg_ref,
            su_ref,
            fd_ref,
            sd_ref,
            fo_ref,
            so_ref,
        ) = refs[4 + count : 27 + count]
        refs = refs[27 + count :]
        gain_one, gain_two, wq_v, wk_v, wv_v, wo_v = refs[:6]
        in_first, out_first, down_first, q_second, kv_second, o_second, gu_second, d_second = refs[6:14]
        cos_ref, sin_ref = refs[14:16]
        (
            tok_all,
            one_ref,
            part,
            land,
            staged,
            landed,
            sums,
            side_own,
            load_sem,
            land_s,
            land_r,
            cot_s,
            cot_r,
            send_sem,
            recv_sem,
            s_sem,
            r_sem,
        ) = refs[16:33]
        side_sems = refs[33:36]
        place = _place()
        c, f, x, core, core_peer, x_peer = place
        hh = 1 - core
        slot = _slot_of(c)
        live = len_ref[slot]
        which = adapter_ref[slot]
        loads = []
        for i in range(count):
            cp = pltpu.make_async_copy(loads_hbm[i], refs[i], load_sem.at[i])
            cp.start()
            loads.append(cp)

        barrier = pltpu.get_barrier_semaphore()
        for j in range(2):
            pl.semaphore_signal(
                barrier, inc=1, device_id=(_block(x, core, j), slot // 2), device_id_type=MESH_ID
            )
        for target in (core_peer, x_peer):
            pl.semaphore_signal(barrier, inc=1, device_id=target, device_id_type=MESH_ID)
        for b in range(4):
            pl.semaphore_signal(
                barrier,
                inc=1,
                device_id=(4 * hh + b, 2 * x + (slot // 2) % 2),
                device_id_type=MESH_ID,
            )
        pl.semaphore_wait(barrier, 8)
        to_f = _owner(c)
        to_h = c // 4
        to_j = (c // 2) % 2
        to_i = c % 2
        moves = []
        for part_row in range(2):
            span = pl.ds(64 * part_row, 64)
            for half in range(2):
                s = 2 * f + half
                cp = _remote(
                    tok_ref.at[half, span],
                    tok_all.at[to_h, to_j, to_i, span],
                    land_s.at[2 * part_row + half],
                    land_r.at[2 * part_row + to_j],
                    (_group_of(s), to_f),
                )
                cp.start()
                moves.append(cp)
        cross = [
            _remote(cot_ref.at[half], cot_peer.at[half], cot_s.at[half], cot_r.at[half], x_peer)
            for half in range(2)
        ]
        cross[0].start()
        cot_moves = []
        for relay in range(2):
            for half in range(2):
                s = 2 * (2 * ((x + relay) % 2) + core) + half
                away = ((c // 2 + c) % 2 + x) % 2
                cot_moves.append(
                    _remote(
                        (cot_peer if relay else cot_ref).at[half],
                        cot_order.at[away * (1 + to_j), (1 - away) * to_j + away],
                        cot_s.at[2 + 2 * relay + half],
                        cot_r.at[2 + 2 * away + to_j],
                        (_group_of(s), 2 * x + 1 - to_h),
                    )
                )
        for cp in loads:
            cp.wait()

        def group_sends(part_row):
            span = pl.ds(64 * part_row, 64)
            for j in range(2):
                pltpu.make_async_copy(
                    tok_all.at[hh, j, (x + j) % 2, span],
                    tok_all.at[hh, j, (x + j) % 2, span],
                    land_r.at[2 * part_row + j],
                ).wait()
                k = 2 * part_row + j
                here = tok_all.at[hh, j, (x + j) % 2, span]
                for base, target in ((0, x_peer), (4, core_peer)):
                    cp = _remote(
                        here, here, send_sem.at[base + k], recv_sem.at[base + k], target
                    )
                    cp.start()
                    sends[base + k] = cp

        sends = {}

        def prepare_first():
            half = HEAD_DIM // 2
            wa_ref[...] = jnp.zeros_like(wa_ref)
            wkv_ref[...] = jnp.zeros_like(wkv_ref)
            sa_ref[...] = jnp.zeros_like(sa_ref)
            for head in range(4):
                for side in range(2):
                    at = head * HEAD_DIM + side * half
                    to = head * lane + side * HALF_PAD
                    wa_ref[:, to : to + half] = wq_v[:, at : at + half]
            for head in range(2):
                for side in range(2):
                    at = head * HEAD_DIM + side * half
                    to = head * lane + side * HALF_PAD
                    wkv_ref[to : to + half, :] = wk_v[at : at + half, :]
                at, to = head * HEAD_DIM, (2 + head) * lane
                wkv_ref[to : to + HEAD_DIM, :] = wv_v[at : at + HEAD_DIM, :]

        def prepare_second():
            half = HEAD_DIM // 2
            own_cols = pl.ds(pl.multiple_of(f * quarter, 128), quarter)
            own_units = pl.ds(pl.multiple_of(f * units, 128), units)
            low = lambda v: (ADAPTER_SCALE * v.astype(F32)).astype(BF16)
            for ref in (fa_ref, fgu_ref, sg_ref, su_ref, fd_ref, sd_ref, fo_ref, so_ref, ow_ref):
                ref[...] = jnp.zeros_like(ref)
            for i in range(3):
                fa_ref[i * RANK : (i + 1) * RANK, :] = in_first[which, i]
            for i in range(2):
                fgu_ref[i * RANK : (i + 1) * RANK, :] = in_first[which, 3 + i]
            all_gu = gu_second.at[:, :, :, own_units]
            sg_ref[:RANK, :] = low(all_gu[which, 0])
            su_ref[RANK : 2 * RANK, :] = low(all_gu[which, 1])
            fd_ref[3 * RANK : 4 * RANK, :] = down_first.at[:, :, own_units][which]
            sd_ref[3 * RANK : 4 * RANK, :] = low(d_second[which])
            so_ref[:RANK, :] = low(o_second[which])
            own_first = out_first.at[:, :, own_cols][which]
            own_q = low(q_second.at[:, :, own_cols][which])
            for head in range(4):
                at = head * HEAD_DIM
                fo_ref[:RANK, head * lane : head * lane + HEAD_DIM] = own_first[:, at : at + HEAD_DIM]
                ow_ref[head * lane : head * lane + HEAD_DIM, :] = wo_v[at : at + HEAD_DIM, :]
                for side in range(2):
                    to = head * lane + side * HALF_PAD
                    sa_ref[:RANK, to : to + half] = own_q[:, at + side * half : at + (side + 1) * half]
            window = pl.ds(pl.multiple_of((3 * f // 2) * 128, 128), 256)
            for i in range(2):
                own_kv = kv_second.at[:, :, :, window][which, i].astype(F32)
                shifted = pltpu.roll(own_kv, 256 - 64, 1)
                own_kv = low(jnp.where(f % 2 == 1, shifted, own_kv))
                for head in range(2):
                    at = head * HEAD_DIM
                    if i:
                        to = (6 + head) * lane
                        sa_ref[2 * RANK : 3 * RANK, to : to + HEAD_DIM] = own_kv[:, at : at + HEAD_DIM]
                    else:
                        for side in range(2):
                            to = (4 + head) * lane + side * HALF_PAD
                            sa_ref[RANK : 2 * RANK, to : to + half] = own_kv[
                                :, at + side * half : at + (side + 1) * half
                            ]

        prepare_first()
        group_sends(0)
        prepare_second()
        group_sends(1)
        for cp in cot_moves[:2]:
            cp.start()
        cross[0].wait_recv()
        cot_moves[2].start()

        def cot_spot(away, j):
            return cot_order.at[(1 + j) if away else 0, 1 if away else j]

        def cot_share():
            for away in range(2):
                for j in range(2):
                    here = cot_spot(away, j)
                    pltpu.make_async_copy(here, here, cot_r.at[2 + 2 * away + j]).wait()
                    there = cot_order.at[1 + j, 0] if away else cot_order.at[3, j]
                    k = 6 + 2 * away + j
                    cp = _remote(here, there, cot_s.at[k], cot_r.at[k], core_peer)
                    cp.start()
                    shared.append(cp)

        shared = []

        def forward(j):
            for part_row in range(2):
                k = 2 * part_row + j
                span = pl.ds(64 * part_row, 64)
                sends[k].wait_recv()
                there = tok_all.at[hh, j, (x + j + 1) % 2, span]
                cp = _remote(there, there, send_sem.at[8 + k], recv_sem.at[8 + k], core_peer)
                cp.start()
                sends[8 + k] = cp
            for part_row in range(2):
                k = 2 * part_row + j
                sends[4 + k].wait_recv()
                sends[8 + k].wait_recv()

        def project_rows(t):
            row = pl.ds(t * block, block)
            v = tok_all[t // 2, t % 2].reshape(block, width).astype(F32)
            factor = lax.rsqrt(jnp.mean(v * v, axis=1, keepdims=True) + EPSILON)
            u = (v * factor * gain_one[...]).astype(BF16)
            one_ref[row, :] = u
            inner = dot_t(u, fa_ref[...]).astype(BF16)
            inner_ref[row, :] = inner
            cos, sin = cos_ref[row, :], sin_ref[row, :]
            for pair in range(4):
                cols = slice(pair * 2 * lane, (pair + 1) * 2 * lane)
                if pair < 2:
                    both = dot(u, wa_ref[:, cols])
                else:
                    both = dot_t(u, wkv_ref[2 * (pair - 2) * lane : 2 * (pair - 1) * lane, :])
                both = both + dot(inner, sa_ref[:, cols])
                for k in range(2):
                    p = both[:, k * lane : (k + 1) * lane]
                    if pair < 3:
                        p = p * cos + pltpu.roll(p, HALF_PAD, 1) * sin
                    qkv_ref[row, (2 * pair + k) * lane : (2 * pair + k + 1) * lane] = p.astype(BF16)

        def attention(t, hook):
            keys = (t + 1) * block
            row = pl.ds(t * block, block)
            qpos = t * block + lax.broadcasted_iota(jnp.int32, (block, keys), 0)
            kpos = lax.broadcasted_iota(jnp.int32, (block, keys), 1)
            allowed = (kpos <= qpos) & (kpos < live)
            stats = jnp.zeros((block, lane), F32)
            lanes = lax.broadcasted_iota(jnp.int32, (block, lane), 1)
            for head in range(4):
                q = qkv_ref[row, head * lane : (head + 1) * lane]
                kv = head // 2
                k = qkv_ref[:keys, (4 + kv) * lane : (5 + kv) * lane]
                v = qkv_ref[:keys, (6 + kv) * lane : (7 + kv) * lane]
                s = jnp.where(allowed, dot_t(q, k) * scale, NEGATIVE)
                top = jnp.max(s, axis=1, keepdims=True)
                p = jnp.where(allowed, jnp.exp(s - top), 0.0)
                total = jnp.sum(p, axis=1, keepdims=True)
                o = dot(p.astype(BF16), v) / total
                att_ref[row, head * lane : (head + 1) * lane] = o.astype(BF16)
                stats = jnp.where(lanes == head, top + jnp.log(total), stats)
                if head == 1 and hook is not None:
                    hook()
            lse_ref[row, :] = stats
            a = att_ref[row, :]
            for at in range(0, width, 256):
                value = dot(a, ow_ref[:, at : at + 256])
                part[t, :, :, at : at + 256] = value.astype(BF16).reshape(2, 128, 256)
            part[t, :, :, width:] = dot_t(a, fo_ref[...]).astype(BF16).reshape(2, 128, SIDE)

        def to_core(t):
            return _remote(part.at[t], land.at[t % 2], s_sem.at[t % 2], r_sem.at[t % 2], core_peer)

        def to_x(j):
            return _remote(staged.at[j], landed.at[j], s_sem.at[2 + j], r_sem.at[2 + j], x_peer)

        def leave(t):
            @pl.when(core == t // 2)
            def _():
                to_core(t).start()

        def combine(t):
            j = t % 2

            @pl.when(core == 1 - t // 2)
            def _():
                to_core(t).wait_recv()
                mine, other = (x + j) % 2, (x + j + 1) % 2
                staged[j] = (part[t, other].astype(F32) + land[j, other].astype(F32)).astype(BF16)
                to_x(j).start()
                sums[j] = part[t, mine].astype(F32) + land[j, mine].astype(F32)

        forward(0)
        cross[1].start()
        project_rows(0)
        project_rows(2)
        attention(0, None)
        leave(0)
        forward(1)
        project_rows(1)
        project_rows(3)
        cross[1].wait_recv()
        cot_moves[3].start()
        attention(1, lambda: combine(0))
        leave(1)
        attention(2, lambda: combine(1))
        leave(2)
        attention(3, lambda: combine(2))
        leave(3)
        combine(3)
        cot_share()
        for t in range(4):

            @pl.when(core == t // 2)
            def _():
                to_core(t).wait_send()

        for j in range(2):
            tok_own[j] = tok_all[hh, j, (x + j) % 2]
        one_cut[...] = one_ref[:, pl.ds(pl.multiple_of(f * quarter, 128), quarter)]
        for j in range(2):
            cp = to_x(j)
            cp.wait_recv()
            sums[j] = sums[j] + landed[j].astype(F32)
            cp.wait_send()
            side_own[j] = sums[j, :, width:].astype(BF16)
        side_first, side_last = _gather_steps([side_own], [side_all], *side_sems, place)
        side_first()
        for j in range(2):
            v = (
                tok_own[j].astype(F32)
                + sums[j, :, :width]
                + dot(side_own[j], so_ref[...])
            )
            sums_resid[j] = v
            factor = lax.rsqrt(jnp.mean(v * v, axis=1, keepdims=True) + EPSILON)
            normed_two[j] = (v * factor * gain_two[...]).astype(BF16)
        for cp in shared:
            cp.wait_recv()
        side_last()
        for cp in moves + cross + cot_moves + shared + list(sends.values()):
            cp.wait_send()

    vmem, hbm = pl.BlockSpec(memory_space=pltpu.VMEM), pl.BlockSpec(memory_space=pl.ANY)
    smem = pl.BlockSpec(memory_space=pltpu.SMEM)
    low = lambda *shape: jax.ShapeDtypeStruct(shape, BF16)
    outs = [
        (jax.ShapeDtypeStruct((2, 128, width), F32), vmem),
        (low(2, 128, width), vmem),
        (low(2, 2, 2, 128, SIDE), hbm),
        (low(2, 128, width), vmem),
        (low(4, 2, 128, width), hbm),
        (low(2, 128, width), hbm),
        (low(rows, 8 * lane), vmem),
        (jax.ShapeDtypeStruct((rows, lane), F32), vmem),
        (low(rows, 4 * lane), vmem),
        (low(rows, quarter), vmem),
        (low(rows, SIDE), vmem),
        (low(width, 4 * lane), vmem),
        (low(4 * lane, width), vmem),
        (low(4 * lane, width), vmem),
        (low(SIDE, 8 * lane), vmem),
        (low(SIDE, width), vmem),
        (low(SIDE, width), vmem),
        (low(SIDE, units), vmem),
        (low(SIDE, units), vmem),
        (low(SIDE, units), vmem),
        (low(SIDE, width), vmem),
        (low(SIDE, 4 * lane), vmem),
        (low(SIDE, width), vmem),
    ]
    own = (2, 128, wide)
    return pl.pallas_call(
        kernel,
        out_shape=[o[0] for o in outs],
        in_specs=[smem, smem] + [hbm] * (2 + count),
        out_specs=[o[1] for o in outs],
        scratch_shapes=[pltpu.VMEM(a.shape, a.dtype) for a in loads_in]
        + [
            pltpu.VMEM((2, 2, 2, 128, width), BF16),
            pltpu.VMEM((rows, width), BF16),
            pltpu.VMEM((4,) + own, BF16),
            pltpu.VMEM((2,) + own, BF16),
            pltpu.VMEM(own, BF16),
            pltpu.VMEM(own, BF16),
            pltpu.VMEM(own, F32),
            pltpu.VMEM((2, 128, SIDE), BF16),
            _sem(count),
            _sem(4),
            _sem(4),
            _sem(10),
            _sem(10),
            _sem(12),
            _sem(12),
            _sem(4),
            _sem(4),
        ]
        + [_sem(2), _sem(6), _sem(6)],
        compiler_params=pltpu.CompilerParams(
            collective_id=cid, has_side_effects=True, vmem_limit_bytes=58 * 1024 * 1024
        ),
        name="front",
    )(lengths, adapters, tokens, cotangent, *loads_in)


def attend_back_call(
    low_own,
    small_own,
    early,
    out_far,
    length,
    own_arrays,
    arrays,
    cid,
):
    qkv = arrays[0]
    width = low_own.shape[-1]
    rows = qkv.shape[0]
    wide = width + SIDE
    step_rows = 256
    scale = HEAD_DIM ** (-0.5)
    lane = PAD_HEAD
    quarter = width // 4
    middle_n = 4 * quarter
    early_n = early.shape[1]
    big = tuple(arrays) + tuple(own_arrays)
    late_n = 4 * quarter
    factor_n = 2 * quarter
    count = len(big)

    def kernel(*refs):
        len_ref, low_ref, small_ref, early_ref, out_ref = refs[:5]
        big_in = refs[5 : 5 + count]
        (
            out_back,
            grad_back,
            early_out,
            middle_out,
            late_out,
            factor_out,
        ) = refs[5 + count : 11 + count]
        refs = refs[11 + count :]
        (
            qkv_ref,
            lse_ref,
            att_ref,
            inner_ref,
            order_ref,
            cos_ref,
            sin_ref,
            ow_ref,
            fo_ref,
            so_ref,
            wa_ref,
            wkv_ref,
            sa_ref,
            fa_ref,
            sd_ref,
            cut_ref,
            inner_qkv_ref,
            cot_ref,
            out_own,
            resid_ref,
            tok_ref,
            grad_resid_ref,
            gain_ref,
        ) = refs[:count]
        (
            low,
            do_ref,
            gio_ref,
            dk_ref,
            dv_ref,
            part,
            land,
            staged,
            landed,
            side_own,
            middle_ref,
            sums,
            side_all,
            grad_ref,
            landed_out,
            small_out,
            late_ref,
            factor_ref,
            out_tok,
            grad_tok,
            early_lines,
            middle_lines,
            load_sem,
            own_sem,
            send_sem,
            recv_sem,
            s_sem,
            r_sem,
        ) = refs[count : count + 28]
        sems = refs[count + 28 :]
        place = _place()
        c, f, x, core, core_peer, x_peer = place
        loads = [
            pltpu.make_async_copy(big_in[i], refs[i], load_sem.at[i]) for i in range(count)
        ]
        for cp in loads:
            cp.start()
        _greet(
            _back_sources(place) + [core_peer, x_peer, _y_peer(place)] + _z_peers(place)
        )
        small_first, small_forward, small_own_here, small_core, small_far, small_last = _order_steps(
            small_ref, small_out, *sems[0:3], place
        )
        early_start, early_across, early_finish = _ctx_first(early_ref, early_lines, *sems[3:6], place)
        early_two = _ctx_second(early_lines, early_out, *sems[6:9], place)
        mid_start, mid_across, mid_finish = _ctx_first(middle_ref, middle_lines, *sems[9:12], place)
        mid_two = _ctx_second(middle_lines, middle_out, *sems[12:15], place)
        late = _ctx_planes(late_ref, late_out, *sems[15:18], place)
        factor = _ctx_planes(factor_ref, factor_out, *sems[25:28], place)
        side_first, side_last = _gather_steps([side_own], [side_all], *sems[18:21], place)
        out_first, out_last = _back_steps(out_tok, out_back, *sems[21:23], place)
        grad_first, grad_last = _back_steps(grad_tok, grad_back, *sems[23:25], place)
        live = len_ref[_slot_of(c)]

        sends = {}
        hh = 1 - core
        local = []
        for j in (1, 0):
            for k, target in ((0, x_peer), (2, core_peer)):
                cp = _remote(
                    low_ref.at[j],
                    low.at[hh, j, (x + j) % 2],
                    send_sem.at[k + j],
                    recv_sem.at[k + j],
                    target,
                )
                cp.start()
                sends[(k, j)] = cp
            if j:
                early_start()
                small_first()
        for j in range(2):
            lc = pltpu.make_async_copy(low_ref.at[j], low.at[hh, j, (x + j) % 2], own_sem.at[j])
            lc.start()
            local.append(lc)
        swaps = [
            _remote(out_ref.at[j], landed_out.at[j], s_sem.at[8 + j], r_sem.at[8 + j], x_peer)
            for j in range(2)
        ]
        dk_ref[...] = jnp.zeros_like(dk_ref)
        dv_ref[...] = jnp.zeros_like(dv_ref)
        for cp in loads:
            cp.wait()
        for lc in local:
            lc.wait()

        def arrive(j):
            sends[(0, j)].wait_recv()
            cp = _remote(
                low.at[hh, j, (x + j + 1) % 2],
                low.at[hh, j, (x + j + 1) % 2],
                send_sem.at[4 + j],
                recv_sem.at[4 + j],
                core_peer,
            )
            cp.start()
            sends[(4, j)] = cp
            sends[(2, j)].wait_recv()
            cp.wait_recv()

        def through_output(t):
            g = low[t // 2, t % 2].reshape(step_rows, width)
            gio = dot_t(g, so_ref[...]).astype(BF16)
            row = pl.ds(t * step_rows, step_rows)
            gio_ref[row, :] = gio
            do_ref[row, :] = (dot_t(g, ow_ref[...]) + dot(gio, fo_ref[...])).astype(BF16)

        def attention(t, hook):
            keys = (t + 1) * step_rows
            row = pl.ds(t * step_rows, step_rows)
            qpos = t * step_rows + lax.broadcasted_iota(jnp.int32, (step_rows, keys), 0)
            kpos = lax.broadcasted_iota(jnp.int32, (step_rows, keys), 1)
            allowed = (kpos <= qpos) & (kpos < live)
            cos, sin = cos_ref[row, :], sin_ref[row, :]
            for head in range(4):
                kv = head // 2
                at = slice(head * lane, (head + 1) * lane)
                q = qkv_ref[row, at]
                k = qkv_ref[:keys, (4 + kv) * lane : (5 + kv) * lane]
                v = qkv_ref[:keys, (6 + kv) * lane : (7 + kv) * lane]
                do = do_ref[row, at]
                s = dot_t(q, k)
                p = jnp.where(allowed, jnp.exp(s * scale - lse_ref[row, head : head + 1]), 0.0)
                dp = dot_t(do, v)
                total = jnp.sum(p * dp, axis=1, keepdims=True)
                ds = (p * (dp - total)).astype(BF16)
                dq = scale * dot(ds, k)
                dq = dq * cos - pltpu.roll(dq, HALF_PAD, 1) * sin
                grad_ref[row, at] = dq.astype(BF16)
                dk_ref[kv, :keys] += dot_rows(ds, q)
                dv_ref[kv, :keys] += dot_rows(p.astype(BF16), do)
                if head == 1 and hook is not None:
                    hook()
            for kv in range(2):
                dk = scale * dk_ref[kv, row, :]
                dk = dk * cos - pltpu.roll(dk, HALF_PAD, 1) * sin
                grad_ref[row, (4 + kv) * lane : (5 + kv) * lane] = dk.astype(BF16)
                grad_ref[row, (6 + kv) * lane : (7 + kv) * lane] = dv_ref[kv, row, :].astype(BF16)
            g = grad_ref[row, :]
            for at in range(0, width, 256):
                value = dot_t(g[:, : 4 * lane], wa_ref[at : at + 256, :])
                value = value + dot(g[:, 4 * lane :], wkv_ref[:, at : at + 256])
                part[t, :, :, at : at + 256] = value.astype(BF16).reshape(2, 128, 256)
            part[t, :, :, width:] = dot_t(g, sa_ref[...]).astype(BF16).reshape(2, 128, SIDE)

        def to_core(t):
            j = t % 2
            return _remote(part.at[t], land.at[j], s_sem.at[j], r_sem.at[j], core_peer)

        def to_x(j):
            return _remote(staged.at[j], landed.at[j], s_sem.at[2 + j], r_sem.at[2 + j], x_peer)

        def leave(t):
            @pl.when(core == t // 2)
            def _():
                to_core(t).start()

        def combine(t):
            j = t % 2

            @pl.when(core == 1 - t // 2)
            def _():
                to_core(t).wait_recv()
                mine, other = (x + j) % 2, (x + j + 1) % 2
                staged[j] = (part[t, other].astype(F32) + land[j, other].astype(F32)).astype(BF16)
                to_x(j).start()
                sums[j] = part[t, mine].astype(F32) + land[j, mine].astype(F32)

        arrive(1)
        early_across()
        through_output(3)
        through_output(1)
        small_own_here()
        for j in range(2):
            small_forward(j)
        def second():
            arrive(0)
            for cp in swaps:
                cp.start()

        attention(3, second)
        leave(3)
        through_output(2)
        through_output(0)
        o_a = dot_rows(gio_ref[...], att_ref[...])[:RANK]
        o_a = jnp.concatenate(
            [o_a[:, head * lane : head * lane + HEAD_DIM] for head in range(4)], axis=1
        )
        middle_ref[:, :quarter] = o_a.astype(BF16)
        own_cols = pl.ds(pl.multiple_of(f * quarter, 128), quarter)
        g = low[:, :, :, :, own_cols].reshape(rows, quarter)
        middle_ref[:, quarter : 2 * quarter] = (ADAPTER_SCALE * dot_rows(inner_ref[...], g)[:RANK]).astype(BF16)
        for j in range(2):
            small_far(j)
        small_core()
        in_gu = jnp.zeros((SIDE, quarter), F32)
        for k in range(4):
            u = order_ref[k, :, :, own_cols].reshape(step_rows, quarter)
            in_gu += dot_rows(small_out[k].reshape(step_rows, SIDE), u)
        middle_ref[:, 2 * quarter : 3 * quarter] = in_gu[:RANK].astype(BF16)
        middle_ref[:, 3 * quarter :] = in_gu[RANK : 2 * RANK].astype(BF16)
        mid_start()
        early_finish()
        early_two[0]()

        def outputs():
            for j in range(2):
                swaps[j].wait()
                total = out_own[j] + landed_out[j].astype(F32)
                side = total[:, width:]
                out_own[j, :, width:] = side
                pos = 128 * _block(x, core, j) + lax.broadcasted_iota(jnp.int32, (128, width), 0)
                value = resid_ref[j] + total[:, :width] + dot(side.astype(BF16), sd_ref[...])
                out_tok[j] = jnp.where(pos < live, value, 0.0).astype(BF16)
                out_first(j)

        def third():
            combine(3)
            mid_across()

        attention(2, third)
        leave(2)
        outputs()
        attention(1, lambda: combine(2))
        leave(1)
        mid_finish()
        mid_two[0]()
        early_two[1]()
        attention(0, lambda: combine(1))
        leave(0)
        combine(0)
        all_b = ADAPTER_SCALE * dot_rows(inner_qkv_ref[...], grad_ref[...])
        half = HEAD_DIM // 2
        pieces = []
        for head in range(6):
            r = slice(0, RANK) if head < 4 else slice(RANK, 2 * RANK)
            for side in range(2):
                to = head * lane + side * HALF_PAD
                pieces.append(all_b[r, to : to + half])
        for head in range(2):
            to = (6 + head) * lane
            pieces.append(all_b[2 * RANK : 3 * RANK, to : to + HEAD_DIM])
        factor_ref[...] = jnp.concatenate(pieces, axis=1).astype(BF16)
        factor[0]()
        mid_two[1]()
        for j in range(2):
            cp = to_x(j)
            cp.wait_recv()
            sums[j] = sums[j] + landed[j].astype(F32)
            side_own[j] = (sums[j, :, width:] + out_own[j, :, width:]).astype(BF16)
        side_first()
        factor[1]()
        side_last()
        in_qkv = dot_rows(side_all[...].reshape(rows, SIDE), cut_ref[...])
        for i in range(3):
            late_ref[:, i * quarter : (i + 1) * quarter] = in_qkv[i * RANK : (i + 1) * RANK].astype(
                BF16
            )
        d_b = jnp.zeros((SIDE, quarter), F32)
        for step in range(4):
            other_x = x if step in (0, 3) else 1 - x
            for i in range(2):
                other_core = (core, 1 - core)[step == 3 or (step in (1, 2) and i == 0)]
                jj = i if step in (0, 3) else step - 1
                pos = 128 * _block(other_x, other_core, jj) + lax.broadcasted_iota(
                    jnp.int32, (128, quarter), 0
                )
                go = cot_ref[step, i, :, own_cols].astype(F32)
                go = jnp.where(pos < live, go, 0.0).astype(BF16)
                d_b += dot_rows(side_all[1 - other_core, jj, (other_x + jj) % 2], go)
        late_ref[:, 3 * quarter :] = (ADAPTER_SCALE * d_b[3 * RANK : 4 * RANK]).astype(BF16)
        late[0]()
        for j in range(2):
            gi = sums[j, :, width:].astype(BF16)
            gn = (sums[j, :, :width] + dot(gi, fa_ref[...])).astype(BF16).astype(F32)
            v = tok_ref[j].astype(F32)
            rms = lax.rsqrt(jnp.mean(v * v, axis=1, keepdims=True) + EPSILON)
            scaled = gn * gain_ref[...]
            mean = jnp.mean(scaled * v, axis=1, keepdims=True)
            grad = grad_resid_ref[j] + rms * scaled - v * (rms * rms * rms) * mean
            grad_tok[j] = grad.astype(BF16)
            grad_first(j)
        late[1]()
        for t in range(4):

            @pl.when(core == t // 2)
            def _():
                to_core(t).wait_send()

        for j in range(2):
            to_x(j).wait_send()
        small_last()
        early_two[2]()
        mid_two[2]()
        factor[2]()
        late[2]()
        out_last()
        grad_last()
        for cp in sends.values():
            cp.wait_send()

    vmem, hbm = pl.BlockSpec(memory_space=pltpu.VMEM), pl.BlockSpec(memory_space=pl.ANY)
    shape = jax.ShapeDtypeStruct
    own = (2, 128, wide)
    return pl.pallas_call(
        kernel,
        out_shape=[
            shape((2, 128, width), BF16),
            shape((2, 128, width), BF16),
            _spread_of(early_n),
            _spread_of(middle_n),
            _spread_of(late_n),
            _spread_of(factor_n),
        ],
        in_specs=[pl.BlockSpec(memory_space=pltpu.SMEM)] + [hbm] * (4 + count),
        out_specs=[hbm] * 6,
        scratch_shapes=[pltpu.VMEM(a.shape, a.dtype) for a in big]
        + [
            pltpu.VMEM((2, 2, 2, 128, width), BF16),
            pltpu.VMEM((rows, 4 * lane), BF16),
            pltpu.VMEM((rows, SIDE), BF16),
            pltpu.VMEM((2, rows, lane), F32),
            pltpu.VMEM((2, rows, lane), F32),
            pltpu.VMEM((4,) + own, BF16),
            pltpu.VMEM((2,) + own, BF16),
            pltpu.VMEM(own, BF16),
            pltpu.VMEM(own, BF16),
            pltpu.VMEM((2, 128, SIDE), BF16),
            pltpu.VMEM((RANK, middle_n), BF16),
            pltpu.VMEM(own, F32),
            pltpu.VMEM((2, 2, 2, 128, SIDE), BF16),
            pltpu.VMEM((rows, 8 * lane), BF16),
            pltpu.VMEM(own, BF16),
            pltpu.VMEM((4, 2, 128, SIDE), BF16),
            pltpu.VMEM((RANK, late_n), BF16),
            pltpu.VMEM((RANK, factor_n), BF16),
            pltpu.VMEM((2, 128, width), BF16),
            pltpu.VMEM((2, 128, width), BF16),
            pltpu.VMEM(_lines_of(early_n), BF16),
            pltpu.VMEM(_lines_of(middle_n), BF16),
            _sem(count),
            _sem(2),
            _sem(6),
            _sem(6),
            _sem(10),
            _sem(10),
        ]
        + [_sem(2), _sem(6), _sem(6)]
        + FIRST_SEMS
        + SECOND_SEMS
        + FIRST_SEMS
        + SECOND_SEMS
        + PLANE_SEMS
        + [_sem(2), _sem(6), _sem(6)]
        + [_sem(2), _sem(2), _sem(2), _sem(2)]
        + PLANE_SEMS,
        compiler_params=pltpu.CompilerParams(
            collective_id=cid, has_side_effects=True, vmem_limit_bytes=62 * 1024 * 1024
        ),
        name="attend_back",
    )(length, low_own, small_own, early, out_far, *big)


def table_call(pieces, out_rows, grad_rows, adapters):
    f32 = lambda *shape: jax.ShapeDtypeStruct(shape, F32)
    choices = 8
    outs = [
        f32(choices, 5, RANK, 1536),
        f32(choices, RANK, 1536),
        f32(choices, RANK, 4096),
        f32(choices, RANK, 1536),
        f32(choices, 2, RANK, 768),
        f32(choices, RANK, 1536),
        f32(choices, 2, RANK, 4096),
        f32(choices, RANK, 1536),
    ]
    plan = (
        ((6, 0, 1024), (6, 1, 1024), (2, None, 1024)),
        ((1, None, 384), (5, None, 384), (0, 3, 384), (0, 4, 384)),
        (
            (0, 0, 384),
            (0, 1, 384),
            (0, 2, 384),
            (7, None, 384),
        ),
        ((3, None, 384), (4, 0, 192), (4, 1, 192)),
    )

    def kernel(which, early_in, middle_in, late_in, factor_in, rows_in, grad_in, *refs):
        outs, rows_out, grad_out = refs[:8], refs[8], refs[9]
        acc, held = refs[10:18], refs[18:22]
        grad_low, grad_full, rows_held, sems, load_sem = refs[22:27]
        loads = []
        for i, src in enumerate((early_in, middle_in, factor_in, late_in)):
            loads.append(pltpu.make_async_copy(src, held[(0, 1, 3, 2)[i]], load_sem.at[i]))
        grad_load = pltpu.make_async_copy(grad_in, grad_low, load_sem.at[4])
        rows_load = pltpu.make_async_copy(rows_in, rows_held, load_sem.at[5])
        for cp in loads + [grad_load, rows_load]:
            cp.start()

        def add(piece, ref):
            def one_slot(origin, carry):
                row = which[origin % 4 + 4 * ((origin // 4 + origin) % 2)]
                for f in range(4):
                    at = 0
                    for out, table, n in plan[piece]:
                        value = ref[origin // 4, f % 2, origin % 4, f // 2, :, at : at + n].astype(F32)
                        cols = slice(f * n, (f + 1) * n)
                        if table is None:
                            acc[out][row, :, cols] += value
                        else:
                            acc[out][row, table, :, cols] += value
                        at += n
                return carry

            lax.fori_loop(0, 8, one_slot, 0)

        def send(out):
            cp = pltpu.make_async_copy(acc[out], outs[out], sems.at[out])
            cp.start()
            return cp

        for out in range(8):
            acc[out][...] = jnp.zeros_like(acc[out])
        loads[0].wait()
        add(0, held[0])
        copies = [send(out) for out in (2, 6)]
        loads[1].wait()
        add(1, held[1])
        copies += [send(out) for out in (1, 5)]
        loads[2].wait()
        add(3, held[3])
        copies += [send(out) for out in (3, 4)]
        loads[3].wait()
        add(2, held[2])
        copies += [send(out) for out in (0, 7)]
        grad_load.wait()
        grad_full[...] = grad_low[...].astype(F32)
        last = pltpu.make_async_copy(grad_full, grad_out, load_sem.at[6])
        last.start()
        rows_load.wait()
        rows_copy = pltpu.make_async_copy(rows_held, rows_out, load_sem.at[7])
        rows_copy.start()
        copies += [last, rows_copy]
        for cp in copies:
            cp.wait()

    hbm = pl.BlockSpec(memory_space=pl.ANY)
    return pl.pallas_call(
        kernel,
        out_shape=outs + [jax.ShapeDtypeStruct(out_rows.shape, BF16), f32(*grad_rows.shape)],
        in_specs=[pl.BlockSpec(memory_space=pltpu.SMEM)] + [hbm] * 6,
        out_specs=[hbm] * 10,
        scratch_shapes=[pltpu.VMEM(o.shape, F32) for o in outs]
        + [pltpu.VMEM(p.shape, BF16) for p in pieces]
        + [pltpu.VMEM(grad_rows.shape, BF16), pltpu.VMEM(grad_rows.shape, F32)]
        + [pltpu.VMEM(out_rows.shape, BF16), _sem(8), _sem(8)],
        compiler_params=pltpu.CompilerParams(vmem_limit_bytes=62 * 1024 * 1024),
        name="tables",
    )(adapters, *pieces, out_rows, grad_rows)


def rope_constants(rows):
    half = HEAD_DIM // 2
    freqs = np.float32(ROPE_BASE) ** (-(np.arange(half, dtype=np.float32) * 2.0 / HEAD_DIM))
    angles = np.arange(rows).astype(np.float32)[:, None] * freqs.astype(np.float32)[None, :]
    cos = np.cos(angles.astype(np.float64)).astype(np.float32)
    sin = np.sin(angles.astype(np.float64)).astype(np.float32)
    gap = np.zeros((rows, HALF_PAD - half), np.float32)
    cosine = np.concatenate([cos, gap, cos, gap], axis=1)
    sine = np.concatenate([-sin, gap, sin, gap], axis=1)
    return jnp.asarray(cosine), jnp.asarray(sine)


def dot(left, right):
    return jnp.dot(left, right, preferred_element_type=F32)


def dot_t(left, right):
    return lax.dot_general(left, right, (((1,), (1,)), ((), ())), preferred_element_type=F32)


def dot_rows(left, right):
    return lax.dot_general(left, right, (((0,), (0,)), ((), ())), preferred_element_type=F32)


def side_pad(value, before=0):
    return jnp.pad(value, ((0, 0), (before, SIDE - before - value.shape[1])))


def blocks(value):
    return value.reshape(2, 2, 2, 128, value.shape[-1])


def own_blocks(value):
    return value.reshape(2, 128, value.shape[-1])


def flat(value):
    return value.reshape(-1, value.shape[-1])


def slot_local(
    tokens,
    cotangent,
    lengths,
    slot_adapter_index,
    attention_norm_gain,
    feedforward_norm_gain,
    query_weight,
    key_weight,
    value_weight,
    output_weight,
    gate_weight,
    up_weight,
    down_weight,
    adapter_input_first,
    adapter_output_first,
    adapter_down_first,
    adapter_query_second,
    adapter_key_value_second,
    adapter_output_second,
    adapter_gate_up_second,
    adapter_down_second,
):
    rows = 4 * 2 * tokens.shape[1]
    cosine, sine = rope_constants(rows)
    turned = lambda t: jnp.swapaxes(t, -1, -2)
    (
        resid,
        normed_two_own,
        inner_o,
        tok_own,
        cot_order,
        _,
        qkv,
        stats,
        attn_b,
        one_cut,
        inner_qkv,
        weight_q,
        weight_kv,
        out_w,
        second_all,
        first_all,
        first_gu,
        second_g,
        second_u,
        first_d,
        second_d,
        first_o,
        second_o,
    ) = front_call(
        tokens,
        cotangent,
        lengths,
        slot_adapter_index,
        (attention_norm_gain[None, :], feedforward_norm_gain[None, :]),
        query_weight,
        turned(key_weight),
        turned(value_weight),
        output_weight,
        (
            turned(adapter_input_first),
            turned(adapter_output_first),
            turned(adapter_down_first),
            adapter_query_second,
            adapter_key_value_second,
            adapter_output_second,
            adapter_gate_up_second,
            adapter_down_second,
        ),
        cosine,
        sine,
        0,
    )
    grad_resid, grad_low_own, small, out_sums, out_far, order, early = feed_forward(
        normed_two_own,
        cot_order,
        resid,
        feedforward_norm_gain[None, :],
        lengths,
        (gate_weight, up_weight, down_weight),
        (first_gu, second_g, second_u, first_d, second_d),
        3,
    )
    out_rows, grad_rows, early, middle, late, factors = attend_back_call(
        grad_low_own,
        small,
        early,
        out_far,
        lengths,
        (out_sums, resid, tok_own, grad_resid, attention_norm_gain[None, :]),
        (
            qkv,
            stats,
            attn_b,
            flat(inner_o),
            order,
            cosine,
            sine,
            out_w,
            first_o,
            second_o,
            weight_q,
            weight_kv,
            second_all,
            first_all,
            second_d,
            one_cut,
            inner_qkv,
            cot_order,
        ),
        10,
    )
    full = table_call((early, middle, late, factors), out_rows, grad_rows, slot_adapter_index)
    turn = lambda t: jnp.swapaxes(t, -1, -2)
    return (
        full[8],
        full[9],
        turn(full[0]),
        turn(full[1]),
        turn(full[2]),
        full[3],
        full[4],
        full[5],
        full[6],
        full[7],
    )


def solution(mesh):
    one_slot = mesh.shape["ctx"] == 8 and mesh.shape["fsdp"] == 4
    return jax.shard_map(
        slot_local if one_slot else local,
        mesh=mesh,
        in_specs=(
            P("fsdp", "ctx", None),
            P("fsdp", "ctx", None),
            P(),
            P(),
            P(),
            P(),
            P(None, "fsdp"),
            P(None, "fsdp"),
            P(None, "fsdp"),
            P("fsdp", None),
            P(None, "fsdp"),
            P(None, "fsdp"),
            P("fsdp", None),
            P(),
            P(),
            P(),
            P(),
            P(),
            P(),
            P(),
            P(),
        ),
        out_specs=(
            P("fsdp", "ctx", None),
            P("fsdp", "ctx", None),
            P(),
            P(),
            P(),
            P(),
            P(),
            P(),
            P(),
            P(),
        ),
        check_vma=False,
    )
```

```python
import math

import jax
import jax.numpy as jnp
import numpy as np
from jax import lax
from jax.experimental import pallas as pl
from jax.experimental.pallas import tpu as pltpu
from jax.sharding import PartitionSpec as P

QUERY_HEADS = 16
KEY_VALUE_HEADS = 8
HEAD_DIM = 96


EPSILON = 1e-05
NEGATIVE = -1e30
ADAPTER_SCALE = 0.5
ROPE_BASE = 100000.0


def from_behind(x, axis, by):
    size = lax.axis_size(axis)
    return lax.ppermute(x, axis, [(i, (i + by) % size) for i in range(size)])


def rope_tables(positions, head_size):
    half_size = head_size // 2
    freqs = ROPE_BASE ** (-(jnp.arange(half_size, dtype=jnp.float32) * 2.0 / head_size))
    angles = positions.astype(jnp.float32)[:, None] * freqs[None, :]
    return (jnp.cos(angles)[:, None, :], jnp.sin(angles)[:, None, :])


def apply_rotation(values, cosine_table, sine_table):
    half_size = values.shape[-1] // 2
    first_half = values[..., :half_size]
    second_half = values[..., half_size:]
    return jnp.concatenate(
        [
            first_half * cosine_table - second_half * sine_table,
            second_half * cosine_table + first_half * sine_table,
        ],
        axis=-1,
    )


def rotate_back(gradient_tree, cosine_table, sine_table):
    half_size = gradient_tree.shape[-1] // 2
    first_half = gradient_tree[..., :half_size]
    second_half = gradient_tree[..., half_size:]
    return jnp.concatenate(
        [
            first_half * cosine_table + second_half * sine_table,
            second_half * cosine_table - first_half * sine_table,
        ],
        axis=-1,
    )


def rms_factor(values):
    return lax.rsqrt(jnp.mean(values * values, axis=-1, keepdims=True) + EPSILON)


def norm_back(values, factor, gain, grad_norm):
    scaled = grad_norm * gain
    return factor * scaled - values * factor**3 * jnp.mean(scaled * values, axis=-1, keepdims=True)


def pick_rows(onehot, table):
    return jnp.einsum("sa,a...->s...", onehot, table, preferred_element_type=jnp.float32).astype(
        jnp.bfloat16
    )


def spread_rows(onehot, gradient_tree):
    return jnp.einsum("sa,s...->a...", onehot, gradient_tree, precision=lax.Precision.HIGHEST)


def direct_product(input_rows, weight_matrix):
    return jnp.einsum("std,do->sto", input_rows, weight_matrix, preferred_element_type=jnp.float32)


def direct_back(gradient_tree, weight_matrix):
    return jnp.einsum(
        "sto,do->std", gradient_tree, weight_matrix, preferred_element_type=jnp.float32
    )


def inner_product_part(input_rows, down):
    return jnp.einsum("std,sdr->str", input_rows, down, preferred_element_type=jnp.float32)


def inner_back(gradient_tree, upward_rows):
    return ADAPTER_SCALE * jnp.einsum(
        "sto,sro->str", gradient_tree, upward_rows, preferred_element_type=jnp.float32
    )


def through_down(grad_inner, down):
    return jnp.einsum("str,sdr->std", grad_inner, down, preferred_element_type=jnp.float32)


def down_grad(input_rows, grad_inner):
    return jnp.einsum("std,str->sdr", input_rows, grad_inner, preferred_element_type=jnp.float32)


def upward_grad(inner_rows, gradient_tree):
    return ADAPTER_SCALE * jnp.einsum(
        "jvp,jvx->jpx", inner_rows, gradient_tree, preferred_element_type=jnp.float32
    )


def upward_apply(inner_rows, upward_rows):
    return ADAPTER_SCALE * jnp.einsum(
        "str,sro->sto", inner_rows, upward_rows, preferred_element_type=jnp.float32
    )


def project(input_rows, weight_matrix, down, upward_rows):
    inner_rows = inner_product_part(input_rows, down).astype(jnp.bfloat16)
    return (
        inner_rows,
        direct_product(input_rows, weight_matrix) + upward_apply(inner_rows, upward_rows),
    )


def project_back(input_rows, grad_output, weight_matrix, down, upward_rows, inner_rows):
    grad_upward = upward_grad(inner_rows, grad_output)
    grad_inner = inner_back(grad_output, upward_rows).astype(jnp.bfloat16)
    grad_down = down_grad(input_rows, grad_inner)
    grad_inputs = direct_back(grad_output, weight_matrix) + through_down(grad_inner, down)
    return (grad_inputs, grad_down, grad_upward)


def allowed_mask(key_start, key_count, query_pos, lengths):
    key_pos = key_start + jnp.arange(key_count, dtype=jnp.int32)
    causal = key_pos[None, :] <= query_pos[:, None]
    live = key_pos[None, :] < lengths[:, None]
    return (causal[None, :, :] & live[:, None, :])[:, None, None, :, :]


def attend_block(state, key_block, value_block, key_start, query_head_rows, query_pos, lengths):
    run_max, run_sum, run_acc = state
    scale = query_head_rows.shape[-1] ** (-0.5)
    scores = (
        jnp.einsum(
            "sqhgd,skhd->shgqk", query_head_rows, key_block, preferred_element_type=jnp.float32
        )
        * scale
    )
    allowed = allowed_mask(key_start, key_block.shape[1], query_pos, lengths)
    new_max = jnp.maximum(run_max, jnp.max(jnp.where(allowed, scores, NEGATIVE), axis=-1))
    weights = jnp.where(allowed, jnp.exp(scores - new_max[..., None]), 0.0)
    factor = jnp.exp(run_max - new_max)
    new_sum = run_sum * factor + jnp.sum(weights, axis=-1)
    update = jnp.einsum(
        "shgqk,skhd->shgqd",
        weights.astype(jnp.bfloat16),
        value_block,
        preferred_element_type=jnp.float32,
    )
    return (new_max, new_sum, run_acc * factor[..., None] + update)


def attend_back(
    key_block,
    value_block,
    key_start,
    query_head_rows,
    grad_heads,
    log_total,
    row_dot,
    query_pos,
    lengths,
):
    scale = query_head_rows.shape[-1] ** (-0.5)
    scores = (
        jnp.einsum(
            "sqhgd,skhd->shgqk", query_head_rows, key_block, preferred_element_type=jnp.float32
        )
        * scale
    )
    allowed = allowed_mask(key_start, key_block.shape[1], query_pos, lengths)
    probs = jnp.where(allowed, jnp.exp(scores - log_total[..., None]), 0.0)
    grad_probs = jnp.einsum(
        "sqhgd,skhd->shgqk", grad_heads, value_block, preferred_element_type=jnp.float32
    )
    grad_scores = (probs * (grad_probs - row_dot[..., None])).astype(jnp.bfloat16)
    grad_query = scale * jnp.einsum(
        "shgqk,skhd->sqhgd", grad_scores, key_block, preferred_element_type=jnp.float32
    )
    grad_key = scale * jnp.einsum(
        "shgqk,sqhgd->skhd", grad_scores, query_head_rows, preferred_element_type=jnp.float32
    )
    grad_value = jnp.einsum(
        "shgqk,sqhgd->skhd",
        probs.astype(jnp.bfloat16),
        grad_heads,
        preferred_element_type=jnp.float32,
    )
    return (grad_query, grad_key, grad_value)


def attend_forward(query_head_rows, key_head_rows, value_head_rows, lengths_used, query_pos):
    slots, rows, kv_heads, group_size, head_size = query_head_rows.shape
    key_flat = key_head_rows.reshape(slots, rows, kv_heads * head_size)
    value_flat = value_head_rows.reshape(slots, rows, kv_heads * head_size)
    stat_shape = (slots, kv_heads, group_size, rows)
    initial = (
        jnp.full(stat_shape, NEGATIVE, jnp.float32),
        jnp.zeros(stat_shape, jnp.float32),
        jnp.zeros(stat_shape + (head_size,), jnp.float32),
    )
    part_keys = lax.all_gather(key_flat, "ctx", axis=1, tiled=True)
    part_values = lax.all_gather(value_flat, "ctx", axis=1, tiled=True)
    piece_rows = part_keys.shape[1]
    part_keys = part_keys.reshape(slots, piece_rows, kv_heads, head_size)
    part_values = part_values.reshape(slots, piece_rows, kv_heads, head_size)
    span_rows = math.gcd(piece_rows, 4 * rows)

    def inner_step(block_index, inner_state):
        sub_keys = lax.dynamic_slice_in_dim(part_keys, block_index * span_rows, span_rows, 1)
        sub_values = lax.dynamic_slice_in_dim(part_values, block_index * span_rows, span_rows, 1)
        return attend_block(
            inner_state,
            sub_keys,
            sub_values,
            block_index * span_rows,
            query_head_rows,
            query_pos,
            lengths_used,
        )

    run_max, run_sum, run_acc = lax.fori_loop(0, piece_rows // span_rows, inner_step, initial)
    log_total = run_max + jnp.log(run_sum)
    attended = jnp.transpose(run_acc / run_sum[..., None], (0, 3, 1, 2, 4))
    return (attended, log_total)


def attend_backward(
    query_head_rows,
    key_head_rows,
    value_head_rows,
    grad_heads,
    attended,
    log_total,
    lengths_used,
    query_pos,
):
    ctx_count = lax.axis_size("ctx")
    own_index = lax.axis_index("ctx")
    rows = query_head_rows.shape[1]
    row_dot = jnp.transpose(
        jnp.sum(grad_heads.astype(jnp.float32) * attended, axis=-1), (0, 2, 3, 1)
    )

    def cycle_step(step_index, carried):
        carried_keys, carried_values, grad_query, grad_key, grad_value = carried
        block_id = (own_index + step_index) % ctx_count
        query_part, key_part, value_part = attend_back(
            carried_keys,
            carried_values,
            block_id * rows,
            query_head_rows,
            grad_heads,
            log_total,
            row_dot,
            query_pos,
            lengths_used,
        )
        grad_key, grad_value = (
            from_behind((grad_key + key_part).astype(jnp.bfloat16), "ctx", -1).astype(jnp.float32),
            from_behind((grad_value + value_part).astype(jnp.bfloat16), "ctx", -1).astype(
                jnp.float32
            ),
        )
        carried_keys, carried_values = from_behind((carried_keys, carried_values), "ctx", -1)
        return (carried_keys, carried_values, grad_query + query_part, grad_key, grad_value)

    key_zeros = jnp.zeros(key_head_rows.shape, jnp.float32)
    start_state = (
        key_head_rows,
        value_head_rows,
        jnp.zeros(query_head_rows.shape, jnp.float32),
        key_zeros,
        key_zeros,
    )
    carried = lax.fori_loop(0, ctx_count, cycle_step, start_state)
    return (carried[2], carried[3], carried[4])


def table_total(rotation_tables):
    return lax.psum(rotation_tables, ("ctx", "fsdp"))


def local(
    tokens,
    cotangent,
    lengths,
    slot_adapter_index,
    attention_norm_gain,
    feedforward_norm_gain,
    query_weight,
    key_weight,
    value_weight,
    output_weight,
    gate_weight,
    up_weight,
    down_weight,
    adapter_input_first,
    adapter_output_first,
    adapter_down_first,
    adapter_query_second,
    adapter_key_value_second,
    adapter_output_second,
    adapter_gate_up_second,
    adapter_down_second,
):
    slot_count, tok_rows, model_width = tokens.shape
    head_groups = QUERY_HEADS // KEY_VALUE_HEADS
    own_index = lax.axis_index("ctx")
    fsdp_index = lax.axis_index("fsdp")
    query_pos = own_index * tok_rows + jnp.arange(tok_rows, dtype=jnp.int32)
    cosine_table, sine_table = rope_tables(query_pos, HEAD_DIM)
    own_lengths = lax.dynamic_slice_in_dim(lengths, fsdp_index * slot_count, slot_count, 0)
    own_adapters = lax.dynamic_slice_in_dim(
        slot_adapter_index, fsdp_index * slot_count, slot_count, 0
    )
    valid = query_pos[None, :] < own_lengths[:, None]
    adapter_labels = jnp.arange(adapter_input_first.shape[0], dtype=jnp.int32)
    onehot_own = own_adapters[:, None] == adapter_labels[None, :]
    owned_low_rank = onehot_own.astype(jnp.bfloat16)
    own_full = onehot_own.astype(jnp.float32)
    tokens_f = tokens.astype(jnp.float32)
    factor_one = rms_factor(tokens_f)
    normed_one = (tokens_f * factor_one * attention_norm_gain).astype(jnp.bfloat16)
    grad_out = jnp.where(valid[..., None], cotangent, jnp.zeros((), jnp.bfloat16))
    input_first = pick_rows(owned_low_rank, adapter_input_first)
    output_second = pick_rows(owned_low_rank, adapter_output_second)
    down_second = pick_rows(owned_low_rank, adapter_down_second)
    output_first = pick_rows(owned_low_rank, adapter_output_first)
    down_first = pick_rows(owned_low_rank, adapter_down_first)
    query_second = pick_rows(owned_low_rank, adapter_query_second)
    key_value_second = pick_rows(owned_low_rank, adapter_key_value_second)
    gate_up_second = pick_rows(owned_low_rank, adapter_gate_up_second)
    weight_q, weight_k, weight_v, weight_gate, weight_up, weight_o, weight_down = (
        lax.all_gather(query_weight, "fsdp", axis=1, tiled=True),
        lax.all_gather(key_weight, "fsdp", axis=1, tiled=True),
        lax.all_gather(value_weight, "fsdp", axis=1, tiled=True),
        lax.all_gather(gate_weight, "fsdp", axis=1, tiled=True),
        lax.all_gather(up_weight, "fsdp", axis=1, tiled=True),
        lax.all_gather(output_weight, "fsdp", axis=0, tiled=True),
        lax.all_gather(down_weight, "fsdp", axis=0, tiled=True),
    )
    inner_q, projected_queries = project(normed_one, weight_q, input_first[:, 0], query_second)
    inner_k, projected_keys = project(
        normed_one, weight_k, input_first[:, 1], key_value_second[:, 0]
    )
    inner_v, projected_values = project(
        normed_one, weight_v, input_first[:, 2], key_value_second[:, 1]
    )
    query_head_rows = apply_rotation(
        projected_queries.reshape(slot_count, tok_rows, -1, HEAD_DIM), cosine_table, sine_table
    ).astype(jnp.bfloat16)
    query_head_rows = query_head_rows.reshape(slot_count, tok_rows, -1, head_groups, HEAD_DIM)
    key_head_rows = apply_rotation(
        projected_keys.reshape(slot_count, tok_rows, -1, HEAD_DIM), cosine_table, sine_table
    ).astype(jnp.bfloat16)
    value_head_rows = projected_values.astype(jnp.bfloat16).reshape(
        slot_count, tok_rows, -1, HEAD_DIM
    )
    attended, log_total = attend_forward(
        query_head_rows, key_head_rows, value_head_rows, own_lengths, query_pos
    )
    attn_b = attended.reshape(slot_count, tok_rows, -1).astype(jnp.bfloat16)
    inner_o, proj_o = project(attn_b, weight_o, output_first, output_second)
    resid = tokens_f + proj_o
    factor_two = rms_factor(resid)
    normed_two = (resid * factor_two * feedforward_norm_gain).astype(jnp.bfloat16)
    inner_gate, gate = project(normed_two, weight_gate, input_first[:, 3], gate_up_second[:, 0])
    inner_up, up_proj = project(normed_two, weight_up, input_first[:, 4], gate_up_second[:, 1])
    sigmoid_gate = jax.nn.sigmoid(gate)
    hidden = (gate * sigmoid_gate * up_proj).astype(jnp.bfloat16)
    inner_down, proj_down = project(hidden, weight_down, down_first, down_second)
    out_tokens = jnp.where(valid[..., None], resid + proj_down, 0.0).astype(jnp.bfloat16)
    grad_hidden, grad_da, grad_db = project_back(
        hidden, grad_out, weight_down, down_first, down_second, inner_down
    )
    grad_gate = (grad_hidden * up_proj * sigmoid_gate * (1.0 + gate * (1.0 - sigmoid_gate))).astype(
        jnp.bfloat16
    )
    grad_up = (grad_hidden * gate * sigmoid_gate).astype(jnp.bfloat16)
    from_gate, grad_ga, grad_gb = project_back(
        normed_two, grad_gate, weight_gate, input_first[:, 3], gate_up_second[:, 0], inner_gate
    )
    from_up, grad_ua, grad_ub = project_back(
        normed_two, grad_up, weight_up, input_first[:, 4], gate_up_second[:, 1], inner_up
    )
    grad_normed_two = (from_gate + from_up).astype(jnp.bfloat16).astype(jnp.float32)
    grad_resid = grad_out.astype(jnp.float32) + norm_back(
        resid, factor_two, feedforward_norm_gain, grad_normed_two
    )
    grad_resid_low = grad_resid.astype(jnp.bfloat16)
    from_attn, grad_oa, grad_ob = project_back(
        attn_b, grad_resid_low, weight_o, output_first, output_second, inner_o
    )
    grad_heads = from_attn.astype(jnp.bfloat16).reshape(attended.shape)
    grad_query, grad_key, grad_value = attend_backward(
        query_head_rows,
        key_head_rows,
        value_head_rows,
        grad_heads,
        attended,
        log_total,
        own_lengths,
        query_pos,
    )
    grad_proj_q = (
        rotate_back(
            grad_query.reshape(slot_count, tok_rows, -1, HEAD_DIM), cosine_table, sine_table
        )
        .astype(jnp.bfloat16)
        .reshape(slot_count, tok_rows, -1)
    )
    grad_proj_k = (
        rotate_back(grad_key, cosine_table, sine_table)
        .astype(jnp.bfloat16)
        .reshape(slot_count, tok_rows, -1)
    )
    grad_proj_v = grad_value.astype(jnp.bfloat16).reshape(slot_count, tok_rows, -1)
    from_query, grad_qa, grad_qb = project_back(
        normed_one, grad_proj_q, weight_q, input_first[:, 0], query_second, inner_q
    )
    from_key, grad_ka, grad_kb = project_back(
        normed_one, grad_proj_k, weight_k, input_first[:, 1], key_value_second[:, 0], inner_k
    )
    from_value, grad_va, grad_vb = project_back(
        normed_one, grad_proj_v, weight_v, input_first[:, 2], key_value_second[:, 1], inner_v
    )
    grad_normed_one = (from_query + from_key + from_value).astype(jnp.bfloat16).astype(jnp.float32)
    grad_tokens = grad_resid + norm_back(tokens_f, factor_one, attention_norm_gain, grad_normed_one)
    slot_grads = (
        jnp.stack([grad_qa, grad_ka, grad_va, grad_ga, grad_ua], axis=1),
        grad_oa,
        grad_da,
        grad_qb,
        jnp.stack([grad_kb, grad_vb], axis=1),
        grad_ob,
        jnp.stack([grad_gb, grad_ub], axis=1),
        grad_db,
    )
    summed = table_total(tuple((spread_rows(own_full, entry_item) for entry_item in slot_grads)))
    return (
        out_tokens,
        grad_tokens,
        summed[0],
        summed[1],
        summed[2],
        summed[3],
        summed[4],
        summed[5],
        summed[6],
        summed[7],
    )


BF16 = jnp.bfloat16
F32 = jnp.float32
MESH_ID = pl.DeviceIdType.MESH
RANK = 16
SIDE = 128
PAD_HEAD = 128
HALF_PAD = 64


def _sem(count):
    return pltpu.SemaphoreType.DMA((count,))


def _place():
    c = lax.axis_index("ctx")
    f = lax.axis_index("fsdp")
    x = f // 2
    core = f % 2
    return c, f, x, core, (c, 2 * x + 1 - core), (c, 2 * (1 - x) + core)


def _slot_of(c):
    return c // 2 + 4 * ((c // 2 + c) % 2)


def _group_of(slot):
    return 2 * (slot % 4) + (slot // 4 + slot) % 2


def _block(x, core, j):
    return 4 * (1 - core) + 2 * j + (x + j) % 2


def _owner(b):
    return 2 * ((b // 2 + b) % 2) + 1 - b // 4


def _greet(targets):
    barrier = pltpu.get_barrier_semaphore()
    for target in targets:
        pl.semaphore_signal(barrier, inc=1, device_id=target, device_id_type=MESH_ID)
    pl.semaphore_wait(barrier, len(targets))


def _remote(src, dst, send, recv, target):
    return pltpu.make_async_remote_copy(
        src_ref=src, dst_ref=dst, send_sem=send, recv_sem=recv, device_id=target, device_id_type=MESH_ID
    )


def _comm_call(kernel, ins, outs, scratch, cid, name, in_space=pl.ANY, out_space=pl.ANY, vmem=None):
    return pl.pallas_call(
        kernel,
        out_shape=outs,
        in_specs=[pl.BlockSpec(memory_space=in_space)] * len(ins),
        out_specs=jax.tree.map(lambda _: pl.BlockSpec(memory_space=out_space), outs),
        scratch_shapes=scratch,
        compiler_params=pltpu.CompilerParams(
            collective_id=cid, has_side_effects=True, vmem_limit_bytes=vmem
        ),
        name=name,
    )(*ins)


def _gather_steps(ins, outs, own_sem, send_sem, recv_sem, place):
    c, f, x, core, core_peer, x_peer = place
    h = 1 - core
    count = len(ins)
    local = []
    sends = []

    def first():
        for base, target in ((0, x_peer), (2 * count, core_peer)):
            for i in range(count):
                for j in range(2):
                    k = base + i * 2 + j
                    cp = _remote(
                        ins[i].at[j], outs[i].at[h, j, (x + j) % 2], send_sem.at[k], recv_sem.at[k], target
                    )
                    cp.start()
                    sends.append(cp)
        for i in range(count):
            for j in range(2):
                lc = pltpu.make_async_copy(
                    ins[i].at[j], outs[i].at[h, j, (x + j) % 2], own_sem.at[i * 2 + j]
                )
                lc.start()
                local.append(lc)

    def last():
        forwards = []
        for i in range(count):
            for j in range(2):
                k = i * 2 + j
                sends[k].wait_recv()
                cp = _remote(
                    outs[i].at[h, j, (x + j + 1) % 2],
                    outs[i].at[h, j, (x + j + 1) % 2],
                    send_sem.at[4 * count + k],
                    recv_sem.at[4 * count + k],
                    core_peer,
                )
                cp.start()
                forwards.append(cp)
        for k in range(2 * count):
            sends[2 * count + k].wait_recv()
            forwards[k].wait_recv()
        for cp in sends + forwards:
            cp.wait_send()
        for lc in local:
            lc.wait()

    return first, last


def _ctx_first(piece, lines, own_sem, send_sem, recv_sem, place):
    c, f, x, core, core_peer, x_peer = place
    z, y = c // 2, c % 2
    sends = []
    local = []

    def start():
        lc = pltpu.make_async_copy(piece, lines.at[z, x], own_sem)
        lc.start()
        local.append(lc)
        cp = _remote(piece, lines.at[z, x], send_sem.at[0], recv_sem.at[0], x_peer)
        cp.start()
        sends.append(cp)

    def spread():
        local[0].wait()
        sends[0].wait_recv()
        for step in range(1, 4):
            cp = _remote(
                lines.at[z],
                lines.at[z],
                send_sem.at[step],
                recv_sem.at[step],
                (2 * ((z + step) % 4) + y, f),
            )
            cp.start()
            sends.append(cp)

    def finish():
        for cp in sends[1:]:
            cp.wait_recv()
        for cp in sends:
            cp.wait_send()

    return start, spread, finish


def _ctx_second(lines, out, own_sem, send_sem, recv_sem, place):
    c, f, x, core, core_peer, x_peer = place
    z, y = c // 2, c % 2
    y_peer = (2 * z + 1 - y, f)
    sends = []
    local = []

    def start():
        lc = pltpu.make_async_copy(lines, out.at[y, core], own_sem)
        lc.start()
        local.append(lc)
        for k, target in ((0, y_peer), (1, core_peer)):
            cp = _remote(lines, out.at[y, core], send_sem.at[k], recv_sem.at[k], target)
            cp.start()
            sends.append(cp)

    def share():
        sends[0].wait_recv()
        cp = _remote(
            out.at[1 - y, core], out.at[1 - y, core], send_sem.at[2], recv_sem.at[2], core_peer
        )
        cp.start()
        sends.append(cp)

    def finish():
        sends[1].wait_recv()
        sends[2].wait_recv()
        for cp in sends:
            cp.wait_send()
        local[0].wait()

    return start, share, finish


def _ctx_planes(piece, out, own_sem, send_sem, recv_sem, place):
    c, f, x, core, core_peer, x_peer = place
    z, y = c // 2, c % 2
    y_peer = (2 * z + 1 - y, f)
    sends = {}
    local = []

    def send(k, src, dst, target):
        cp = _remote(src, dst, send_sem.at[k], recv_sem.at[k], target)
        cp.start()
        sends[k] = cp

    def spot(yy, zz):
        return out.at[yy, core, zz, x]

    def start():
        lc = pltpu.make_async_copy(piece, spot(y, z), own_sem)
        lc.start()
        local.append(lc)
        for step in range(1, 4):
            send(step, piece, spot(y, z), (2 * ((z + step) % 4) + y, f))
        send(4, piece, spot(y, z), y_peer)
        send(8, piece, spot(y, z), x_peer)

    def forward():
        for step in range(1, 4):
            sends[step].wait_recv()
            at = spot(y, (z + 4 - step) % 4)
            send(4 + step, at, at, y_peer)
            send(8 + step, at, at, x_peer)
        for step in range(4):
            sends[4 + step].wait_recv()
            at = spot(1 - y, (z + 4 - step) % 4)
            send(12 + step, at, at, x_peer)

    def finish():
        local[0].wait()
        for half in range(2):
            for step in range(4):
                sends[8 + 4 * half + step].wait_recv()
            yy = 1 - y if half else y
            send(16 + half, out.at[yy, core], out.at[yy, core], core_peer)
        for half in range(2):
            sends[16 + half].wait_recv()
        for cp in sends.values():
            cp.wait_send()

    return start, forward, finish


def _z_peers(place):
    c, f = place[:2]
    return [(2 * ((c // 2 + step) % 4) + c % 2, f) for step in range(1, 4)]


def _y_peer(place):
    c, f = place[:2]
    return (2 * (c // 2) + 1 - c % 2, f)


def _lines_of(n):
    return (4, 2, RANK, n)


def _spread_of(n):
    return jax.ShapeDtypeStruct((2, 2, 4, 2, RANK, n), BF16)


FIRST_SEMS = [pltpu.SemaphoreType.DMA(()), _sem(4), _sem(4)]
SECOND_SEMS = [pltpu.SemaphoreType.DMA(()), _sem(3), _sem(3)]
PLANE_SEMS = [pltpu.SemaphoreType.DMA(()), _sem(18), _sem(18)]


def _order_steps(own, order, own_sem, send_sem, recv_sem, place):
    core_peer, x_peer = place[4:]
    sends, local, forwards = [], [], []

    def first():
        for j in range(2):
            cp = _remote(own.at[j], order.at[1 + j, 1], send_sem.at[j], recv_sem.at[j], x_peer)
            cp.start()
            sends.append(cp)
        for j in range(2):
            cp = _remote(
                own.at[j], order.at[3, j], send_sem.at[2 + j], recv_sem.at[2 + j], core_peer
            )
            cp.start()
            sends.append(cp)
        for j in range(2):
            lc = pltpu.make_async_copy(own.at[j], order.at[0, j], own_sem.at[j])
            lc.start()
            local.append(lc)

    def forward(j):
        sends[j].wait_recv()
        cp = _remote(
            order.at[1 + j, 1],
            order.at[1 + j, 0],
            send_sem.at[4 + j],
            recv_sem.at[4 + j],
            core_peer,
        )
        cp.start()
        forwards.append(cp)

    def own_here():
        for lc in local:
            lc.wait()

    def core_here():
        for j in range(2):
            sends[2 + j].wait_recv()

    def far_here(j):
        forwards[j].wait_recv()

    def last():
        for cp in sends + forwards:
            cp.wait_send()

    return first, forward, own_here, core_here, far_here, last


def _order_all(own, order, sems, place):
    first, forward, own_here, core_here, far_here, last = _order_steps(own, order, *sems, place)
    first()
    own_here()
    for j in range(2):
        forward(j)
    core_here()
    for j in range(2):
        far_here(j)
    last()


def feed_forward(own, cot, resid, gain, length, weights, adapters, cid):
    gate_w, up_w, down_w = weights
    width, units = gate_w.shape
    wide = width + SIDE
    tile = 256

    loads_in = tuple(weights) + tuple(adapters) + (cot,)
    count = len(loads_in)

    def kernel(*refs):
        len_ref, own_ref, resid_ref, gain_ref = refs[:4]
        loads_hbm = refs[4 : 4 + count]
        outs_hbm = refs[4 + count : 11 + count]
        mirrors = refs[len(refs) - 8 : len(refs) - 1]
        grad_resid, grad_low, small, out_own, out_far, order, early = mirrors
        flush_sem = refs[len(refs) - 1]
        refs = refs[11 + count : len(refs) - 8]
        flushed = []

        def flush(*places):
            for at in places:
                cp = pltpu.make_async_copy(mirrors[at], outs_hbm[at], flush_sem.at[at])
                cp.start()
                flushed.append(cp)

        gate_ref, up_ref, down_ref, first_ref, sg_ref, su_ref, fd_ref, sd_ref, go_ref = refs[:count]
        (
            sums,
            hid_s,
            gg_s,
            gu_s,
            in_s,
            gid_s,
            part,
            out_part,
            near,
            out_near,
            far,
            out_land,
            staged,
            landed,
            load_sem,
            own_sem,
            send_sem,
            recv_sem,
            s_sem,
            r_sem,
        ) = refs[count:]
        place = _place()
        core_peer, x_peer = place[4:]
        loads = []
        for i in range(count):
            cp = pltpu.make_async_copy(loads_hbm[i], refs[i], load_sem.at[i])
            cp.start()
            loads.append(cp)
        _greet([core_peer, x_peer])
        first, forward, own_here, core_here, far_here, last = _order_steps(
            own_ref, order, own_sem, send_sem, recv_sem, place
        )
        first()
        copies = []
        c, f, x, core = place[:4]
        live = len_ref[_slot_of(c)]

        def masked(step):
            other_x = x if step in (0, 3) else 1 - x
            pieces = []
            for k in range(2):
                other_core = (core, 1 - core)[step == 3 or (step in (1, 2) and k == 0)]
                j = k if step in (0, 3) else step - 1
                pos = 128 * _block(other_x, other_core, j) + lax.broadcasted_iota(jnp.int32, (128, width), 0)
                pieces.append(jnp.where(pos < live, go_ref[step, k].astype(F32), 0.0).astype(BF16))
            return pieces

        def work(step):
            rows = order[step].reshape(2 * 128, width)
            pieces = masked(step)
            for k in range(2):
                go_ref[step, k] = pieces[k]
            go = go_ref[step].reshape(2 * 128, width)
            inner = dot_t(rows, first_ref[...]).astype(BF16)
            gid = dot_t(go, sd_ref[...]).astype(BF16)
            in_s[step] = inner
            gid_s[step] = gid
            for at in range(0, units, tile):
                cols = slice(at, at + tile)
                gate = dot(rows, gate_ref[:, cols]) + dot(inner, sg_ref[:, cols])
                up = dot(rows, up_ref[:, cols]) + dot(inner, su_ref[:, cols])
                grad = dot_t(go, down_ref[cols, :]) + dot(gid, fd_ref[:, cols])
                sig = 0.5 * jnp.tanh(0.5 * gate) + 0.5
                silu = gate * sig
                hid_s[step, :, cols] = (silu * up).astype(BF16)
                gg_s[step, :, cols] = (grad * up * sig * (1.0 + gate * (1.0 - sig))).astype(BF16)
                gu_s[step, :, cols] = (grad * silu).astype(BF16)
            gg, gu = gg_s[step], gu_s[step]
            for at in range(0, width, tile):
                cols = slice(at, at + tile)
                value = dot_t(gg, gate_ref[cols, :]) + dot_t(gu, up_ref[cols, :])
                if step == 0:
                    sums[:, :, cols] = value.reshape(2, 128, tile)
                else:
                    part[step - 1, :, :, cols] = value.astype(BF16).reshape(2, 128, tile)
            value = dot_t(gg, sg_ref[...]) + dot_t(gu, su_ref[...])
            if step == 0:
                sums[:, :, width:] = value.reshape(2, 128, SIDE)
            else:
                part[step - 1, :, :, width:] = value.astype(BF16).reshape(2, 128, SIDE)

        def down(step):
            hid = hid_s[step]
            for at in range(0, width, tile):
                cols = slice(at, at + tile)
                out = dot(hid, down_ref[:, cols])
                if step == 0:
                    out_own[:, :, cols] = out.reshape(2, 128, tile)
                else:
                    out_part[step - 1, :, :, cols] = out.astype(BF16).reshape(2, 128, tile)
            out = dot_t(hid, fd_ref[...])
            if step == 0:
                out_own[:, :, width:] = out.reshape(2, 128, SIDE)
            else:
                out_part[step - 1, :, :, width:] = out.astype(BF16).reshape(2, 128, SIDE)

        def send(src, dst, k, target):
            cp = _remote(src, dst, s_sem.at[k], r_sem.at[k], target)
            cp.start()
            copies.append(cp)
            return cp

        own_here()
        for cp in loads:
            cp.wait()
        work(0)
        across, out_cps = [], []

        def leave(j, cp):
            cp.wait_recv()
            staged[j] = (part[j, 1].astype(F32) + far[j].astype(F32)).astype(BF16)
            across.append(send(staged.at[j], landed.at[j], 6 + j, x_peer))

        for j in range(2):
            forward(j)
            far_here(j)
            work(1 + j)
            cp = send(part.at[j, 0], far.at[j], 2 + j, core_peer)
            down(1 + j)
            out_cps.append(send(out_part.at[j, 0], out_land.at[j], 4 + j, core_peer))
            leave(j, cp)
        core_here()
        flush(5)
        work(3)
        near_cp = [send(part.at[2], near, 0, core_peer)]
        down(3)
        near_cp.append(send(out_part.at[2], out_near, 1, core_peer))
        down(0)
        for j in range(2):
            out_cps[j].wait_recv()
            out_far[j] = (out_part[j, 1].astype(F32) + out_land[j].astype(F32)).astype(BF16)
        for cp in near_cp:
            cp.wait_recv()
        sums[...] = sums[...] + near[...].astype(F32)
        out_own[...] = out_own[...] + out_near[...].astype(F32)
        for at in range(0, units, 512):
            cols = slice(at, at + 512)
            g = jnp.zeros((SIDE, 512), F32)
            u = jnp.zeros((SIDE, 512), F32)
            d = jnp.zeros((SIDE, 512), F32)
            for step in range(4):
                g += dot_rows(in_s[step], gg_s[step, :, cols])
                u += dot_rows(in_s[step], gu_s[step, :, cols])
                d += dot_rows(gid_s[step], hid_s[step, :, cols])
            early[:, at : at + 512] = (ADAPTER_SCALE * g[:RANK]).astype(BF16)
            early[:, units + at : units + at + 512] = (ADAPTER_SCALE * u[RANK : 2 * RANK]).astype(BF16)
            early[:, 2 * units + at : 2 * units + at + 512] = d[3 * RANK : 4 * RANK].astype(BF16)
        flush(3, 4, 6)
        for j in range(2):
            across[j].wait_recv()
            total = sums[j] + landed[j].astype(F32)
            gi = total[:, width:].astype(BF16)
            small[j] = gi
            gn = (total[:, :width] + dot(gi, first_ref[...])).astype(BF16).astype(F32)
            v = resid_ref[j]
            factor = lax.rsqrt(jnp.mean(v * v, axis=1, keepdims=True) + EPSILON)
            scaled = gn * gain_ref[...].reshape(1, width)
            mean = jnp.mean(scaled * v, axis=1, keepdims=True)
            grad = go_ref[0, j].astype(F32) + factor * scaled - v * (factor * factor * factor) * mean
            grad_resid[j] = grad
            grad_low[j] = grad.astype(BF16)
        flush(0, 1, 2)
        last()
        for cp in copies:
            cp.wait_send()
        for cp in flushed:
            cp.wait()

    vmem = pl.BlockSpec(memory_space=pltpu.VMEM)
    rows = (2, 128, wide)
    f32 = lambda *shape: jax.ShapeDtypeStruct(shape, F32)
    outs = [
        f32(2, 128, width),
        jax.ShapeDtypeStruct((2, 128, width), BF16),
        jax.ShapeDtypeStruct((2, 128, SIDE), BF16),
        f32(*rows),
        jax.ShapeDtypeStruct(rows, BF16),
        jax.ShapeDtypeStruct((4, 2, 128, width), BF16),
        jax.ShapeDtypeStruct((RANK, 3 * units), BF16),
    ]
    hbm = pl.BlockSpec(memory_space=pl.ANY)
    return pl.pallas_call(
        kernel,
        out_shape=outs,
        in_specs=[pl.BlockSpec(memory_space=pltpu.SMEM), vmem, vmem, vmem] + [hbm] * count,
        out_specs=[hbm] * len(outs),
        scratch_shapes=[pltpu.VMEM(a.shape, a.dtype) for a in loads_in]
        + [pltpu.VMEM(rows, F32)]
        + [pltpu.VMEM((4, 256, units), BF16)] * 3
        + [pltpu.VMEM((4, 256, SIDE), BF16)] * 2
        + [pltpu.VMEM((3,) + rows, BF16)] * 2
        + [pltpu.VMEM(rows, BF16)] * 6
        + [_sem(count), _sem(2), _sem(6), _sem(6), _sem(8), _sem(8)]
        + [pltpu.VMEM(o.shape, o.dtype) for o in outs]
        + [_sem(len(outs))],
        compiler_params=pltpu.CompilerParams(
            collective_id=cid, has_side_effects=True, vmem_limit_bytes=58 * 1024 * 1024
        ),
        name="feed_forward",
    )(length, own, resid, gain, *loads_in)


def _back_steps(src, dst, out_s, out_r, place):
    c, f, x, core = place[:4]
    slot = _slot_of(c)
    place_in = slot % 2

    def move(j):
        return _remote(
            src.at[j],
            dst.at[place_in],
            out_s.at[j],
            out_r.at[place_in],
            (_block(x, core, j), slot // 2),
        )

    def first(j):
        move(j).start()

    def last():
        for half in range(2):
            pltpu.make_async_copy(dst.at[half], dst.at[half], out_r.at[half]).wait()
        for j in range(2):
            move(j).wait_send()

    return first, last


def _back_sources(place):
    c, f = place[:2]
    return [(_group_of(2 * f + half), _owner(c)) for half in range(2)]


def front_call(
    tokens,
    cotangent,
    lengths,
    adapters,
    gains,
    wq,
    wk,
    wv,
    wo,
    tables,
    cosine,
    sine,
    cid,
):
    width = tokens.shape[-1]
    rows = cosine.shape[0]
    wide = width + SIDE
    block = 256
    scale = HEAD_DIM ** (-0.5)
    lane = PAD_HEAD
    units = tables[6].shape[-1] // 4
    quarter = width // 4
    loads_in = gains + (wq, wk, wv, wo) + tables + (cosine, sine)
    count = len(loads_in)

    vmem, hbm = pl.BlockSpec(memory_space=pltpu.VMEM), pl.BlockSpec(memory_space=pl.ANY)
    smem = pl.BlockSpec(memory_space=pltpu.SMEM)
    low = lambda *shape: jax.ShapeDtypeStruct(shape, BF16)
    outs = [
        (jax.ShapeDtypeStruct((2, 128, width), F32), vmem),
        (low(2, 128, width), vmem),
        (low(2, 2, 2, 128, SIDE), hbm),
        (low(2, 128, width), vmem),
        (low(4, 2, 128, width), hbm),
        (low(2, 128, width), hbm),
        (low(rows, 8 * lane), vmem),
        (jax.ShapeDtypeStruct((rows, lane), F32), vmem),
        (low(rows, 4 * lane), vmem),
        (low(rows, quarter), vmem),
        (low(rows, SIDE), vmem),
        (low(width, 4 * lane), vmem),
        (low(4 * lane, width), vmem),
        (low(4 * lane, width), vmem),
        (low(SIDE, 8 * lane), vmem),
        (low(SIDE, width), vmem),
        (low(SIDE, width), vmem),
        (low(SIDE, units), vmem),
        (low(SIDE, units), vmem),
        (low(SIDE, units), vmem),
        (low(SIDE, width), vmem),
        (low(SIDE, 4 * lane), vmem),
        (low(SIDE, width), vmem),
    ]
    mirror_of = []
    for o in outs:
        mirror_of.append(sum(m >= 0 for m in mirror_of) if o[1] is vmem else -1)
    mirrored = sum(m >= 0 for m in mirror_of) + 1

    def kernel(*refs):
        len_ref, adapter_ref, tok_ref, cot_ref = refs[:4]
        loads_hbm = refs[4 : 4 + count]
        (
            sums_resid,
            normed_two,
            side_all,
            tok_own,
            cot_order,
            cot_peer,
            qkv_ref,
            lse_ref,
            att_ref,
            one_cut,
            inner_ref,
            wa_ref,
            wkv_ref,
            ow_ref,
            sa_ref,
            fa_ref,
            fgu_ref,
            sg_ref,
            su_ref,
            fd_ref,
            sd_ref,
            fo_ref,
            so_ref,
        ) = [
            refs[len(refs) - mirrored + k] if k >= 0 else out
            for k, out in zip(mirror_of, refs[4 + count : 27 + count])
        ]
        outs_hbm = refs[4 + count : 27 + count]
        mirrors = refs[len(refs) - mirrored : len(refs) - 1]
        flush_sem = refs[len(refs) - 1]
        refs = refs[27 + count :]
        flushed = []

        def flush(*places):
            for at in places:
                n = mirror_of[at]
                cp = pltpu.make_async_copy(mirrors[n], outs_hbm[at], flush_sem.at[n])
                cp.start()
                flushed.append(cp)

        gain_one, gain_two, wq_v, wk_v, wv_v, wo_v = refs[:6]
        in_first, out_first, down_first, q_second, kv_second, o_second, gu_second, d_second = refs[6:14]
        cos_ref, sin_ref = refs[14:16]
        (
            tok_all,
            one_ref,
            part,
            land,
            staged,
            landed,
            sums,
            side_own,
            load_sem,
            land_s,
            land_r,
            cot_s,
            cot_r,
            send_sem,
            recv_sem,
            s_sem,
            r_sem,
        ) = refs[16:33]
        side_sems = refs[33:36]
        place = _place()
        c, f, x, core, core_peer, x_peer = place
        hh = 1 - core
        slot = _slot_of(c)
        live = len_ref[slot]
        which = adapter_ref[slot]
        loads = []
        for i in range(count):
            cp = pltpu.make_async_copy(loads_hbm[i], refs[i], load_sem.at[i])
            cp.start()
            loads.append(cp)

        barrier = pltpu.get_barrier_semaphore()
        for j in range(2):
            pl.semaphore_signal(
                barrier, inc=1, device_id=(_block(x, core, j), slot // 2), device_id_type=MESH_ID
            )
        for target in (core_peer, x_peer):
            pl.semaphore_signal(barrier, inc=1, device_id=target, device_id_type=MESH_ID)
        for b in range(4):
            pl.semaphore_signal(
                barrier,
                inc=1,
                device_id=(4 * hh + b, 2 * x + (slot // 2) % 2),
                device_id_type=MESH_ID,
            )
        pl.semaphore_wait(barrier, 8)
        to_f = _owner(c)
        to_h = c // 4
        to_j = (c // 2) % 2
        to_i = c % 2
        moves = []
        for part_row in range(2):
            span = pl.ds(64 * part_row, 64)
            for half in range(2):
                s = 2 * f + half
                cp = _remote(
                    tok_ref.at[half, span],
                    tok_all.at[to_h, to_j, to_i, span],
                    land_s.at[2 * part_row + half],
                    land_r.at[2 * part_row + to_j],
                    (_group_of(s), to_f),
                )
                cp.start()
                moves.append(cp)
        cross = [
            _remote(cot_ref.at[half], cot_peer.at[half], cot_s.at[half], cot_r.at[half], x_peer)
            for half in range(2)
        ]
        cross[0].start()
        cot_moves = []
        for relay in range(2):
            for half in range(2):
                s = 2 * (2 * ((x + relay) % 2) + core) + half
                away = ((c // 2 + c) % 2 + x) % 2
                cot_moves.append(
                    _remote(
                        (cot_peer if relay else cot_ref).at[half],
                        cot_order.at[away * (1 + to_j), (1 - away) * to_j + away],
                        cot_s.at[2 + 2 * relay + half],
                        cot_r.at[2 + 2 * away + to_j],
                        (_group_of(s), 2 * x + 1 - to_h),
                    )
                )
        for cp in loads:
            cp.wait()

        def group_sends(part_row):
            span = pl.ds(64 * part_row, 64)
            for j in range(2):
                pltpu.make_async_copy(
                    tok_all.at[hh, j, (x + j) % 2, span],
                    tok_all.at[hh, j, (x + j) % 2, span],
                    land_r.at[2 * part_row + j],
                ).wait()
                k = 2 * part_row + j
                here = tok_all.at[hh, j, (x + j) % 2, span]
                for base, target in ((0, x_peer), (4, core_peer)):
                    cp = _remote(
                        here, here, send_sem.at[base + k], recv_sem.at[base + k], target
                    )
                    cp.start()
                    sends[base + k] = cp

        sends = {}

        def prepare_first():
            half = HEAD_DIM // 2
            wa_ref[...] = jnp.zeros_like(wa_ref)
            wkv_ref[...] = jnp.zeros_like(wkv_ref)
            sa_ref[...] = jnp.zeros_like(sa_ref)
            for head in range(4):
                for side in range(2):
                    at = head * HEAD_DIM + side * half
                    to = head * lane + side * HALF_PAD
                    wa_ref[:, to : to + half] = wq_v[:, at : at + half]
            for head in range(2):
                for side in range(2):
                    at = head * HEAD_DIM + side * half
                    to = head * lane + side * HALF_PAD
                    wkv_ref[to : to + half, :] = wk_v[at : at + half, :]
                at, to = head * HEAD_DIM, (2 + head) * lane
                wkv_ref[to : to + HEAD_DIM, :] = wv_v[at : at + HEAD_DIM, :]

        def prepare_second():
            half = HEAD_DIM // 2
            own_cols = pl.ds(pl.multiple_of(f * quarter, 128), quarter)
            own_units = pl.ds(pl.multiple_of(f * units, 128), units)
            low = lambda v: (ADAPTER_SCALE * v.astype(F32)).astype(BF16)
            for ref in (fa_ref, fgu_ref, sg_ref, su_ref, fd_ref, sd_ref, fo_ref, so_ref, ow_ref):
                ref[...] = jnp.zeros_like(ref)
            for i in range(3):
                fa_ref[i * RANK : (i + 1) * RANK, :] = in_first[which, i]
            for i in range(2):
                fgu_ref[i * RANK : (i + 1) * RANK, :] = in_first[which, 3 + i]
            all_gu = gu_second.at[:, :, :, own_units]
            sg_ref[:RANK, :] = low(all_gu[which, 0])
            su_ref[RANK : 2 * RANK, :] = low(all_gu[which, 1])
            fd_ref[3 * RANK : 4 * RANK, :] = down_first.at[:, :, own_units][which]
            sd_ref[3 * RANK : 4 * RANK, :] = low(d_second[which])
            so_ref[:RANK, :] = low(o_second[which])
            own_first = out_first.at[:, :, own_cols][which]
            own_q = low(q_second.at[:, :, own_cols][which])
            for head in range(4):
                at = head * HEAD_DIM
                fo_ref[:RANK, head * lane : head * lane + HEAD_DIM] = own_first[:, at : at + HEAD_DIM]
                ow_ref[head * lane : head * lane + HEAD_DIM, :] = wo_v[at : at + HEAD_DIM, :]
                for side in range(2):
                    to = head * lane + side * HALF_PAD
                    sa_ref[:RANK, to : to + half] = own_q[:, at + side * half : at + (side + 1) * half]
            window = pl.ds(pl.multiple_of((3 * f // 2) * 128, 128), 256)
            for i in range(2):
                own_kv = kv_second.at[:, :, :, window][which, i].astype(F32)
                shifted = pltpu.roll(own_kv, 256 - 64, 1)
                own_kv = low(jnp.where(f % 2 == 1, shifted, own_kv))
                for head in range(2):
                    at = head * HEAD_DIM
                    if i:
                        to = (6 + head) * lane
                        sa_ref[2 * RANK : 3 * RANK, to : to + HEAD_DIM] = own_kv[:, at : at + HEAD_DIM]
                    else:
                        for side in range(2):
                            to = (4 + head) * lane + side * HALF_PAD
                            sa_ref[RANK : 2 * RANK, to : to + half] = own_kv[
                                :, at + side * half : at + (side + 1) * half
                            ]

        prepare_first()
        group_sends(0)
        prepare_second()
        flush(*range(11, 23))
        group_sends(1)
        for cp in cot_moves[:2]:
            cp.start()
        cross[0].wait_recv()
        cot_moves[2].start()

        def cot_spot(away, j):
            return cot_order.at[(1 + j) if away else 0, 1 if away else j]

        def cot_share():
            for away in range(2):
                for j in range(2):
                    here = cot_spot(away, j)
                    pltpu.make_async_copy(here, here, cot_r.at[2 + 2 * away + j]).wait()
                    there = cot_order.at[1 + j, 0] if away else cot_order.at[3, j]
                    k = 6 + 2 * away + j
                    cp = _remote(here, there, cot_s.at[k], cot_r.at[k], core_peer)
                    cp.start()
                    shared.append(cp)

        shared = []

        def forward(j):
            for part_row in range(2):
                k = 2 * part_row + j
                span = pl.ds(64 * part_row, 64)
                sends[k].wait_recv()
                there = tok_all.at[hh, j, (x + j + 1) % 2, span]
                cp = _remote(there, there, send_sem.at[8 + k], recv_sem.at[8 + k], core_peer)
                cp.start()
                sends[8 + k] = cp
            for part_row in range(2):
                k = 2 * part_row + j
                sends[4 + k].wait_recv()
                sends[8 + k].wait_recv()

        def project_rows(t):
            row = pl.ds(t * block, block)
            v = tok_all[t // 2, t % 2].reshape(block, width).astype(F32)
            factor = lax.rsqrt(jnp.mean(v * v, axis=1, keepdims=True) + EPSILON)
            u = (v * factor * gain_one[...].reshape(1, width)).astype(BF16)
            one_ref[row, :] = u
            inner = dot_t(u, fa_ref[...]).astype(BF16)
            inner_ref[row, :] = inner
            cos, sin = cos_ref[row, :], sin_ref[row, :]
            for pair in range(4):
                cols = slice(pair * 2 * lane, (pair + 1) * 2 * lane)
                if pair < 2:
                    both = dot(u, wa_ref[:, cols])
                else:
                    both = dot_t(u, wkv_ref[2 * (pair - 2) * lane : 2 * (pair - 1) * lane, :])
                both = both + dot(inner, sa_ref[:, cols])
                for k in range(2):
                    p = both[:, k * lane : (k + 1) * lane]
                    if pair < 3:
                        p = p * cos + pltpu.roll(p, HALF_PAD, 1) * sin
                    qkv_ref[row, (2 * pair + k) * lane : (2 * pair + k + 1) * lane] = p.astype(BF16)

        def attention(t, hook):
            keys = (t + 1) * block
            row = pl.ds(t * block, block)
            qpos = t * block + lax.broadcasted_iota(jnp.int32, (block, keys), 0)
            kpos = lax.broadcasted_iota(jnp.int32, (block, keys), 1)
            allowed = (kpos <= qpos) & (kpos < live)
            stats = jnp.zeros((block, lane), F32)
            lanes = lax.broadcasted_iota(jnp.int32, (block, lane), 1)
            for head in range(4):
                q = qkv_ref[row, head * lane : (head + 1) * lane]
                kv = head // 2
                k = qkv_ref[:keys, (4 + kv) * lane : (5 + kv) * lane]
                v = qkv_ref[:keys, (6 + kv) * lane : (7 + kv) * lane]
                s = jnp.where(allowed, dot_t(q, k) * scale, NEGATIVE)
                top = jnp.max(s, axis=1, keepdims=True)
                p = jnp.where(allowed, jnp.exp(s - top), 0.0)
                total = jnp.sum(p, axis=1, keepdims=True)
                o = dot(p.astype(BF16), v) / total
                att_ref[row, head * lane : (head + 1) * lane] = o.astype(BF16)
                stats = jnp.where(lanes == head, top + jnp.log(total), stats)
                if head == 1 and hook is not None:
                    hook()
            lse_ref[row, :] = stats
            a = att_ref[row, :]
            for at in range(0, width, 256):
                value = dot(a, ow_ref[:, at : at + 256])
                part[t, :, :, at : at + 256] = value.astype(BF16).reshape(2, 128, 256)
            part[t, :, :, width:] = dot_t(a, fo_ref[...]).astype(BF16).reshape(2, 128, SIDE)

        def to_core(t):
            return _remote(part.at[t], land.at[t % 2], s_sem.at[t % 2], r_sem.at[t % 2], core_peer)

        def to_x(j):
            return _remote(staged.at[j], landed.at[j], s_sem.at[2 + j], r_sem.at[2 + j], x_peer)

        def leave(t):
            @pl.when(core == t // 2)
            def _():
                to_core(t).start()

        def combine(t):
            j = t % 2

            @pl.when(core == 1 - t // 2)
            def _():
                to_core(t).wait_recv()
                mine, other = (x + j) % 2, (x + j + 1) % 2
                staged[j] = (part[t, other].astype(F32) + land[j, other].astype(F32)).astype(BF16)
                to_x(j).start()
                sums[j] = part[t, mine].astype(F32) + land[j, mine].astype(F32)

        forward(0)
        cross[1].start()
        project_rows(0)
        project_rows(2)
        attention(0, None)
        leave(0)
        forward(1)
        project_rows(1)
        project_rows(3)
        cross[1].wait_recv()
        cot_moves[3].start()
        attention(1, lambda: combine(0))
        leave(1)
        attention(2, lambda: combine(1))
        leave(2)
        attention(3, lambda: combine(2))
        leave(3)
        combine(3)
        cot_share()
        for t in range(4):

            @pl.when(core == t // 2)
            def _():
                to_core(t).wait_send()

        for j in range(2):
            tok_own[j] = tok_all[hh, j, (x + j) % 2]
        one_cut[...] = one_ref[:, pl.ds(pl.multiple_of(f * quarter, 128), quarter)]
        for j in range(2):
            cp = to_x(j)
            cp.wait_recv()
            sums[j] = sums[j] + landed[j].astype(F32)
            cp.wait_send()
            side_own[j] = sums[j, :, width:].astype(BF16)
        side_first, side_last = _gather_steps([side_own], [side_all], *side_sems, place)
        side_first()
        flush(3, 6, 7, 8, 9, 10)
        for j in range(2):
            v = (
                tok_own[j].astype(F32)
                + sums[j, :, :width]
                + dot(side_own[j], so_ref[...])
            )
            sums_resid[j] = v
            factor = lax.rsqrt(jnp.mean(v * v, axis=1, keepdims=True) + EPSILON)
            normed_two[j] = (v * factor * gain_two[...].reshape(1, width)).astype(BF16)
        flush(0, 1)
        for cp in shared:
            cp.wait_recv()
        side_last()
        for cp in flushed:
            cp.wait()
        for cp in moves + cross + cot_moves + shared + list(sends.values()):
            cp.wait_send()

    own = (2, 128, wide)
    return pl.pallas_call(
        kernel,
        out_shape=[o[0] for o in outs],
        in_specs=[smem, smem] + [hbm] * (2 + count),
        out_specs=[hbm for o in outs],
        scratch_shapes=[pltpu.VMEM(a.shape, a.dtype) for a in loads_in]
        + [
            pltpu.VMEM((2, 2, 2, 128, width), BF16),
            pltpu.VMEM((rows, width), BF16),
            pltpu.VMEM((4,) + own, BF16),
            pltpu.VMEM((2,) + own, BF16),
            pltpu.VMEM(own, BF16),
            pltpu.VMEM(own, BF16),
            pltpu.VMEM(own, F32),
            pltpu.VMEM((2, 128, SIDE), BF16),
            _sem(count),
            _sem(4),
            _sem(4),
            _sem(10),
            _sem(10),
            _sem(12),
            _sem(12),
            _sem(4),
            _sem(4),
        ]
        + [_sem(2), _sem(6), _sem(6)]
        + [pltpu.VMEM(o[0].shape, o[0].dtype) for o in outs if o[1] is vmem]
        + [_sem(mirrored - 1)],
        compiler_params=pltpu.CompilerParams(
            collective_id=cid, has_side_effects=True, vmem_limit_bytes=58 * 1024 * 1024
        ),
        name="front",
    )(lengths, adapters, tokens, cotangent, *loads_in)


def attend_back_call(
    low_own,
    small_own,
    early,
    out_far,
    length,
    own_arrays,
    arrays,
    cid,
):
    qkv = arrays[0]
    width = low_own.shape[-1]
    rows = qkv.shape[0]
    wide = width + SIDE
    step_rows = 256
    scale = HEAD_DIM ** (-0.5)
    lane = PAD_HEAD
    quarter = width // 4
    middle_n = 4 * quarter
    early_n = early.shape[1]
    big = tuple(arrays) + tuple(own_arrays)
    late_n = 4 * quarter
    factor_n = 2 * quarter
    count = len(big)

    def kernel(*refs):
        len_ref, low_ref, small_ref, early_ref, out_ref = refs[:5]
        big_in = refs[5 : 5 + count]
        (
            out_back,
            grad_back,
            early_out,
            middle_out,
            late_out,
            factor_out,
        ) = refs[5 + count : 11 + count]
        refs = refs[11 + count :]
        (
            qkv_ref,
            lse_ref,
            att_ref,
            inner_ref,
            order_ref,
            cos_ref,
            sin_ref,
            ow_ref,
            fo_ref,
            so_ref,
            wa_ref,
            wkv_ref,
            sa_ref,
            fa_ref,
            sd_ref,
            cut_ref,
            inner_qkv_ref,
            cot_ref,
            out_own,
            resid_ref,
            tok_ref,
            grad_resid_ref,
            gain_ref,
        ) = refs[:count]
        (
            low,
            do_ref,
            gio_ref,
            dk_ref,
            dv_ref,
            part,
            land,
            staged,
            landed,
            side_own,
            middle_ref,
            sums,
            side_all,
            grad_ref,
            landed_out,
            small_out,
            late_ref,
            factor_ref,
            out_tok,
            grad_tok,
            early_lines,
            middle_lines,
            load_sem,
            own_sem,
            send_sem,
            recv_sem,
            s_sem,
            r_sem,
        ) = refs[count : count + 28]
        sems = refs[count + 28 :]
        place = _place()
        c, f, x, core, core_peer, x_peer = place
        loads = [
            pltpu.make_async_copy(big_in[i], refs[i], load_sem.at[i]) for i in range(count)
        ]
        for cp in loads:
            cp.start()
        _greet(
            _back_sources(place) + [core_peer, x_peer, _y_peer(place)] + _z_peers(place)
        )
        small_first, small_forward, small_own_here, small_core, small_far, small_last = _order_steps(
            small_ref, small_out, *sems[0:3], place
        )
        early_start, early_across, early_finish = _ctx_first(early_ref, early_lines, *sems[3:6], place)
        early_two = _ctx_second(early_lines, early_out, *sems[6:9], place)
        mid_start, mid_across, mid_finish = _ctx_first(middle_ref, middle_lines, *sems[9:12], place)
        mid_two = _ctx_second(middle_lines, middle_out, *sems[12:15], place)
        late = _ctx_planes(late_ref, late_out, *sems[15:18], place)
        factor = _ctx_planes(factor_ref, factor_out, *sems[25:28], place)
        side_first, side_last = _gather_steps([side_own], [side_all], *sems[18:21], place)
        out_first, out_last = _back_steps(out_tok, out_back, *sems[21:23], place)
        grad_first, grad_last = _back_steps(grad_tok, grad_back, *sems[23:25], place)
        live = len_ref[_slot_of(c)]

        sends = {}
        hh = 1 - core
        local = []
        for j in (1, 0):
            for k, target in ((0, x_peer), (2, core_peer)):
                cp = _remote(
                    low_ref.at[j],
                    low.at[hh, j, (x + j) % 2],
                    send_sem.at[k + j],
                    recv_sem.at[k + j],
                    target,
                )
                cp.start()
                sends[(k, j)] = cp
            if j:
                early_start()
                small_first()
        for j in range(2):
            lc = pltpu.make_async_copy(low_ref.at[j], low.at[hh, j, (x + j) % 2], own_sem.at[j])
            lc.start()
            local.append(lc)
        swaps = [
            _remote(out_ref.at[j], landed_out.at[j], s_sem.at[8 + j], r_sem.at[8 + j], x_peer)
            for j in range(2)
        ]
        dk_ref[...] = jnp.zeros_like(dk_ref)
        dv_ref[...] = jnp.zeros_like(dv_ref)
        for cp in loads:
            cp.wait()
        for lc in local:
            lc.wait()

        def arrive(j):
            sends[(0, j)].wait_recv()
            cp = _remote(
                low.at[hh, j, (x + j + 1) % 2],
                low.at[hh, j, (x + j + 1) % 2],
                send_sem.at[4 + j],
                recv_sem.at[4 + j],
                core_peer,
            )
            cp.start()
            sends[(4, j)] = cp
            sends[(2, j)].wait_recv()
            cp.wait_recv()

        def through_output(t):
            g = low[t // 2, t % 2].reshape(step_rows, width)
            gio = dot_t(g, so_ref[...]).astype(BF16)
            row = pl.ds(t * step_rows, step_rows)
            gio_ref[row, :] = gio
            do_ref[row, :] = (dot_t(g, ow_ref[...]) + dot(gio, fo_ref[...])).astype(BF16)

        def attention(t, hook):
            keys = (t + 1) * step_rows
            row = pl.ds(t * step_rows, step_rows)
            qpos = t * step_rows + lax.broadcasted_iota(jnp.int32, (step_rows, keys), 0)
            kpos = lax.broadcasted_iota(jnp.int32, (step_rows, keys), 1)
            allowed = (kpos <= qpos) & (kpos < live)
            cos, sin = cos_ref[row, :], sin_ref[row, :]
            for head in range(4):
                kv = head // 2
                at = slice(head * lane, (head + 1) * lane)
                q = qkv_ref[row, at]
                k = qkv_ref[:keys, (4 + kv) * lane : (5 + kv) * lane]
                v = qkv_ref[:keys, (6 + kv) * lane : (7 + kv) * lane]
                do = do_ref[row, at]
                s = dot_t(q, k)
                p = jnp.where(allowed, jnp.exp(s * scale - lse_ref[row, head : head + 1]), 0.0)
                dp = dot_t(do, v)
                total = jnp.sum(p * dp, axis=1, keepdims=True)
                ds = (p * (dp - total)).astype(BF16)
                dq = scale * dot(ds, k)
                dq = dq * cos - pltpu.roll(dq, HALF_PAD, 1) * sin
                grad_ref[row, at] = dq.astype(BF16)
                dk_ref[kv, :keys] += dot_rows(ds, q)
                dv_ref[kv, :keys] += dot_rows(p.astype(BF16), do)
                if head == 1 and hook is not None:
                    hook()
            for kv in range(2):
                dk = scale * dk_ref[kv, row, :]
                dk = dk * cos - pltpu.roll(dk, HALF_PAD, 1) * sin
                grad_ref[row, (4 + kv) * lane : (5 + kv) * lane] = dk.astype(BF16)
                grad_ref[row, (6 + kv) * lane : (7 + kv) * lane] = dv_ref[kv, row, :].astype(BF16)
            g = grad_ref[row, :]
            for at in range(0, width, 256):
                value = dot_t(g[:, : 4 * lane], wa_ref[at : at + 256, :])
                value = value + dot(g[:, 4 * lane :], wkv_ref[:, at : at + 256])
                part[t, :, :, at : at + 256] = value.astype(BF16).reshape(2, 128, 256)
            part[t, :, :, width:] = dot_t(g, sa_ref[...]).astype(BF16).reshape(2, 128, SIDE)

        def to_core(t):
            j = t % 2
            return _remote(part.at[t], land.at[j], s_sem.at[j], r_sem.at[j], core_peer)

        def to_x(j, narrow):
            cols = pl.ds(width, SIDE) if narrow else pl.ds(0, width)
            n = 2 + 2 * narrow + j
            return _remote(
                staged.at[j, :, cols], landed.at[j, :, cols], s_sem.at[n], r_sem.at[n], x_peer
            )

        def leave(t):
            @pl.when(core == t // 2)
            def _():
                to_core(t).start()

        def combine(t):
            j = t % 2

            @pl.when(core == 1 - t // 2)
            def _():
                to_core(t).wait_recv()
                mine, other = (x + j) % 2, (x + j + 1) % 2
                for cols, narrow in ((slice(width, wide), 1), (slice(0, width), 0)):
                    staged[j, :, cols] = (
                        part[t, other, :, cols].astype(F32) + land[j, other, :, cols].astype(F32)
                    ).astype(BF16)
                    to_x(j, narrow).start()
                sums[j] = part[t, mine].astype(F32) + land[j, mine].astype(F32)

        arrive(1)
        early_across()
        through_output(3)
        through_output(1)
        small_own_here()
        for j in range(2):
            small_forward(j)
        def second():
            arrive(0)
            for cp in swaps:
                cp.start()

        attention(3, second)
        leave(3)
        through_output(2)
        through_output(0)
        o_a = dot_rows(gio_ref[...], att_ref[...])[:RANK]
        o_a = jnp.concatenate(
            [o_a[:, head * lane : head * lane + HEAD_DIM] for head in range(4)], axis=1
        )
        middle_ref[:, :quarter] = o_a.astype(BF16)
        own_cols = pl.ds(pl.multiple_of(f * quarter, 128), quarter)
        g = low[:, :, :, :, own_cols].reshape(rows, quarter)
        middle_ref[:, quarter : 2 * quarter] = (ADAPTER_SCALE * dot_rows(inner_ref[...], g)[:RANK]).astype(BF16)
        for j in range(2):
            small_far(j)
        small_core()
        in_gu = jnp.zeros((SIDE, quarter), F32)
        for k in range(4):
            u = order_ref[k, :, :, own_cols].reshape(step_rows, quarter)
            in_gu += dot_rows(small_out[k].reshape(step_rows, SIDE), u)
        middle_ref[:, 2 * quarter : 3 * quarter] = in_gu[:RANK].astype(BF16)
        middle_ref[:, 3 * quarter :] = in_gu[RANK : 2 * RANK].astype(BF16)
        mid_start()
        early_finish()
        early_two[0]()

        def outputs():
            for j in range(2):
                swaps[j].wait()
                total = out_own[j] + landed_out[j].astype(F32)
                side = total[:, width:]
                out_own[j, :, width:] = side
                pos = 128 * _block(x, core, j) + lax.broadcasted_iota(jnp.int32, (128, width), 0)
                value = resid_ref[j] + total[:, :width] + dot(side.astype(BF16), sd_ref[...])
                out_tok[j] = jnp.where(pos < live, value, 0.0).astype(BF16)
                out_first(j)

        def third():
            combine(3)
            mid_across()

        attention(2, third)
        leave(2)
        outputs()
        attention(1, lambda: combine(2))
        leave(1)
        mid_finish()
        mid_two[0]()
        early_two[1]()
        attention(0, lambda: combine(1))
        leave(0)
        combine(0)
        def token_rows():
            for j in range(2):
                to_x(j, 0).wait_recv()
                gi = sums[j, :, width:].astype(BF16)
                total = sums[j, :, :width] + landed[j, :, :width].astype(F32)
                gn = (total + dot(gi, fa_ref[...])).astype(BF16).astype(F32)
                v = tok_ref[j].astype(F32)
                rms = lax.rsqrt(jnp.mean(v * v, axis=1, keepdims=True) + EPSILON)
                scaled = gn * gain_ref[...].reshape(1, width)
                mean = jnp.mean(scaled * v, axis=1, keepdims=True)
                grad = grad_resid_ref[j] + rms * scaled - v * (rms * rms * rms) * mean
                grad_tok[j] = grad.astype(BF16)
                grad_first(j)

        for j in range(2):
            to_x(j, 1).wait_recv()
            sums[j, :, width:] = sums[j, :, width:] + landed[j, :, width:].astype(F32)
            side_own[j] = (sums[j, :, width:] + out_own[j, :, width:]).astype(BF16)
        side_first()

        all_b = ADAPTER_SCALE * dot_rows(inner_qkv_ref[...], grad_ref[...])
        half = HEAD_DIM // 2
        pieces = []
        for head in range(6):
            r = slice(0, RANK) if head < 4 else slice(RANK, 2 * RANK)
            for side in range(2):
                to = head * lane + side * HALF_PAD
                pieces.append(all_b[r, to : to + half])
        for head in range(2):
            to = (6 + head) * lane
            pieces.append(all_b[2 * RANK : 3 * RANK, to : to + HEAD_DIM])
        factor_ref[...] = jnp.concatenate(pieces, axis=1).astype(BF16)
        factor[0]()
        mid_two[1]()
        factor[1]()
        side_last()
        in_qkv = dot_rows(side_all[...].reshape(rows, SIDE), cut_ref[...])
        for i in range(3):
            late_ref[:, i * quarter : (i + 1) * quarter] = in_qkv[i * RANK : (i + 1) * RANK].astype(
                BF16
            )
        d_b = jnp.zeros((SIDE, quarter), F32)
        for step in range(4):
            other_x = x if step in (0, 3) else 1 - x
            for i in range(2):
                other_core = (core, 1 - core)[step == 3 or (step in (1, 2) and i == 0)]
                jj = i if step in (0, 3) else step - 1
                pos = 128 * _block(other_x, other_core, jj) + lax.broadcasted_iota(
                    jnp.int32, (128, quarter), 0
                )
                go = cot_ref[step, i, :, own_cols].astype(F32)
                go = jnp.where(pos < live, go, 0.0).astype(BF16)
                d_b += dot_rows(side_all[1 - other_core, jj, (other_x + jj) % 2], go)
        late_ref[:, 3 * quarter :] = (ADAPTER_SCALE * d_b[3 * RANK : 4 * RANK]).astype(BF16)
        late[0]()

        token_rows()
        late[1]()
        for t in range(4):

            @pl.when(core == t // 2)
            def _():
                to_core(t).wait_send()

        for j in range(2):
            to_x(j, 0).wait_send()
            to_x(j, 1).wait_send()
        small_last()
        early_two[2]()
        mid_two[2]()
        factor[2]()
        late[2]()
        out_last()
        grad_last()
        for cp in sends.values():
            cp.wait_send()

    vmem, hbm = pl.BlockSpec(memory_space=pltpu.VMEM), pl.BlockSpec(memory_space=pl.ANY)
    shape = jax.ShapeDtypeStruct
    own = (2, 128, wide)
    return pl.pallas_call(
        kernel,
        out_shape=[
            shape((2, 128, width), BF16),
            shape((2, 128, width), BF16),
            _spread_of(early_n),
            _spread_of(middle_n),
            _spread_of(late_n),
            _spread_of(factor_n),
        ],
        in_specs=[pl.BlockSpec(memory_space=pltpu.SMEM)] + [hbm] * (4 + count),
        out_specs=[hbm] * 6,
        scratch_shapes=[pltpu.VMEM(a.shape, a.dtype) for a in big]
        + [
            pltpu.VMEM((2, 2, 2, 128, width), BF16),
            pltpu.VMEM((rows, 4 * lane), BF16),
            pltpu.VMEM((rows, SIDE), BF16),
            pltpu.VMEM((2, rows, lane), F32),
            pltpu.VMEM((2, rows, lane), F32),
            pltpu.VMEM((4,) + own, BF16),
            pltpu.VMEM((2,) + own, BF16),
            pltpu.VMEM(own, BF16),
            pltpu.VMEM(own, BF16),
            pltpu.VMEM((2, 128, SIDE), BF16),
            pltpu.VMEM((RANK, middle_n), BF16),
            pltpu.VMEM(own, F32),
            pltpu.VMEM((2, 2, 2, 128, SIDE), BF16),
            pltpu.VMEM((rows, 8 * lane), BF16),
            pltpu.VMEM(own, BF16),
            pltpu.VMEM((4, 2, 128, SIDE), BF16),
            pltpu.VMEM((RANK, late_n), BF16),
            pltpu.VMEM((RANK, factor_n), BF16),
            pltpu.VMEM((2, 128, width), BF16),
            pltpu.VMEM((2, 128, width), BF16),
            pltpu.VMEM(_lines_of(early_n), BF16),
            pltpu.VMEM(_lines_of(middle_n), BF16),
            _sem(count),
            _sem(2),
            _sem(6),
            _sem(6),
            _sem(10),
            _sem(10),
        ]
        + [_sem(2), _sem(6), _sem(6)]
        + FIRST_SEMS
        + SECOND_SEMS
        + FIRST_SEMS
        + SECOND_SEMS
        + PLANE_SEMS
        + [_sem(2), _sem(6), _sem(6)]
        + [_sem(2), _sem(2), _sem(2), _sem(2)]
        + PLANE_SEMS,
        compiler_params=pltpu.CompilerParams(
            collective_id=cid, has_side_effects=True, vmem_limit_bytes=62 * 1024 * 1024
        ),
        name="attend_back",
    )(length, low_own, small_own, early, out_far, *big)


def table_call(pieces, out_rows, grad_rows, adapters):
    f32 = lambda *shape: jax.ShapeDtypeStruct(shape, F32)
    choices = 8
    outs = [
        f32(choices, 5, RANK, 1536),
        f32(choices, RANK, 1536),
        f32(choices, RANK, 4096),
        f32(choices, RANK, 1536),
        f32(choices, 2, RANK, 768),
        f32(choices, RANK, 1536),
        f32(choices, 2, RANK, 4096),
        f32(choices, RANK, 1536),
    ]
    plan = (
        ((6, 0, 1024), (6, 1, 1024), (2, None, 1024)),
        ((1, None, 384), (5, None, 384), (0, 3, 384), (0, 4, 384)),
        (
            (0, 0, 384),
            (0, 1, 384),
            (0, 2, 384),
            (7, None, 384),
        ),
        ((3, None, 384), (4, 0, 192), (4, 1, 192)),
    )

    def kernel(which, early_in, middle_in, late_in, factor_in, rows_in, grad_in, *refs):
        outs, rows_out, grad_out = refs[:8], refs[8], refs[9]
        acc, held = refs[10:18], refs[18:22]
        grad_low, grad_full, rows_held, sems, load_sem = refs[22:27]
        loads = []
        for i, src in enumerate((early_in, middle_in, factor_in, late_in)):
            loads.append(pltpu.make_async_copy(src, held[(0, 1, 3, 2)[i]], load_sem.at[i]))
        grad_load = pltpu.make_async_copy(grad_in, grad_low, load_sem.at[4])
        rows_load = pltpu.make_async_copy(rows_in, rows_held, load_sem.at[5])
        for cp in loads + [grad_load, rows_load]:
            cp.start()

        def add(piece, ref):
            def one_slot(origin, carry):
                row = which[origin % 4 + 4 * ((origin // 4 + origin) % 2)]
                for f in range(4):
                    at = 0
                    for out, table, n in plan[piece]:
                        value = ref[origin // 4, f % 2, origin % 4, f // 2, :, at : at + n].astype(F32)
                        cols = slice(f * n, (f + 1) * n)
                        if table is None:
                            acc[out][row, :, cols] += value
                        else:
                            acc[out][row, table, :, cols] += value
                        at += n
                return carry

            lax.fori_loop(0, 8, one_slot, 0)

        def send(out):
            cp = pltpu.make_async_copy(acc[out], outs[out], sems.at[out])
            cp.start()
            return cp

        for out in range(8):
            acc[out][...] = jnp.zeros_like(acc[out])
        loads[0].wait()
        add(0, held[0])
        copies = [send(out) for out in (2, 6)]
        loads[1].wait()
        add(1, held[1])
        copies += [send(out) for out in (1, 5)]
        loads[2].wait()
        add(3, held[3])
        copies += [send(out) for out in (3, 4)]
        loads[3].wait()
        add(2, held[2])
        copies += [send(out) for out in (0, 7)]
        grad_load.wait()
        grad_full[...] = grad_low[...].astype(F32)
        last = pltpu.make_async_copy(grad_full, grad_out, load_sem.at[6])
        last.start()
        rows_load.wait()
        rows_copy = pltpu.make_async_copy(rows_held, rows_out, load_sem.at[7])
        rows_copy.start()
        copies += [last, rows_copy]
        for cp in copies:
            cp.wait()

    hbm = pl.BlockSpec(memory_space=pl.ANY)
    return pl.pallas_call(
        kernel,
        out_shape=outs + [jax.ShapeDtypeStruct(out_rows.shape, BF16), f32(*grad_rows.shape)],
        in_specs=[pl.BlockSpec(memory_space=pltpu.SMEM)] + [hbm] * 6,
        out_specs=[hbm] * 10,
        scratch_shapes=[pltpu.VMEM(o.shape, F32) for o in outs]
        + [pltpu.VMEM(p.shape, BF16) for p in pieces]
        + [pltpu.VMEM(grad_rows.shape, BF16), pltpu.VMEM(grad_rows.shape, F32)]
        + [pltpu.VMEM(out_rows.shape, BF16), _sem(8), _sem(8)],
        compiler_params=pltpu.CompilerParams(vmem_limit_bytes=62 * 1024 * 1024),
        name="tables",
    )(adapters, *pieces, out_rows, grad_rows)


def rope_constants(rows):
    half = HEAD_DIM // 2
    freqs = np.float32(ROPE_BASE) ** (-(np.arange(half, dtype=np.float32) * 2.0 / HEAD_DIM))
    angles = np.arange(rows).astype(np.float32)[:, None] * freqs.astype(np.float32)[None, :]
    cos = np.cos(angles.astype(np.float64)).astype(np.float32)
    sin = np.sin(angles.astype(np.float64)).astype(np.float32)
    gap = np.zeros((rows, HALF_PAD - half), np.float32)
    cosine = np.concatenate([cos, gap, cos, gap], axis=1)
    sine = np.concatenate([-sin, gap, sin, gap], axis=1)
    return jnp.asarray(cosine), jnp.asarray(sine)


def dot(left, right):
    return jnp.dot(left, right, preferred_element_type=F32)


def dot_t(left, right):
    return lax.dot_general(left, right, (((1,), (1,)), ((), ())), preferred_element_type=F32)


def dot_rows(left, right):
    return lax.dot_general(left, right, (((0,), (0,)), ((), ())), preferred_element_type=F32)


def side_pad(value, before=0):
    return jnp.pad(value, ((0, 0), (before, SIDE - before - value.shape[1])))


def blocks(value):
    return value.reshape(2, 2, 2, 128, value.shape[-1])


def own_blocks(value):
    return value.reshape(2, 128, value.shape[-1])


def flat(value):
    return value.reshape(-1, value.shape[-1])


def slot_local(
    tokens,
    cotangent,
    lengths,
    slot_adapter_index,
    attention_norm_gain,
    feedforward_norm_gain,
    query_weight,
    key_weight,
    value_weight,
    output_weight,
    gate_weight,
    up_weight,
    down_weight,
    adapter_input_first,
    adapter_output_first,
    adapter_down_first,
    adapter_query_second,
    adapter_key_value_second,
    adapter_output_second,
    adapter_gate_up_second,
    adapter_down_second,
):
    rows = 4 * 2 * tokens.shape[1]
    cosine, sine = rope_constants(rows)
    turned = lambda t: jnp.swapaxes(t, -1, -2)
    (
        resid,
        normed_two_own,
        inner_o,
        tok_own,
        cot_order,
        _,
        qkv,
        stats,
        attn_b,
        one_cut,
        inner_qkv,
        weight_q,
        weight_kv,
        out_w,
        second_all,
        first_all,
        first_gu,
        second_g,
        second_u,
        first_d,
        second_d,
        first_o,
        second_o,
    ) = front_call(
        tokens,
        cotangent,
        lengths,
        slot_adapter_index,
        (attention_norm_gain, feedforward_norm_gain),
        query_weight,
        turned(key_weight),
        turned(value_weight),
        output_weight,
        (
            turned(adapter_input_first),
            turned(adapter_output_first),
            turned(adapter_down_first),
            adapter_query_second,
            adapter_key_value_second,
            adapter_output_second,
            adapter_gate_up_second,
            adapter_down_second,
        ),
        cosine,
        sine,
        0,
    )
    grad_resid, grad_low_own, small, out_sums, out_far, order, early = feed_forward(
        normed_two_own,
        cot_order,
        resid,
        feedforward_norm_gain,
        lengths,
        (gate_weight, up_weight, down_weight),
        (first_gu, second_g, second_u, first_d, second_d),
        3,
    )
    out_rows, grad_rows, early, middle, late, factors = attend_back_call(
        grad_low_own,
        small,
        early,
        out_far,
        lengths,
        (out_sums, resid, tok_own, grad_resid, attention_norm_gain),
        (
            qkv,
            stats,
            attn_b,
            flat(inner_o),
            order,
            cosine,
            sine,
            out_w,
            first_o,
            second_o,
            weight_q,
            weight_kv,
            second_all,
            first_all,
            second_d,
            one_cut,
            inner_qkv,
            cot_order,
        ),
        10,
    )
    full = table_call((early, middle, late, factors), out_rows, grad_rows, slot_adapter_index)
    turn = lambda t: jnp.swapaxes(t, -1, -2)
    return (
        full[8],
        full[9],
        turn(full[0]),
        turn(full[1]),
        turn(full[2]),
        full[3],
        full[4],
        full[5],
        full[6],
        full[7],
    )


def solution(mesh):
    one_slot = mesh.shape["ctx"] == 8 and mesh.shape["fsdp"] == 4
    return jax.shard_map(
        slot_local if one_slot else local,
        mesh=mesh,
        in_specs=(
            P("fsdp", "ctx", None),
            P("fsdp", "ctx", None),
            P(),
            P(),
            P(),
            P(),
            P(None, "fsdp"),
            P(None, "fsdp"),
            P(None, "fsdp"),
            P("fsdp", None),
            P(None, "fsdp"),
            P(None, "fsdp"),
            P("fsdp", None),
            P(),
            P(),
            P(),
            P(),
            P(),
            P(),
            P(),
            P(),
        ),
        out_specs=(
            P("fsdp", "ctx", None),
            P("fsdp", "ctx", None),
            P(),
            P(),
            P(),
            P(),
            P(),
            P(),
            P(),
            P(),
        ),
        check_vma=False,
    )
```

```python
import math

import jax
import jax.numpy as jnp
import numpy as np
from jax import lax
from jax.experimental import pallas as pl
from jax.experimental.pallas import tpu as pltpu
from jax.sharding import PartitionSpec as P

QUERY_HEADS = 16
KEY_VALUE_HEADS = 8
HEAD_DIM = 96


EPSILON = 1e-05
NEGATIVE = -1e30
ADAPTER_SCALE = 0.5
ROPE_BASE = 100000.0


def from_behind(x, axis, by):
    size = lax.axis_size(axis)
    return lax.ppermute(x, axis, [(i, (i + by) % size) for i in range(size)])


def rope_tables(positions, head_size):
    half_size = head_size // 2
    freqs = ROPE_BASE ** (-(jnp.arange(half_size, dtype=jnp.float32) * 2.0 / head_size))
    angles = positions.astype(jnp.float32)[:, None] * freqs[None, :]
    return (jnp.cos(angles)[:, None, :], jnp.sin(angles)[:, None, :])


def apply_rotation(values, cosine_table, sine_table):
    half_size = values.shape[-1] // 2
    first_half = values[..., :half_size]
    second_half = values[..., half_size:]
    return jnp.concatenate(
        [
            first_half * cosine_table - second_half * sine_table,
            second_half * cosine_table + first_half * sine_table,
        ],
        axis=-1,
    )


def rotate_back(gradient_tree, cosine_table, sine_table):
    half_size = gradient_tree.shape[-1] // 2
    first_half = gradient_tree[..., :half_size]
    second_half = gradient_tree[..., half_size:]
    return jnp.concatenate(
        [
            first_half * cosine_table + second_half * sine_table,
            second_half * cosine_table - first_half * sine_table,
        ],
        axis=-1,
    )


def rms_factor(values):
    return lax.rsqrt(jnp.mean(values * values, axis=-1, keepdims=True) + EPSILON)


def norm_back(values, factor, gain, grad_norm):
    scaled = grad_norm * gain
    return factor * scaled - values * factor**3 * jnp.mean(scaled * values, axis=-1, keepdims=True)


def pick_rows(onehot, table):
    return jnp.einsum("sa,a...->s...", onehot, table, preferred_element_type=jnp.float32).astype(
        jnp.bfloat16
    )


def spread_rows(onehot, gradient_tree):
    return jnp.einsum("sa,s...->a...", onehot, gradient_tree, precision=lax.Precision.HIGHEST)


def direct_product(input_rows, weight_matrix):
    return jnp.einsum("std,do->sto", input_rows, weight_matrix, preferred_element_type=jnp.float32)


def direct_back(gradient_tree, weight_matrix):
    return jnp.einsum(
        "sto,do->std", gradient_tree, weight_matrix, preferred_element_type=jnp.float32
    )


def inner_product_part(input_rows, down):
    return jnp.einsum("std,sdr->str", input_rows, down, preferred_element_type=jnp.float32)


def inner_back(gradient_tree, upward_rows):
    return ADAPTER_SCALE * jnp.einsum(
        "sto,sro->str", gradient_tree, upward_rows, preferred_element_type=jnp.float32
    )


def through_down(grad_inner, down):
    return jnp.einsum("str,sdr->std", grad_inner, down, preferred_element_type=jnp.float32)


def down_grad(input_rows, grad_inner):
    return jnp.einsum("std,str->sdr", input_rows, grad_inner, preferred_element_type=jnp.float32)


def upward_grad(inner_rows, gradient_tree):
    return ADAPTER_SCALE * jnp.einsum(
        "jvp,jvx->jpx", inner_rows, gradient_tree, preferred_element_type=jnp.float32
    )


def upward_apply(inner_rows, upward_rows):
    return ADAPTER_SCALE * jnp.einsum(
        "str,sro->sto", inner_rows, upward_rows, preferred_element_type=jnp.float32
    )


def project(input_rows, weight_matrix, down, upward_rows):
    inner_rows = inner_product_part(input_rows, down).astype(jnp.bfloat16)
    return (
        inner_rows,
        direct_product(input_rows, weight_matrix) + upward_apply(inner_rows, upward_rows),
    )


def project_back(input_rows, grad_output, weight_matrix, down, upward_rows, inner_rows):
    grad_upward = upward_grad(inner_rows, grad_output)
    grad_inner = inner_back(grad_output, upward_rows).astype(jnp.bfloat16)
    grad_down = down_grad(input_rows, grad_inner)
    grad_inputs = direct_back(grad_output, weight_matrix) + through_down(grad_inner, down)
    return (grad_inputs, grad_down, grad_upward)


def allowed_mask(key_start, key_count, query_pos, lengths):
    key_pos = key_start + jnp.arange(key_count, dtype=jnp.int32)
    causal = key_pos[None, :] <= query_pos[:, None]
    live = key_pos[None, :] < lengths[:, None]
    return (causal[None, :, :] & live[:, None, :])[:, None, None, :, :]


def attend_block(state, key_block, value_block, key_start, query_head_rows, query_pos, lengths):
    run_max, run_sum, run_acc = state
    scale = query_head_rows.shape[-1] ** (-0.5)
    scores = (
        jnp.einsum(
            "sqhgd,skhd->shgqk", query_head_rows, key_block, preferred_element_type=jnp.float32
        )
        * scale
    )
    allowed = allowed_mask(key_start, key_block.shape[1], query_pos, lengths)
    new_max = jnp.maximum(run_max, jnp.max(jnp.where(allowed, scores, NEGATIVE), axis=-1))
    weights = jnp.where(allowed, jnp.exp(scores - new_max[..., None]), 0.0)
    factor = jnp.exp(run_max - new_max)
    new_sum = run_sum * factor + jnp.sum(weights, axis=-1)
    update = jnp.einsum(
        "shgqk,skhd->shgqd",
        weights.astype(jnp.bfloat16),
        value_block,
        preferred_element_type=jnp.float32,
    )
    return (new_max, new_sum, run_acc * factor[..., None] + update)


def attend_back(
    key_block,
    value_block,
    key_start,
    query_head_rows,
    grad_heads,
    log_total,
    row_dot,
    query_pos,
    lengths,
):
    scale = query_head_rows.shape[-1] ** (-0.5)
    scores = (
        jnp.einsum(
            "sqhgd,skhd->shgqk", query_head_rows, key_block, preferred_element_type=jnp.float32
        )
        * scale
    )
    allowed = allowed_mask(key_start, key_block.shape[1], query_pos, lengths)
    probs = jnp.where(allowed, jnp.exp(scores - log_total[..., None]), 0.0)
    grad_probs = jnp.einsum(
        "sqhgd,skhd->shgqk", grad_heads, value_block, preferred_element_type=jnp.float32
    )
    grad_scores = (probs * (grad_probs - row_dot[..., None])).astype(jnp.bfloat16)
    grad_query = scale * jnp.einsum(
        "shgqk,skhd->sqhgd", grad_scores, key_block, preferred_element_type=jnp.float32
    )
    grad_key = scale * jnp.einsum(
        "shgqk,sqhgd->skhd", grad_scores, query_head_rows, preferred_element_type=jnp.float32
    )
    grad_value = jnp.einsum(
        "shgqk,sqhgd->skhd",
        probs.astype(jnp.bfloat16),
        grad_heads,
        preferred_element_type=jnp.float32,
    )
    return (grad_query, grad_key, grad_value)


def attend_forward(query_head_rows, key_head_rows, value_head_rows, lengths_used, query_pos):
    slots, rows, kv_heads, group_size, head_size = query_head_rows.shape
    key_flat = key_head_rows.reshape(slots, rows, kv_heads * head_size)
    value_flat = value_head_rows.reshape(slots, rows, kv_heads * head_size)
    stat_shape = (slots, kv_heads, group_size, rows)
    initial = (
        jnp.full(stat_shape, NEGATIVE, jnp.float32),
        jnp.zeros(stat_shape, jnp.float32),
        jnp.zeros(stat_shape + (head_size,), jnp.float32),
    )
    part_keys = lax.all_gather(key_flat, "ctx", axis=1, tiled=True)
    part_values = lax.all_gather(value_flat, "ctx", axis=1, tiled=True)
    piece_rows = part_keys.shape[1]
    part_keys = part_keys.reshape(slots, piece_rows, kv_heads, head_size)
    part_values = part_values.reshape(slots, piece_rows, kv_heads, head_size)
    span_rows = math.gcd(piece_rows, 4 * rows)

    def inner_step(block_index, inner_state):
        sub_keys = lax.dynamic_slice_in_dim(part_keys, block_index * span_rows, span_rows, 1)
        sub_values = lax.dynamic_slice_in_dim(part_values, block_index * span_rows, span_rows, 1)
        return attend_block(
            inner_state,
            sub_keys,
            sub_values,
            block_index * span_rows,
            query_head_rows,
            query_pos,
            lengths_used,
        )

    run_max, run_sum, run_acc = lax.fori_loop(0, piece_rows // span_rows, inner_step, initial)
    log_total = run_max + jnp.log(run_sum)
    attended = jnp.transpose(run_acc / run_sum[..., None], (0, 3, 1, 2, 4))
    return (attended, log_total)


def attend_backward(
    query_head_rows,
    key_head_rows,
    value_head_rows,
    grad_heads,
    attended,
    log_total,
    lengths_used,
    query_pos,
):
    ctx_count = lax.axis_size("ctx")
    own_index = lax.axis_index("ctx")
    rows = query_head_rows.shape[1]
    row_dot = jnp.transpose(
        jnp.sum(grad_heads.astype(jnp.float32) * attended, axis=-1), (0, 2, 3, 1)
    )

    def cycle_step(step_index, carried):
        carried_keys, carried_values, grad_query, grad_key, grad_value = carried
        block_id = (own_index + step_index) % ctx_count
        query_part, key_part, value_part = attend_back(
            carried_keys,
            carried_values,
            block_id * rows,
            query_head_rows,
            grad_heads,
            log_total,
            row_dot,
            query_pos,
            lengths_used,
        )
        grad_key, grad_value = (
            from_behind((grad_key + key_part).astype(jnp.bfloat16), "ctx", -1).astype(jnp.float32),
            from_behind((grad_value + value_part).astype(jnp.bfloat16), "ctx", -1).astype(
                jnp.float32
            ),
        )
        carried_keys, carried_values = from_behind((carried_keys, carried_values), "ctx", -1)
        return (carried_keys, carried_values, grad_query + query_part, grad_key, grad_value)

    key_zeros = jnp.zeros(key_head_rows.shape, jnp.float32)
    start_state = (
        key_head_rows,
        value_head_rows,
        jnp.zeros(query_head_rows.shape, jnp.float32),
        key_zeros,
        key_zeros,
    )
    carried = lax.fori_loop(0, ctx_count, cycle_step, start_state)
    return (carried[2], carried[3], carried[4])


def table_total(rotation_tables):
    return lax.psum(rotation_tables, ("ctx", "fsdp"))


def local(
    tokens,
    cotangent,
    lengths,
    slot_adapter_index,
    attention_norm_gain,
    feedforward_norm_gain,
    query_weight,
    key_weight,
    value_weight,
    output_weight,
    gate_weight,
    up_weight,
    down_weight,
    adapter_input_first,
    adapter_output_first,
    adapter_down_first,
    adapter_query_second,
    adapter_key_value_second,
    adapter_output_second,
    adapter_gate_up_second,
    adapter_down_second,
):
    slot_count, tok_rows, model_width = tokens.shape
    head_groups = QUERY_HEADS // KEY_VALUE_HEADS
    own_index = lax.axis_index("ctx")
    fsdp_index = lax.axis_index("fsdp")
    query_pos = own_index * tok_rows + jnp.arange(tok_rows, dtype=jnp.int32)
    cosine_table, sine_table = rope_tables(query_pos, HEAD_DIM)
    own_lengths = lax.dynamic_slice_in_dim(lengths, fsdp_index * slot_count, slot_count, 0)
    own_adapters = lax.dynamic_slice_in_dim(
        slot_adapter_index, fsdp_index * slot_count, slot_count, 0
    )
    valid = query_pos[None, :] < own_lengths[:, None]
    adapter_labels = jnp.arange(adapter_input_first.shape[0], dtype=jnp.int32)
    onehot_own = own_adapters[:, None] == adapter_labels[None, :]
    owned_low_rank = onehot_own.astype(jnp.bfloat16)
    own_full = onehot_own.astype(jnp.float32)
    tokens_f = tokens.astype(jnp.float32)
    factor_one = rms_factor(tokens_f)
    normed_one = (tokens_f * factor_one * attention_norm_gain).astype(jnp.bfloat16)
    grad_out = jnp.where(valid[..., None], cotangent, jnp.zeros((), jnp.bfloat16))
    input_first = pick_rows(owned_low_rank, adapter_input_first)
    output_second = pick_rows(owned_low_rank, adapter_output_second)
    down_second = pick_rows(owned_low_rank, adapter_down_second)
    output_first = pick_rows(owned_low_rank, adapter_output_first)
    down_first = pick_rows(owned_low_rank, adapter_down_first)
    query_second = pick_rows(owned_low_rank, adapter_query_second)
    key_value_second = pick_rows(owned_low_rank, adapter_key_value_second)
    gate_up_second = pick_rows(owned_low_rank, adapter_gate_up_second)
    weight_q, weight_k, weight_v, weight_gate, weight_up, weight_o, weight_down = (
        lax.all_gather(query_weight, "fsdp", axis=1, tiled=True),
        lax.all_gather(key_weight, "fsdp", axis=1, tiled=True),
        lax.all_gather(value_weight, "fsdp", axis=1, tiled=True),
        lax.all_gather(gate_weight, "fsdp", axis=1, tiled=True),
        lax.all_gather(up_weight, "fsdp", axis=1, tiled=True),
        lax.all_gather(output_weight, "fsdp", axis=0, tiled=True),
        lax.all_gather(down_weight, "fsdp", axis=0, tiled=True),
    )
    inner_q, projected_queries = project(normed_one, weight_q, input_first[:, 0], query_second)
    inner_k, projected_keys = project(
        normed_one, weight_k, input_first[:, 1], key_value_second[:, 0]
    )
    inner_v, projected_values = project(
        normed_one, weight_v, input_first[:, 2], key_value_second[:, 1]
    )
    query_head_rows = apply_rotation(
        projected_queries.reshape(slot_count, tok_rows, -1, HEAD_DIM), cosine_table, sine_table
    ).astype(jnp.bfloat16)
    query_head_rows = query_head_rows.reshape(slot_count, tok_rows, -1, head_groups, HEAD_DIM)
    key_head_rows = apply_rotation(
        projected_keys.reshape(slot_count, tok_rows, -1, HEAD_DIM), cosine_table, sine_table
    ).astype(jnp.bfloat16)
    value_head_rows = projected_values.astype(jnp.bfloat16).reshape(
        slot_count, tok_rows, -1, HEAD_DIM
    )
    attended, log_total = attend_forward(
        query_head_rows, key_head_rows, value_head_rows, own_lengths, query_pos
    )
    attn_b = attended.reshape(slot_count, tok_rows, -1).astype(jnp.bfloat16)
    inner_o, proj_o = project(attn_b, weight_o, output_first, output_second)
    resid = tokens_f + proj_o
    factor_two = rms_factor(resid)
    normed_two = (resid * factor_two * feedforward_norm_gain).astype(jnp.bfloat16)
    inner_gate, gate = project(normed_two, weight_gate, input_first[:, 3], gate_up_second[:, 0])
    inner_up, up_proj = project(normed_two, weight_up, input_first[:, 4], gate_up_second[:, 1])
    sigmoid_gate = jax.nn.sigmoid(gate)
    hidden = (gate * sigmoid_gate * up_proj).astype(jnp.bfloat16)
    inner_down, proj_down = project(hidden, weight_down, down_first, down_second)
    out_tokens = jnp.where(valid[..., None], resid + proj_down, 0.0).astype(jnp.bfloat16)
    grad_hidden, grad_da, grad_db = project_back(
        hidden, grad_out, weight_down, down_first, down_second, inner_down
    )
    grad_gate = (grad_hidden * up_proj * sigmoid_gate * (1.0 + gate * (1.0 - sigmoid_gate))).astype(
        jnp.bfloat16
    )
    grad_up = (grad_hidden * gate * sigmoid_gate).astype(jnp.bfloat16)
    from_gate, grad_ga, grad_gb = project_back(
        normed_two, grad_gate, weight_gate, input_first[:, 3], gate_up_second[:, 0], inner_gate
    )
    from_up, grad_ua, grad_ub = project_back(
        normed_two, grad_up, weight_up, input_first[:, 4], gate_up_second[:, 1], inner_up
    )
    grad_normed_two = (from_gate + from_up).astype(jnp.bfloat16).astype(jnp.float32)
    grad_resid = grad_out.astype(jnp.float32) + norm_back(
        resid, factor_two, feedforward_norm_gain, grad_normed_two
    )
    grad_resid_low = grad_resid.astype(jnp.bfloat16)
    from_attn, grad_oa, grad_ob = project_back(
        attn_b, grad_resid_low, weight_o, output_first, output_second, inner_o
    )
    grad_heads = from_attn.astype(jnp.bfloat16).reshape(attended.shape)
    grad_query, grad_key, grad_value = attend_backward(
        query_head_rows,
        key_head_rows,
        value_head_rows,
        grad_heads,
        attended,
        log_total,
        own_lengths,
        query_pos,
    )
    grad_proj_q = (
        rotate_back(
            grad_query.reshape(slot_count, tok_rows, -1, HEAD_DIM), cosine_table, sine_table
        )
        .astype(jnp.bfloat16)
        .reshape(slot_count, tok_rows, -1)
    )
    grad_proj_k = (
        rotate_back(grad_key, cosine_table, sine_table)
        .astype(jnp.bfloat16)
        .reshape(slot_count, tok_rows, -1)
    )
    grad_proj_v = grad_value.astype(jnp.bfloat16).reshape(slot_count, tok_rows, -1)
    from_query, grad_qa, grad_qb = project_back(
        normed_one, grad_proj_q, weight_q, input_first[:, 0], query_second, inner_q
    )
    from_key, grad_ka, grad_kb = project_back(
        normed_one, grad_proj_k, weight_k, input_first[:, 1], key_value_second[:, 0], inner_k
    )
    from_value, grad_va, grad_vb = project_back(
        normed_one, grad_proj_v, weight_v, input_first[:, 2], key_value_second[:, 1], inner_v
    )
    grad_normed_one = (from_query + from_key + from_value).astype(jnp.bfloat16).astype(jnp.float32)
    grad_tokens = grad_resid + norm_back(tokens_f, factor_one, attention_norm_gain, grad_normed_one)
    slot_grads = (
        jnp.stack([grad_qa, grad_ka, grad_va, grad_ga, grad_ua], axis=1),
        grad_oa,
        grad_da,
        grad_qb,
        jnp.stack([grad_kb, grad_vb], axis=1),
        grad_ob,
        jnp.stack([grad_gb, grad_ub], axis=1),
        grad_db,
    )
    summed = table_total(tuple((spread_rows(own_full, entry_item) for entry_item in slot_grads)))
    return (
        out_tokens,
        grad_tokens,
        summed[0],
        summed[1],
        summed[2],
        summed[3],
        summed[4],
        summed[5],
        summed[6],
        summed[7],
    )


BF16 = jnp.bfloat16
F32 = jnp.float32
MESH_ID = pl.DeviceIdType.MESH
RANK = 16
SIDE = 128
PAD_HEAD = 128
HALF_PAD = 64


def _sem(count):
    return pltpu.SemaphoreType.DMA((count,))


def _place():
    c = lax.axis_index("ctx")
    f = lax.axis_index("fsdp")
    x = f // 2
    core = f % 2
    return c, f, x, core, (c, 2 * x + 1 - core), (c, 2 * (1 - x) + core)


def _slot_of(c):
    return c // 2 + 4 * ((c // 2 + c) % 2)


def _group_of(slot):
    return 2 * (slot % 4) + (slot // 4 + slot) % 2


def _block(x, core, j):
    return 4 * (1 - core) + 2 * j + (x + j) % 2


def _owner(b):
    return 2 * ((b // 2 + b) % 2) + 1 - b // 4


def _greet(targets):
    barrier = pltpu.get_barrier_semaphore()
    for target in targets:
        pl.semaphore_signal(barrier, inc=1, device_id=target, device_id_type=MESH_ID)
    pl.semaphore_wait(barrier, len(targets))


def _remote(src, dst, send, recv, target):
    return pltpu.make_async_remote_copy(
        src_ref=src, dst_ref=dst, send_sem=send, recv_sem=recv, device_id=target, device_id_type=MESH_ID
    )


def _comm_call(kernel, ins, outs, scratch, cid, name, in_space=pl.ANY, out_space=pl.ANY, vmem=None):
    return pl.pallas_call(
        kernel,
        out_shape=outs,
        in_specs=[pl.BlockSpec(memory_space=in_space)] * len(ins),
        out_specs=jax.tree.map(lambda _: pl.BlockSpec(memory_space=out_space), outs),
        scratch_shapes=scratch,
        compiler_params=pltpu.CompilerParams(
            collective_id=cid, has_side_effects=True, vmem_limit_bytes=vmem
        ),
        name=name,
    )(*ins)


def _gather_steps(ins, outs, own_sem, send_sem, recv_sem, place):
    c, f, x, core, core_peer, x_peer = place
    h = 1 - core
    count = len(ins)
    local = []
    sends = []

    def first():
        for base, target in ((0, x_peer), (2 * count, core_peer)):
            for i in range(count):
                for j in range(2):
                    k = base + i * 2 + j
                    cp = _remote(
                        ins[i].at[j], outs[i].at[h, j, (x + j) % 2], send_sem.at[k], recv_sem.at[k], target
                    )
                    cp.start()
                    sends.append(cp)
        for i in range(count):
            for j in range(2):
                lc = pltpu.make_async_copy(
                    ins[i].at[j], outs[i].at[h, j, (x + j) % 2], own_sem.at[i * 2 + j]
                )
                lc.start()
                local.append(lc)

    def last():
        forwards = []
        for i in range(count):
            for j in range(2):
                k = i * 2 + j
                sends[k].wait_recv()
                cp = _remote(
                    outs[i].at[h, j, (x + j + 1) % 2],
                    outs[i].at[h, j, (x + j + 1) % 2],
                    send_sem.at[4 * count + k],
                    recv_sem.at[4 * count + k],
                    core_peer,
                )
                cp.start()
                forwards.append(cp)
        for k in range(2 * count):
            sends[2 * count + k].wait_recv()
            forwards[k].wait_recv()
        for cp in sends + forwards:
            cp.wait_send()
        for lc in local:
            lc.wait()

    return first, last


def _ctx_first(piece, lines, own_sem, send_sem, recv_sem, place):
    c, f, x, core, core_peer, x_peer = place
    z, y = c // 2, c % 2
    sends = []
    local = []

    def start():
        lc = pltpu.make_async_copy(piece, lines.at[z, x], own_sem)
        lc.start()
        local.append(lc)
        cp = _remote(piece, lines.at[z, x], send_sem.at[0], recv_sem.at[0], x_peer)
        cp.start()
        sends.append(cp)

    def spread():
        local[0].wait()
        sends[0].wait_recv()
        for step in range(1, 4):
            cp = _remote(
                lines.at[z],
                lines.at[z],
                send_sem.at[step],
                recv_sem.at[step],
                (2 * ((z + step) % 4) + y, f),
            )
            cp.start()
            sends.append(cp)

    def finish():
        for cp in sends[1:]:
            cp.wait_recv()
        for cp in sends:
            cp.wait_send()

    return start, spread, finish


def _ctx_second(lines, out, own_sem, send_sem, recv_sem, place):
    c, f, x, core, core_peer, x_peer = place
    z, y = c // 2, c % 2
    y_peer = (2 * z + 1 - y, f)
    sends = []
    local = []

    def start():
        lc = pltpu.make_async_copy(lines, out.at[y, core], own_sem)
        lc.start()
        local.append(lc)
        for k, target in ((0, y_peer), (1, core_peer)):
            cp = _remote(lines, out.at[y, core], send_sem.at[k], recv_sem.at[k], target)
            cp.start()
            sends.append(cp)

    def share():
        sends[0].wait_recv()
        cp = _remote(
            out.at[1 - y, core], out.at[1 - y, core], send_sem.at[2], recv_sem.at[2], core_peer
        )
        cp.start()
        sends.append(cp)

    def finish():
        sends[1].wait_recv()
        sends[2].wait_recv()
        for cp in sends:
            cp.wait_send()
        local[0].wait()

    return start, share, finish


def _ctx_planes(piece, out, own_sem, send_sem, recv_sem, place):
    c, f, x, core, core_peer, x_peer = place
    z, y = c // 2, c % 2
    y_peer = (2 * z + 1 - y, f)
    sends = {}
    local = []

    def send(k, src, dst, target):
        cp = _remote(src, dst, send_sem.at[k], recv_sem.at[k], target)
        cp.start()
        sends[k] = cp

    def spot(yy, zz):
        return out.at[yy, core, zz, x]

    def start():
        lc = pltpu.make_async_copy(piece, spot(y, z), own_sem)
        lc.start()
        local.append(lc)
        for step in range(1, 4):
            send(step, piece, spot(y, z), (2 * ((z + step) % 4) + y, f))
        send(4, piece, spot(y, z), y_peer)
        send(8, piece, spot(y, z), x_peer)

    def forward():
        for step in range(1, 4):
            sends[step].wait_recv()
            at = spot(y, (z + 4 - step) % 4)
            send(4 + step, at, at, y_peer)
            send(8 + step, at, at, x_peer)
        for step in range(4):
            sends[4 + step].wait_recv()
            at = spot(1 - y, (z + 4 - step) % 4)
            send(12 + step, at, at, x_peer)

    def finish():
        local[0].wait()
        for half in range(2):
            for step in range(4):
                sends[8 + 4 * half + step].wait_recv()
            yy = 1 - y if half else y
            send(16 + half, out.at[yy, core], out.at[yy, core], core_peer)
        for half in range(2):
            sends[16 + half].wait_recv()
        for cp in sends.values():
            cp.wait_send()

    return start, forward, finish


def _z_peers(place):
    c, f = place[:2]
    return [(2 * ((c // 2 + step) % 4) + c % 2, f) for step in range(1, 4)]


def _y_peer(place):
    c, f = place[:2]
    return (2 * (c // 2) + 1 - c % 2, f)


def _lines_of(n):
    return (4, 2, RANK, n)


def _spread_of(n):
    return jax.ShapeDtypeStruct((2, 2, 4, 2, RANK, n), BF16)


FIRST_SEMS = [pltpu.SemaphoreType.DMA(()), _sem(4), _sem(4)]
SECOND_SEMS = [pltpu.SemaphoreType.DMA(()), _sem(3), _sem(3)]
PLANE_SEMS = [pltpu.SemaphoreType.DMA(()), _sem(18), _sem(18)]


def _order_steps(own, order, own_sem, send_sem, recv_sem, place):
    core_peer, x_peer = place[4:]
    sends, local, forwards = [], [], []

    def first():
        for j in range(2):
            cp = _remote(own.at[j], order.at[1 + j, 1], send_sem.at[j], recv_sem.at[j], x_peer)
            cp.start()
            sends.append(cp)
        for j in range(2):
            cp = _remote(
                own.at[j], order.at[3, j], send_sem.at[2 + j], recv_sem.at[2 + j], core_peer
            )
            cp.start()
            sends.append(cp)
        for j in range(2):
            lc = pltpu.make_async_copy(own.at[j], order.at[0, j], own_sem.at[j])
            lc.start()
            local.append(lc)

    def forward(j):
        sends[j].wait_recv()
        cp = _remote(
            order.at[1 + j, 1],
            order.at[1 + j, 0],
            send_sem.at[4 + j],
            recv_sem.at[4 + j],
            core_peer,
        )
        cp.start()
        forwards.append(cp)

    def own_here():
        for lc in local:
            lc.wait()

    def core_here():
        for j in range(2):
            sends[2 + j].wait_recv()

    def far_here(j):
        forwards[j].wait_recv()

    def last():
        for cp in sends + forwards:
            cp.wait_send()

    return first, forward, own_here, core_here, far_here, last


def _order_all(own, order, sems, place):
    first, forward, own_here, core_here, far_here, last = _order_steps(own, order, *sems, place)
    first()
    own_here()
    for j in range(2):
        forward(j)
    core_here()
    for j in range(2):
        far_here(j)
    last()


def feed_forward(own, cot, resid, gain, length, weights, adapters, cid):
    gate_w, up_w, down_w = weights
    width, units = gate_w.shape
    wide = width + SIDE
    tile = 256

    loads_in = tuple(weights) + tuple(adapters) + (cot,)
    count = len(loads_in)

    def kernel(*refs):
        len_ref, own_ref, resid_ref, gain_ref = refs[:4]
        loads_hbm = refs[4 : 4 + count]
        outs_hbm = refs[4 + count : 11 + count]
        mirrors = refs[len(refs) - 8 : len(refs) - 1]
        grad_resid, grad_low, small, out_own, out_far, order, early = mirrors
        flush_sem = refs[len(refs) - 1]
        refs = refs[11 + count : len(refs) - 8]
        flushed = []

        def flush(*places):
            for at in places:
                cp = pltpu.make_async_copy(mirrors[at], outs_hbm[at], flush_sem.at[at])
                cp.start()
                flushed.append(cp)

        gate_ref, up_ref, down_ref, first_ref, sg_ref, su_ref, fd_ref, sd_ref, go_ref = refs[:count]
        (
            sums,
            hid_s,
            gg_s,
            gu_s,
            in_s,
            gid_s,
            part,
            out_part,
            near,
            out_near,
            far,
            out_land,
            staged,
            landed,
            load_sem,
            send_sem,
            recv_sem,
            s_sem,
            r_sem,
        ) = refs[count:]
        place = _place()
        core_peer, x_peer = place[4:]
        loads = []
        for i in range(count):
            cp = pltpu.make_async_copy(loads_hbm[i], refs[i], load_sem.at[i])
            cp.start()
            loads.append(cp)
        _greet([core_peer, x_peer])
        c, f, x, core = place[:4]
        live = len_ref[_slot_of(c)]

        def masked(step, middle):
            other_x = x + middle * (1 - 2 * x)
            pieces = []
            for i in range(2):
                other_core = core + (step // 3 + middle * (1 - i)) * (1 - 2 * core)
                j = (1 - middle) * i + middle * (step - 1)
                pos = 128 * _block(other_x, other_core, j) + lax.broadcasted_iota(
                    jnp.int32, (128, width), 0
                )
                pieces.append(jnp.where(pos < live, go_ref[step, i].astype(F32), 0.0).astype(BF16))
            return pieces

        def work(step, middle):
            rows = order[step].reshape(2 * 128, width)
            pieces = masked(step, middle)
            for k in range(2):
                go_ref[step, k] = pieces[k]
            go = go_ref[step].reshape(2 * 128, width)
            inner = dot_t(rows, first_ref[...]).astype(BF16)
            gid = dot_t(go, sd_ref[...]).astype(BF16)
            in_s[step] = inner
            gid_s[step] = gid
            for at in range(0, units, tile):
                cols = slice(at, at + tile)
                gate = dot(rows, gate_ref[:, cols]) + dot(inner, sg_ref[:, cols])
                up = dot(rows, up_ref[:, cols]) + dot(inner, su_ref[:, cols])
                grad = dot_t(go, down_ref[cols, :]) + dot(gid, fd_ref[:, cols])
                sig = 0.5 * jnp.tanh(0.5 * gate) + 0.5
                silu = gate * sig
                hid_s[step, :, cols] = (silu * up).astype(BF16)
                gg_s[step, :, cols] = (grad * up * sig * (1.0 + gate * (1.0 - sig))).astype(BF16)
                gu_s[step, :, cols] = (grad * silu).astype(BF16)
            gg, gu = gg_s[step], gu_s[step]
            for at in range(0, width, tile):
                cols = slice(at, at + tile)
                value = dot_t(gg, gate_ref[cols, :]) + dot_t(gu, up_ref[cols, :])
                part[step, :, :, cols] = value.astype(BF16).reshape(2, 128, tile)
            value = dot_t(gg, sg_ref[...]) + dot_t(gu, su_ref[...])
            part[step, :, :, width:] = value.astype(BF16).reshape(2, 128, SIDE)

        def down(step):
            hid = hid_s[step]
            for at in range(0, width, tile):
                cols = slice(at, at + tile)
                out = dot(hid, down_ref[:, cols])
                out_part[step, :, :, cols] = out.astype(BF16).reshape(2, 128, tile)
            out = dot_t(hid, fd_ref[...])
            out_part[step, :, :, width:] = out.astype(BF16).reshape(2, 128, SIDE)

        def sent(src, dst, n, target):
            return _remote(src, dst, s_sem.at[n], r_sem.at[n], target)

        def from_x(j):
            return _remote(own_ref.at[j], order.at[1 + j, 1], send_sem.at[j], recv_sem.at[j], x_peer)

        def from_core(j):
            return _remote(
                own_ref.at[j], order.at[3, j], send_sem.at[2 + j], recv_sem.at[2 + j], core_peer
            )

        def from_far(j):
            return _remote(
                order.at[1 + j, 1],
                order.at[1 + j, 0],
                send_sem.at[4 + j],
                recv_sem.at[4 + j],
                core_peer,
            )

        def far_sum(j):
            return sent(part.at[1 + j, 0], far.at[j], 2 + j, core_peer)

        def far_out(j):
            return sent(out_part.at[1 + j, 0], out_land.at[j], 4 + j, core_peer)

        def near_sum():
            return sent(part.at[3], near, 0, core_peer)

        def near_out():
            return sent(out_part.at[3], out_near, 1, core_peer)

        def across(j):
            return sent(staged.at[j], landed.at[j], 6 + j, x_peer)

        for j in range(2):
            from_x(j).start()
        for j in range(2):
            from_core(j).start()
        for j in range(2):
            order[0, j] = own_ref[j]
        for cp in loads:
            cp.wait()

        def one_step(step, carry):
            middle = ((step + 1) // 2) % 2

            @pl.when(middle == 1)
            def _():
                j = step - 1
                from_x(j).wait_recv()
                from_far(j).start()
                from_far(j).wait_recv()

            @pl.when(step == 3)
            def _():
                for j in range(2):
                    from_core(j).wait_recv()

            work(step, middle)

            @pl.when(middle == 1)
            def _():
                far_sum(step - 1).start()

            @pl.when(step == 3)
            def _():
                near_sum().start()

            down(step)

            @pl.when(middle == 1)
            def _():
                j = step - 1
                far_out(j).start()
                far_sum(j).wait_recv()
                staged[j] = (part[1 + j, 1].astype(F32) + far[j].astype(F32)).astype(BF16)
                across(j).start()

            @pl.when(step == 3)
            def _():
                near_out().start()

            return carry

        lax.fori_loop(0, 4, one_step, 0)
        flush(5)
        for j in range(2):
            far_out(j).wait_recv()
            out_far[j] = (out_part[1 + j, 1].astype(F32) + out_land[j].astype(F32)).astype(BF16)
        near_sum().wait_recv()
        near_out().wait_recv()
        sums[...] = part[0].astype(F32) + near[...].astype(F32)
        out_own[...] = out_part[0].astype(F32) + out_near[...].astype(F32)
        for at in range(0, units, 512):
            cols = slice(at, at + 512)
            g = jnp.zeros((SIDE, 512), F32)
            u = jnp.zeros((SIDE, 512), F32)
            d = jnp.zeros((SIDE, 512), F32)
            for step in range(4):
                g += dot_rows(in_s[step], gg_s[step, :, cols])
                u += dot_rows(in_s[step], gu_s[step, :, cols])
                d += dot_rows(gid_s[step], hid_s[step, :, cols])
            early[:, at : at + 512] = (ADAPTER_SCALE * g[:RANK]).astype(BF16)
            early[:, units + at : units + at + 512] = (ADAPTER_SCALE * u[RANK : 2 * RANK]).astype(BF16)
            early[:, 2 * units + at : 2 * units + at + 512] = d[3 * RANK : 4 * RANK].astype(BF16)
        flush(3, 4, 6)
        for j in range(2):
            across(j).wait_recv()
            total = sums[j] + landed[j].astype(F32)
            gi = total[:, width:].astype(BF16)
            small[j] = gi
            gn = (total[:, :width] + dot(gi, first_ref[...])).astype(BF16).astype(F32)
            v = resid_ref[j]
            factor = lax.rsqrt(jnp.mean(v * v, axis=1, keepdims=True) + EPSILON)
            scaled = gn * gain_ref[...].reshape(1, width)
            mean = jnp.mean(scaled * v, axis=1, keepdims=True)
            grad = go_ref[0, j].astype(F32) + factor * scaled - v * (factor * factor * factor) * mean
            grad_resid[j] = grad
            grad_low[j] = grad.astype(BF16)
        flush(0, 1, 2)
        for j in range(2):
            for cp in (from_x(j), from_core(j), from_far(j), far_sum(j), far_out(j), across(j)):
                cp.wait_send()
        near_sum().wait_send()
        near_out().wait_send()
        for cp in flushed:
            cp.wait()

    vmem = pl.BlockSpec(memory_space=pltpu.VMEM)
    rows = (2, 128, wide)
    f32 = lambda *shape: jax.ShapeDtypeStruct(shape, F32)
    outs = [
        f32(2, 128, width),
        jax.ShapeDtypeStruct((2, 128, width), BF16),
        jax.ShapeDtypeStruct((2, 128, SIDE), BF16),
        f32(*rows),
        jax.ShapeDtypeStruct(rows, BF16),
        jax.ShapeDtypeStruct((4, 2, 128, width), BF16),
        jax.ShapeDtypeStruct((RANK, 3 * units), BF16),
    ]
    hbm = pl.BlockSpec(memory_space=pl.ANY)
    return pl.pallas_call(
        kernel,
        out_shape=outs,
        in_specs=[pl.BlockSpec(memory_space=pltpu.SMEM), vmem, vmem, vmem] + [hbm] * count,
        out_specs=[hbm] * len(outs),
        scratch_shapes=[pltpu.VMEM(a.shape, a.dtype) for a in loads_in]
        + [pltpu.VMEM(rows, F32)]
        + [pltpu.VMEM((4, 256, units), BF16)] * 3
        + [pltpu.VMEM((4, 256, SIDE), BF16)] * 2
        + [pltpu.VMEM((4,) + rows, BF16)] * 2
        + [pltpu.VMEM(rows, BF16)] * 6
        + [_sem(count), _sem(6), _sem(6), _sem(8), _sem(8)]
        + [pltpu.VMEM(o.shape, o.dtype) for o in outs]
        + [_sem(len(outs))],
        compiler_params=pltpu.CompilerParams(
            collective_id=cid, has_side_effects=True, vmem_limit_bytes=58 * 1024 * 1024
        ),
        name="feed_forward",
    )(length, own, resid, gain, *loads_in)


def _back_steps(src, dst, out_s, out_r, place):
    c, f, x, core = place[:4]
    slot = _slot_of(c)
    place_in = slot % 2

    def move(j):
        return _remote(
            src.at[j],
            dst.at[place_in],
            out_s.at[j],
            out_r.at[place_in],
            (_block(x, core, j), slot // 2),
        )

    def first(j):
        move(j).start()

    def last():
        for half in range(2):
            pltpu.make_async_copy(dst.at[half], dst.at[half], out_r.at[half]).wait()
        for j in range(2):
            move(j).wait_send()

    return first, last


def _back_sources(place):
    c, f = place[:2]
    return [(_group_of(2 * f + half), _owner(c)) for half in range(2)]


def front_call(
    tokens,
    cotangent,
    lengths,
    adapters,
    gains,
    wq,
    wk,
    wv,
    wo,
    tables,
    cosine,
    sine,
    cid,
):
    width = tokens.shape[-1]
    rows = cosine.shape[0]
    wide = width + SIDE
    block = 256
    scale = HEAD_DIM ** (-0.5)
    lane = PAD_HEAD
    units = tables[6].shape[-1] // 4
    quarter = width // 4
    loads_in = gains + (wq, wk, wv, wo) + tables + (cosine, sine)
    count = len(loads_in)

    vmem, hbm = pl.BlockSpec(memory_space=pltpu.VMEM), pl.BlockSpec(memory_space=pl.ANY)
    smem = pl.BlockSpec(memory_space=pltpu.SMEM)
    low = lambda *shape: jax.ShapeDtypeStruct(shape, BF16)
    outs = [
        (jax.ShapeDtypeStruct((2, 128, width), F32), vmem),
        (low(2, 128, width), vmem),
        (low(2, 2, 2, 128, SIDE), hbm),
        (low(2, 128, width), vmem),
        (low(4, 2, 128, width), hbm),
        (low(2, 128, width), hbm),
        (low(rows, 8 * lane), vmem),
        (jax.ShapeDtypeStruct((rows, lane), F32), vmem),
        (low(rows, 4 * lane), vmem),
        (low(rows, quarter), vmem),
        (low(rows, SIDE), vmem),
        (low(width, 4 * lane), vmem),
        (low(4 * lane, width), vmem),
        (low(4 * lane, width), vmem),
        (low(SIDE, 8 * lane), vmem),
        (low(SIDE, width), vmem),
        (low(SIDE, width), vmem),
        (low(SIDE, units), vmem),
        (low(SIDE, units), vmem),
        (low(SIDE, units), vmem),
        (low(SIDE, width), vmem),
        (low(SIDE, 4 * lane), vmem),
        (low(SIDE, width), vmem),
    ]
    mirror_of = []
    for o in outs:
        mirror_of.append(sum(m >= 0 for m in mirror_of) if o[1] is vmem else -1)
    mirrored = sum(m >= 0 for m in mirror_of) + 1

    def kernel(*refs):
        len_ref, adapter_ref, tok_ref, cot_ref = refs[:4]
        loads_hbm = refs[4 : 4 + count]
        (
            sums_resid,
            normed_two,
            side_all,
            tok_own,
            cot_order,
            cot_peer,
            qkv_ref,
            lse_ref,
            att_ref,
            one_cut,
            inner_ref,
            wa_ref,
            wkv_ref,
            ow_ref,
            sa_ref,
            fa_ref,
            fgu_ref,
            sg_ref,
            su_ref,
            fd_ref,
            sd_ref,
            fo_ref,
            so_ref,
        ) = [
            refs[len(refs) - mirrored + k] if k >= 0 else out
            for k, out in zip(mirror_of, refs[4 + count : 27 + count])
        ]
        outs_hbm = refs[4 + count : 27 + count]
        mirrors = refs[len(refs) - mirrored : len(refs) - 1]
        flush_sem = refs[len(refs) - 1]
        refs = refs[27 + count :]
        flushed = []

        def flush(*places):
            for at in places:
                n = mirror_of[at]
                cp = pltpu.make_async_copy(mirrors[n], outs_hbm[at], flush_sem.at[n])
                cp.start()
                flushed.append(cp)

        gain_one, gain_two, wq_v, wk_v, wv_v, wo_v = refs[:6]
        in_first, out_first, down_first, q_second, kv_second, o_second, gu_second, d_second = refs[6:14]
        cos_ref, sin_ref = refs[14:16]
        (
            tok_all,
            one_ref,
            part,
            land,
            staged,
            landed,
            sums,
            side_own,
            load_sem,
            land_s,
            land_r,
            cot_s,
            cot_r,
            send_sem,
            recv_sem,
            s_sem,
            r_sem,
        ) = refs[16:33]
        side_sems = refs[33:36]
        place = _place()
        c, f, x, core, core_peer, x_peer = place
        hh = 1 - core
        slot = _slot_of(c)
        live = len_ref[slot]
        which = adapter_ref[slot]
        loads = []
        for i in range(count):
            cp = pltpu.make_async_copy(loads_hbm[i], refs[i], load_sem.at[i])
            cp.start()
            loads.append(cp)

        barrier = pltpu.get_barrier_semaphore()
        for j in range(2):
            pl.semaphore_signal(
                barrier, inc=1, device_id=(_block(x, core, j), slot // 2), device_id_type=MESH_ID
            )
        for target in (core_peer, x_peer):
            pl.semaphore_signal(barrier, inc=1, device_id=target, device_id_type=MESH_ID)
        for b in range(4):
            pl.semaphore_signal(
                barrier,
                inc=1,
                device_id=(4 * hh + b, 2 * x + (slot // 2) % 2),
                device_id_type=MESH_ID,
            )
        pl.semaphore_wait(barrier, 8)
        to_f = _owner(c)
        to_h = c // 4
        to_j = (c // 2) % 2
        to_i = c % 2
        moves = []
        for part_row in range(2):
            span = pl.ds(64 * part_row, 64)
            for half in range(2):
                s = 2 * f + half
                cp = _remote(
                    tok_ref.at[half, span],
                    tok_all.at[to_h, to_j, to_i, span],
                    land_s.at[2 * part_row + half],
                    land_r.at[2 * part_row + to_j],
                    (_group_of(s), to_f),
                )
                cp.start()
                moves.append(cp)
        cross = [
            _remote(cot_ref.at[half], cot_peer.at[half], cot_s.at[half], cot_r.at[half], x_peer)
            for half in range(2)
        ]
        cross[0].start()
        cot_moves = []
        for relay in range(2):
            for half in range(2):
                s = 2 * (2 * ((x + relay) % 2) + core) + half
                away = ((c // 2 + c) % 2 + x) % 2
                cot_moves.append(
                    _remote(
                        (cot_peer if relay else cot_ref).at[half],
                        cot_order.at[away * (1 + to_j), (1 - away) * to_j + away],
                        cot_s.at[2 + 2 * relay + half],
                        cot_r.at[2 + 2 * away + to_j],
                        (_group_of(s), 2 * x + 1 - to_h),
                    )
                )
        for cp in loads:
            cp.wait()

        def group_sends(part_row):
            span = pl.ds(64 * part_row, 64)
            for j in range(2):
                pltpu.make_async_copy(
                    tok_all.at[hh, j, (x + j) % 2, span],
                    tok_all.at[hh, j, (x + j) % 2, span],
                    land_r.at[2 * part_row + j],
                ).wait()
                k = 2 * part_row + j
                here = tok_all.at[hh, j, (x + j) % 2, span]
                for base, target in ((0, x_peer), (4, core_peer)):
                    cp = _remote(
                        here, here, send_sem.at[base + k], recv_sem.at[base + k], target
                    )
                    cp.start()
                    sends[base + k] = cp

        sends = {}

        def prepare_first():
            half = HEAD_DIM // 2
            wa_ref[...] = jnp.zeros_like(wa_ref)
            wkv_ref[...] = jnp.zeros_like(wkv_ref)
            sa_ref[...] = jnp.zeros_like(sa_ref)
            for head in range(4):
                for side in range(2):
                    at = head * HEAD_DIM + side * half
                    to = head * lane + side * HALF_PAD
                    wa_ref[:, to : to + half] = wq_v[:, at : at + half]
            for head in range(2):
                for side in range(2):
                    at = head * HEAD_DIM + side * half
                    to = head * lane + side * HALF_PAD
                    wkv_ref[to : to + half, :] = wk_v[at : at + half, :]
                at, to = head * HEAD_DIM, (2 + head) * lane
                wkv_ref[to : to + HEAD_DIM, :] = wv_v[at : at + HEAD_DIM, :]

        def prepare_second():
            half = HEAD_DIM // 2
            own_cols = pl.ds(pl.multiple_of(f * quarter, 128), quarter)
            own_units = pl.ds(pl.multiple_of(f * units, 128), units)
            low = lambda v: (ADAPTER_SCALE * v.astype(F32)).astype(BF16)
            for ref in (fa_ref, fgu_ref, sg_ref, su_ref, fd_ref, sd_ref, fo_ref, so_ref, ow_ref):
                ref[...] = jnp.zeros_like(ref)
            for i in range(3):
                fa_ref[i * RANK : (i + 1) * RANK, :] = in_first[which, i]
            for i in range(2):
                fgu_ref[i * RANK : (i + 1) * RANK, :] = in_first[which, 3 + i]
            all_gu = gu_second.at[:, :, :, own_units]
            sg_ref[:RANK, :] = low(all_gu[which, 0])
            su_ref[RANK : 2 * RANK, :] = low(all_gu[which, 1])
            fd_ref[3 * RANK : 4 * RANK, :] = down_first.at[:, :, own_units][which]
            sd_ref[3 * RANK : 4 * RANK, :] = low(d_second[which])
            so_ref[:RANK, :] = low(o_second[which])
            own_first = out_first.at[:, :, own_cols][which]
            own_q = low(q_second.at[:, :, own_cols][which])
            for head in range(4):
                at = head * HEAD_DIM
                fo_ref[:RANK, head * lane : head * lane + HEAD_DIM] = own_first[:, at : at + HEAD_DIM]
                ow_ref[head * lane : head * lane + HEAD_DIM, :] = wo_v[at : at + HEAD_DIM, :]
                for side in range(2):
                    to = head * lane + side * HALF_PAD
                    sa_ref[:RANK, to : to + half] = own_q[:, at + side * half : at + (side + 1) * half]
            window = pl.ds(pl.multiple_of((3 * f // 2) * 128, 128), 256)
            for i in range(2):
                own_kv = kv_second.at[:, :, :, window][which, i].astype(F32)
                shifted = pltpu.roll(own_kv, 256 - 64, 1)
                own_kv = low(jnp.where(f % 2 == 1, shifted, own_kv))
                for head in range(2):
                    at = head * HEAD_DIM
                    if i:
                        to = (6 + head) * lane
                        sa_ref[2 * RANK : 3 * RANK, to : to + HEAD_DIM] = own_kv[:, at : at + HEAD_DIM]
                    else:
                        for side in range(2):
                            to = (4 + head) * lane + side * HALF_PAD
                            sa_ref[RANK : 2 * RANK, to : to + half] = own_kv[
                                :, at + side * half : at + (side + 1) * half
                            ]

        prepare_first()
        group_sends(0)
        prepare_second()
        flush(*range(11, 23))
        group_sends(1)
        for cp in cot_moves[:2]:
            cp.start()
        cross[0].wait_recv()
        cot_moves[2].start()

        def cot_spot(away, j):
            return cot_order.at[(1 + j) if away else 0, 1 if away else j]

        def cot_share():
            for away in range(2):
                for j in range(2):
                    here = cot_spot(away, j)
                    pltpu.make_async_copy(here, here, cot_r.at[2 + 2 * away + j]).wait()
                    there = cot_order.at[1 + j, 0] if away else cot_order.at[3, j]
                    k = 6 + 2 * away + j
                    cp = _remote(here, there, cot_s.at[k], cot_r.at[k], core_peer)
                    cp.start()
                    shared.append(cp)

        shared = []

        def forward(j):
            for part_row in range(2):
                k = 2 * part_row + j
                span = pl.ds(64 * part_row, 64)
                sends[k].wait_recv()
                there = tok_all.at[hh, j, (x + j + 1) % 2, span]
                cp = _remote(there, there, send_sem.at[8 + k], recv_sem.at[8 + k], core_peer)
                cp.start()
                sends[8 + k] = cp
            for part_row in range(2):
                k = 2 * part_row + j
                sends[4 + k].wait_recv()
                sends[8 + k].wait_recv()

        def project_rows(t):
            row = pl.ds(t * block, block)
            v = tok_all[t // 2, t % 2].reshape(block, width).astype(F32)
            factor = lax.rsqrt(jnp.mean(v * v, axis=1, keepdims=True) + EPSILON)
            u = (v * factor * gain_one[...].reshape(1, width)).astype(BF16)
            one_ref[row, :] = u
            inner = dot_t(u, fa_ref[...]).astype(BF16)
            inner_ref[row, :] = inner
            cos, sin = cos_ref[row, :], sin_ref[row, :]
            for pair in range(4):
                cols = slice(pair * 2 * lane, (pair + 1) * 2 * lane)
                if pair < 2:
                    both = dot(u, wa_ref[:, cols])
                else:
                    both = dot_t(u, wkv_ref[2 * (pair - 2) * lane : 2 * (pair - 1) * lane, :])
                both = both + dot(inner, sa_ref[:, cols])
                for k in range(2):
                    p = both[:, k * lane : (k + 1) * lane]
                    if pair < 3:
                        p = p * cos + pltpu.roll(p, HALF_PAD, 1) * sin
                    qkv_ref[row, (2 * pair + k) * lane : (2 * pair + k + 1) * lane] = p.astype(BF16)

        def attention(t, hook):
            keys = (t + 1) * block
            row = pl.ds(t * block, block)
            qpos = t * block + lax.broadcasted_iota(jnp.int32, (block, keys), 0)
            kpos = lax.broadcasted_iota(jnp.int32, (block, keys), 1)
            allowed = (kpos <= qpos) & (kpos < live)
            stats = jnp.zeros((block, lane), F32)
            lanes = lax.broadcasted_iota(jnp.int32, (block, lane), 1)
            for head in range(4):
                q = qkv_ref[row, head * lane : (head + 1) * lane]
                kv = head // 2
                k = qkv_ref[:keys, (4 + kv) * lane : (5 + kv) * lane]
                v = qkv_ref[:keys, (6 + kv) * lane : (7 + kv) * lane]
                s = jnp.where(allowed, dot_t(q, k) * scale, NEGATIVE)
                top = jnp.max(s, axis=1, keepdims=True)
                p = jnp.where(allowed, jnp.exp(s - top), 0.0)
                total = jnp.sum(p, axis=1, keepdims=True)
                o = dot(p.astype(BF16), v) / total
                att_ref[row, head * lane : (head + 1) * lane] = o.astype(BF16)
                stats = jnp.where(lanes == head, top + jnp.log(total), stats)
                if head == 1 and hook is not None:
                    hook()
            lse_ref[row, :] = stats
            a = att_ref[row, :]
            for at in range(0, width, 256):
                value = dot(a, ow_ref[:, at : at + 256])
                part[t, :, :, at : at + 256] = value.astype(BF16).reshape(2, 128, 256)
            part[t, :, :, width:] = dot_t(a, fo_ref[...]).astype(BF16).reshape(2, 128, SIDE)

        def to_core(t):
            return _remote(part.at[t], land.at[t % 2], s_sem.at[t % 2], r_sem.at[t % 2], core_peer)

        def to_x(j):
            return _remote(staged.at[j], landed.at[j], s_sem.at[2 + j], r_sem.at[2 + j], x_peer)

        def leave(t):
            @pl.when(core == t // 2)
            def _():
                to_core(t).start()

        def combine(t):
            j = t % 2

            @pl.when(core == 1 - t // 2)
            def _():
                to_core(t).wait_recv()
                mine, other = (x + j) % 2, (x + j + 1) % 2
                staged[j] = (part[t, other].astype(F32) + land[j, other].astype(F32)).astype(BF16)
                to_x(j).start()
                sums[j] = part[t, mine].astype(F32) + land[j, mine].astype(F32)

        forward(0)
        cross[1].start()
        project_rows(0)
        project_rows(2)
        attention(0, None)
        leave(0)
        forward(1)
        project_rows(1)
        project_rows(3)
        cross[1].wait_recv()
        cot_moves[3].start()
        attention(1, lambda: combine(0))
        leave(1)
        attention(2, lambda: combine(1))
        leave(2)
        attention(3, lambda: combine(2))
        leave(3)
        combine(3)
        cot_share()
        for t in range(4):

            @pl.when(core == t // 2)
            def _():
                to_core(t).wait_send()

        for j in range(2):
            tok_own[j] = tok_all[hh, j, (x + j) % 2]
        one_cut[...] = one_ref[:, pl.ds(pl.multiple_of(f * quarter, 128), quarter)]
        for j in range(2):
            cp = to_x(j)
            cp.wait_recv()
            sums[j] = sums[j] + landed[j].astype(F32)
            cp.wait_send()
            side_own[j] = sums[j, :, width:].astype(BF16)
        side_first, side_last = _gather_steps([side_own], [side_all], *side_sems, place)
        side_first()
        flush(3, 6, 7, 8, 9, 10)
        for j in range(2):
            v = (
                tok_own[j].astype(F32)
                + sums[j, :, :width]
                + dot(side_own[j], so_ref[...])
            )
            sums_resid[j] = v
            factor = lax.rsqrt(jnp.mean(v * v, axis=1, keepdims=True) + EPSILON)
            normed_two[j] = (v * factor * gain_two[...].reshape(1, width)).astype(BF16)
        flush(0, 1)
        for cp in shared:
            cp.wait_recv()
        side_last()
        for cp in flushed:
            cp.wait()
        for cp in moves + cross + cot_moves + shared + list(sends.values()):
            cp.wait_send()

    own = (2, 128, wide)
    return pl.pallas_call(
        kernel,
        out_shape=[o[0] for o in outs],
        in_specs=[smem, smem] + [hbm] * (2 + count),
        out_specs=[hbm for o in outs],
        scratch_shapes=[pltpu.VMEM(a.shape, a.dtype) for a in loads_in]
        + [
            pltpu.VMEM((2, 2, 2, 128, width), BF16),
            pltpu.VMEM((rows, width), BF16),
            pltpu.VMEM((4,) + own, BF16),
            pltpu.VMEM((2,) + own, BF16),
            pltpu.VMEM(own, BF16),
            pltpu.VMEM(own, BF16),
            pltpu.VMEM(own, F32),
            pltpu.VMEM((2, 128, SIDE), BF16),
            _sem(count),
            _sem(4),
            _sem(4),
            _sem(10),
            _sem(10),
            _sem(12),
            _sem(12),
            _sem(4),
            _sem(4),
        ]
        + [_sem(2), _sem(6), _sem(6)]
        + [pltpu.VMEM(o[0].shape, o[0].dtype) for o in outs if o[1] is vmem]
        + [_sem(mirrored - 1)],
        compiler_params=pltpu.CompilerParams(
            collective_id=cid, has_side_effects=True, vmem_limit_bytes=58 * 1024 * 1024
        ),
        name="front",
    )(lengths, adapters, tokens, cotangent, *loads_in)


def attend_back_call(
    low_own,
    small_own,
    early,
    out_far,
    length,
    own_arrays,
    arrays,
    cid,
):
    qkv = arrays[0]
    width = low_own.shape[-1]
    rows = qkv.shape[0]
    wide = width + SIDE
    step_rows = 256
    scale = HEAD_DIM ** (-0.5)
    lane = PAD_HEAD
    quarter = width // 4
    middle_n = 4 * quarter
    early_n = early.shape[1]
    big = tuple(arrays) + tuple(own_arrays)
    late_n = 4 * quarter
    factor_n = 2 * quarter
    count = len(big)

    def kernel(*refs):
        len_ref, low_ref, small_ref, early_ref, out_ref = refs[:5]
        big_in = refs[5 : 5 + count]
        (
            out_back,
            grad_back,
            early_out,
            middle_out,
            late_out,
            factor_out,
        ) = refs[5 + count : 11 + count]
        refs = refs[11 + count :]
        (
            qkv_ref,
            lse_ref,
            att_ref,
            inner_ref,
            order_ref,
            cos_ref,
            sin_ref,
            ow_ref,
            fo_ref,
            so_ref,
            wa_ref,
            wkv_ref,
            sa_ref,
            fa_ref,
            sd_ref,
            cut_ref,
            inner_qkv_ref,
            cot_ref,
            out_own,
            resid_ref,
            tok_ref,
            grad_resid_ref,
            gain_ref,
        ) = refs[:count]
        (
            low,
            do_ref,
            gio_ref,
            dk_ref,
            dv_ref,
            part,
            land,
            staged,
            landed,
            side_own,
            middle_ref,
            sums,
            side_all,
            grad_ref,
            landed_out,
            small_out,
            late_ref,
            factor_ref,
            out_tok,
            grad_tok,
            early_lines,
            middle_lines,
            load_sem,
            own_sem,
            send_sem,
            recv_sem,
            s_sem,
            r_sem,
        ) = refs[count : count + 28]
        sems = refs[count + 28 :]
        place = _place()
        c, f, x, core, core_peer, x_peer = place
        loads = [
            pltpu.make_async_copy(big_in[i], refs[i], load_sem.at[i]) for i in range(count)
        ]
        for cp in loads:
            cp.start()
        _greet(
            _back_sources(place) + [core_peer, x_peer, _y_peer(place)] + _z_peers(place)
        )
        small_first, small_forward, small_own_here, small_core, small_far, small_last = _order_steps(
            small_ref, small_out, *sems[0:3], place
        )
        early_start, early_across, early_finish = _ctx_first(early_ref, early_lines, *sems[3:6], place)
        early_two = _ctx_second(early_lines, early_out, *sems[6:9], place)
        mid_start, mid_across, mid_finish = _ctx_first(middle_ref, middle_lines, *sems[9:12], place)
        mid_two = _ctx_second(middle_lines, middle_out, *sems[12:15], place)
        late = _ctx_planes(late_ref, late_out, *sems[15:18], place)
        factor = _ctx_planes(factor_ref, factor_out, *sems[25:28], place)
        side_first, side_last = _gather_steps([side_own], [side_all], *sems[18:21], place)
        out_first, out_last = _back_steps(out_tok, out_back, *sems[21:23], place)
        grad_first, grad_last = _back_steps(grad_tok, grad_back, *sems[23:25], place)
        live = len_ref[_slot_of(c)]

        sends = {}
        hh = 1 - core
        local = []
        for j in (1, 0):
            for k, target in ((0, x_peer), (2, core_peer)):
                cp = _remote(
                    low_ref.at[j],
                    low.at[hh, j, (x + j) % 2],
                    send_sem.at[k + j],
                    recv_sem.at[k + j],
                    target,
                )
                cp.start()
                sends[(k, j)] = cp
            if j:
                early_start()
                small_first()
        for j in range(2):
            lc = pltpu.make_async_copy(low_ref.at[j], low.at[hh, j, (x + j) % 2], own_sem.at[j])
            lc.start()
            local.append(lc)
        swaps = [
            _remote(out_ref.at[j], landed_out.at[j], s_sem.at[8 + j], r_sem.at[8 + j], x_peer)
            for j in range(2)
        ]
        dk_ref[...] = jnp.zeros_like(dk_ref)
        dv_ref[...] = jnp.zeros_like(dv_ref)
        for cp in loads:
            cp.wait()
        for lc in local:
            lc.wait()

        def arrive(j):
            sends[(0, j)].wait_recv()
            cp = _remote(
                low.at[hh, j, (x + j + 1) % 2],
                low.at[hh, j, (x + j + 1) % 2],
                send_sem.at[4 + j],
                recv_sem.at[4 + j],
                core_peer,
            )
            cp.start()
            sends[(4, j)] = cp
            sends[(2, j)].wait_recv()
            cp.wait_recv()

        def through_output(t):
            g = low[t // 2, t % 2].reshape(step_rows, width)
            gio = dot_t(g, so_ref[...]).astype(BF16)
            row = pl.ds(t * step_rows, step_rows)
            gio_ref[row, :] = gio
            do_ref[row, :] = (dot_t(g, ow_ref[...]) + dot(gio, fo_ref[...])).astype(BF16)

        def attention(t, hook):
            keys = (t + 1) * step_rows
            row = pl.ds(t * step_rows, step_rows)
            qpos = t * step_rows + lax.broadcasted_iota(jnp.int32, (step_rows, keys), 0)
            kpos = lax.broadcasted_iota(jnp.int32, (step_rows, keys), 1)
            allowed = (kpos <= qpos) & (kpos < live)
            cos, sin = cos_ref[row, :], sin_ref[row, :]
            for head in range(4):
                kv = head // 2
                at = slice(head * lane, (head + 1) * lane)
                q = qkv_ref[row, at]
                k = qkv_ref[:keys, (4 + kv) * lane : (5 + kv) * lane]
                v = qkv_ref[:keys, (6 + kv) * lane : (7 + kv) * lane]
                do = do_ref[row, at]
                s = dot_t(q, k)
                p = jnp.where(allowed, jnp.exp(s * scale - lse_ref[row, head : head + 1]), 0.0)
                dp = dot_t(do, v)
                total = jnp.sum(p * dp, axis=1, keepdims=True)
                ds = (p * (dp - total)).astype(BF16)
                dq = scale * dot(ds, k)
                dq = dq * cos - pltpu.roll(dq, HALF_PAD, 1) * sin
                grad_ref[row, at] = dq.astype(BF16)
                dk_ref[kv, :keys] += dot_rows(ds, q)
                dv_ref[kv, :keys] += dot_rows(p.astype(BF16), do)
                if head == 1 and hook is not None:
                    hook()
            for kv in range(2):
                dk = scale * dk_ref[kv, row, :]
                dk = dk * cos - pltpu.roll(dk, HALF_PAD, 1) * sin
                grad_ref[row, (4 + kv) * lane : (5 + kv) * lane] = dk.astype(BF16)
                grad_ref[row, (6 + kv) * lane : (7 + kv) * lane] = dv_ref[kv, row, :].astype(BF16)
            g = grad_ref[row, :]
            for at in range(0, width, 256):
                value = dot_t(g[:, : 4 * lane], wa_ref[at : at + 256, :])
                value = value + dot(g[:, 4 * lane :], wkv_ref[:, at : at + 256])
                part[t, :, :, at : at + 256] = value.astype(BF16).reshape(2, 128, 256)
            part[t, :, :, width:] = dot_t(g, sa_ref[...]).astype(BF16).reshape(2, 128, SIDE)

        def to_core(t):
            j = t % 2
            return _remote(part.at[t], land.at[j], s_sem.at[j], r_sem.at[j], core_peer)

        def to_x(j, narrow):
            cols = pl.ds(width, SIDE) if narrow else pl.ds(0, width)
            n = 2 + 2 * narrow + j
            return _remote(
                staged.at[j, :, cols], landed.at[j, :, cols], s_sem.at[n], r_sem.at[n], x_peer
            )

        def leave(t):
            @pl.when(core == t // 2)
            def _():
                to_core(t).start()

        def combine(t):
            j = t % 2

            @pl.when(core == 1 - t // 2)
            def _():
                to_core(t).wait_recv()
                mine, other = (x + j) % 2, (x + j + 1) % 2
                for cols, narrow in ((slice(width, wide), 1), (slice(0, width), 0)):
                    staged[j, :, cols] = (
                        part[t, other, :, cols].astype(F32) + land[j, other, :, cols].astype(F32)
                    ).astype(BF16)
                    to_x(j, narrow).start()
                sums[j] = part[t, mine].astype(F32) + land[j, mine].astype(F32)

        arrive(1)
        early_across()
        through_output(3)
        through_output(1)
        small_own_here()
        for j in range(2):
            small_forward(j)
        def second():
            arrive(0)
            for cp in swaps:
                cp.start()

        attention(3, second)
        leave(3)
        through_output(2)
        through_output(0)
        o_a = dot_rows(gio_ref[...], att_ref[...])[:RANK]
        o_a = jnp.concatenate(
            [o_a[:, head * lane : head * lane + HEAD_DIM] for head in range(4)], axis=1
        )
        middle_ref[:, :quarter] = o_a.astype(BF16)
        own_cols = pl.ds(pl.multiple_of(f * quarter, 128), quarter)
        g = low[:, :, :, :, own_cols].reshape(rows, quarter)
        middle_ref[:, quarter : 2 * quarter] = (ADAPTER_SCALE * dot_rows(inner_ref[...], g)[:RANK]).astype(BF16)
        for j in range(2):
            small_far(j)
        small_core()
        in_gu = jnp.zeros((SIDE, quarter), F32)
        for k in range(4):
            u = order_ref[k, :, :, own_cols].reshape(step_rows, quarter)
            in_gu += dot_rows(small_out[k].reshape(step_rows, SIDE), u)
        middle_ref[:, 2 * quarter : 3 * quarter] = in_gu[:RANK].astype(BF16)
        middle_ref[:, 3 * quarter :] = in_gu[RANK : 2 * RANK].astype(BF16)
        mid_start()
        early_finish()
        early_two[0]()

        def outputs():
            for j in range(2):
                swaps[j].wait()
                total = out_own[j] + landed_out[j].astype(F32)
                side = total[:, width:]
                out_own[j, :, width:] = side
                pos = 128 * _block(x, core, j) + lax.broadcasted_iota(jnp.int32, (128, width), 0)
                value = resid_ref[j] + total[:, :width] + dot(side.astype(BF16), sd_ref[...])
                out_tok[j] = jnp.where(pos < live, value, 0.0).astype(BF16)
                out_first(j)

        def third():
            combine(3)
            mid_across()

        attention(2, third)
        leave(2)
        outputs()
        attention(1, lambda: combine(2))
        leave(1)
        mid_finish()
        mid_two[0]()
        early_two[1]()
        attention(0, lambda: combine(1))
        leave(0)
        combine(0)
        def token_rows():
            for j in range(2):
                to_x(j, 0).wait_recv()
                gi = sums[j, :, width:].astype(BF16)
                total = sums[j, :, :width] + landed[j, :, :width].astype(F32)
                gn = (total + dot(gi, fa_ref[...])).astype(BF16).astype(F32)
                v = tok_ref[j].astype(F32)
                rms = lax.rsqrt(jnp.mean(v * v, axis=1, keepdims=True) + EPSILON)
                scaled = gn * gain_ref[...].reshape(1, width)
                mean = jnp.mean(scaled * v, axis=1, keepdims=True)
                grad = grad_resid_ref[j] + rms * scaled - v * (rms * rms * rms) * mean
                grad_tok[j] = grad.astype(BF16)
                grad_first(j)

        for j in range(2):
            to_x(j, 1).wait_recv()
            sums[j, :, width:] = sums[j, :, width:] + landed[j, :, width:].astype(F32)
            side_own[j] = (sums[j, :, width:] + out_own[j, :, width:]).astype(BF16)
        side_first()

        all_b = ADAPTER_SCALE * dot_rows(inner_qkv_ref[...], grad_ref[...])
        half = HEAD_DIM // 2
        pieces = []
        for head in range(6):
            r = slice(0, RANK) if head < 4 else slice(RANK, 2 * RANK)
            for side in range(2):
                to = head * lane + side * HALF_PAD
                pieces.append(all_b[r, to : to + half])
        for head in range(2):
            to = (6 + head) * lane
            pieces.append(all_b[2 * RANK : 3 * RANK, to : to + HEAD_DIM])
        factor_ref[...] = jnp.concatenate(pieces, axis=1).astype(BF16)
        factor[0]()
        mid_two[1]()
        factor[1]()
        side_last()
        in_qkv = dot_rows(side_all[...].reshape(rows, SIDE), cut_ref[...])
        for i in range(3):
            late_ref[:, i * quarter : (i + 1) * quarter] = in_qkv[i * RANK : (i + 1) * RANK].astype(
                BF16
            )
        d_b = jnp.zeros((SIDE, quarter), F32)
        for step in range(4):
            other_x = x if step in (0, 3) else 1 - x
            for i in range(2):
                other_core = (core, 1 - core)[step == 3 or (step in (1, 2) and i == 0)]
                jj = i if step in (0, 3) else step - 1
                pos = 128 * _block(other_x, other_core, jj) + lax.broadcasted_iota(
                    jnp.int32, (128, quarter), 0
                )
                go = cot_ref[step, i, :, own_cols].astype(F32)
                go = jnp.where(pos < live, go, 0.0).astype(BF16)
                d_b += dot_rows(side_all[1 - other_core, jj, (other_x + jj) % 2], go)
        late_ref[:, 3 * quarter :] = (ADAPTER_SCALE * d_b[3 * RANK : 4 * RANK]).astype(BF16)
        late[0]()

        token_rows()
        late[1]()
        for t in range(4):

            @pl.when(core == t // 2)
            def _():
                to_core(t).wait_send()

        for j in range(2):
            to_x(j, 0).wait_send()
            to_x(j, 1).wait_send()
        small_last()
        early_two[2]()
        mid_two[2]()
        factor[2]()
        late[2]()
        out_last()
        grad_last()
        for cp in sends.values():
            cp.wait_send()

    vmem, hbm = pl.BlockSpec(memory_space=pltpu.VMEM), pl.BlockSpec(memory_space=pl.ANY)
    shape = jax.ShapeDtypeStruct
    own = (2, 128, wide)
    return pl.pallas_call(
        kernel,
        out_shape=[
            shape((2, 128, width), BF16),
            shape((2, 128, width), BF16),
            _spread_of(early_n),
            _spread_of(middle_n),
            _spread_of(late_n),
            _spread_of(factor_n),
        ],
        in_specs=[pl.BlockSpec(memory_space=pltpu.SMEM)] + [hbm] * (4 + count),
        out_specs=[hbm] * 6,
        scratch_shapes=[pltpu.VMEM(a.shape, a.dtype) for a in big]
        + [
            pltpu.VMEM((2, 2, 2, 128, width), BF16),
            pltpu.VMEM((rows, 4 * lane), BF16),
            pltpu.VMEM((rows, SIDE), BF16),
            pltpu.VMEM((2, rows, lane), F32),
            pltpu.VMEM((2, rows, lane), F32),
            pltpu.VMEM((4,) + own, BF16),
            pltpu.VMEM((2,) + own, BF16),
            pltpu.VMEM(own, BF16),
            pltpu.VMEM(own, BF16),
            pltpu.VMEM((2, 128, SIDE), BF16),
            pltpu.VMEM((RANK, middle_n), BF16),
            pltpu.VMEM(own, F32),
            pltpu.VMEM((2, 2, 2, 128, SIDE), BF16),
            pltpu.VMEM((rows, 8 * lane), BF16),
            pltpu.VMEM(own, BF16),
            pltpu.VMEM((4, 2, 128, SIDE), BF16),
            pltpu.VMEM((RANK, late_n), BF16),
            pltpu.VMEM((RANK, factor_n), BF16),
            pltpu.VMEM((2, 128, width), BF16),
            pltpu.VMEM((2, 128, width), BF16),
            pltpu.VMEM(_lines_of(early_n), BF16),
            pltpu.VMEM(_lines_of(middle_n), BF16),
            _sem(count),
            _sem(2),
            _sem(6),
            _sem(6),
            _sem(10),
            _sem(10),
        ]
        + [_sem(2), _sem(6), _sem(6)]
        + FIRST_SEMS
        + SECOND_SEMS
        + FIRST_SEMS
        + SECOND_SEMS
        + PLANE_SEMS
        + [_sem(2), _sem(6), _sem(6)]
        + [_sem(2), _sem(2), _sem(2), _sem(2)]
        + PLANE_SEMS,
        compiler_params=pltpu.CompilerParams(
            collective_id=cid, has_side_effects=True, vmem_limit_bytes=62 * 1024 * 1024
        ),
        name="attend_back",
    )(length, low_own, small_own, early, out_far, *big)


def table_call(pieces, out_rows, grad_rows, adapters):
    f32 = lambda *shape: jax.ShapeDtypeStruct(shape, F32)
    choices = 8
    outs = [
        f32(choices, 5, RANK, 1536),
        f32(choices, RANK, 1536),
        f32(choices, RANK, 4096),
        f32(choices, RANK, 1536),
        f32(choices, 2, RANK, 768),
        f32(choices, RANK, 1536),
        f32(choices, 2, RANK, 4096),
        f32(choices, RANK, 1536),
    ]
    plan = (
        ((6, 0, 1024), (6, 1, 1024), (2, None, 1024)),
        ((1, None, 384), (5, None, 384), (0, 3, 384), (0, 4, 384)),
        (
            (0, 0, 384),
            (0, 1, 384),
            (0, 2, 384),
            (7, None, 384),
        ),
        ((3, None, 384), (4, 0, 192), (4, 1, 192)),
    )

    def kernel(which, early_in, middle_in, late_in, factor_in, rows_in, grad_in, *refs):
        outs, rows_out, grad_out = refs[:8], refs[8], refs[9]
        acc, held = refs[10:18], refs[18:22]
        grad_low, grad_full, rows_held, sems, load_sem = refs[22:27]
        loads = []
        for i, src in enumerate((early_in, middle_in, factor_in, late_in)):
            loads.append(pltpu.make_async_copy(src, held[(0, 1, 3, 2)[i]], load_sem.at[i]))
        grad_load = pltpu.make_async_copy(grad_in, grad_low, load_sem.at[4])
        rows_load = pltpu.make_async_copy(rows_in, rows_held, load_sem.at[5])
        for cp in loads + [grad_load, rows_load]:
            cp.start()

        def add(piece, ref):
            def one_slot(origin, carry):
                row = which[origin % 4 + 4 * ((origin // 4 + origin) % 2)]
                for f in range(4):
                    at = 0
                    for out, table, n in plan[piece]:
                        value = ref[origin // 4, f % 2, origin % 4, f // 2, :, at : at + n].astype(F32)
                        cols = slice(f * n, (f + 1) * n)
                        if table is None:
                            acc[out][row, :, cols] += value
                        else:
                            acc[out][row, table, :, cols] += value
                        at += n
                return carry

            lax.fori_loop(0, 8, one_slot, 0)

        def send(out):
            cp = pltpu.make_async_copy(acc[out], outs[out], sems.at[out])
            cp.start()
            return cp

        def clear(*which_out):
            for out in which_out:
                acc[out][...] = jnp.zeros_like(acc[out])

        clear(2, 6)
        loads[0].wait()
        add(0, held[0])
        copies = [send(out) for out in (2, 6)]
        clear(0, 1, 5)
        loads[1].wait()
        add(1, held[1])
        copies += [send(out) for out in (1, 5)]
        clear(3, 4, 7)
        loads[2].wait()
        add(3, held[3])
        copies += [send(out) for out in (3, 4)]
        loads[3].wait()
        add(2, held[2])
        copies += [send(out) for out in (0, 7)]
        grad_load.wait()
        grad_full[...] = grad_low[...].astype(F32)
        last = pltpu.make_async_copy(grad_full, grad_out, load_sem.at[6])
        last.start()
        rows_load.wait()
        rows_copy = pltpu.make_async_copy(rows_held, rows_out, load_sem.at[7])
        rows_copy.start()
        copies += [last, rows_copy]
        for cp in copies:
            cp.wait()

    hbm = pl.BlockSpec(memory_space=pl.ANY)
    return pl.pallas_call(
        kernel,
        out_shape=outs + [jax.ShapeDtypeStruct(out_rows.shape, BF16), f32(*grad_rows.shape)],
        in_specs=[pl.BlockSpec(memory_space=pltpu.SMEM)] + [hbm] * 6,
        out_specs=[hbm] * 10,
        scratch_shapes=[pltpu.VMEM(o.shape, F32) for o in outs]
        + [pltpu.VMEM(p.shape, BF16) for p in pieces]
        + [pltpu.VMEM(grad_rows.shape, BF16), pltpu.VMEM(grad_rows.shape, F32)]
        + [pltpu.VMEM(out_rows.shape, BF16), _sem(8), _sem(8)],
        compiler_params=pltpu.CompilerParams(vmem_limit_bytes=62 * 1024 * 1024),
        name="tables",
    )(adapters, *pieces, out_rows, grad_rows)


def rope_constants(rows):
    half = HEAD_DIM // 2
    freqs = np.float32(ROPE_BASE) ** (-(np.arange(half, dtype=np.float32) * 2.0 / HEAD_DIM))
    angles = np.arange(rows).astype(np.float32)[:, None] * freqs.astype(np.float32)[None, :]
    cos = np.cos(angles.astype(np.float64)).astype(np.float32)
    sin = np.sin(angles.astype(np.float64)).astype(np.float32)
    gap = np.zeros((rows, HALF_PAD - half), np.float32)
    cosine = np.concatenate([cos, gap, cos, gap], axis=1)
    sine = np.concatenate([-sin, gap, sin, gap], axis=1)
    return jnp.asarray(cosine), jnp.asarray(sine)


def dot(left, right):
    return jnp.dot(left, right, preferred_element_type=F32)


def dot_t(left, right):
    return lax.dot_general(left, right, (((1,), (1,)), ((), ())), preferred_element_type=F32)


def dot_rows(left, right):
    return lax.dot_general(left, right, (((0,), (0,)), ((), ())), preferred_element_type=F32)


def side_pad(value, before=0):
    return jnp.pad(value, ((0, 0), (before, SIDE - before - value.shape[1])))


def blocks(value):
    return value.reshape(2, 2, 2, 128, value.shape[-1])


def own_blocks(value):
    return value.reshape(2, 128, value.shape[-1])


def flat(value):
    return value.reshape(-1, value.shape[-1])


def slot_local(
    tokens,
    cotangent,
    lengths,
    slot_adapter_index,
    attention_norm_gain,
    feedforward_norm_gain,
    query_weight,
    key_weight,
    value_weight,
    output_weight,
    gate_weight,
    up_weight,
    down_weight,
    adapter_input_first,
    adapter_output_first,
    adapter_down_first,
    adapter_query_second,
    adapter_key_value_second,
    adapter_output_second,
    adapter_gate_up_second,
    adapter_down_second,
):
    rows = 4 * 2 * tokens.shape[1]
    cosine, sine = rope_constants(rows)
    turned = lambda t: jnp.swapaxes(t, -1, -2)
    (
        resid,
        normed_two_own,
        inner_o,
        tok_own,
        cot_order,
        _,
        qkv,
        stats,
        attn_b,
        one_cut,
        inner_qkv,
        weight_q,
        weight_kv,
        out_w,
        second_all,
        first_all,
        first_gu,
        second_g,
        second_u,
        first_d,
        second_d,
        first_o,
        second_o,
    ) = front_call(
        tokens,
        cotangent,
        lengths,
        slot_adapter_index,
        (attention_norm_gain, feedforward_norm_gain),
        query_weight,
        turned(key_weight),
        turned(value_weight),
        output_weight,
        (
            turned(adapter_input_first),
            turned(adapter_output_first),
            turned(adapter_down_first),
            adapter_query_second,
            adapter_key_value_second,
            adapter_output_second,
            adapter_gate_up_second,
            adapter_down_second,
        ),
        cosine,
        sine,
        0,
    )
    grad_resid, grad_low_own, small, out_sums, out_far, order, early = feed_forward(
        normed_two_own,
        cot_order,
        resid,
        feedforward_norm_gain,
        lengths,
        (gate_weight, up_weight, down_weight),
        (first_gu, second_g, second_u, first_d, second_d),
        3,
    )
    out_rows, grad_rows, early, middle, late, factors = attend_back_call(
        grad_low_own,
        small,
        early,
        out_far,
        lengths,
        (out_sums, resid, tok_own, grad_resid, attention_norm_gain),
        (
            qkv,
            stats,
            attn_b,
            flat(inner_o),
            order,
            cosine,
            sine,
            out_w,
            first_o,
            second_o,
            weight_q,
            weight_kv,
            second_all,
            first_all,
            second_d,
            one_cut,
            inner_qkv,
            cot_order,
        ),
        10,
    )
    full = table_call((early, middle, late, factors), out_rows, grad_rows, slot_adapter_index)
    turn = lambda t: jnp.swapaxes(t, -1, -2)
    return (
        full[8],
        full[9],
        turn(full[0]),
        turn(full[1]),
        turn(full[2]),
        full[3],
        full[4],
        full[5],
        full[6],
        full[7],
    )


def solution(mesh):
    one_slot = mesh.shape["ctx"] == 8 and mesh.shape["fsdp"] == 4
    return jax.shard_map(
        slot_local if one_slot else local,
        mesh=mesh,
        in_specs=(
            P("fsdp", "ctx", None),
            P("fsdp", "ctx", None),
            P(),
            P(),
            P(),
            P(),
            P(None, "fsdp"),
            P(None, "fsdp"),
            P(None, "fsdp"),
            P("fsdp", None),
            P(None, "fsdp"),
            P(None, "fsdp"),
            P("fsdp", None),
            P(),
            P(),
            P(),
            P(),
            P(),
            P(),
            P(),
            P(),
        ),
        out_specs=(
            P("fsdp", "ctx", None),
            P("fsdp", "ctx", None),
            P(),
            P(),
            P(),
            P(),
            P(),
            P(),
            P(),
            P(),
        ),
        check_vma=False,
    )
```

```python
import math

import jax
import jax.numpy as jnp
import numpy as np
from jax import lax
from jax.experimental import pallas as pl
from jax.experimental.pallas import tpu as pltpu
from jax.sharding import PartitionSpec as P

QUERY_HEADS = 16
KEY_VALUE_HEADS = 8
HEAD_DIM = 96


EPSILON = 1e-05
NEGATIVE = -1e30
ADAPTER_SCALE = 0.5
ROPE_BASE = 100000.0


def from_behind(x, axis, by):
    size = lax.axis_size(axis)
    return lax.ppermute(x, axis, [(i, (i + by) % size) for i in range(size)])


def rope_tables(positions, head_size):
    half_size = head_size // 2
    freqs = ROPE_BASE ** (-(jnp.arange(half_size, dtype=jnp.float32) * 2.0 / head_size))
    angles = positions.astype(jnp.float32)[:, None] * freqs[None, :]
    return (jnp.cos(angles)[:, None, :], jnp.sin(angles)[:, None, :])


def apply_rotation(values, cosine_table, sine_table):
    half_size = values.shape[-1] // 2
    first_half = values[..., :half_size]
    second_half = values[..., half_size:]
    return jnp.concatenate(
        [
            first_half * cosine_table - second_half * sine_table,
            second_half * cosine_table + first_half * sine_table,
        ],
        axis=-1,
    )


def rotate_back(gradient_tree, cosine_table, sine_table):
    half_size = gradient_tree.shape[-1] // 2
    first_half = gradient_tree[..., :half_size]
    second_half = gradient_tree[..., half_size:]
    return jnp.concatenate(
        [
            first_half * cosine_table + second_half * sine_table,
            second_half * cosine_table - first_half * sine_table,
        ],
        axis=-1,
    )


def rms_factor(values):
    return lax.rsqrt(jnp.mean(values * values, axis=-1, keepdims=True) + EPSILON)


def norm_back(values, factor, gain, grad_norm):
    scaled = grad_norm * gain
    return factor * scaled - values * factor**3 * jnp.mean(scaled * values, axis=-1, keepdims=True)


def pick_rows(onehot, table):
    return jnp.einsum("sa,a...->s...", onehot, table, preferred_element_type=jnp.float32).astype(
        jnp.bfloat16
    )


def spread_rows(onehot, gradient_tree):
    return jnp.einsum("sa,s...->a...", onehot, gradient_tree, precision=lax.Precision.HIGHEST)


def direct_product(input_rows, weight_matrix):
    return jnp.einsum("std,do->sto", input_rows, weight_matrix, preferred_element_type=jnp.float32)


def direct_back(gradient_tree, weight_matrix):
    return jnp.einsum(
        "sto,do->std", gradient_tree, weight_matrix, preferred_element_type=jnp.float32
    )


def inner_product_part(input_rows, down):
    return jnp.einsum("std,sdr->str", input_rows, down, preferred_element_type=jnp.float32)


def inner_back(gradient_tree, upward_rows):
    return ADAPTER_SCALE * jnp.einsum(
        "sto,sro->str", gradient_tree, upward_rows, preferred_element_type=jnp.float32
    )


def through_down(grad_inner, down):
    return jnp.einsum("str,sdr->std", grad_inner, down, preferred_element_type=jnp.float32)


def down_grad(input_rows, grad_inner):
    return jnp.einsum("std,str->sdr", input_rows, grad_inner, preferred_element_type=jnp.float32)


def upward_grad(inner_rows, gradient_tree):
    return ADAPTER_SCALE * jnp.einsum(
        "jvp,jvx->jpx", inner_rows, gradient_tree, preferred_element_type=jnp.float32
    )


def upward_apply(inner_rows, upward_rows):
    return ADAPTER_SCALE * jnp.einsum(
        "str,sro->sto", inner_rows, upward_rows, preferred_element_type=jnp.float32
    )


def project(input_rows, weight_matrix, down, upward_rows):
    inner_rows = inner_product_part(input_rows, down).astype(jnp.bfloat16)
    return (
        inner_rows,
        direct_product(input_rows, weight_matrix) + upward_apply(inner_rows, upward_rows),
    )


def project_back(input_rows, grad_output, weight_matrix, down, upward_rows, inner_rows):
    grad_upward = upward_grad(inner_rows, grad_output)
    grad_inner = inner_back(grad_output, upward_rows).astype(jnp.bfloat16)
    grad_down = down_grad(input_rows, grad_inner)
    grad_inputs = direct_back(grad_output, weight_matrix) + through_down(grad_inner, down)
    return (grad_inputs, grad_down, grad_upward)


def allowed_mask(key_start, key_count, query_pos, lengths):
    key_pos = key_start + jnp.arange(key_count, dtype=jnp.int32)
    causal = key_pos[None, :] <= query_pos[:, None]
    live = key_pos[None, :] < lengths[:, None]
    return (causal[None, :, :] & live[:, None, :])[:, None, None, :, :]


def attend_block(state, key_block, value_block, key_start, query_head_rows, query_pos, lengths):
    run_max, run_sum, run_acc = state
    scale = query_head_rows.shape[-1] ** (-0.5)
    scores = (
        jnp.einsum(
            "sqhgd,skhd->shgqk", query_head_rows, key_block, preferred_element_type=jnp.float32
        )
        * scale
    )
    allowed = allowed_mask(key_start, key_block.shape[1], query_pos, lengths)
    new_max = jnp.maximum(run_max, jnp.max(jnp.where(allowed, scores, NEGATIVE), axis=-1))
    weights = jnp.where(allowed, jnp.exp(scores - new_max[..., None]), 0.0)
    factor = jnp.exp(run_max - new_max)
    new_sum = run_sum * factor + jnp.sum(weights, axis=-1)
    update = jnp.einsum(
        "shgqk,skhd->shgqd",
        weights.astype(jnp.bfloat16),
        value_block,
        preferred_element_type=jnp.float32,
    )
    return (new_max, new_sum, run_acc * factor[..., None] + update)


def attend_back(
    key_block,
    value_block,
    key_start,
    query_head_rows,
    grad_heads,
    log_total,
    row_dot,
    query_pos,
    lengths,
):
    scale = query_head_rows.shape[-1] ** (-0.5)
    scores = (
        jnp.einsum(
            "sqhgd,skhd->shgqk", query_head_rows, key_block, preferred_element_type=jnp.float32
        )
        * scale
    )
    allowed = allowed_mask(key_start, key_block.shape[1], query_pos, lengths)
    probs = jnp.where(allowed, jnp.exp(scores - log_total[..., None]), 0.0)
    grad_probs = jnp.einsum(
        "sqhgd,skhd->shgqk", grad_heads, value_block, preferred_element_type=jnp.float32
    )
    grad_scores = (probs * (grad_probs - row_dot[..., None])).astype(jnp.bfloat16)
    grad_query = scale * jnp.einsum(
        "shgqk,skhd->sqhgd", grad_scores, key_block, preferred_element_type=jnp.float32
    )
    grad_key = scale * jnp.einsum(
        "shgqk,sqhgd->skhd", grad_scores, query_head_rows, preferred_element_type=jnp.float32
    )
    grad_value = jnp.einsum(
        "shgqk,sqhgd->skhd",
        probs.astype(jnp.bfloat16),
        grad_heads,
        preferred_element_type=jnp.float32,
    )
    return (grad_query, grad_key, grad_value)


def attend_forward(query_head_rows, key_head_rows, value_head_rows, lengths_used, query_pos):
    slots, rows, kv_heads, group_size, head_size = query_head_rows.shape
    key_flat = key_head_rows.reshape(slots, rows, kv_heads * head_size)
    value_flat = value_head_rows.reshape(slots, rows, kv_heads * head_size)
    stat_shape = (slots, kv_heads, group_size, rows)
    initial = (
        jnp.full(stat_shape, NEGATIVE, jnp.float32),
        jnp.zeros(stat_shape, jnp.float32),
        jnp.zeros(stat_shape + (head_size,), jnp.float32),
    )
    part_keys = lax.all_gather(key_flat, "ctx", axis=1, tiled=True)
    part_values = lax.all_gather(value_flat, "ctx", axis=1, tiled=True)
    piece_rows = part_keys.shape[1]
    part_keys = part_keys.reshape(slots, piece_rows, kv_heads, head_size)
    part_values = part_values.reshape(slots, piece_rows, kv_heads, head_size)
    span_rows = math.gcd(piece_rows, 4 * rows)

    def inner_step(block_index, inner_state):
        sub_keys = lax.dynamic_slice_in_dim(part_keys, block_index * span_rows, span_rows, 1)
        sub_values = lax.dynamic_slice_in_dim(part_values, block_index * span_rows, span_rows, 1)
        return attend_block(
            inner_state,
            sub_keys,
            sub_values,
            block_index * span_rows,
            query_head_rows,
            query_pos,
            lengths_used,
        )

    run_max, run_sum, run_acc = lax.fori_loop(0, piece_rows // span_rows, inner_step, initial)
    log_total = run_max + jnp.log(run_sum)
    attended = jnp.transpose(run_acc / run_sum[..., None], (0, 3, 1, 2, 4))
    return (attended, log_total)


def attend_backward(
    query_head_rows,
    key_head_rows,
    value_head_rows,
    grad_heads,
    attended,
    log_total,
    lengths_used,
    query_pos,
):
    ctx_count = lax.axis_size("ctx")
    own_index = lax.axis_index("ctx")
    rows = query_head_rows.shape[1]
    row_dot = jnp.transpose(
        jnp.sum(grad_heads.astype(jnp.float32) * attended, axis=-1), (0, 2, 3, 1)
    )

    def cycle_step(step_index, carried):
        carried_keys, carried_values, grad_query, grad_key, grad_value = carried
        block_id = (own_index + step_index) % ctx_count
        query_part, key_part, value_part = attend_back(
            carried_keys,
            carried_values,
            block_id * rows,
            query_head_rows,
            grad_heads,
            log_total,
            row_dot,
            query_pos,
            lengths_used,
        )
        grad_key, grad_value = (
            from_behind((grad_key + key_part).astype(jnp.bfloat16), "ctx", -1).astype(jnp.float32),
            from_behind((grad_value + value_part).astype(jnp.bfloat16), "ctx", -1).astype(
                jnp.float32
            ),
        )
        carried_keys, carried_values = from_behind((carried_keys, carried_values), "ctx", -1)
        return (carried_keys, carried_values, grad_query + query_part, grad_key, grad_value)

    key_zeros = jnp.zeros(key_head_rows.shape, jnp.float32)
    start_state = (
        key_head_rows,
        value_head_rows,
        jnp.zeros(query_head_rows.shape, jnp.float32),
        key_zeros,
        key_zeros,
    )
    carried = lax.fori_loop(0, ctx_count, cycle_step, start_state)
    return (carried[2], carried[3], carried[4])


def table_total(rotation_tables):
    return lax.psum(rotation_tables, ("ctx", "fsdp"))


def local(
    tokens,
    cotangent,
    lengths,
    slot_adapter_index,
    attention_norm_gain,
    feedforward_norm_gain,
    query_weight,
    key_weight,
    value_weight,
    output_weight,
    gate_weight,
    up_weight,
    down_weight,
    adapter_input_first,
    adapter_output_first,
    adapter_down_first,
    adapter_query_second,
    adapter_key_value_second,
    adapter_output_second,
    adapter_gate_up_second,
    adapter_down_second,
):
    slot_count, tok_rows, model_width = tokens.shape
    head_groups = QUERY_HEADS // KEY_VALUE_HEADS
    own_index = lax.axis_index("ctx")
    fsdp_index = lax.axis_index("fsdp")
    query_pos = own_index * tok_rows + jnp.arange(tok_rows, dtype=jnp.int32)
    cosine_table, sine_table = rope_tables(query_pos, HEAD_DIM)
    own_lengths = lax.dynamic_slice_in_dim(lengths, fsdp_index * slot_count, slot_count, 0)
    own_adapters = lax.dynamic_slice_in_dim(
        slot_adapter_index, fsdp_index * slot_count, slot_count, 0
    )
    valid = query_pos[None, :] < own_lengths[:, None]
    adapter_labels = jnp.arange(adapter_input_first.shape[0], dtype=jnp.int32)
    onehot_own = own_adapters[:, None] == adapter_labels[None, :]
    owned_low_rank = onehot_own.astype(jnp.bfloat16)
    own_full = onehot_own.astype(jnp.float32)
    tokens_f = tokens.astype(jnp.float32)
    factor_one = rms_factor(tokens_f)
    normed_one = (tokens_f * factor_one * attention_norm_gain).astype(jnp.bfloat16)
    grad_out = jnp.where(valid[..., None], cotangent, jnp.zeros((), jnp.bfloat16))
    input_first = pick_rows(owned_low_rank, adapter_input_first)
    output_second = pick_rows(owned_low_rank, adapter_output_second)
    down_second = pick_rows(owned_low_rank, adapter_down_second)
    output_first = pick_rows(owned_low_rank, adapter_output_first)
    down_first = pick_rows(owned_low_rank, adapter_down_first)
    query_second = pick_rows(owned_low_rank, adapter_query_second)
    key_value_second = pick_rows(owned_low_rank, adapter_key_value_second)
    gate_up_second = pick_rows(owned_low_rank, adapter_gate_up_second)
    weight_q, weight_k, weight_v, weight_gate, weight_up, weight_o, weight_down = (
        lax.all_gather(query_weight, "fsdp", axis=1, tiled=True),
        lax.all_gather(key_weight, "fsdp", axis=1, tiled=True),
        lax.all_gather(value_weight, "fsdp", axis=1, tiled=True),
        lax.all_gather(gate_weight, "fsdp", axis=1, tiled=True),
        lax.all_gather(up_weight, "fsdp", axis=1, tiled=True),
        lax.all_gather(output_weight, "fsdp", axis=0, tiled=True),
        lax.all_gather(down_weight, "fsdp", axis=0, tiled=True),
    )
    inner_q, projected_queries = project(normed_one, weight_q, input_first[:, 0], query_second)
    inner_k, projected_keys = project(
        normed_one, weight_k, input_first[:, 1], key_value_second[:, 0]
    )
    inner_v, projected_values = project(
        normed_one, weight_v, input_first[:, 2], key_value_second[:, 1]
    )
    query_head_rows = apply_rotation(
        projected_queries.reshape(slot_count, tok_rows, -1, HEAD_DIM), cosine_table, sine_table
    ).astype(jnp.bfloat16)
    query_head_rows = query_head_rows.reshape(slot_count, tok_rows, -1, head_groups, HEAD_DIM)
    key_head_rows = apply_rotation(
        projected_keys.reshape(slot_count, tok_rows, -1, HEAD_DIM), cosine_table, sine_table
    ).astype(jnp.bfloat16)
    value_head_rows = projected_values.astype(jnp.bfloat16).reshape(
        slot_count, tok_rows, -1, HEAD_DIM
    )
    attended, log_total = attend_forward(
        query_head_rows, key_head_rows, value_head_rows, own_lengths, query_pos
    )
    attn_b = attended.reshape(slot_count, tok_rows, -1).astype(jnp.bfloat16)
    inner_o, proj_o = project(attn_b, weight_o, output_first, output_second)
    resid = tokens_f + proj_o
    factor_two = rms_factor(resid)
    normed_two = (resid * factor_two * feedforward_norm_gain).astype(jnp.bfloat16)
    inner_gate, gate = project(normed_two, weight_gate, input_first[:, 3], gate_up_second[:, 0])
    inner_up, up_proj = project(normed_two, weight_up, input_first[:, 4], gate_up_second[:, 1])
    sigmoid_gate = jax.nn.sigmoid(gate)
    hidden = (gate * sigmoid_gate * up_proj).astype(jnp.bfloat16)
    inner_down, proj_down = project(hidden, weight_down, down_first, down_second)
    out_tokens = jnp.where(valid[..., None], resid + proj_down, 0.0).astype(jnp.bfloat16)
    grad_hidden, grad_da, grad_db = project_back(
        hidden, grad_out, weight_down, down_first, down_second, inner_down
    )
    grad_gate = (grad_hidden * up_proj * sigmoid_gate * (1.0 + gate * (1.0 - sigmoid_gate))).astype(
        jnp.bfloat16
    )
    grad_up = (grad_hidden * gate * sigmoid_gate).astype(jnp.bfloat16)
    from_gate, grad_ga, grad_gb = project_back(
        normed_two, grad_gate, weight_gate, input_first[:, 3], gate_up_second[:, 0], inner_gate
    )
    from_up, grad_ua, grad_ub = project_back(
        normed_two, grad_up, weight_up, input_first[:, 4], gate_up_second[:, 1], inner_up
    )
    grad_normed_two = (from_gate + from_up).astype(jnp.bfloat16).astype(jnp.float32)
    grad_resid = grad_out.astype(jnp.float32) + norm_back(
        resid, factor_two, feedforward_norm_gain, grad_normed_two
    )
    grad_resid_low = grad_resid.astype(jnp.bfloat16)
    from_attn, grad_oa, grad_ob = project_back(
        attn_b, grad_resid_low, weight_o, output_first, output_second, inner_o
    )
    grad_heads = from_attn.astype(jnp.bfloat16).reshape(attended.shape)
    grad_query, grad_key, grad_value = attend_backward(
        query_head_rows,
        key_head_rows,
        value_head_rows,
        grad_heads,
        attended,
        log_total,
        own_lengths,
        query_pos,
    )
    grad_proj_q = (
        rotate_back(
            grad_query.reshape(slot_count, tok_rows, -1, HEAD_DIM), cosine_table, sine_table
        )
        .astype(jnp.bfloat16)
        .reshape(slot_count, tok_rows, -1)
    )
    grad_proj_k = (
        rotate_back(grad_key, cosine_table, sine_table)
        .astype(jnp.bfloat16)
        .reshape(slot_count, tok_rows, -1)
    )
    grad_proj_v = grad_value.astype(jnp.bfloat16).reshape(slot_count, tok_rows, -1)
    from_query, grad_qa, grad_qb = project_back(
        normed_one, grad_proj_q, weight_q, input_first[:, 0], query_second, inner_q
    )
    from_key, grad_ka, grad_kb = project_back(
        normed_one, grad_proj_k, weight_k, input_first[:, 1], key_value_second[:, 0], inner_k
    )
    from_value, grad_va, grad_vb = project_back(
        normed_one, grad_proj_v, weight_v, input_first[:, 2], key_value_second[:, 1], inner_v
    )
    grad_normed_one = (from_query + from_key + from_value).astype(jnp.bfloat16).astype(jnp.float32)
    grad_tokens = grad_resid + norm_back(tokens_f, factor_one, attention_norm_gain, grad_normed_one)
    slot_grads = (
        jnp.stack([grad_qa, grad_ka, grad_va, grad_ga, grad_ua], axis=1),
        grad_oa,
        grad_da,
        grad_qb,
        jnp.stack([grad_kb, grad_vb], axis=1),
        grad_ob,
        jnp.stack([grad_gb, grad_ub], axis=1),
        grad_db,
    )
    summed = table_total(tuple((spread_rows(own_full, entry_item) for entry_item in slot_grads)))
    return (
        out_tokens,
        grad_tokens,
        summed[0],
        summed[1],
        summed[2],
        summed[3],
        summed[4],
        summed[5],
        summed[6],
        summed[7],
    )


BF16 = jnp.bfloat16
F32 = jnp.float32
MESH_ID = pl.DeviceIdType.MESH
RANK = 16
SIDE = 128
PAD_HEAD = 128
HALF_PAD = 64


def _sem(count):
    return pltpu.SemaphoreType.DMA((count,))


def _place():
    c = lax.axis_index("ctx")
    f = lax.axis_index("fsdp")
    x = f // 2
    core = f % 2
    return c, f, x, core, (c, 2 * x + 1 - core), (c, 2 * (1 - x) + core)


def _slot_of(c):
    return c // 2 + 4 * ((c // 2 + c) % 2)


def _group_of(slot):
    return 2 * (slot % 4) + (slot // 4 + slot) % 2


def _block(x, core, j):
    return 4 * (1 - core) + 2 * j + (x + j) % 2


def _owner(b):
    return 2 * ((b // 2 + b) % 2) + 1 - b // 4


def _greet(targets):
    barrier = pltpu.get_barrier_semaphore()
    for target in targets:
        pl.semaphore_signal(barrier, inc=1, device_id=target, device_id_type=MESH_ID)
    pl.semaphore_wait(barrier, len(targets))


def _remote(src, dst, send, recv, target):
    return pltpu.make_async_remote_copy(
        src_ref=src, dst_ref=dst, send_sem=send, recv_sem=recv, device_id=target, device_id_type=MESH_ID
    )


def _comm_call(kernel, ins, outs, scratch, cid, name, in_space=pl.ANY, out_space=pl.ANY, vmem=None):
    return pl.pallas_call(
        kernel,
        out_shape=outs,
        in_specs=[pl.BlockSpec(memory_space=in_space)] * len(ins),
        out_specs=jax.tree.map(lambda _: pl.BlockSpec(memory_space=out_space), outs),
        scratch_shapes=scratch,
        compiler_params=pltpu.CompilerParams(
            collective_id=cid, has_side_effects=True, vmem_limit_bytes=vmem
        ),
        name=name,
    )(*ins)


def _gather_steps(ins, outs, own_sem, send_sem, recv_sem, place):
    c, f, x, core, core_peer, x_peer = place
    h = 1 - core
    count = len(ins)
    local = []
    sends = []

    def first():
        for base, target in ((0, x_peer), (2 * count, core_peer)):
            for i in range(count):
                for j in range(2):
                    k = base + i * 2 + j
                    cp = _remote(
                        ins[i].at[j], outs[i].at[h, j, (x + j) % 2], send_sem.at[k], recv_sem.at[k], target
                    )
                    cp.start()
                    sends.append(cp)
        for i in range(count):
            for j in range(2):
                lc = pltpu.make_async_copy(
                    ins[i].at[j], outs[i].at[h, j, (x + j) % 2], own_sem.at[i * 2 + j]
                )
                lc.start()
                local.append(lc)

    def last():
        forwards = []
        for i in range(count):
            for j in range(2):
                k = i * 2 + j
                sends[k].wait_recv()
                cp = _remote(
                    outs[i].at[h, j, (x + j + 1) % 2],
                    outs[i].at[h, j, (x + j + 1) % 2],
                    send_sem.at[4 * count + k],
                    recv_sem.at[4 * count + k],
                    core_peer,
                )
                cp.start()
                forwards.append(cp)
        for k in range(2 * count):
            sends[2 * count + k].wait_recv()
            forwards[k].wait_recv()
        for cp in sends + forwards:
            cp.wait_send()
        for lc in local:
            lc.wait()

    return first, last


def _ctx_first(piece, lines, own_sem, send_sem, recv_sem, place):
    c, f, x, core, core_peer, x_peer = place
    z, y = c // 2, c % 2
    sends = []
    local = []

    def start():
        lc = pltpu.make_async_copy(piece, lines.at[z, x], own_sem)
        lc.start()
        local.append(lc)
        cp = _remote(piece, lines.at[z, x], send_sem.at[0], recv_sem.at[0], x_peer)
        cp.start()
        sends.append(cp)

    def spread():
        local[0].wait()
        sends[0].wait_recv()
        for step in range(1, 4):
            cp = _remote(
                lines.at[z],
                lines.at[z],
                send_sem.at[step],
                recv_sem.at[step],
                (2 * ((z + step) % 4) + y, f),
            )
            cp.start()
            sends.append(cp)

    def finish():
        for cp in sends[1:]:
            cp.wait_recv()
        for cp in sends:
            cp.wait_send()

    return start, spread, finish


def _ctx_second(lines, out, own_sem, send_sem, recv_sem, place):
    c, f, x, core, core_peer, x_peer = place
    z, y = c // 2, c % 2
    y_peer = (2 * z + 1 - y, f)
    sends = []
    local = []

    def start():
        lc = pltpu.make_async_copy(lines, out.at[y, core], own_sem)
        lc.start()
        local.append(lc)
        for k, target in ((0, y_peer), (1, core_peer)):
            cp = _remote(lines, out.at[y, core], send_sem.at[k], recv_sem.at[k], target)
            cp.start()
            sends.append(cp)

    def share():
        sends[0].wait_recv()
        cp = _remote(
            out.at[1 - y, core], out.at[1 - y, core], send_sem.at[2], recv_sem.at[2], core_peer
        )
        cp.start()
        sends.append(cp)

    def finish():
        sends[1].wait_recv()
        sends[2].wait_recv()
        for cp in sends:
            cp.wait_send()
        local[0].wait()

    return start, share, finish


def _ctx_planes(piece, out, own_sem, send_sem, recv_sem, place):
    c, f, x, core, core_peer, x_peer = place
    z, y = c // 2, c % 2
    y_peer = (2 * z + 1 - y, f)
    sends = {}
    local = []

    def send(k, src, dst, target):
        cp = _remote(src, dst, send_sem.at[k], recv_sem.at[k], target)
        cp.start()
        sends[k] = cp

    def spot(yy, zz):
        return out.at[yy, core, zz, x]

    def start():
        lc = pltpu.make_async_copy(piece, spot(y, z), own_sem)
        lc.start()
        local.append(lc)
        for step in range(1, 4):
            send(step, piece, spot(y, z), (2 * ((z + step) % 4) + y, f))
        send(4, piece, spot(y, z), y_peer)
        send(8, piece, spot(y, z), x_peer)

    def forward():
        for step in range(1, 4):
            sends[step].wait_recv()
            at = spot(y, (z + 4 - step) % 4)
            send(4 + step, at, at, y_peer)
            send(8 + step, at, at, x_peer)
        for step in range(4):
            sends[4 + step].wait_recv()
            at = spot(1 - y, (z + 4 - step) % 4)
            send(12 + step, at, at, x_peer)

    def finish():
        local[0].wait()
        for half in range(2):
            for step in range(4):
                sends[8 + 4 * half + step].wait_recv()
            yy = 1 - y if half else y
            send(16 + half, out.at[yy, core], out.at[yy, core], core_peer)
        for half in range(2):
            sends[16 + half].wait_recv()
        for cp in sends.values():
            cp.wait_send()

    return start, forward, finish


def _z_peers(place):
    c, f = place[:2]
    return [(2 * ((c // 2 + step) % 4) + c % 2, f) for step in range(1, 4)]


def _y_peer(place):
    c, f = place[:2]
    return (2 * (c // 2) + 1 - c % 2, f)


def _lines_of(n):
    return (4, 2, RANK, n)


def _spread_of(n):
    return jax.ShapeDtypeStruct((2, 2, 4, 2, RANK, n), BF16)


FIRST_SEMS = [pltpu.SemaphoreType.DMA(()), _sem(4), _sem(4)]
SECOND_SEMS = [pltpu.SemaphoreType.DMA(()), _sem(3), _sem(3)]
PLANE_SEMS = [pltpu.SemaphoreType.DMA(()), _sem(18), _sem(18)]


def _order_steps(own, order, own_sem, send_sem, recv_sem, place):
    core_peer, x_peer = place[4:]
    sends, local, forwards = [], [], []

    def first():
        for j in range(2):
            cp = _remote(own.at[j], order.at[1 + j, 1], send_sem.at[j], recv_sem.at[j], x_peer)
            cp.start()
            sends.append(cp)
        for j in range(2):
            cp = _remote(
                own.at[j], order.at[3, j], send_sem.at[2 + j], recv_sem.at[2 + j], core_peer
            )
            cp.start()
            sends.append(cp)
        for j in range(2):
            lc = pltpu.make_async_copy(own.at[j], order.at[0, j], own_sem.at[j])
            lc.start()
            local.append(lc)

    def forward(j):
        sends[j].wait_recv()
        cp = _remote(
            order.at[1 + j, 1],
            order.at[1 + j, 0],
            send_sem.at[4 + j],
            recv_sem.at[4 + j],
            core_peer,
        )
        cp.start()
        forwards.append(cp)

    def own_here():
        for lc in local:
            lc.wait()

    def core_here():
        for j in range(2):
            sends[2 + j].wait_recv()

    def far_here(j):
        forwards[j].wait_recv()

    def last():
        for cp in sends + forwards:
            cp.wait_send()

    return first, forward, own_here, core_here, far_here, last


def _order_all(own, order, sems, place):
    first, forward, own_here, core_here, far_here, last = _order_steps(own, order, *sems, place)
    first()
    own_here()
    for j in range(2):
        forward(j)
    core_here()
    for j in range(2):
        far_here(j)
    last()


def feed_forward(own, cot, resid, gain, length, weights, adapters, cid):
    gate_w, up_w, down_w = weights
    width, units = gate_w.shape
    wide = width + SIDE
    tile = 256

    loads_in = tuple(weights) + tuple(adapters) + (cot,)
    count = len(loads_in)

    def kernel(*refs):
        len_ref, own_ref, resid_ref, gain_ref = refs[:4]
        loads_hbm = refs[4 : 4 + count]
        outs_hbm = refs[4 + count : 11 + count]
        mirrors = refs[len(refs) - 8 : len(refs) - 1]
        grad_resid, grad_low, small, out_own, out_far, order, early = mirrors
        flush_sem = refs[len(refs) - 1]
        refs = refs[11 + count : len(refs) - 8]
        flushed = []

        def flush(*places):
            for at in places:
                cp = pltpu.make_async_copy(mirrors[at], outs_hbm[at], flush_sem.at[at])
                cp.start()
                flushed.append(cp)

        gate_ref, up_ref, down_ref, first_ref, sg_ref, su_ref, fd_ref, sd_ref, go_ref = refs[:count]
        (
            sums,
            hid_s,
            gg_s,
            gu_s,
            in_s,
            gid_s,
            part,
            out_part,
            near,
            out_near,
            far,
            out_land,
            staged,
            landed,
            load_sem,
            send_sem,
            recv_sem,
            s_sem,
            r_sem,
        ) = refs[count:]
        place = _place()
        core_peer, x_peer = place[4:]
        loads = []
        for i in range(count):
            cp = pltpu.make_async_copy(loads_hbm[i], refs[i], load_sem.at[i])
            cp.start()
            loads.append(cp)
        _greet([core_peer, x_peer])
        c, f, x, core = place[:4]
        live = len_ref[_slot_of(c)]

        def masked(step, middle):
            other_x = x + middle * (1 - 2 * x)
            pieces = []
            for i in range(2):
                other_core = core + (step // 3 + middle * (1 - i)) * (1 - 2 * core)
                j = (1 - middle) * i + middle * (step - 1)
                pos = 128 * _block(other_x, other_core, j) + lax.broadcasted_iota(
                    jnp.int32, (128, width), 0
                )
                pieces.append(jnp.where(pos < live, go_ref[step, i].astype(F32), 0.0).astype(BF16))
            return pieces

        def work(step, middle):
            rows = order[step].reshape(2 * 128, width)
            pieces = masked(step, middle)
            for k in range(2):
                go_ref[step, k] = pieces[k]
            go = go_ref[step].reshape(2 * 128, width)
            inner = dot_t(rows, first_ref[...]).astype(BF16)
            gid = dot_t(go, sd_ref[...]).astype(BF16)
            in_s[step] = inner
            gid_s[step] = gid
            for at in range(0, units, tile):
                cols = slice(at, at + tile)
                gate = dot(rows, gate_ref[:, cols]) + dot(inner, sg_ref[:, cols])
                up = dot(rows, up_ref[:, cols]) + dot(inner, su_ref[:, cols])
                grad = dot_t(go, down_ref[cols, :]) + dot(gid, fd_ref[:, cols])
                sig = 0.5 * jnp.tanh(0.5 * gate) + 0.5
                silu = gate * sig
                hid_s[step, :, cols] = (silu * up).astype(BF16)
                gg_s[step, :, cols] = (grad * up * sig * (1.0 + gate * (1.0 - sig))).astype(BF16)
                gu_s[step, :, cols] = (grad * silu).astype(BF16)
            gg, gu = gg_s[step], gu_s[step]
            for at in range(0, width, tile):
                cols = slice(at, at + tile)
                value = dot_t(gg, gate_ref[cols, :]) + dot_t(gu, up_ref[cols, :])
                part[step, :, :, cols] = value.astype(BF16).reshape(2, 128, tile)
            value = dot_t(gg, sg_ref[...]) + dot_t(gu, su_ref[...])
            part[step, :, :, width:] = value.astype(BF16).reshape(2, 128, SIDE)

        def down(step):
            hid = hid_s[step]
            for at in range(0, width, tile):
                cols = slice(at, at + tile)
                out = dot(hid, down_ref[:, cols])
                out_part[step, :, :, cols] = out.astype(BF16).reshape(2, 128, tile)
            out = dot_t(hid, fd_ref[...])
            out_part[step, :, :, width:] = out.astype(BF16).reshape(2, 128, SIDE)

        def sent(src, dst, n, target):
            return _remote(src, dst, s_sem.at[n], r_sem.at[n], target)

        def from_x(j):
            return _remote(own_ref.at[j], order.at[1 + j, 1], send_sem.at[j], recv_sem.at[j], x_peer)

        def from_core(j):
            return _remote(
                own_ref.at[j], order.at[3, j], send_sem.at[2 + j], recv_sem.at[2 + j], core_peer
            )

        def from_far(j):
            return _remote(
                order.at[1 + j, 1],
                order.at[1 + j, 0],
                send_sem.at[4 + j],
                recv_sem.at[4 + j],
                core_peer,
            )

        def far_sum(j):
            return sent(part.at[1 + j, 0], far.at[j], 2 + j, core_peer)

        def far_out(j):
            return sent(out_part.at[1 + j, 0], out_land.at[j], 4 + j, core_peer)

        def near_sum():
            return sent(part.at[3], near, 0, core_peer)

        def near_out():
            return sent(out_part.at[3], out_near, 1, core_peer)

        def across(j):
            return sent(staged.at[j], landed.at[j], 6 + j, x_peer)

        for j in range(2):
            from_x(j).start()
        for j in range(2):
            from_core(j).start()
        for j in range(2):
            order[0, j] = own_ref[j]
        for cp in loads:
            cp.wait()

        def one_step(step, carry):
            middle = ((step + 1) // 2) % 2

            @pl.when(middle == 1)
            def _():
                j = step - 1
                from_x(j).wait_recv()
                from_far(j).start()
                from_far(j).wait_recv()

            @pl.when(step == 3)
            def _():
                for j in range(2):
                    from_core(j).wait_recv()

            work(step, middle)

            @pl.when(middle == 1)
            def _():
                far_sum(step - 1).start()

            @pl.when(step == 3)
            def _():
                near_sum().start()

            down(step)

            @pl.when(middle == 1)
            def _():
                j = step - 1
                far_out(j).start()
                far_sum(j).wait_recv()
                staged[j] = (part[1 + j, 1].astype(F32) + far[j].astype(F32)).astype(BF16)
                across(j).start()

            @pl.when(step == 3)
            def _():
                near_out().start()

            return carry

        lax.fori_loop(0, 4, one_step, 0)
        flush(5)
        for j in range(2):
            far_out(j).wait_recv()
            out_far[j] = (out_part[1 + j, 1].astype(F32) + out_land[j].astype(F32)).astype(BF16)
        near_sum().wait_recv()
        near_out().wait_recv()
        sums[...] = part[0].astype(F32) + near[...].astype(F32)
        out_own[...] = out_part[0].astype(F32) + out_near[...].astype(F32)
        for at in range(0, units, 512):
            cols = slice(at, at + 512)
            g = jnp.zeros((SIDE, 512), F32)
            u = jnp.zeros((SIDE, 512), F32)
            d = jnp.zeros((SIDE, 512), F32)
            for step in range(4):
                g += dot_rows(in_s[step], gg_s[step, :, cols])
                u += dot_rows(in_s[step], gu_s[step, :, cols])
                d += dot_rows(gid_s[step], hid_s[step, :, cols])
            early[:, at : at + 512] = (ADAPTER_SCALE * g[:RANK]).astype(BF16)
            early[:, units + at : units + at + 512] = (ADAPTER_SCALE * u[RANK : 2 * RANK]).astype(BF16)
            early[:, 2 * units + at : 2 * units + at + 512] = d[3 * RANK : 4 * RANK].astype(BF16)
        flush(3, 4, 6)
        for j in range(2):
            across(j).wait_recv()
            total = sums[j] + landed[j].astype(F32)
            gi = total[:, width:].astype(BF16)
            small[j] = gi
            gn = (total[:, :width] + dot(gi, first_ref[...])).astype(BF16).astype(F32)
            v = resid_ref[j]
            factor = lax.rsqrt(jnp.mean(v * v, axis=1, keepdims=True) + EPSILON)
            scaled = gn * gain_ref[...].reshape(1, width)
            mean = jnp.mean(scaled * v, axis=1, keepdims=True)
            grad = go_ref[0, j].astype(F32) + factor * scaled - v * (factor * factor * factor) * mean
            grad_resid[j] = grad
            grad_low[j] = grad.astype(BF16)
        flush(0, 1, 2)
        for j in range(2):
            for cp in (from_x(j), from_core(j), from_far(j), far_sum(j), far_out(j), across(j)):
                cp.wait_send()
        near_sum().wait_send()
        near_out().wait_send()
        for cp in flushed:
            cp.wait()

    vmem = pl.BlockSpec(memory_space=pltpu.VMEM)
    rows = (2, 128, wide)
    f32 = lambda *shape: jax.ShapeDtypeStruct(shape, F32)
    outs = [
        f32(2, 128, width),
        jax.ShapeDtypeStruct((2, 128, width), BF16),
        jax.ShapeDtypeStruct((2, 128, SIDE), BF16),
        f32(*rows),
        jax.ShapeDtypeStruct(rows, BF16),
        jax.ShapeDtypeStruct((4, 2, 128, width), BF16),
        jax.ShapeDtypeStruct((RANK, 3 * units), BF16),
    ]
    hbm = pl.BlockSpec(memory_space=pl.ANY)
    return pl.pallas_call(
        kernel,
        out_shape=outs,
        in_specs=[pl.BlockSpec(memory_space=pltpu.SMEM), vmem, vmem, vmem] + [hbm] * count,
        out_specs=[hbm] * len(outs),
        scratch_shapes=[pltpu.VMEM(a.shape, a.dtype) for a in loads_in]
        + [pltpu.VMEM(rows, F32)]
        + [pltpu.VMEM((4, 256, units), BF16)] * 3
        + [pltpu.VMEM((4, 256, SIDE), BF16)] * 2
        + [pltpu.VMEM((4,) + rows, BF16)] * 2
        + [pltpu.VMEM(rows, BF16)] * 6
        + [_sem(count), _sem(6), _sem(6), _sem(8), _sem(8)]
        + [pltpu.VMEM(o.shape, o.dtype) for o in outs]
        + [_sem(len(outs))],
        compiler_params=pltpu.CompilerParams(
            collective_id=cid, has_side_effects=True, vmem_limit_bytes=58 * 1024 * 1024
        ),
        name="feed_forward",
    )(length, own, resid, gain, *loads_in)


def _back_steps(src, dst, out_s, out_r, place):
    c, f, x, core = place[:4]
    slot = _slot_of(c)
    place_in = slot % 2

    def move(j):
        return _remote(
            src.at[j],
            dst.at[place_in],
            out_s.at[j],
            out_r.at[place_in],
            (_block(x, core, j), slot // 2),
        )

    def first(j):
        move(j).start()

    def last():
        for half in range(2):
            pltpu.make_async_copy(dst.at[half], dst.at[half], out_r.at[half]).wait()
        for j in range(2):
            move(j).wait_send()

    return first, last


def _back_sources(place):
    c, f = place[:2]
    return [(_group_of(2 * f + half), _owner(c)) for half in range(2)]


def front_call(
    tokens,
    cotangent,
    lengths,
    adapters,
    gains,
    wq,
    wk,
    wv,
    wo,
    tables,
    cosine,
    sine,
    cid,
):
    width = tokens.shape[-1]
    rows = cosine.shape[0]
    wide = width + SIDE
    block = 256
    scale = HEAD_DIM ** (-0.5)
    lane = PAD_HEAD
    units = tables[6].shape[-1] // 4
    quarter = width // 4
    loads_in = gains + (wq, wk, wv, wo) + tables + (cosine, sine)
    count = len(loads_in)

    vmem, hbm = pl.BlockSpec(memory_space=pltpu.VMEM), pl.BlockSpec(memory_space=pl.ANY)
    smem = pl.BlockSpec(memory_space=pltpu.SMEM)
    low = lambda *shape: jax.ShapeDtypeStruct(shape, BF16)
    outs = [
        (jax.ShapeDtypeStruct((2, 128, width), F32), vmem),
        (low(2, 128, width), vmem),
        (low(2, 2, 2, 128, SIDE), hbm),
        (low(2, 128, width), vmem),
        (low(4, 2, 128, width), hbm),
        (low(2, 128, width), hbm),
        (low(rows, 8 * lane), vmem),
        (jax.ShapeDtypeStruct((rows, lane), F32), vmem),
        (low(rows, 4 * lane), vmem),
        (low(rows, quarter), vmem),
        (low(rows, SIDE), vmem),
        (low(width, 4 * lane), vmem),
        (low(4 * lane, width), vmem),
        (low(4 * lane, width), vmem),
        (low(SIDE, 8 * lane), vmem),
        (low(SIDE, width), vmem),
        (low(SIDE, width), vmem),
        (low(SIDE, units), vmem),
        (low(SIDE, units), vmem),
        (low(SIDE, units), vmem),
        (low(SIDE, width), vmem),
        (low(SIDE, 4 * lane), vmem),
        (low(SIDE, width), vmem),
    ]
    mirror_of = []
    for o in outs:
        mirror_of.append(sum(m >= 0 for m in mirror_of) if o[1] is vmem else -1)
    mirrored = sum(m >= 0 for m in mirror_of) + 1

    def kernel(*refs):
        len_ref, adapter_ref, tok_ref, cot_ref = refs[:4]
        loads_hbm = refs[4 : 4 + count]
        (
            sums_resid,
            normed_two,
            side_all,
            tok_own,
            cot_order,
            cot_peer,
            qkv_ref,
            lse_ref,
            att_ref,
            one_cut,
            inner_ref,
            wa_ref,
            wkv_ref,
            ow_ref,
            sa_ref,
            fa_ref,
            fgu_ref,
            sg_ref,
            su_ref,
            fd_ref,
            sd_ref,
            fo_ref,
            so_ref,
        ) = [
            refs[len(refs) - mirrored + k] if k >= 0 else out
            for k, out in zip(mirror_of, refs[4 + count : 27 + count])
        ]
        outs_hbm = refs[4 + count : 27 + count]
        mirrors = refs[len(refs) - mirrored : len(refs) - 1]
        flush_sem = refs[len(refs) - 1]
        refs = refs[27 + count :]
        flushed = []

        def flush(*places):
            for at in places:
                n = mirror_of[at]
                cp = pltpu.make_async_copy(mirrors[n], outs_hbm[at], flush_sem.at[n])
                cp.start()
                flushed.append(cp)

        gain_one, gain_two, wq_v, wk_v, wv_v, wo_v = refs[:6]
        in_first, out_first, down_first, q_second, kv_second, o_second, gu_second, d_second = refs[6:14]
        cos_ref, sin_ref = refs[14:16]
        (
            tok_all,
            one_ref,
            part,
            land,
            staged,
            landed,
            sums,
            side_own,
            load_sem,
            land_s,
            land_r,
            cot_s,
            cot_r,
            send_sem,
            recv_sem,
            s_sem,
            r_sem,
        ) = refs[16:33]
        side_sems = refs[33:36]
        place = _place()
        c, f, x, core, core_peer, x_peer = place
        hh = 1 - core
        slot = _slot_of(c)
        live = len_ref[slot]
        which = adapter_ref[slot]
        loads = []
        for i in range(count):
            cp = pltpu.make_async_copy(loads_hbm[i], refs[i], load_sem.at[i])
            cp.start()
            loads.append(cp)

        barrier = pltpu.get_barrier_semaphore()
        for j in range(2):
            pl.semaphore_signal(
                barrier, inc=1, device_id=(_block(x, core, j), slot // 2), device_id_type=MESH_ID
            )
        for target in (core_peer, x_peer):
            pl.semaphore_signal(barrier, inc=1, device_id=target, device_id_type=MESH_ID)
        for b in range(4):
            pl.semaphore_signal(
                barrier,
                inc=1,
                device_id=(4 * hh + b, 2 * x + (slot // 2) % 2),
                device_id_type=MESH_ID,
            )
        pl.semaphore_wait(barrier, 8)
        to_f = _owner(c)
        to_h = c // 4
        to_j = (c // 2) % 2
        to_i = c % 2
        moves = []
        for part_row in range(2):
            span = pl.ds(64 * part_row, 64)
            for half in range(2):
                s = 2 * f + half
                cp = _remote(
                    tok_ref.at[half, span],
                    tok_all.at[to_h, to_j, to_i, span],
                    land_s.at[2 * part_row + half],
                    land_r.at[2 * part_row + to_j],
                    (_group_of(s), to_f),
                )
                cp.start()
                moves.append(cp)
        cross = [
            _remote(cot_ref.at[half], cot_peer.at[half], cot_s.at[half], cot_r.at[half], x_peer)
            for half in range(2)
        ]
        cross[0].start()
        cot_moves = []
        for relay in range(2):
            for half in range(2):
                s = 2 * (2 * ((x + relay) % 2) + core) + half
                away = ((c // 2 + c) % 2 + x) % 2
                cot_moves.append(
                    _remote(
                        (cot_peer if relay else cot_ref).at[half],
                        cot_order.at[away * (1 + to_j), (1 - away) * to_j + away],
                        cot_s.at[2 + 2 * relay + half],
                        cot_r.at[2 + 2 * away + to_j],
                        (_group_of(s), 2 * x + 1 - to_h),
                    )
                )
        for cp in loads:
            cp.wait()

        def group_sends(part_row):
            span = pl.ds(64 * part_row, 64)
            for j in range(2):
                pltpu.make_async_copy(
                    tok_all.at[hh, j, (x + j) % 2, span],
                    tok_all.at[hh, j, (x + j) % 2, span],
                    land_r.at[2 * part_row + j],
                ).wait()
                k = 2 * part_row + j
                here = tok_all.at[hh, j, (x + j) % 2, span]
                for base, target in ((0, x_peer), (4, core_peer)):
                    cp = _remote(
                        here, here, send_sem.at[base + k], recv_sem.at[base + k], target
                    )
                    cp.start()
                    sends[base + k] = cp

        sends = {}

        def prepare_first():
            half = HEAD_DIM // 2
            wa_ref[...] = jnp.zeros_like(wa_ref)
            wkv_ref[...] = jnp.zeros_like(wkv_ref)
            sa_ref[...] = jnp.zeros_like(sa_ref)
            for head in range(4):
                for side in range(2):
                    at = head * HEAD_DIM + side * half
                    to = head * lane + side * HALF_PAD
                    wa_ref[:, to : to + half] = wq_v[:, at : at + half]
            for head in range(2):
                for side in range(2):
                    at = head * HEAD_DIM + side * half
                    to = head * lane + side * HALF_PAD
                    wkv_ref[to : to + half, :] = wk_v[at : at + half, :]
                at, to = head * HEAD_DIM, (2 + head) * lane
                wkv_ref[to : to + HEAD_DIM, :] = wv_v[at : at + HEAD_DIM, :]

        def prepare_second():
            half = HEAD_DIM // 2
            own_cols = pl.ds(pl.multiple_of(f * quarter, 128), quarter)
            own_units = pl.ds(pl.multiple_of(f * units, 128), units)
            low = lambda v: (ADAPTER_SCALE * v.astype(F32)).astype(BF16)
            for ref in (fa_ref, fgu_ref, sg_ref, su_ref, fd_ref, sd_ref, fo_ref, so_ref, ow_ref):
                ref[...] = jnp.zeros_like(ref)
            for i in range(3):
                fa_ref[i * RANK : (i + 1) * RANK, :] = in_first[which, i]
            for i in range(2):
                fgu_ref[i * RANK : (i + 1) * RANK, :] = in_first[which, 3 + i]
            all_gu = gu_second.at[:, :, :, own_units]
            sg_ref[:RANK, :] = low(all_gu[which, 0])
            su_ref[RANK : 2 * RANK, :] = low(all_gu[which, 1])
            fd_ref[3 * RANK : 4 * RANK, :] = down_first.at[:, :, own_units][which]
            sd_ref[3 * RANK : 4 * RANK, :] = low(d_second[which])
            so_ref[:RANK, :] = low(o_second[which])
            own_first = out_first.at[:, :, own_cols][which]
            own_q = low(q_second.at[:, :, own_cols][which])
            for head in range(4):
                at = head * HEAD_DIM
                fo_ref[:RANK, head * lane : head * lane + HEAD_DIM] = own_first[:, at : at + HEAD_DIM]
                ow_ref[head * lane : head * lane + HEAD_DIM, :] = wo_v[at : at + HEAD_DIM, :]
                for side in range(2):
                    to = head * lane + side * HALF_PAD
                    sa_ref[:RANK, to : to + half] = own_q[:, at + side * half : at + (side + 1) * half]
            window = pl.ds(pl.multiple_of((3 * f // 2) * 128, 128), 256)
            for i in range(2):
                own_kv = kv_second.at[:, :, :, window][which, i].astype(F32)
                shifted = pltpu.roll(own_kv, 256 - 64, 1)
                own_kv = low(jnp.where(f % 2 == 1, shifted, own_kv))
                for head in range(2):
                    at = head * HEAD_DIM
                    if i:
                        to = (6 + head) * lane
                        sa_ref[2 * RANK : 3 * RANK, to : to + HEAD_DIM] = own_kv[:, at : at + HEAD_DIM]
                    else:
                        for side in range(2):
                            to = (4 + head) * lane + side * HALF_PAD
                            sa_ref[RANK : 2 * RANK, to : to + half] = own_kv[
                                :, at + side * half : at + (side + 1) * half
                            ]

        prepare_first()
        group_sends(0)
        prepare_second()
        flush(*range(11, 23))
        group_sends(1)
        for cp in cot_moves[:2]:
            cp.start()
        cross[0].wait_recv()
        cot_moves[2].start()

        def cot_spot(away, j):
            return cot_order.at[(1 + j) if away else 0, 1 if away else j]

        def cot_share():
            for away in range(2):
                for j in range(2):
                    here = cot_spot(away, j)
                    pltpu.make_async_copy(here, here, cot_r.at[2 + 2 * away + j]).wait()
                    there = cot_order.at[1 + j, 0] if away else cot_order.at[3, j]
                    k = 6 + 2 * away + j
                    cp = _remote(here, there, cot_s.at[k], cot_r.at[k], core_peer)
                    cp.start()
                    shared.append(cp)

        shared = []

        def forward(j):
            for part_row in range(2):
                k = 2 * part_row + j
                span = pl.ds(64 * part_row, 64)
                sends[k].wait_recv()
                there = tok_all.at[hh, j, (x + j + 1) % 2, span]
                cp = _remote(there, there, send_sem.at[8 + k], recv_sem.at[8 + k], core_peer)
                cp.start()
                sends[8 + k] = cp
            for part_row in range(2):
                k = 2 * part_row + j
                sends[4 + k].wait_recv()
                sends[8 + k].wait_recv()

        def project_rows(t):
            row = pl.ds(t * block, block)
            v = tok_all[t // 2, t % 2].reshape(block, width).astype(F32)
            factor = lax.rsqrt(jnp.mean(v * v, axis=1, keepdims=True) + EPSILON)
            u = (v * factor * gain_one[...].reshape(1, width)).astype(BF16)
            one_ref[row, :] = u
            inner = dot_t(u, fa_ref[...]).astype(BF16)
            inner_ref[row, :] = inner
            cos, sin = cos_ref[row, :], sin_ref[row, :]
            for pair in range(4):
                cols = slice(pair * 2 * lane, (pair + 1) * 2 * lane)
                if pair < 2:
                    both = dot(u, wa_ref[:, cols])
                else:
                    both = dot_t(u, wkv_ref[2 * (pair - 2) * lane : 2 * (pair - 1) * lane, :])
                both = both + dot(inner, sa_ref[:, cols])
                for k in range(2):
                    p = both[:, k * lane : (k + 1) * lane]
                    if pair < 3:
                        p = p * cos + pltpu.roll(p, HALF_PAD, 1) * sin
                    qkv_ref[row, (2 * pair + k) * lane : (2 * pair + k + 1) * lane] = p.astype(BF16)

        def attention(t, hook):
            keys = (t + 1) * block
            row = pl.ds(t * block, block)
            qpos = t * block + lax.broadcasted_iota(jnp.int32, (block, keys), 0)
            kpos = lax.broadcasted_iota(jnp.int32, (block, keys), 1)
            allowed = (kpos <= qpos) & (kpos < live)
            stats = jnp.zeros((block, lane), F32)
            lanes = lax.broadcasted_iota(jnp.int32, (block, lane), 1)
            for head in range(4):
                q = qkv_ref[row, head * lane : (head + 1) * lane]
                kv = head // 2
                k = qkv_ref[:keys, (4 + kv) * lane : (5 + kv) * lane]
                v = qkv_ref[:keys, (6 + kv) * lane : (7 + kv) * lane]
                s = jnp.where(allowed, dot_t(q, k) * scale, NEGATIVE)
                top = jnp.max(s, axis=1, keepdims=True)
                p = jnp.where(allowed, jnp.exp(s - top), 0.0)
                total = jnp.sum(p, axis=1, keepdims=True)
                o = dot(p.astype(BF16), v) / total
                att_ref[row, head * lane : (head + 1) * lane] = o.astype(BF16)
                stats = jnp.where(lanes == head, top + jnp.log(total), stats)
                if head == 1 and hook is not None:
                    hook()
            lse_ref[row, :] = stats
            a = att_ref[row, :]
            for at in range(0, width, 256):
                value = dot(a, ow_ref[:, at : at + 256])
                part[t, :, :, at : at + 256] = value.astype(BF16).reshape(2, 128, 256)
            part[t, :, :, width:] = dot_t(a, fo_ref[...]).astype(BF16).reshape(2, 128, SIDE)

        def to_core(t):
            return _remote(part.at[t], land.at[t % 2], s_sem.at[t % 2], r_sem.at[t % 2], core_peer)

        def to_x(j):
            return _remote(staged.at[j], landed.at[j], s_sem.at[2 + j], r_sem.at[2 + j], x_peer)

        def leave(t):
            @pl.when(core == t // 2)
            def _():
                to_core(t).start()

        def combine(t):
            j = t % 2

            @pl.when(core == 1 - t // 2)
            def _():
                to_core(t).wait_recv()
                mine, other = (x + j) % 2, (x + j + 1) % 2
                staged[j] = (part[t, other].astype(F32) + land[j, other].astype(F32)).astype(BF16)
                to_x(j).start()
                sums[j] = part[t, mine].astype(F32) + land[j, mine].astype(F32)

        forward(0)
        cross[1].start()
        project_rows(0)
        project_rows(2)
        attention(0, None)
        leave(0)
        forward(1)
        project_rows(1)
        project_rows(3)
        cross[1].wait_recv()
        cot_moves[3].start()
        attention(1, lambda: combine(0))
        leave(1)
        attention(2, lambda: combine(1))
        leave(2)
        attention(3, lambda: combine(2))
        leave(3)
        combine(3)
        cot_share()
        for t in range(4):

            @pl.when(core == t // 2)
            def _():
                to_core(t).wait_send()

        for j in range(2):
            tok_own[j] = tok_all[hh, j, (x + j) % 2]
        one_cut[...] = one_ref[:, pl.ds(pl.multiple_of(f * quarter, 128), quarter)]
        for j in range(2):
            cp = to_x(j)
            cp.wait_recv()
            sums[j] = sums[j] + landed[j].astype(F32)
            cp.wait_send()
            side_own[j] = sums[j, :, width:].astype(BF16)
        side_first, side_last = _gather_steps([side_own], [side_all], *side_sems, place)
        side_first()
        flush(3, 6, 7, 8, 9, 10)
        for j in range(2):
            v = (
                tok_own[j].astype(F32)
                + sums[j, :, :width]
                + dot(side_own[j], so_ref[...])
            )
            sums_resid[j] = v
            factor = lax.rsqrt(jnp.mean(v * v, axis=1, keepdims=True) + EPSILON)
            normed_two[j] = (v * factor * gain_two[...].reshape(1, width)).astype(BF16)
        flush(0, 1)
        for cp in shared:
            cp.wait_recv()
        side_last()
        for cp in flushed:
            cp.wait()
        for cp in moves + cross + cot_moves + shared + list(sends.values()):
            cp.wait_send()

    own = (2, 128, wide)
    return pl.pallas_call(
        kernel,
        out_shape=[o[0] for o in outs],
        in_specs=[smem, smem] + [hbm] * (2 + count),
        out_specs=[hbm for o in outs],
        scratch_shapes=[pltpu.VMEM(a.shape, a.dtype) for a in loads_in]
        + [
            pltpu.VMEM((2, 2, 2, 128, width), BF16),
            pltpu.VMEM((rows, width), BF16),
            pltpu.VMEM((4,) + own, BF16),
            pltpu.VMEM((2,) + own, BF16),
            pltpu.VMEM(own, BF16),
            pltpu.VMEM(own, BF16),
            pltpu.VMEM(own, F32),
            pltpu.VMEM((2, 128, SIDE), BF16),
            _sem(count),
            _sem(4),
            _sem(4),
            _sem(10),
            _sem(10),
            _sem(12),
            _sem(12),
            _sem(4),
            _sem(4),
        ]
        + [_sem(2), _sem(6), _sem(6)]
        + [pltpu.VMEM(o[0].shape, o[0].dtype) for o in outs if o[1] is vmem]
        + [_sem(mirrored - 1)],
        compiler_params=pltpu.CompilerParams(
            collective_id=cid, has_side_effects=True, vmem_limit_bytes=58 * 1024 * 1024
        ),
        name="front",
    )(lengths, adapters, tokens, cotangent, *loads_in)


def attend_back_call(
    low_own,
    small_own,
    early,
    out_far,
    length,
    own_arrays,
    arrays,
    cid,
):
    qkv = arrays[0]
    width = low_own.shape[-1]
    rows = qkv.shape[0]
    wide = width + SIDE
    step_rows = 256
    scale = HEAD_DIM ** (-0.5)
    lane = PAD_HEAD
    quarter = width // 4
    middle_n = 4 * quarter
    early_n = early.shape[1]
    big = tuple(arrays) + tuple(own_arrays)
    late_n = 4 * quarter
    factor_n = 2 * quarter
    count = len(big)

    def kernel(*refs):
        len_ref, low_ref, small_ref, early_ref, out_ref = refs[:5]
        big_in = refs[5 : 5 + count]
        (
            out_back,
            grad_back,
            early_out,
            middle_out,
            late_out,
            factor_out,
        ) = refs[5 + count : 11 + count]
        refs = refs[11 + count :]
        (
            qkv_ref,
            lse_ref,
            att_ref,
            inner_ref,
            order_ref,
            cos_ref,
            sin_ref,
            ow_ref,
            fo_ref,
            so_ref,
            wa_ref,
            wkv_ref,
            sa_ref,
            fa_ref,
            sd_ref,
            cut_ref,
            inner_qkv_ref,
            cot_ref,
            out_own,
            resid_ref,
            tok_ref,
            grad_resid_ref,
            gain_ref,
        ) = refs[:count]
        (
            low,
            do_ref,
            gio_ref,
            dk_ref,
            dv_ref,
            part,
            land,
            staged,
            landed,
            side_own,
            middle_ref,
            sums,
            side_all,
            grad_ref,
            landed_out,
            small_out,
            late_ref,
            factor_ref,
            out_tok,
            grad_tok,
            early_lines,
            middle_lines,
            load_sem,
            own_sem,
            send_sem,
            recv_sem,
            s_sem,
            r_sem,
        ) = refs[count : count + 28]
        sems = refs[count + 28 :]
        place = _place()
        c, f, x, core, core_peer, x_peer = place
        loads = [
            pltpu.make_async_copy(big_in[i], refs[i], load_sem.at[i]) for i in range(count)
        ]
        for cp in loads:
            cp.start()
        _greet(
            _back_sources(place) + [core_peer, x_peer, _y_peer(place)] + _z_peers(place)
        )
        small_first, small_forward, small_own_here, small_core, small_far, small_last = _order_steps(
            small_ref, small_out, *sems[0:3], place
        )
        early_start, early_across, early_finish = _ctx_first(early_ref, early_lines, *sems[3:6], place)
        early_two = _ctx_second(early_lines, early_out, *sems[6:9], place)
        mid_start, mid_across, mid_finish = _ctx_first(middle_ref, middle_lines, *sems[9:12], place)
        mid_two = _ctx_second(middle_lines, middle_out, *sems[12:15], place)
        late = _ctx_planes(late_ref, late_out, *sems[15:18], place)
        factor = _ctx_planes(factor_ref, factor_out, *sems[25:28], place)
        side_first, side_last = _gather_steps([side_own], [side_all], *sems[18:21], place)
        out_first, out_last = _back_steps(out_tok, out_back, *sems[21:23], place)
        grad_first, grad_last = _back_steps(grad_tok, grad_back, *sems[23:25], place)
        live = len_ref[_slot_of(c)]

        sends = {}
        hh = 1 - core
        local = []
        for j in (1, 0):
            for k, target in ((0, x_peer), (2, core_peer)):
                cp = _remote(
                    low_ref.at[j],
                    low.at[hh, j, (x + j) % 2],
                    send_sem.at[k + j],
                    recv_sem.at[k + j],
                    target,
                )
                cp.start()
                sends[(k, j)] = cp
            if j:
                early_start()
                small_first()
        for j in range(2):
            lc = pltpu.make_async_copy(low_ref.at[j], low.at[hh, j, (x + j) % 2], own_sem.at[j])
            lc.start()
            local.append(lc)
        swaps = [
            _remote(out_ref.at[j], landed_out.at[j], s_sem.at[8 + j], r_sem.at[8 + j], x_peer)
            for j in range(2)
        ]
        dk_ref[...] = jnp.zeros_like(dk_ref)
        dv_ref[...] = jnp.zeros_like(dv_ref)
        for cp in loads:
            cp.wait()
        for lc in local:
            lc.wait()

        def arrive(j):
            sends[(0, j)].wait_recv()
            cp = _remote(
                low.at[hh, j, (x + j + 1) % 2],
                low.at[hh, j, (x + j + 1) % 2],
                send_sem.at[4 + j],
                recv_sem.at[4 + j],
                core_peer,
            )
            cp.start()
            sends[(4, j)] = cp
            sends[(2, j)].wait_recv()
            cp.wait_recv()

        def through_output(t):
            g = low[t // 2, t % 2].reshape(step_rows, width)
            gio = dot_t(g, so_ref[...]).astype(BF16)
            row = pl.ds(t * step_rows, step_rows)
            gio_ref[row, :] = gio
            do_ref[row, :] = (dot_t(g, ow_ref[...]) + dot(gio, fo_ref[...])).astype(BF16)

        def attention(t, hook):
            keys = (t + 1) * step_rows
            row = pl.ds(t * step_rows, step_rows)
            qpos = t * step_rows + lax.broadcasted_iota(jnp.int32, (step_rows, keys), 0)
            kpos = lax.broadcasted_iota(jnp.int32, (step_rows, keys), 1)
            allowed = (kpos <= qpos) & (kpos < live)
            cos, sin = cos_ref[row, :], sin_ref[row, :]
            for head in range(4):
                kv = head // 2
                at = slice(head * lane, (head + 1) * lane)
                q = qkv_ref[row, at]
                k = qkv_ref[:keys, (4 + kv) * lane : (5 + kv) * lane]
                v = qkv_ref[:keys, (6 + kv) * lane : (7 + kv) * lane]
                do = do_ref[row, at]
                s = dot_t(q, k)
                p = jnp.where(allowed, jnp.exp(s * scale - lse_ref[row, head : head + 1]), 0.0)
                dp = dot_t(do, v)
                total = jnp.sum(p * dp, axis=1, keepdims=True)
                ds = (p * (dp - total)).astype(BF16)
                dq = scale * dot(ds, k)
                dq = dq * cos - pltpu.roll(dq, HALF_PAD, 1) * sin
                grad_ref[row, at] = dq.astype(BF16)
                dk_ref[kv, :keys] += dot_rows(ds, q)
                dv_ref[kv, :keys] += dot_rows(p.astype(BF16), do)
                if head == 1 and hook is not None:
                    hook()
            for kv in range(2):
                dk = scale * dk_ref[kv, row, :]
                dk = dk * cos - pltpu.roll(dk, HALF_PAD, 1) * sin
                grad_ref[row, (4 + kv) * lane : (5 + kv) * lane] = dk.astype(BF16)
                grad_ref[row, (6 + kv) * lane : (7 + kv) * lane] = dv_ref[kv, row, :].astype(BF16)
            g = grad_ref[row, :]
            for at in range(0, width, 256):
                value = dot_t(g[:, : 4 * lane], wa_ref[at : at + 256, :])
                value = value + dot(g[:, 4 * lane :], wkv_ref[:, at : at + 256])
                part[t, :, :, at : at + 256] = value.astype(BF16).reshape(2, 128, 256)
            part[t, :, :, width:] = dot_t(g, sa_ref[...]).astype(BF16).reshape(2, 128, SIDE)

        def to_core(t):
            j = t % 2
            return _remote(part.at[t], land.at[j], s_sem.at[j], r_sem.at[j], core_peer)

        def to_x(j, narrow):
            cols = pl.ds(width, SIDE) if narrow else pl.ds(0, width)
            n = 2 + 2 * narrow + j
            return _remote(
                staged.at[j, :, cols], landed.at[j, :, cols], s_sem.at[n], r_sem.at[n], x_peer
            )

        def leave(t):
            @pl.when(core == t // 2)
            def _():
                to_core(t).start()

        def combine(t):
            j = t % 2

            @pl.when(core == 1 - t // 2)
            def _():
                to_core(t).wait_recv()
                mine, other = (x + j) % 2, (x + j + 1) % 2
                for cols, narrow in ((slice(width, wide), 1), (slice(0, width), 0)):
                    staged[j, :, cols] = (
                        part[t, other, :, cols].astype(F32) + land[j, other, :, cols].astype(F32)
                    ).astype(BF16)
                    to_x(j, narrow).start()
                sums[j] = part[t, mine].astype(F32) + land[j, mine].astype(F32)

        arrive(1)
        early_across()
        through_output(3)
        through_output(1)
        small_own_here()
        for j in range(2):
            small_forward(j)
        def second():
            arrive(0)
            for cp in swaps:
                cp.start()

        attention(3, second)
        leave(3)
        through_output(2)
        through_output(0)
        o_a = dot_rows(gio_ref[...], att_ref[...])[:RANK]
        o_a = jnp.concatenate(
            [o_a[:, head * lane : head * lane + HEAD_DIM] for head in range(4)], axis=1
        )
        middle_ref[:, :quarter] = o_a.astype(BF16)
        own_cols = pl.ds(pl.multiple_of(f * quarter, 128), quarter)
        g = low[:, :, :, :, own_cols].reshape(rows, quarter)
        middle_ref[:, quarter : 2 * quarter] = (ADAPTER_SCALE * dot_rows(inner_ref[...], g)[:RANK]).astype(BF16)
        for j in range(2):
            small_far(j)
        small_core()
        in_gu = jnp.zeros((SIDE, quarter), F32)
        for k in range(4):
            u = order_ref[k, :, :, own_cols].reshape(step_rows, quarter)
            in_gu += dot_rows(small_out[k].reshape(step_rows, SIDE), u)
        middle_ref[:, 2 * quarter : 3 * quarter] = in_gu[:RANK].astype(BF16)
        middle_ref[:, 3 * quarter :] = in_gu[RANK : 2 * RANK].astype(BF16)
        mid_start()
        early_finish()
        early_two[0]()

        def outputs():
            for j in range(2):
                swaps[j].wait()
                total = out_own[j] + landed_out[j].astype(F32)
                side = total[:, width:]
                out_own[j, :, width:] = side
                pos = 128 * _block(x, core, j) + lax.broadcasted_iota(jnp.int32, (128, width), 0)
                value = resid_ref[j] + total[:, :width] + dot(side.astype(BF16), sd_ref[...])
                out_tok[j] = jnp.where(pos < live, value, 0.0).astype(BF16)
                out_first(j)

        def third():
            combine(3)
            mid_across()

        attention(2, third)
        leave(2)
        outputs()
        attention(1, lambda: combine(2))
        leave(1)
        attention(0, lambda: combine(1))
        leave(0)
        mid_finish()
        mid_two[0]()
        early_two[1]()
        combine(0)
        def token_rows():
            for j in range(2):
                to_x(j, 0).wait_recv()
                gi = sums[j, :, width:].astype(BF16)
                total = sums[j, :, :width] + landed[j, :, :width].astype(F32)
                gn = (total + dot(gi, fa_ref[...])).astype(BF16).astype(F32)
                v = tok_ref[j].astype(F32)
                rms = lax.rsqrt(jnp.mean(v * v, axis=1, keepdims=True) + EPSILON)
                scaled = gn * gain_ref[...].reshape(1, width)
                mean = jnp.mean(scaled * v, axis=1, keepdims=True)
                grad = grad_resid_ref[j] + rms * scaled - v * (rms * rms * rms) * mean
                grad_tok[j] = grad.astype(BF16)
                grad_first(j)

        for j in range(2):
            to_x(j, 1).wait_recv()
            sums[j, :, width:] = sums[j, :, width:] + landed[j, :, width:].astype(F32)
            side_own[j] = (sums[j, :, width:] + out_own[j, :, width:]).astype(BF16)
        side_first()

        all_b = ADAPTER_SCALE * dot_rows(inner_qkv_ref[...], grad_ref[...])
        half = HEAD_DIM // 2
        pieces = []
        for head in range(6):
            r = slice(0, RANK) if head < 4 else slice(RANK, 2 * RANK)
            for side in range(2):
                to = head * lane + side * HALF_PAD
                pieces.append(all_b[r, to : to + half])
        for head in range(2):
            to = (6 + head) * lane
            pieces.append(all_b[2 * RANK : 3 * RANK, to : to + HEAD_DIM])
        factor_ref[...] = jnp.concatenate(pieces, axis=1).astype(BF16)
        factor[0]()
        mid_two[1]()
        side_last()
        in_qkv = dot_rows(side_all[...].reshape(rows, SIDE), cut_ref[...])
        for i in range(3):
            late_ref[:, i * quarter : (i + 1) * quarter] = in_qkv[i * RANK : (i + 1) * RANK].astype(
                BF16
            )
        d_b = jnp.zeros((SIDE, quarter), F32)
        for step in range(4):
            other_x = x if step in (0, 3) else 1 - x
            for i in range(2):
                other_core = (core, 1 - core)[step == 3 or (step in (1, 2) and i == 0)]
                jj = i if step in (0, 3) else step - 1
                pos = 128 * _block(other_x, other_core, jj) + lax.broadcasted_iota(
                    jnp.int32, (128, quarter), 0
                )
                go = cot_ref[step, i, :, own_cols].astype(F32)
                go = jnp.where(pos < live, go, 0.0).astype(BF16)
                d_b += dot_rows(side_all[1 - other_core, jj, (other_x + jj) % 2], go)
        late_ref[:, 3 * quarter :] = (ADAPTER_SCALE * d_b[3 * RANK : 4 * RANK]).astype(BF16)
        late[0]()
        factor[1]()

        token_rows()
        late[1]()
        for t in range(4):

            @pl.when(core == t // 2)
            def _():
                to_core(t).wait_send()

        for j in range(2):
            to_x(j, 0).wait_send()
            to_x(j, 1).wait_send()
        small_last()
        early_two[2]()
        mid_two[2]()
        factor[2]()
        late[2]()
        out_last()
        grad_last()
        for cp in sends.values():
            cp.wait_send()

    vmem, hbm = pl.BlockSpec(memory_space=pltpu.VMEM), pl.BlockSpec(memory_space=pl.ANY)
    shape = jax.ShapeDtypeStruct
    own = (2, 128, wide)
    return pl.pallas_call(
        kernel,
        out_shape=[
            shape((2, 128, width), BF16),
            shape((2, 128, width), BF16),
            _spread_of(early_n),
            _spread_of(middle_n),
            _spread_of(late_n),
            _spread_of(factor_n),
        ],
        in_specs=[pl.BlockSpec(memory_space=pltpu.SMEM)] + [hbm] * (4 + count),
        out_specs=[hbm] * 6,
        scratch_shapes=[pltpu.VMEM(a.shape, a.dtype) for a in big]
        + [
            pltpu.VMEM((2, 2, 2, 128, width), BF16),
            pltpu.VMEM((rows, 4 * lane), BF16),
            pltpu.VMEM((rows, SIDE), BF16),
            pltpu.VMEM((2, rows, lane), F32),
            pltpu.VMEM((2, rows, lane), F32),
            pltpu.VMEM((4,) + own, BF16),
            pltpu.VMEM((2,) + own, BF16),
            pltpu.VMEM(own, BF16),
            pltpu.VMEM(own, BF16),
            pltpu.VMEM((2, 128, SIDE), BF16),
            pltpu.VMEM((RANK, middle_n), BF16),
            pltpu.VMEM(own, F32),
            pltpu.VMEM((2, 2, 2, 128, SIDE), BF16),
            pltpu.VMEM((rows, 8 * lane), BF16),
            pltpu.VMEM(own, BF16),
            pltpu.VMEM((4, 2, 128, SIDE), BF16),
            pltpu.VMEM((RANK, late_n), BF16),
            pltpu.VMEM((RANK, factor_n), BF16),
            pltpu.VMEM((2, 128, width), BF16),
            pltpu.VMEM((2, 128, width), BF16),
            pltpu.VMEM(_lines_of(early_n), BF16),
            pltpu.VMEM(_lines_of(middle_n), BF16),
            _sem(count),
            _sem(2),
            _sem(6),
            _sem(6),
            _sem(10),
            _sem(10),
        ]
        + [_sem(2), _sem(6), _sem(6)]
        + FIRST_SEMS
        + SECOND_SEMS
        + FIRST_SEMS
        + SECOND_SEMS
        + PLANE_SEMS
        + [_sem(2), _sem(6), _sem(6)]
        + [_sem(2), _sem(2), _sem(2), _sem(2)]
        + PLANE_SEMS,
        compiler_params=pltpu.CompilerParams(
            collective_id=cid, has_side_effects=True, vmem_limit_bytes=62 * 1024 * 1024
        ),
        name="attend_back",
    )(length, low_own, small_own, early, out_far, *big)


def table_call(pieces, out_rows, grad_rows, adapters):
    f32 = lambda *shape: jax.ShapeDtypeStruct(shape, F32)
    choices = 8
    outs = [
        f32(choices, 5, RANK, 1536),
        f32(choices, RANK, 1536),
        f32(choices, RANK, 4096),
        f32(choices, RANK, 1536),
        f32(choices, 2, RANK, 768),
        f32(choices, RANK, 1536),
        f32(choices, 2, RANK, 4096),
        f32(choices, RANK, 1536),
    ]
    plan = (
        ((6, 0, 1024), (6, 1, 1024), (2, None, 1024)),
        ((1, None, 384), (5, None, 384), (0, 3, 384), (0, 4, 384)),
        (
            (0, 0, 384),
            (0, 1, 384),
            (0, 2, 384),
            (7, None, 384),
        ),
        ((3, None, 384), (4, 0, 192), (4, 1, 192)),
    )

    def kernel(which, early_in, middle_in, late_in, factor_in, rows_in, grad_in, *refs):
        outs, rows_out, grad_out = refs[:8], refs[8], refs[9]
        acc, held = refs[10:18], refs[18:22]
        grad_low, grad_full, rows_held, sems, load_sem = refs[22:27]
        loads = []
        for i, src in enumerate((early_in, middle_in, factor_in, late_in)):
            loads.append(pltpu.make_async_copy(src, held[(0, 1, 3, 2)[i]], load_sem.at[i]))
        grad_load = pltpu.make_async_copy(grad_in, grad_low, load_sem.at[4])
        rows_load = pltpu.make_async_copy(rows_in, rows_held, load_sem.at[5])
        for cp in loads + [grad_load, rows_load]:
            cp.start()

        def add(piece, ref):
            def one_slot(origin, carry):
                row = which[origin % 4 + 4 * ((origin // 4 + origin) % 2)]
                for f in range(4):
                    at = 0
                    for out, table, n in plan[piece]:
                        value = ref[origin // 4, f % 2, origin % 4, f // 2, :, at : at + n].astype(F32)
                        cols = slice(f * n, (f + 1) * n)
                        if table is None:
                            acc[out][row, :, cols] += value
                        else:
                            acc[out][row, table, :, cols] += value
                        at += n
                return carry

            lax.fori_loop(0, 8, one_slot, 0)

        def send(out):
            cp = pltpu.make_async_copy(acc[out], outs[out], sems.at[out])
            cp.start()
            return cp

        def clear(*which_out):
            for out in which_out:
                acc[out][...] = jnp.zeros_like(acc[out])

        clear(2, 6)
        loads[0].wait()
        add(0, held[0])
        copies = [send(out) for out in (2, 6)]
        clear(0, 1, 5)
        loads[1].wait()
        add(1, held[1])
        copies += [send(out) for out in (1, 5)]
        clear(3, 4, 7)
        loads[2].wait()
        add(3, held[3])
        copies += [send(out) for out in (3, 4)]
        loads[3].wait()
        add(2, held[2])
        copies += [send(out) for out in (0, 7)]
        grad_load.wait()
        grad_full[...] = grad_low[...].astype(F32)
        last = pltpu.make_async_copy(grad_full, grad_out, load_sem.at[6])
        last.start()
        rows_load.wait()
        rows_copy = pltpu.make_async_copy(rows_held, rows_out, load_sem.at[7])
        rows_copy.start()
        copies += [last, rows_copy]
        for cp in copies:
            cp.wait()

    hbm = pl.BlockSpec(memory_space=pl.ANY)
    return pl.pallas_call(
        kernel,
        out_shape=outs + [jax.ShapeDtypeStruct(out_rows.shape, BF16), f32(*grad_rows.shape)],
        in_specs=[pl.BlockSpec(memory_space=pltpu.SMEM)] + [hbm] * 6,
        out_specs=[hbm] * 10,
        scratch_shapes=[pltpu.VMEM(o.shape, F32) for o in outs]
        + [pltpu.VMEM(p.shape, BF16) for p in pieces]
        + [pltpu.VMEM(grad_rows.shape, BF16), pltpu.VMEM(grad_rows.shape, F32)]
        + [pltpu.VMEM(out_rows.shape, BF16), _sem(8), _sem(8)],
        compiler_params=pltpu.CompilerParams(vmem_limit_bytes=62 * 1024 * 1024),
        name="tables",
    )(adapters, *pieces, out_rows, grad_rows)


def rope_constants(rows):
    half = HEAD_DIM // 2
    freqs = np.float32(ROPE_BASE) ** (-(np.arange(half, dtype=np.float32) * 2.0 / HEAD_DIM))
    angles = np.arange(rows).astype(np.float32)[:, None] * freqs.astype(np.float32)[None, :]
    cos = np.cos(angles.astype(np.float64)).astype(np.float32)
    sin = np.sin(angles.astype(np.float64)).astype(np.float32)
    gap = np.zeros((rows, HALF_PAD - half), np.float32)
    cosine = np.concatenate([cos, gap, cos, gap], axis=1)
    sine = np.concatenate([-sin, gap, sin, gap], axis=1)
    return jnp.asarray(cosine), jnp.asarray(sine)


def dot(left, right):
    return jnp.dot(left, right, preferred_element_type=F32)


def dot_t(left, right):
    return lax.dot_general(left, right, (((1,), (1,)), ((), ())), preferred_element_type=F32)


def dot_rows(left, right):
    return lax.dot_general(left, right, (((0,), (0,)), ((), ())), preferred_element_type=F32)


def side_pad(value, before=0):
    return jnp.pad(value, ((0, 0), (before, SIDE - before - value.shape[1])))


def blocks(value):
    return value.reshape(2, 2, 2, 128, value.shape[-1])


def own_blocks(value):
    return value.reshape(2, 128, value.shape[-1])


def flat(value):
    return value.reshape(-1, value.shape[-1])


def slot_local(
    tokens,
    cotangent,
    lengths,
    slot_adapter_index,
    attention_norm_gain,
    feedforward_norm_gain,
    query_weight,
    key_weight,
    value_weight,
    output_weight,
    gate_weight,
    up_weight,
    down_weight,
    adapter_input_first,
    adapter_output_first,
    adapter_down_first,
    adapter_query_second,
    adapter_key_value_second,
    adapter_output_second,
    adapter_gate_up_second,
    adapter_down_second,
):
    rows = 4 * 2 * tokens.shape[1]
    cosine, sine = rope_constants(rows)
    turned = lambda t: jnp.swapaxes(t, -1, -2)
    (
        resid,
        normed_two_own,
        inner_o,
        tok_own,
        cot_order,
        _,
        qkv,
        stats,
        attn_b,
        one_cut,
        inner_qkv,
        weight_q,
        weight_kv,
        out_w,
        second_all,
        first_all,
        first_gu,
        second_g,
        second_u,
        first_d,
        second_d,
        first_o,
        second_o,
    ) = front_call(
        tokens,
        cotangent,
        lengths,
        slot_adapter_index,
        (attention_norm_gain, feedforward_norm_gain),
        query_weight,
        turned(key_weight),
        turned(value_weight),
        output_weight,
        (
            turned(adapter_input_first),
            turned(adapter_output_first),
            turned(adapter_down_first),
            adapter_query_second,
            adapter_key_value_second,
            adapter_output_second,
            adapter_gate_up_second,
            adapter_down_second,
        ),
        cosine,
        sine,
        0,
    )
    grad_resid, grad_low_own, small, out_sums, out_far, order, early = feed_forward(
        normed_two_own,
        cot_order,
        resid,
        feedforward_norm_gain,
        lengths,
        (gate_weight, up_weight, down_weight),
        (first_gu, second_g, second_u, first_d, second_d),
        3,
    )
    out_rows, grad_rows, early, middle, late, factors = attend_back_call(
        grad_low_own,
        small,
        early,
        out_far,
        lengths,
        (out_sums, resid, tok_own, grad_resid, attention_norm_gain),
        (
            qkv,
            stats,
            attn_b,
            flat(inner_o),
            order,
            cosine,
            sine,
            out_w,
            first_o,
            second_o,
            weight_q,
            weight_kv,
            second_all,
            first_all,
            second_d,
            one_cut,
            inner_qkv,
            cot_order,
        ),
        10,
    )
    full = table_call((early, middle, late, factors), out_rows, grad_rows, slot_adapter_index)
    turn = lambda t: jnp.swapaxes(t, -1, -2)
    return (
        full[8],
        full[9],
        turn(full[0]),
        turn(full[1]),
        turn(full[2]),
        full[3],
        full[4],
        full[5],
        full[6],
        full[7],
    )


def solution(mesh):
    one_slot = mesh.shape["ctx"] == 8 and mesh.shape["fsdp"] == 4
    return jax.shard_map(
        slot_local if one_slot else local,
        mesh=mesh,
        in_specs=(
            P("fsdp", "ctx", None),
            P("fsdp", "ctx", None),
            P(),
            P(),
            P(),
            P(),
            P(None, "fsdp"),
            P(None, "fsdp"),
            P(None, "fsdp"),
            P("fsdp", None),
            P(None, "fsdp"),
            P(None, "fsdp"),
            P("fsdp", None),
            P(),
            P(),
            P(),
            P(),
            P(),
            P(),
            P(),
            P(),
        ),
        out_specs=(
            P("fsdp", "ctx", None),
            P("fsdp", "ctx", None),
            P(),
            P(),
            P(),
            P(),
            P(),
            P(),
            P(),
            P(),
        ),
        check_vma=False,
    )
```
